32 devices in a mesh: wide: 8 (over z, x), grp: 4 (over y, core).
Axes of the slice: x: 2, y: 2, z: 4, core: 2. Of those that a mesh axis runs over, the one named last changes fastest.
Arguments:
- images: bfloat16 [64, 196, 768], P(('wide', 'grp')), may hold values from -6 to 6
- slot_mask: int32 [64], P(('wide', 'grp')), may hold values from 0 to 1
- labels: int32 [64], P(('wide', 'grp')), may hold values from 0 to 999
- patch_weight: float32 [768, 768], P(('wide', 'grp')), may hold values from -0.21875 to 0.21875
- patch_moment: float32 [768, 768], P(('wide', 'grp')), may hold values from -1.335144e-05 to 1.335144e-05
- patch_square: float32 [768, 768], P(('wide', 'grp')), may hold values from 2.1972157e-11 to 8.788863e-11
- triple_weight: float32 [3, 768, 2304], P(None, ('wide', 'grp')), may hold values from -0.21875 to 0.21875
- triple_moment: float32 [3, 768, 2304], P(None, ('wide', 'grp')), may hold values from -1.335144e-05 to 1.335144e-05
- triple_square: float32 [3, 768, 2304], P(None, ('wide', 'grp')), may hold values from 2.1972157e-11 to 8.788863e-11
- output_weight: float32 [3, 768, 768], P(None, ('wide', 'grp')), may hold values from -1.75 to 1.75
- output_moment: float32 [3, 768, 768], P(None, ('wide', 'grp')), may hold values from -1.335144e-05 to 1.335144e-05
- output_square: float32 [3, 768, 768], P(None, ('wide', 'grp')), may hold values from 2.1972157e-11 to 8.788863e-11
- expand_weight: float32 [3, 768, 3072], P(None, ('wide', 'grp')), may hold values from -0.21875 to 0.21875
- expand_moment: float32 [3, 768, 3072], P(None, ('wide', 'grp')), may hold values from -1.335144e-05 to 1.335144e-05
- expand_square: float32 [3, 768, 3072], P(None, ('wide', 'grp')), may hold values from 2.1972157e-11 to 8.788863e-11
- shrink_weight: float32 [3, 3072, 768], P(None, ('wide', 'grp')), may hold values from -0.109375 to 0.109375
- shrink_moment: float32 [3, 3072, 768], P(None, ('wide', 'grp')), may hold values from -1.335144e-05 to 1.335144e-05
- shrink_square: float32 [3, 3072, 768], P(None, ('wide', 'grp')), may hold values from 2.1972157e-11 to 8.788863e-11
- vector_weight: float32 [213, 768], replicated, may hold values from -0.9 to 2.5
- vector_moment: float32 [213, 768], replicated, may hold values from -6.1035156e-05 to 6.1035156e-05
- vector_square: float32 [213, 768], replicated, may hold values from 5.4930394e-10 to 2.1972157e-09
- head_weight: float32 [769, 1000], replicated, may hold values from -0.21875 to 0.21875
- head_moment: float32 [769, 1000], replicated, may hold values from -6.1035156e-05 to 6.1035156e-05
- head_square: float32 [769, 1000], replicated, may hold values from 5.4930394e-10 to 2.1972157e-09
Outputs:
- loss_sum: float32 [], replicated
- image_total: float32 [], replicated
- grad_norm: float32 [], replicated
- patch_master: float32 [768, 768], P(('wide', 'grp'))
- patch_first: float32 [768, 768], P(('wide', 'grp'))
- patch_second: float32 [768, 768], P(('wide', 'grp'))
- triple_master: float32 [3, 768, 2304], P(None, ('wide', 'grp'))
- triple_first: float32 [3, 768, 2304], P(None, ('wide', 'grp'))
- triple_second: float32 [3, 768, 2304], P(None, ('wide', 'grp'))
- output_master: float32 [3, 768, 768], P(None, ('wide', 'grp'))
- output_first: float32 [3, 768, 768], P(None, ('wide', 'grp'))
- output_second: float32 [3, 768, 768], P(None, ('wide', 'grp'))
- expand_master: float32 [3, 768, 3072], P(None, ('wide', 'grp'))
- expand_first: float32 [3, 768, 3072], P(None, ('wide', 'grp'))
- expand_second: float32 [3, 768, 3072], P(None, ('wide', 'grp'))
- shrink_master: float32 [3, 3072, 768], P(None, ('wide', 'grp'))
- shrink_first: float32 [3, 3072, 768], P(None, ('wide', 'grp'))
- shrink_second: float32 [3, 3072, 768], P(None, ('wide', 'grp'))
- vector_master: float32 [213, 768], replicated
- vector_first: float32 [213, 768], replicated
- vector_second: float32 [213, 768], replicated
- head_master: float32 [769, 1000], replicated
- head_first: float32 [769, 1000], replicated
- head_second: float32 [769, 1000], replicated
- head_bias_grad: float32 [1000], replicated
The draws below stay inside these ranges and needn't reach their ends.
All inputs are finite; a program needn't handle non-finite values.
Results may differ from the reference program's by a relative error of at most 0.023.
Values may be sent and summed in bfloat16 or wider, within the bound.
A program may use at most 448 MiB of HBM per device.

```python
import math
import jax
import jax.numpy as jnp
from jax import lax

D = 768
HEADS = 12
HEAD_DIM = 64
FF = 3072
PATCHES = 196
PATCH_IN = 768
CLASSES = 1000
LAYERS = 3
STEP_INDEX = 10
IMG_DEV = 2
S = 197
VECTORS = 213
IMAGES = 64
SLOTS_WIDE = 8
PARAMS = 22756072


def draw_slot_mask(key, part):
    key = jax.random.fold_in(key, 7)
    wide_count = IMAGES // SLOTS_WIDE
    group_count = SLOTS_WIDE // IMG_DEV
    wide_span = max(wide_count - 1, 1)
    group_span = max(group_count - 1, 1)
    slot_ids = jnp.arange(IMAGES, dtype=jnp.int32)
    wide_at = slot_ids // SLOTS_WIDE
    group_at = slot_ids % SLOTS_WIDE // IMG_DEV
    chance = (wide_span + 2 * wide_at) * (group_span + 2 * group_at)
    coins = jax.random.randint(key, (IMAGES,), 0, 9 * wide_span * group_span)
    return (coins < chance).astype(jnp.int32)


def draw_vector_weight(key, part):
    key = jax.random.fold_in(key, 11)
    noise_key, factor_key = jax.random.split(key)
    noise = jax.random.truncated_normal(noise_key, -3.0, 3.0, (VECTORS, D))
    ramp = 0.6 + 1.2 * jnp.arange(D, dtype=jnp.float32) / (D - 1)
    factor = jax.random.uniform(factor_key, (VECTORS, D), minval=0.8, maxval=1.25)
    row_ids = jnp.arange(VECTORS)[:, None]
    is_gain = (row_ids >= S + 2) & ((row_ids - S) % 2 == 0)
    return jnp.where(is_gain, ramp[None, :] * factor, 0.3 * noise).astype(jnp.float32)


def with_ends(array, rng, low, top_value):
    dims = array.shape
    spot = [jax.random.randint(jax.random.fold_in(rng, axis), (), 0, dims[axis]) for axis in range(len(dims))]
    array = array.at[tuple(spot)].set(low)
    longest = dims.index(max(dims))
    spot[longest] = (spot[longest] + 1) % dims[longest]
    return array.at[tuple(spot)].set(top_value)


def shard_levels(stream_key, shape, cuts, low, largest):
    gain, own = 1.0, jax.random.fold_in(stream_key, 6)
    for dim, blocks in cuts:
        steps = jnp.exp(jax.random.uniform(jax.random.fold_in(own, dim), (blocks,), jnp.float32, low / len(cuts), largest / len(cuts)))
        gain = gain * jnp.repeat(steps, shape[dim] // blocks).reshape([-1 if axis == dim else 1 for axis in range(len(shape))])
    return gain


def scatter_about(key, shape, scale, limit, cuts=(), held_as=jnp.bfloat16):
    gain = shard_levels(key, shape, cuts, -0.22, 0.18) if cuts else 1.0
    result = jax.random.normal(key, shape, jnp.float32) * scale * gain
    return jnp.minimum(jnp.maximum(result, -limit), limit).astype(held_as)


def setup_inputs(seed: int = 0) -> dict:
    key_list = jax.random.split(jax.random.key(seed), 25)
    images = scatter_about(key_list[0], (IMAGES, PATCHES, PATCH_IN), 1.0, 6.0, ((0, 32),))
    slot_mask = draw_slot_mask(jax.random.fold_in(key_list[24], 71), 0)
    labels = with_ends(jax.random.randint(key_list[2], (IMAGES,), 0, CLASSES), jax.random.fold_in(key_list[2], 1), 0, CLASSES - 1).astype(jnp.int32)
    patch_weight = scatter_about(key_list[3], (PATCH_IN, D), PATCH_IN ** -0.5, 0.21875, ((0, 32),), jnp.float32)
    patch_moment = scatter_about(key_list[4], (PATCH_IN, D), (0.011 / PARAMS ** 0.5), 1.33514404296875e-05, ((0, 32),), jnp.float32)
    patch_square = jnp.clip(jnp.exp(math.log(8.788862693176469e-11) - 1.3862944 * jax.random.uniform(key_list[5], (PATCH_IN, D), jnp.float32) ** shard_levels(key_list[5], (PATCH_IN, D), ((0, 32),), -0.2, 0.2)), 2.1972156732941173e-11, 8.788862693176469e-11)
    triple_weight = scatter_about(key_list[6], (LAYERS, D, 3 * D), D ** -0.5, 0.21875, ((1, 32),), jnp.float32)
    triple_moment = scatter_about(key_list[7], (LAYERS, D, 3 * D), (0.011 / PARAMS ** 0.5), 1.33514404296875e-05, ((1, 32),), jnp.float32)
    triple_square = jnp.clip(jnp.exp(math.log(8.788862693176469e-11) - 1.3862944 * jax.random.uniform(key_list[8], (LAYERS, D, 3 * D), jnp.float32) ** shard_levels(key_list[8], (LAYERS, D, 3 * D), ((1, 32),), -0.2, 0.2)), 2.1972156732941173e-11, 8.788862693176469e-11)
    output_weight = scatter_about(key_list[9], (LAYERS, D, D), (D // 64) ** -0.5, 1.75, ((1, 32),), jnp.float32)
    output_moment = scatter_about(key_list[10], (LAYERS, D, D), (0.011 / PARAMS ** 0.5), 1.33514404296875e-05, ((1, 32),), jnp.float32)
    output_square = jnp.clip(jnp.exp(math.log(8.788862693176469e-11) - 1.3862944 * jax.random.uniform(key_list[11], (LAYERS, D, D), jnp.float32) ** shard_levels(key_list[11], (LAYERS, D, D), ((1, 32),), -0.2, 0.2)), 2.1972156732941173e-11, 8.788862693176469e-11)
    expand_weight = scatter_about(key_list[12], (LAYERS, D, FF), D ** -0.5, 0.21875, ((1, 32),), jnp.float32)
    expand_moment = scatter_about(key_list[13], (LAYERS, D, FF), (0.011 / PARAMS ** 0.5), 1.33514404296875e-05, ((1, 32),), jnp.float32)
    expand_square = jnp.clip(jnp.exp(math.log(8.788862693176469e-11) - 1.3862944 * jax.random.uniform(key_list[14], (LAYERS, D, FF), jnp.float32) ** shard_levels(key_list[14], (LAYERS, D, FF), ((1, 32),), -0.2, 0.2)), 2.1972156732941173e-11, 8.788862693176469e-11)
    shrink_weight = scatter_about(key_list[15], (LAYERS, FF, D), FF ** -0.5, 0.109375, ((1, 32),), jnp.float32)
    shrink_moment = scatter_about(key_list[16], (LAYERS, FF, D), (0.011 / PARAMS ** 0.5), 1.33514404296875e-05, ((1, 32),), jnp.float32)
    shrink_square = jnp.clip(jnp.exp(math.log(8.788862693176469e-11) - 1.3862944 * jax.random.uniform(key_list[17], (LAYERS, FF, D), jnp.float32) ** shard_levels(key_list[17], (LAYERS, FF, D), ((1, 32),), -0.2, 0.2)), 2.1972156732941173e-11, 8.788862693176469e-11)
    vector_weight = draw_vector_weight(jax.random.fold_in(key_list[24], 71), 0)
    vector_moment = scatter_about(key_list[19], (VECTORS, D), (0.055 / PARAMS ** 0.5), 6.103515625e-05, (), jnp.float32)
    vector_square = jnp.clip(jnp.exp(jax.random.uniform(key_list[20], (VECTORS, D), jnp.float32, math.log(5.493039356707641e-10), math.log(2.1972157426830563e-09))), 5.493039356707641e-10, 2.1972157426830563e-09)
    head_weight = scatter_about(key_list[21], (D + 1, CLASSES), D ** -0.5, 0.21875, (), jnp.float32)
    head_moment = scatter_about(key_list[22], (D + 1, CLASSES), (0.055 / PARAMS ** 0.5), 6.103515625e-05, (), jnp.float32)
    head_square = jnp.clip(jnp.exp(jax.random.uniform(key_list[23], (D + 1, CLASSES), jnp.float32, math.log(5.493039356707641e-10), math.log(2.1972157426830563e-09))), 5.493039356707641e-10, 2.1972157426830563e-09)
    return {"images": images, "slot_mask": slot_mask, "labels": labels, "patch_weight": patch_weight, "patch_moment": patch_moment, "patch_square": patch_square, "triple_weight": triple_weight, "triple_moment": triple_moment, "triple_square": triple_square, "output_weight": output_weight, "output_moment": output_moment, "output_square": output_square, "expand_weight": expand_weight, "expand_moment": expand_moment, "expand_square": expand_square, "shrink_weight": shrink_weight, "shrink_moment": shrink_moment, "shrink_square": shrink_square, "vector_weight": vector_weight, "vector_moment": vector_moment, "vector_square": vector_square, "head_weight": head_weight, "head_moment": head_moment, "head_square": head_square}


@jax.custom_vjp
def low(v):
    return lax.optimization_barrier(v.astype(jnp.bfloat16)).astype(jnp.float32)

@jax.custom_vjp
def low_back(v):
    return v

def low_keep(v):
    return (low(v), None)

def low_pass(kept, grad):
    return (grad,)

def back_keep(v):
    return (v, None)

def back_low(kept, grad):
    return (low(grad),)
low.defvjp(low_keep, low_pass)
low_back.defvjp(back_keep, back_low)
EPS_NORM = 1e-06
CLIP = 0.1
BETA_ONE = 0.9
BETA_TWO = 0.95
ADAM_EPS = 1e-08
DECAY = 0.05
RATE_MATRIX = 0.03
RATE_OUTPUT = 0.2
RATE_VECTOR = 0.3
SMOOTH = 0.1

def normalize(values, gain_row, shift_row):
    center = values - lax.optimization_barrier(jnp.mean(values, -1, keepdims=True))
    spread = lax.optimization_barrier(jnp.mean(center * center, -1, keepdims=True))
    return center * lax.rsqrt(spread + EPS_NORM) * gain_row + shift_row

def product(form, left, right):
    return jnp.einsum(form, left, right, precision=lax.Precision.HIGHEST)

def adam_update(master, moment, square, gradient, step_rate):
    moment_new = BETA_ONE * moment + (1.0 - BETA_ONE) * gradient
    square_new = BETA_TWO * square + (1.0 - BETA_TWO) * gradient * gradient
    moment_hat = moment_new / (1.0 - BETA_ONE ** STEP_INDEX)
    square_hat = square_new / (1.0 - BETA_TWO ** STEP_INDEX)
    master_new = master - step_rate * (moment_hat / (jnp.sqrt(square_hat) + ADAM_EPS) + DECAY * master)
    return (master_new, moment_new, square_new)

def group_loss(params, pieces, weight_img, label_ids):
    patch_c, triple_c, output_c, expand_c, shrink_c, vectors, head_c = params
    count_img = pieces.shape[0]
    embedded = low_back(product('bnp,pd->bnd', pieces, patch_c)) + vectors[S + 1]
    opening = jnp.broadcast_to(vectors[S], (count_img, 1, D))
    hidden = jnp.concatenate([opening, embedded], axis=1) + vectors[:S]
    for layer_at in range(LAYERS):
        base_at = S + 2 + 4 * layer_at
        normed = low(normalize(hidden, vectors[base_at], vectors[base_at + 1]))
        triple = low_back(low(product('bsd,de->bse', normed, triple_c[layer_at])))
        split_heads = triple.reshape(count_img, S, 3, HEADS, HEAD_DIM)
        scores = low_back(product('bqhd,bkhd->bhqk', split_heads[:, :, 0], split_heads[:, :, 1]) * HEAD_DIM ** (-0.5))
        probs = low(jax.nn.softmax(scores, axis=-1))
        attended = product('bhqk,bkhd->bqhd', probs, split_heads[:, :, 2]).reshape(count_img, S, D)
        attended = low_back(low(attended))
        hidden = hidden + low_back(product('bsd,de->bse', attended, output_c[layer_at]))
        normed_two = low(normalize(hidden, vectors[base_at + 2], vectors[base_at + 3]))
        expanded = low_back(product('bsd,df->bsf', normed_two, expand_c[layer_at]))
        active = low(jax.nn.gelu(expanded, approximate=False))
        hidden = hidden + low_back(product('bsf,fd->bsd', active, shrink_c[layer_at]))
    final_at = S + 2 + 4 * LAYERS
    feature = low(normalize(hidden[:, 0], vectors[final_at], vectors[final_at + 1]))
    logits = low_back(product('bd,dc->bc', feature, head_c[:D]) + head_c[D])
    log_prob = jax.nn.log_softmax(logits, axis=-1)
    target = (1.0 - SMOOTH) * jax.nn.one_hot(label_ids, CLASSES, dtype=jnp.float32) + SMOOTH / CLASSES
    return jnp.sum(weight_img * -lax.optimization_barrier(jnp.sum(target * log_prob, axis=-1)))

def reference(images, slot_mask, labels, patch_weight, patch_moment, patch_square, triple_weight, triple_moment, triple_square, output_weight, output_moment, output_square, expand_weight, expand_moment, expand_square, shrink_weight, shrink_moment, shrink_square, vector_weight, vector_moment, vector_square, head_weight, head_moment, head_square):
    image_total = jnp.sum(slot_mask.astype(jnp.float32))
    copies = (low(patch_weight), low(triple_weight), low(output_weight), low(expand_weight), low(shrink_weight), vector_weight, jnp.concatenate([low(head_weight[:D]), head_weight[D:]], axis=0))
    group_size = 16
    group_count = IMAGES // group_size
    pieces_all = images.astype(jnp.float32).reshape(group_count, group_size, PATCHES, PATCH_IN)
    weights_all = slot_mask.astype(jnp.float32).reshape(group_count, group_size)
    labels_all = labels.reshape(group_count, group_size)
    checked = jax.checkpoint(group_loss)

    def objective(*params):

        def advance(running, inputs):
            return (running + checked(params, inputs[0], inputs[1], inputs[2]), None)
        loss_all, unused = lax.scan(advance, jnp.zeros((), jnp.float32), (pieces_all, weights_all, labels_all))
        return (loss_all / image_total, loss_all)
    mean_loss, backward, loss_sum = jax.vjp(objective, *copies, has_aux=True)
    grads = backward(jnp.ones((), jnp.float32))
    grad_norm = jnp.sqrt(jnp.sum(jnp.stack([jnp.sum(member * member) for member in grads])))
    clip_scale = CLIP / jnp.maximum(grad_norm, CLIP)
    patch_new = adam_update(patch_weight, patch_moment, patch_square, grads[0] * clip_scale, RATE_MATRIX)
    triple_new = adam_update(triple_weight, triple_moment, triple_square, grads[1] * clip_scale, RATE_MATRIX)
    output_new = adam_update(output_weight, output_moment, output_square, grads[2] * clip_scale, RATE_OUTPUT)
    expand_new = adam_update(expand_weight, expand_moment, expand_square, grads[3] * clip_scale, RATE_MATRIX)
    shrink_new = adam_update(shrink_weight, shrink_moment, shrink_square, grads[4] * clip_scale, RATE_MATRIX)
    vector_new = adam_update(vector_weight, vector_moment, vector_square, grads[5] * clip_scale, RATE_VECTOR)
    head_clipped = grads[6] * clip_scale
    head_new = adam_update(head_weight, head_moment, head_square, head_clipped, RATE_MATRIX)
    return (loss_sum, image_total, grad_norm, patch_new[0], patch_new[1], patch_new[2], triple_new[0], triple_new[1], triple_new[2], output_new[0], output_new[1], output_new[2], expand_new[0], expand_new[1], expand_new[2], shrink_new[0], shrink_new[1], shrink_new[2], vector_new[0], vector_new[1], vector_new[2], head_new[0], head_new[1], head_new[2], head_clipped[D])
```

```python
import functools
from types import SimpleNamespace

import jax
import jax.numpy as jnp
from jax import lax
from jax.experimental import pallas as pl
from jax.experimental.pallas import tpu as pltpu
from jax.sharding import PartitionSpec as P

D = 768
HEADS = 12
HEAD_DIM = 64
FF = 3072
CLASSES = 1000
LAYERS = 3
STEP_INDEX = 10
S = 197
PAD = 208

EPS_NORM = 1e-06
CLIP = 0.1
BETA_ONE = 0.9
BETA_TWO = 0.95
ADAM_EPS = 1e-08
DECAY = 0.05
RATE_MATRIX = 0.03
RATE_OUTPUT = 0.2
RATE_VECTOR = 0.3
SMOOTH = 0.1

F32 = jnp.float32
BF = jnp.bfloat16
NN = (((1,), (0,)), ((), ()))
NT = (((1,), (1,)), ((), ()))
TN = (((0,), (0,)), ((), ()))
VMEM_SPEC = pl.BlockSpec(memory_space=pltpu.VMEM)
ANY_SPEC = pl.BlockSpec(memory_space=pl.ANY)
LIMIT = 61 * 1024 * 1024


def dot(left, right, form=NN):
    return lax.dot_general(left, right, form, preferred_element_type=F32)


def normalize(values, gain_row, shift_row):
    center = values - jnp.mean(values, -1, keepdims=True)
    spread = jnp.mean(center * center, -1, keepdims=True)
    return center * lax.rsqrt(spread + EPS_NORM) * gain_row + shift_row


def normalize_back(values, gain_row, grad):
    center = values - jnp.mean(values, -1, keepdims=True)
    spread = jnp.mean(center * center, -1, keepdims=True)
    scale = lax.rsqrt(spread + EPS_NORM)
    unit = center * scale
    d_unit = grad * gain_row
    d_values = scale * (
        d_unit
        - jnp.mean(d_unit, -1, keepdims=True)
        - unit * jnp.mean(d_unit * unit, -1, keepdims=True)
    )
    return (
        d_values,
        jnp.sum(grad * unit, 0, keepdims=True),
        jnp.sum(grad, 0, keepdims=True),
    )


def gelu_and_slope(u):
    x = jnp.abs(u) * 0.7071067811865476
    t = 1.0 / (1.0 + 0.3275911 * x)
    series = t * (
        0.254829592
        + t * (-0.284496736 + t * (1.421413741 + t * (-1.453152027 + t * 1.061405429)))
    )
    bell = jnp.exp(-0.5 * u * u)
    tail = 0.5 * series * bell
    share = jnp.where(u >= 0.0, 1.0 - tail, tail)
    return u * share, share + u * bell * 0.3989422804014327


class Plan:
    def __init__(self, mesh):
        self.wide, self.grp = mesh.shape["wide"], mesh.shape["grp"]
        self.n = self.wide * self.grp
        self.cube = self.wide == 8 and self.grp == 4

    def where(self):
        if not self.cube:
            return 0, 0, 0, 0
        wide, grp = lax.axis_index("wide"), lax.axis_index("grp")
        return wide // 2, wide % 2, grp // 2, grp % 2


CHIPS = (4, 2, 2)
BLOCK = D // 16
BLOCK_FF = FF // 32


def cols_shape(columns):
    return CHIPS + (BLOCK, columns)


ROWS_SHAPE = CHIPS + (2, BLOCK_FF, D)


def cut_of(columns):
    return (columns // 2 + 127) // 128 * 128


class Gather:
    def __init__(self, plan, by_cols, block, whole, send, recv):
        self.z, self.x, self.y, self.c = plan.where()
        self.by_cols, self.block, self.whole = by_cols, block, whole
        self.send, self.recv = send, recv
        self.width = block.shape[-1]

    def region(self, z, x, y, start, width):
        if self.by_cols:
            first = pl.multiple_of(self.c * self.width + start, 128)
            return self.whole.at[z, x, y, :, pl.ds(first, width)]
        return self.whole.at[z, x, y, self.c, :, pl.ds(start, width)]

    def copy(self, at):
        z, x, y, c = self.z, self.x, self.y, self.c
        width, cut, line = self.width, cut_of(self.width), slice(None)
        if at < 3:
            src, dst = self.block, self.region(z, x, y, 0, width)
            to = (jnp.bitwise_xor(z, at + 1) * 2 + x, y * 2 + c)
        else:
            src = dst = (
                lambda: self.region(line, x, y, 0, width),
                lambda: self.region(line, x, y, 0, width),
                lambda: self.region(line, x, 1 - y, 0, cut),
                lambda: self.region(line, 1 - x, y, cut, width - cut),
                lambda: self.region(line, x, y, 0, width),
                lambda: self.region(line, 1 - x, y, 0, width),
                lambda: self.region(line, x, 1 - y, 0, width),
                lambda: self.region(line, 1 - x, 1 - y, 0, cut),
                lambda: self.region(line, 1 - x, 1 - y, cut, width - cut),
            )[at - 3]()
            over_x, over_y, over_c = (z * 2 + 1 - x, y * 2 + c), (z * 2 + x, (1 - y) * 2 + c), (z * 2 + x, y * 2 + 1 - c)
            to = (over_x, over_y, over_x, over_y, over_c, over_c, over_c, over_c, over_c)[at - 3]
        return pltpu.make_async_remote_copy(
            src_ref=src,
            dst_ref=dst,
            send_sem=self.send.at[at],
            recv_sem=self.recv.at[at],
            device_id=to,
            device_id_type=pl.DeviceIdType.MESH,
        )

    def keep(self):
        here = self.region(self.z, self.x, self.y, 0, self.width)
        return pltpu.make_async_copy(self.block, here, self.send.at[12])

    def start(self, *which):
        for at in which:
            self.copy(at).start()

    def arrived(self, *which):
        for at in which:
            self.copy(at).wait_recv()

    def stage0(self):
        self.start(0, 1, 2)
        self.keep().start()

    def stage1(self):
        self.arrived(0, 1, 2)
        self.keep().wait()
        self.start(3, 4, 7)

    def stage2(self):
        self.arrived(3, 4)
        self.start(5, 6, 8, 9)

    def stage3(self):
        self.arrived(5, 6)
        self.start(10, 11)

    def finish(self):
        self.arrived(7, 8, 9, 10, 11)
        for at in range(12):
            self.copy(at).wait_send()


def cube_barrier(plan):
    z, x, y, c = plan.where()
    barrier = pltpu.get_barrier_semaphore()
    partners = [(jnp.bitwise_xor(z, k) * 2 + x, y * 2 + c) for k in (1, 2, 3)]
    partners += [
        (z * 2 + 1 - x, y * 2 + c),
        (z * 2 + x, (1 - y) * 2 + c),
        (z * 2 + x, y * 2 + 1 - c),
    ]
    for partner in partners:
        pl.semaphore_signal(barrier, inc=1, device_id=partner, device_id_type=pl.DeviceIdType.MESH)
    pl.semaphore_wait(barrier, len(partners))


def load(source, target, sem):
    copy = pltpu.make_async_copy(source, target, sem)
    copy.start()
    return copy


def start_all(copies):
    for copy in copies:
        copy.start()


def wait_all(copies):
    for copy in copies:
        copy.wait()


def weight(ref, first, width):
    cols = pl.ds(first if isinstance(first, int) else pl.multiple_of(first, 128), width)
    return ref[:, :, :, :, cols].reshape(D, width)


class SmallGather:
    def __init__(self, plan, block, whole, send, recv):
        self.z, self.x, self.y, self.c = plan.where()
        self.block, self.whole, self.send, self.recv = block, whole, send, recv

    def copy(self, at):
        z, x, y, c = self.z, self.x, self.y, self.c
        line = slice(None)
        if at < 3:
            src, dst = self.block, self.whole.at[z, x, y, c]
            to = (jnp.bitwise_xor(z, at + 1) * 2 + x, y * 2 + c)
        elif at == 3:
            src = dst = self.whole.at[line, x, y, c]
            to = (z * 2 + 1 - x, y * 2 + c)
        elif at == 4:
            src = dst = self.whole.at[line, line, y, c]
            to = (z * 2 + x, (1 - y) * 2 + c)
        else:
            src = dst = self.whole.at[line, line, line, c]
            to = (z * 2 + x, y * 2 + 1 - c)
        return pltpu.make_async_remote_copy(
            src_ref=src,
            dst_ref=dst,
            send_sem=self.send.at[at],
            recv_sem=self.recv.at[at],
            device_id=to,
            device_id_type=pl.DeviceIdType.MESH,
        )

    def keep(self):
        here = self.whole.at[self.z, self.x, self.y, self.c]
        return pltpu.make_async_copy(self.block, here, self.send.at[6])

    def stage0(self):
        for at in range(3):
            self.copy(at).start()
        self.keep().start()

    def stage1(self):
        for at in range(3):
            self.copy(at).wait_recv()
        self.keep().wait()
        self.copy(3).start()

    def stage2(self):
        self.copy(3).wait_recv()
        self.copy(4).start()

    def stage3(self):
        self.copy(4).wait_recv()
        self.copy(5).start()

    def finish(self):
        self.copy(5).wait_recv()
        for at in range(6):
            self.copy(at).wait_send()


FF_TILE = 512
HALF = BLOCK // 2
WIDTH = FF // 2
HEAD_ROWS = 16
HEAD_BLOCK = 32
FINAL = S + 2 + 4 * LAYERS


def saved_shapes(rows):
    heads = rows // PAD * HEADS
    return dict(
        h=((rows, D), F32),
        a=((rows, D), BF),
        t=((rows, 3 * D), BF),
        o=((rows, D), BF),
        p=((heads, PAD, PAD), BF),
        h1=((rows, D), F32),
        m=((rows, D), BF),
        z=((rows, FF), BF),
        slope=((rows, FF), BF),
    )


SAVED = tuple(saved_shapes(PAD))


def row(ref, at):
    return ref[pl.ds(at, 1)]


def share_shards(plan, r):
    z, x, y, c = plan.where()
    r.joined_f[:, :, : 3 * D] = r.triple[...]
    r.joined_f[:, :, 3 * D :] = r.output[...]
    mine = pl.ds(pl.multiple_of(c * HALF, 8), HALF)

    def part(core, width):
        return pl.ds(pl.multiple_of(core * width, 128), width)

    moves = [
        (r.patch.at[:, part(1 - c, D // 2)], r.patch_f.at[mine]),
        (r.joined_f.at[:, :, part(1 - c, WIDTH)], r.joined_b.at[:, mine]),
        (r.expand.at[:, :, part(1 - c, WIDTH)], r.expand_b.at[:, mine]),
    ]
    copies = [
        pltpu.make_async_remote_copy(
            src_ref=src,
            dst_ref=dst,
            send_sem=r.share_send.at[i],
            recv_sem=r.share_recv.at[i],
            device_id=(z * 2 + x, y * 2 + 1 - c),
            device_id_type=pl.DeviceIdType.MESH,
        )
        for i, (src, dst) in enumerate(moves)
    ]
    start_all(copies)
    r.patch_f[mine] = r.patch[:, part(c, D // 2)]
    r.joined_b[:, mine] = r.joined_f[:, :, part(c, WIDTH)]
    r.expand_b[:, mine] = r.expand[:, :, part(c, WIDTH)]
    r.shrink_block[...] = r.shrink[...].astype(BF)
    for copy, src, dst in zip(
        copies,
        (r.patch_f, r.joined_b, r.expand_b),
        (r.patch_block, r.joined_block, r.expand_block),
    ):
        copy.wait_recv()
        dst[...] = src[...].astype(BF)
    for copy in copies:
        copy.wait_send()


def head_part(r, image_total):
    images = r.h.shape[0] // PAD
    table = r.head[:D].astype(BF)
    r.first[...] = jnp.zeros_like(r.first)
    for image in range(images):
        r.first[image : image + 1] = r.h[image * PAD : image * PAD + 1]
    first = r.first[...]
    gain, shift = r.vectors[FINAL : FINAL + 1], r.vectors[FINAL + 1 : FINAL + 2]
    feature = normalize(first, gain, shift).astype(BF)
    logits = dot(feature, table) + r.head[D : D + 1]
    ids = lax.broadcasted_iota(jnp.int32, logits.shape, 1)
    shifted = logits - jnp.max(logits, -1, keepdims=True)
    log_prob = shifted - jnp.log(jnp.sum(jnp.exp(shifted), -1, keepdims=True))
    target = jnp.where(ids == r.labels[...], 1.0 - SMOOTH, 0.0) + SMOOTH / CLASSES
    weights = r.weights[...]
    loss = jnp.sum(weights * -jnp.sum(target * log_prob, -1, keepdims=True))
    d_logits = ((weights / image_total) * (jnp.exp(log_prob) - target)).astype(BF)
    d_feature = dot(d_logits, table, NT)
    r.d_logits[...] = jnp.zeros_like(r.d_logits)
    r.d_logits[:, :CLASSES] = d_logits.astype(F32)
    r.head_block[...] = jnp.zeros_like(r.head_block)
    feature = feature.astype(F32)
    for image in range(images):
        for j in range(6):
            at = image * 14 + j
            r.head_block[at : at + 1] = feature[image : image + 1, j * 128 : j * 128 + 128]
        for j in range(8):
            at = image * 14 + 6 + j
            r.head_block[at : at + 1] = r.d_logits[image : image + 1, j * 128 : j * 128 + 128]
    d_first, d_gain, d_shift = normalize_back(first, gain, d_feature)
    r.g[...] = jnp.zeros_like(r.g)
    for image in range(images):
        r.g[image * PAD : image * PAD + 1] = d_first[image : image + 1]
    r.tail[...] = jnp.zeros_like(r.tail)
    r.tail[0:1] = jnp.full((1, D), loss, F32)
    r.tail[1:2] = d_gain
    r.tail[2:3] = d_shift


def forward_kernel(plan, names, *refs):
    r = SimpleNamespace(**dict(zip(names, refs)))
    cube = plan.cube
    images = r.images.shape[0]
    patch, joined, expand, shrink = range(4)
    wholes = (r.patch_whole, r.joined_whole, r.expand_whole, r.shrink_whole)
    weights = (r.patch_w, r.joined_w, r.expand_w, r.shrink_w)
    if cube:
        blocks = (r.patch_block, r.joined_block, r.expand_block, r.shrink_block)
        cube_barrier(plan)
        share_shards(plan, r)
        r.count[...] = jnp.full((8, 128), jnp.sum(r.weights[...]), F32)
        counting = SmallGather(plan, r.count, r.counts, r.count_send, r.count_recv)

    def unit(kind, layer):
        if kind == patch:
            return Gather(plan, True, blocks[0], wholes[0], r.send.at[0], r.recv.at[0])
        at = 3 * layer + kind
        block, whole = blocks[kind].at[layer], wholes[kind].at[layer]
        return Gather(plan, kind != shrink, block, whole, r.send.at[at], r.recv.at[at])

    def ready(kind, layer):
        if cube:
            unit(kind, layer).finish()
        whole = wholes[kind] if kind == patch else wholes[kind].at[layer]
        return load(whole, weights[kind], r.loads.at[kind])

    held = (r.h, r.a, r.t, r.o, r.p, r.h1, r.m, r.z, r.slope)
    kept = (r.keep_h, r.keep_a, r.keep_t, r.keep_o, r.keep_p, r.keep_h1, r.keep_m, r.keep_z, r.keep_slope)
    h_, a_, t_, o_, p_, h1_, m_, z_, slope_ = range(9)

    def saves(layer, *which):
        return [pltpu.make_async_copy(held[k], kept[k].at[layer], r.saves.at[k]) for k in which]

    if cube:
        unit(patch, 0).stage0()
        counting.stage0()
        unit(joined, 0).stage0()
        unit(patch, 0).stage1()
        unit(expand, 0).stage0()
        unit(joined, 0).stage1()
        unit(patch, 0).stage2()
        unit(shrink, 0).stage0()
        unit(expand, 0).stage1()
        unit(joined, 0).stage2()
        unit(patch, 0).stage3()
    ready(patch, 0).wait()
    for image in range(images):
        at = image * PAD
        r.h[at : at + 1] = r.vectors[0:1] + r.vectors[S : S + 1]
        embedded = dot(r.images[image], weight(r.patch_w, 0, D))
        r.h[at + 1 : at + S] = embedded + r.vectors[S + 1 : S + 2] + r.vectors[1:S]
        r.h[at + S : at + PAD] = jnp.zeros((PAD - S, D), F32)

    low_lane = lax.broadcasted_iota(jnp.int32, (PAD, 128), 1) < HEAD_DIM
    real_key = lax.broadcasted_iota(jnp.int32, (PAD, PAD), 0) < S

    @pl.loop(0, LAYERS)
    def _(layer):
        more = layer < LAYERS - 1
        base = S + 2 + 4 * layer
        if cube:
            pl.when(more)(lambda: unit(joined, layer + 1).stage0())
            unit(shrink, layer).stage1()
            unit(expand, layer).stage2()
            unit(joined, layer).stage3()
        start_all(saves(layer, h_))

        @pl.when(layer > 0)
        def _():
            wait_all(saves(layer, a_, t_, o_, p_, h1_, m_))

        r.a[...] = normalize(r.h[...], row(r.vectors, base), row(r.vectors, base + 1)).astype(BF)
        ready(joined, layer).wait()

        @pl.loop(0, 3)
        def _(j):
            cols = pl.ds(pl.multiple_of(j * D, 128), D)
            r.t[:, cols] = dot(r.a[...], weight(r.joined_w, j * D, D)).astype(BF)

        start_all(saves(layer, a_, t_))

        @pl.loop(0, images * (HEADS // 2))
        def _(step):
            image, pair = step // (HEADS // 2), step % (HEADS // 2)
            rows = pl.ds(pl.multiple_of(image * PAD, 16), PAD)
            lanes = [pl.ds(pl.multiple_of(pair * 128 + part * D, 128), 128) for part in range(3)]
            q, key, v = (r.t[rows, lane] for lane in lanes)
            zero = jnp.zeros_like(key)
            outs = []
            for which in range(2):
                part = jnp.where(low_lane, key, zero) if which == 0 else jnp.where(low_lane, zero, key)
                scores = dot(part, q, NT) * HEAD_DIM**-0.5
                scores = jnp.where(real_key, scores, -1e30)
                top = jnp.max(scores, 0, keepdims=True)
                e = jnp.exp(scores - top)
                p = (e * (1.0 / jnp.sum(e, 0, keepdims=True))).astype(BF)
                r.p[step * 2 + which] = p
                outs.append(dot(p, v, TN))
            r.o[rows, lanes[0]] = jnp.where(low_lane, outs[0], outs[1]).astype(BF)

        start_all(saves(layer, o_, p_))
        r.h1[...] = r.h[...] + dot(r.o[...], weight(r.joined_w, 3 * D, D))
        start_all(saves(layer, h1_))
        if cube:
            @pl.when(more)
            def _():
                unit(expand, layer + 1).stage0()
                unit(joined, layer + 1).stage1()

            unit(shrink, layer).stage2()
            unit(expand, layer).stage3()
            pl.when(layer == 0)(counting.stage1)
            pl.when(layer == 1)(counting.stage3)
        r.m[...] = normalize(r.h1[...], row(r.vectors, base + 2), row(r.vectors, base + 3)).astype(BF)
        start_all(saves(layer, m_))
        wait_all(saves(layer, h_))
        r.h[...] = r.h1[...]

        @pl.when(layer > 0)
        def _():
            wait_all(saves(layer, z_, slope_))

        ready(expand, layer).wait()

        @pl.loop(0, FF // FF_TILE)
        def _(j):
            cols = pl.ds(pl.multiple_of(j * FF_TILE, 128), FF_TILE)
            u = dot(r.m[...], weight(r.expand_w, j * FF_TILE, FF_TILE))
            z, slope = gelu_and_slope(u)
            r.z[:, cols] = z.astype(BF)
            r.slope[:, cols] = slope.astype(BF)

        start_all(saves(layer, z_, slope_))
        if cube:
            @pl.when(more)
            def _():
                unit(shrink, layer + 1).stage0()
                unit(expand, layer + 1).stage1()
                unit(joined, layer + 1).stage2()

            unit(shrink, layer).stage3()
            pl.when(layer == 0)(counting.stage2)
            pl.when(layer == 1)(counting.finish)
        ready(shrink, layer).wait()

        @pl.loop(0, 4)
        def _(j):
            cols = pl.ds(pl.multiple_of(j * D, 128), D)
            r.h[...] += dot(r.z[:, cols], r.shrink_w[j].reshape(D, D))

    if cube:
        r.total[...] = jnp.sum(r.counts[...].reshape(-1, 8, 128), 0)
        image_total = r.total[0:1, 0:1]
    else:
        image_total = r.count_in[0:1, 0:1]
    head_part(r, image_total)
    wait_all(saves(LAYERS - 1, a_, t_, o_, p_, h1_, m_, z_, slope_))


def pallas(kernel, name, inputs, outputs, scratch, **params):
    names = list(inputs) + list(outputs) + list(scratch)
    outs = pl.pallas_call(
        functools.partial(kernel, names),
        out_shape=[jax.ShapeDtypeStruct(shape, kind) for shape, kind, _ in outputs.values()],
        in_specs=[spec for _, spec in inputs.values()],
        out_specs=[spec for _, _, spec in outputs.values()],
        scratch_shapes=list(scratch.values()),
        compiler_params=pltpu.CompilerParams(vmem_limit_bytes=LIMIT, **params),
        name=name,
    )(*[value for value, _ in inputs.values()])
    return SimpleNamespace(**dict(zip(outputs, outs)))


def given_in(spec, **values):
    return {name: (value, spec) for name, value in values.items()}


def vmem(kind, **shapes):
    return {name: pltpu.VMEM(shape, kind) for name, shape in shapes.items()}


def dma(**counts):
    return {name: pltpu.SemaphoreType.DMA(count) for name, count in counts.items()}


def forward(plan, shards, args, gathered, count):
    rows = args["images"].shape[0] * PAD
    shapes = saved_shapes(rows)
    whole = dict(
        patch_whole=cols_shape(D),
        joined_whole=(LAYERS,) + cols_shape(FF),
        expand_whole=(LAYERS,) + cols_shape(FF),
        shrink_whole=(LAYERS,) + ROWS_SHAPE,
    )
    inputs = given_in(VMEM_SPEC, **args)
    outputs = {}
    if plan.cube:
        inputs.update(given_in(VMEM_SPEC, **shards))
        outputs.update({name: (shape, BF, ANY_SPEC) for name, shape in whole.items()})
    else:
        inputs.update(given_in(ANY_SPEC, **dict(zip(whole, gathered))))
        inputs.update(given_in(VMEM_SPEC, count_in=count))
    for name, (shape, kind) in shapes.items():
        outputs["keep_" + name] = ((LAYERS,) + shape, kind, ANY_SPEC)
    outputs.update(
        g=((rows, D), F32, VMEM_SPEC),
        tail=((8, D), F32, VMEM_SPEC),
        head_block=((HEAD_BLOCK, 128), F32, VMEM_SPEC),
        total=((8, 128), F32, VMEM_SPEC),
    )
    scratch = vmem(
        BF,
        patch_w=cols_shape(D),
        joined_w=cols_shape(FF),
        expand_w=cols_shape(FF),
        shrink_w=ROWS_SHAPE,
    )
    scratch.update({name: pltpu.VMEM(shape, kind) for name, (shape, kind) in shapes.items()})
    scratch.update(vmem(F32, first=(HEAD_ROWS, D), d_logits=(HEAD_ROWS, 1024)))
    scratch.update(dma(saves=(9,), loads=(4,)))
    extra = {}
    if plan.cube:
        scratch.update(
            vmem(
                F32,
                joined_f=(LAYERS, HALF, FF),
                joined_b=(LAYERS, BLOCK, WIDTH),
                expand_b=(LAYERS, BLOCK, WIDTH),
                patch_f=(BLOCK, D // 2),
                count=(8, 128),
                counts=CHIPS + (2, 8, 128),
            )
        )
        scratch.update(
            vmem(
                BF,
                patch_block=(BLOCK, D // 2),
                joined_block=(LAYERS, BLOCK, WIDTH),
                expand_block=(LAYERS, BLOCK, WIDTH),
                shrink_block=(LAYERS, BLOCK_FF, D),
            )
        )
        scratch.update(
            dma(send=(10, 13), recv=(10, 12), share_send=(3,), share_recv=(3,), count_send=(7,), count_recv=(7,))
        )
        extra = dict(collective_id=1, has_side_effects=True)
    got = pallas(functools.partial(forward_kernel, plan), "forward", inputs, outputs, scratch, **extra)
    if not plan.cube:
        for name, value in zip(whole, gathered):
            setattr(got, name, value)
        got.total = count
    return got


UNITS = 3 * LAYERS
TAIL = 512
SEND = 4
VEC_ROWS = 256


def relative(plan):
    z, x, y, c = plan.where()
    return c, (z * 2 + x) * 2 + y


def place(plan, slot, core, chip):
    my_core, my_chip = relative(plan)
    at = jnp.bitwise_xor(my_chip, chip)
    other = jnp.bitwise_xor(my_core, core)
    return slot + (SEND - slot) * other, at // 4, at % 4


def store_cols(plan, out, slot, tile, width, value, half=WIDTH):
    per_half = half // width
    lanes = pl.ds(pl.multiple_of((tile % per_half) * width, 128), width)
    for b in range(16):
        rows = value[b * BLOCK : (b + 1) * BLOCK].astype(BF)
        out[(*place(plan, slot, tile // per_half, b), slice(None), lanes)] = rows


def store_rows(plan, out, slot, tile, value):
    for b in range(4):
        at = place(plan, slot, b % 2, tile * 2 + b // 2)
        for part in range(2):
            first = b * BLOCK_FF + part * BLOCK
            out[(*at, slice(None), pl.ds(part * D, D))] = value[first : first + BLOCK].astype(BF)


def store_vectors(plan, out, slot, value):
    for b in range(32):
        rows = value[b * 8 : b * 8 + 8]
        block = jnp.concatenate([rows[:, j * 128 : j * 128 + 128] for j in range(6)], 0)
        out[(*place(plan, slot, b % 2, b // 2), slice(None), pl.ds(D // 2, 128))] = block.astype(BF)


class Reduce:
    def __init__(self, plan, bufs, unit, width=WIDTH):
        self.plan, self.bufs, self.unit, self.width = plan, bufs, unit, width
        self.z, self.x, self.y, self.c = plan.where()
        self.cut = width // 2
        self.slot, self.three, self.two = unit % 4, unit % 3, unit % 2

    def copy(self, at):
        z, x, y, c = self.z, self.x, self.y, self.c
        bufs, slot, three, width, cut = self.bufs, self.slot, self.three, self.width, self.cut
        line = slice(None)
        full, left, right = pl.ds(0, width), pl.ds(0, cut), pl.ds(cut, width - cut)
        over_x, over_y, over_c = (
            (z * 2 + 1 - x, y * 2 + c),
            (z * 2 + x, (1 - y) * 2 + c),
            (z * 2 + x, y * 2 + 1 - c),
        )
        unit = bufs.unit
        if at == 0:
            src, dst, to = unit.at[SEND, :, :, :, full], bufs.core.at[:, :, :, full], over_c
        elif at == 1:
            src, dst, to = unit.at[slot, :, 3, :, left], bufs.near.at[three, :, :, left], over_x
        elif at == 2:
            src, dst, to = unit.at[slot, :, 3, :, right], bufs.far.at[three, :, :, left], over_y
        elif at == 3:
            src, dst, to = unit.at[slot, :, 1, :, full], bufs.y.at[three, :, :, full], over_y
        elif at == 4:
            src, dst, to = unit.at[slot, :, 2, :, full], bufs.x.at[three, :, :, full], over_x
        elif at < 8:
            k = at - 4
            src = bufs.line.at[self.two, k, :, full]
            dst = bufs.z.at[slot, k - 1, :, full]
            to = (jnp.bitwise_xor(z, k) * 2 + x, y * 2 + c)
        else:
            rows = pl.ds(pl.multiple_of((1 - c) * HALF, 8), HALF)
            if width == WIDTH:
                src, dst = bufs.total.at[self.two, rows], bufs.owned.at[self.unit, c]
            else:
                cols = pl.ds(0, D // 2)
                src, dst = bufs.total.at[self.two, rows, cols], bufs.patch.at[c]
            to = over_c
        return pltpu.make_async_remote_copy(
            src_ref=src,
            dst_ref=dst,
            send_sem=bufs.send.at[slot, at],
            recv_sem=bufs.recv.at[slot, at],
            device_id=to,
            device_id_type=pl.DeviceIdType.MESH,
        )

    def own(self, by_rows):
        bufs, c = self.bufs, self.c
        sem = bufs.send
        if by_rows:
            return [
                pltpu.make_async_copy(
                    bufs.total.at[self.two, pl.ds(part * HALF, HALF)],
                    bufs.owned.at[self.unit, part],
                    sem.at[self.slot, 9 + part],
                )
                for part in range(2)
            ]
        rows = pl.ds(pl.multiple_of(c * HALF, 8), HALF)
        if self.width == WIDTH:
            src, dst = bufs.total.at[self.two, rows], bufs.owned.at[self.unit, c]
        else:
            src, dst = bufs.total.at[self.two, rows, pl.ds(0, D // 2)], bufs.patch.at[c]
        return [pltpu.make_async_copy(src, dst, sem.at[self.slot, 9])]

    def credit(self):
        return self.bufs.credit

    def stage0(self):
        @pl.when(self.unit > 0)
        def _():
            pl.semaphore_wait(self.credit(), 1)

        self.copy(0).start()

    def stage1(self):
        unit, core, slot = self.bufs.unit, self.bufs.core, self.slot
        cols = pl.ds(0, self.width)
        self.copy(0).wait_recv()

        def add(z, chip):
            both = unit[slot, z, chip, :, cols].astype(F32) + core[z, chip, :, cols].astype(F32)
            unit[slot, z, chip, :, cols] = both.astype(BF)

        pl.loop(0, 4)(lambda z: add(z, 3))
        self.copy(1).start()
        self.copy(2).start()
        pl.loop(0, 12)(lambda i: add(i // 3, i % 3))

        @pl.when(self.unit < UNITS)
        def _():
            z, x, y, c = self.z, self.x, self.y, self.c
            pl.semaphore_signal(
                self.credit(),
                inc=1,
                device_id=(z * 2 + x, y * 2 + 1 - c),
                device_id_type=pl.DeviceIdType.MESH,
            )

    def stage2(self):
        unit, slot, cut = self.bufs.unit, self.slot, self.cut
        left, right = pl.ds(0, cut), pl.ds(cut, self.width - cut)
        self.copy(1).wait_recv()
        self.copy(2).wait_recv()

        @pl.loop(0, 4)
        def _(z):
            for chip, cols, landed in ((1, left, self.bufs.near), (2, right, self.bufs.far)):
                got = landed[self.three, z, :, left].astype(F32)
                unit[slot, z, chip, :, cols] = (unit[slot, z, chip, :, cols].astype(F32) + got).astype(BF)

        self.copy(3).start()
        self.copy(4).start()
        self.copy(1).wait_send()
        self.copy(2).wait_send()

    def stage3(self):
        bufs, cols = self.bufs, pl.ds(0, self.width)
        self.copy(3).wait_recv()
        self.copy(4).wait_recv()

        @pl.loop(0, 4)
        def _(z):
            bufs.line[self.two, z, :, cols] = (
                bufs.unit[self.slot, z, 0, :, cols].astype(F32)
                + bufs.y[self.three, z, :, cols].astype(F32)
                + bufs.x[self.three, z, :, cols].astype(F32)
            ).astype(BF)

        for at in (5, 6, 7):
            self.copy(at).start()
        self.copy(3).wait_send()
        self.copy(4).wait_send()

    def stage4(self, by_rows):
        bufs, cols = self.bufs, pl.ds(0, self.width)
        for at in (5, 6, 7):
            self.copy(at).wait_recv()
        total = bufs.line[self.two, 0, :, cols].astype(F32)
        for k in range(3):
            total = total + bufs.z[self.slot, k, :, cols].astype(F32)
        bufs.total[self.two, :, cols] = total
        bufs.squares[0:1, cols] += jnp.sum(total * total, 0, keepdims=True)
        if not by_rows:
            self.copy(8).start()
        start_all(self.own(by_rows))
        for at in (5, 6, 7):
            self.copy(at).wait_send()

    def stage5(self, by_rows):
        if not by_rows:
            self.copy(8).wait()
        wait_all(self.own(by_rows))


def backward_kernel(plan, names, *refs):
    r = SimpleNamespace(**dict(zip(names, refs)))
    cube = plan.cube
    images = r.images.shape[0]
    loads = [
        (r.keep_z, r.vm_z),
        (r.shrink_whole, r.shrink_w),
        (r.keep_slope, r.vm_slope),
        (r.expand_whole, r.expand_w),
        (r.keep_m, r.vm_m),
        (r.keep_h1, r.vm_h1),
        (r.keep_o, r.vm_o),
        (r.keep_t, r.vm_t),
        (r.keep_p, r.vm_p),
        (r.keep_a, r.vm_a),
        (r.keep_h, r.vm_h),
        (r.joined_whole, r.expand_w),
    ]
    z_, shrink_, slope_, expand_, m_, h1_, o_, t_, p_, a_, h_, joined_ = range(12)
    top = LAYERS - 1

    def fetch(which, layer):
        src, dst = loads[which]
        return pltpu.make_async_copy(src.at[layer], dst, r.loads.at[which])

    def start(layer, *which):
        for k in which:
            fetch(k, layer).start()

    def wait(layer, *which):
        for k in which:
            fetch(k, layer).wait()

    first_g = load(r.g_in, r.g, r.loads.at[joined_ + 1])
    start(top, *range(joined_))
    if cube:
        cube_barrier(plan)
        r.squares[...] = jnp.zeros_like(r.squares)
        head_rows = SmallGather(plan, r.head_block, r.head_rows, r.head_send, r.head_recv)
        head_rows.stage0()
    r.vectors[...] = jnp.zeros_like(r.vectors)
    r.vectors[FINAL : FINAL + 2] = r.tail_in[1:3]
    first_g.wait()

    def tick(it, kind):
        unit = 3 * it + kind
        if not cube:
            copies = [
                pltpu.make_async_copy(r.unit.at[(unit % 4, SEND)[i]], r.full.at[unit, i], r.loads.at[joined_ + 1 + i])
                for i in range(2)
            ]
            start_all(copies)
            wait_all(copies)
            return

        def when(back, do):
            if kind >= back:
                do()
            else:
                pl.when(unit >= back)(do)

        def by_rows(back):
            return (kind - back) % 3 == 0

        when(1, lambda: Reduce(plan, r, unit - 1).stage1())
        Reduce(plan, r, unit).stage0()
        when(2, lambda: Reduce(plan, r, unit - 2).stage2())
        when(3, lambda: Reduce(plan, r, unit - 3).stage3())
        when(5, lambda: Reduce(plan, r, unit - 5).stage5(by_rows(5)))
        when(4, lambda: Reduce(plan, r, unit - 4).stage4(by_rows(4)))

    def sent(unit):
        if cube:
            pl.when(unit > 0)(lambda: Reduce(plan, r, unit - 1).copy(0).wait_send())

    low_lane = lax.broadcasted_iota(jnp.int32, (PAD, 128), 1) < HEAD_DIM
    scale = HEAD_DIM**-0.5

    @pl.loop(0, LAYERS)
    def _(it):
        layer = top - it
        below = it < LAYERS - 1
        base = S + 2 + 4 * layer
        r.gr[...] = r.g[...].astype(BF)
        wait(layer, z_)
        slot = (3 * it) % 4
        sent(3 * it)

        @pl.loop(0, 8)
        def _(j):
            cols = pl.ds(pl.multiple_of(j * (D // 2), 128), D // 2)
            store_rows(plan, r.unit, slot, j, dot(r.vm_z[:, cols], r.gr[...], TN))

        tick(it, 0)
        if cube:
            pl.when(it == 0)(head_rows.stage1)
            pl.when(it == 1)(head_rows.finish)
        wait(layer, shrink_, slope_, expand_, m_, h1_)
        pl.when(below)(lambda: start(layer - 1, z_))
        slot_e = (3 * it + 1) % 4
        r.g1[...] = jnp.zeros_like(r.g1)
        sent(3 * it + 1)

        @pl.loop(0, 4)
        def _(j):
            cols = pl.ds(pl.multiple_of(j * D, 128), D)
            dz = dot(r.gr[...], r.shrink_w[j].reshape(D, D), NT)
            du = (dz * r.vm_slope[:, cols].astype(F32)).astype(BF)
            r.g1[...] += dot(du, weight(r.expand_w, j * D, D), NT)
            store_cols(plan, r.unit, slot_e, j, D, dot(r.vm_m[...], du, TN))

        start(layer, joined_)
        pl.when(below)(lambda: start(layer - 1, shrink_, slope_, m_))
        tick(it, 1)
        if cube:
            pl.when(it == 0)(head_rows.stage2)
        d_h1, d_gain, d_shift = normalize_back(r.vm_h1[...], row(r.params, base + 2), r.g1[...])
        r.g1[...] = r.g[...] + d_h1
        r.vectors[pl.ds(base + 2, 1)] = d_gain
        r.vectors[pl.ds(base + 3, 1)] = d_shift
        pl.when(below)(lambda: start(layer - 1, h1_))

        r.gr[...] = r.g1[...].astype(BF)
        slot_t = (3 * it + 2) % 4
        wait(layer, o_)
        sent(3 * it + 2)
        store_cols(plan, r.unit, slot_t, 3, D, dot(r.vm_o[...], r.gr[...], TN))
        wait(layer, joined_)
        r.do[...] = dot(r.gr[...], weight(r.expand_w, 3 * D, D), NT).astype(BF)
        wait(layer, t_, p_, a_, h_)

        @pl.loop(0, images * (HEADS // 2))
        def _(step):
            image, pair = step // (HEADS // 2), step % (HEADS // 2)
            rows = pl.ds(pl.multiple_of(image * PAD, 16), PAD)
            lanes = [pl.ds(pl.multiple_of(pair * 128 + part * D, 128), 128) for part in range(3)]
            q, key, v = (r.vm_t[rows, lane] for lane in lanes)
            do = r.do[rows, lanes[0]]
            zero = jnp.zeros_like(v)
            dqs, dks, dvs = [], [], []
            for which in range(2):
                part = jnp.where(low_lane, v, zero) if which == 0 else jnp.where(low_lane, zero, v)
                p_low = r.vm_p[step * 2 + which]
                p = p_low.astype(F32)
                dvs.append(dot(p_low, do))
                dp = dot(part, do, NT)
                ds = (p * (dp - jnp.sum(p * dp, 0, keepdims=True))).astype(BF)
                dqs.append(dot(ds, key, TN))
                dks.append(dot(ds, q))
            r.dt[rows, lanes[0]] = (jnp.where(low_lane, dqs[0], dqs[1]) * scale).astype(BF)
            r.dt[rows, lanes[1]] = (jnp.where(low_lane, dks[0], dks[1]) * scale).astype(BF)
            r.dt[rows, lanes[2]] = jnp.where(low_lane, dvs[0], dvs[1]).astype(BF)

        pl.when(below)(lambda: start(layer - 1, o_, t_, p_))
        r.g[...] = jnp.zeros_like(r.g)

        @pl.loop(0, 3)
        def _(j):
            cols = pl.ds(pl.multiple_of(j * D, 128), D)
            store_cols(plan, r.unit, slot_t, j, D, dot(r.vm_a[...], r.dt[:, cols], TN))
            r.g[...] += dot(r.dt[:, cols], weight(r.expand_w, j * D, D), NT)

        tick(it, 2)
        if cube:
            pl.when(it == 0)(head_rows.stage3)
        d_h, d_gain, d_shift = normalize_back(r.vm_h[...], row(r.params, base), r.g[...])
        r.g[...] = r.g1[...] + d_h
        r.vectors[pl.ds(base, 1)] = d_gain
        r.vectors[pl.ds(base + 1, 1)] = d_shift
        pl.when(below)(lambda: start(layer - 1, a_, h_, expand_))

    slot = UNITS % 4
    sent(jnp.int32(UNITS))
    for part in range(2):
        half = D // 2
        value = jnp.zeros((D, half), F32)
        for image in range(images):
            rows = r.g[image * PAD + 1 : image * PAD + S, part * half : (part + 1) * half]
            value = value + dot(r.images[image], rows.astype(BF), TN)
        store_cols(plan, r.unit, slot, part, half, value, half)
    pos = r.g[:PAD]
    for image in range(1, images):
        pos = pos + r.g[image * PAD : (image + 1) * PAD]
    r.vectors[:S] = pos[:S]
    r.vectors[S : S + 1] = pos[:1]
    r.vectors[S + 1 : S + 2] = jnp.sum(pos[1:S], 0, keepdims=True)
    if not cube:
        copies = [
            pltpu.make_async_copy(r.unit.at[(slot, SEND)[i]], r.full.at[UNITS, i], r.loads.at[i])
            for i in range(2)
        ]
        copies.append(pltpu.make_async_copy(r.vectors, r.vector_rows, r.loads.at[2]))
        start_all(copies)
        wait_all(copies)
        return
    store_vectors(plan, r.unit, slot, r.vectors[...])

    def stage(unit, which):
        width = WIDTH if unit < UNITS else TAIL
        done = Reduce(plan, r, jnp.int32(unit), width)
        by_rows = unit % 3 == 0 and unit < UNITS
        (
            done.stage0,
            done.stage1,
            done.stage2,
            done.stage3,
            lambda: done.stage4(by_rows),
            lambda: done.stage5(by_rows),
        )[which]()

    for ahead in range(5):
        for which in (1, 0, 2, 3, 5, 4):
            unit = UNITS + ahead - which
            if unit <= UNITS:
                stage(unit, which)
    r.tail_block[:BLOCK] = r.total[UNITS % 2, :, D // 2 : TAIL]
    line = lax.broadcasted_iota(jnp.int32, (8, 128), 0)
    squares, loss = jnp.sum(r.squares[...]), r.tail_in[0:1, 0:128]
    r.tail_block[BLOCK:] = jnp.where(line == 0, squares, jnp.where(line == 1, loss, 0.0))
    gather = SmallGather(plan, r.tail_block, r.vector_rows, r.tail_send, r.tail_recv)
    gather.stage0()
    gather.stage1()
    gather.stage2()
    gather.stage3()
    stage(UNITS, 5)
    Reduce(plan, r, jnp.int32(UNITS), TAIL).copy(0).wait_send()
    gather.finish()


def backward(plan, images, params, done):
    rows = done.g.shape[0]
    shapes = saved_shapes(rows)
    inputs = given_in(VMEM_SPEC, images=images, params=params, tail_in=done.tail)
    if plan.cube:
        inputs.update(given_in(VMEM_SPEC, head_block=done.head_block))
    inputs.update(
        given_in(
            ANY_SPEC,
            g_in=done.g,
            joined_whole=done.joined_whole,
            expand_whole=done.expand_whole,
            shrink_whole=done.shrink_whole,
        )
    )
    inputs.update({"keep_" + name: (getattr(done, "keep_" + name), ANY_SPEC) for name in SAVED})
    if plan.cube:
        outputs = dict(
            owned=((UNITS, 2, HALF, WIDTH), F32, ANY_SPEC),
            patch=((2, HALF, D // 2), F32, ANY_SPEC),
            vector_rows=(CHIPS + (2, BLOCK + 8, 128), F32, ANY_SPEC),
            head_rows=(CHIPS + (2, HEAD_BLOCK, 128), F32, ANY_SPEC),
        )
    else:
        outputs = dict(
            full=((UNITS + 1, 2, 4, 4, BLOCK, WIDTH), BF, ANY_SPEC),
            vector_rows=((VEC_ROWS, D), F32, ANY_SPEC),
        )
    scratch = {"vm_" + name: pltpu.VMEM(shape, kind) for name, (shape, kind) in shapes.items()}
    scratch.update(
        vmem(
            BF,
            expand_w=cols_shape(FF),
            shrink_w=ROWS_SHAPE,
            gr=(rows, D),
            do=(rows, D),
            dt=(rows, 3 * D),
            unit=(SEND + 1, 4, 4, BLOCK, WIDTH),
        )
    )
    scratch.update(vmem(F32, g=(rows, D), g1=(rows, D), vectors=(VEC_ROWS, D)))
    scratch.update(dma(loads=(15,)))
    extra = {}
    if plan.cube:
        scratch.update(
            vmem(
                BF,
                core=(4, 4, BLOCK, WIDTH),
                near=(3, 4, BLOCK, WIDTH // 2),
                far=(3, 4, BLOCK, WIDTH // 2),
                x=(3, 4, BLOCK, WIDTH),
                y=(3, 4, BLOCK, WIDTH),
                z=(4, 3, BLOCK, WIDTH),
                line=(2, 4, BLOCK, WIDTH),
            )
        )
        scratch.update(
            vmem(F32, total=(2, BLOCK, WIDTH), squares=(8, WIDTH), tail_block=(BLOCK + 8, 128))
        )
        scratch.update(
            dma(send=(4, 11), recv=(4, 11), head_send=(7,), head_recv=(7,), tail_send=(7,), tail_recv=(7,))
        )
        scratch.update(credit=pltpu.SemaphoreType.REGULAR)
        extra = dict(collective_id=2, has_side_effects=True)
    return pallas(functools.partial(backward_kernel, plan), "backward", inputs, outputs, scratch, **extra)


PARAMS = ("patch", "triple", "output", "expand", "shrink", "vector", "head")
KINDS = ("w_", "m_", "s_")


def adam_update(master, moment, square, gradient, step_rate):
    moment_new = BETA_ONE * moment + (1.0 - BETA_ONE) * gradient
    square_new = BETA_TWO * square + (1.0 - BETA_TWO) * gradient * gradient
    moment_hat = moment_new / (1.0 - BETA_ONE**STEP_INDEX)
    square_hat = square_new / (1.0 - BETA_TWO**STEP_INDEX)
    master_new = master - step_rate * (
        moment_hat / (jnp.sqrt(square_hat) + ADAM_EPS) + DECAY * master
    )
    return (master_new, moment_new, square_new)


def head_matrices(ref, images):
    def take(first, count):
        devices = ref.shape[0] // HEAD_BLOCK
        pieces = [
            jnp.concatenate(
                [
                    ref[pl.ds(image * 14 + first + j, devices, stride=HEAD_BLOCK), :]
                    for j in range(count)
                ],
                1,
            )
            for image in range(images)
        ]
        return jnp.concatenate(pieces, 0).astype(BF)

    return take(0, 6), take(6, 8)


def update_kernel(images, names, *refs):
    r = SimpleNamespace(**dict(zip(names, refs)))
    named = dict(zip(names, refs))
    groups = [
        [(named[kind + name], named["vm_" + kind + name], named["to_" + kind + name]) for kind in KINDS]
        for name in PARAMS
    ]
    patch, triple, output, expand, shrink, vector, head = range(7)

    def moves(group, back):
        return [
            pltpu.make_async_copy(*((buf, out) if back else (src, buf)), r.sems.at[3 * group + k])
            for k, (src, buf, out) in enumerate(groups[group])
        ]

    order = (head, shrink, expand, triple, output, patch, vector)
    for group in order:
        start_all(moves(group, False))

    tile = jnp.sum(r.tails[:, BLOCK:, :], 0)
    features, d_logits = head_matrices(r.head_rows, images)
    r.features[...] = features
    r.d_logits[...] = d_logits
    alike = (dot(features, features, NT) + 1.0) * dot(d_logits, d_logits, NT)
    norm = jnp.sqrt(tile[0:1, 0:1] + jnp.sum(alike))
    clip = CLIP / jnp.maximum(norm, CLIP)
    line = lax.broadcasted_iota(jnp.int32, (8, 128), 0)
    r.scalars[...] = jnp.where(line == 0, norm, tile[1:2])

    def step(group, at, gradient, rate):
        bufs = [buf for _, buf, _ in groups[group]]
        new = adam_update(*[buf[at] for buf in bufs], gradient * clip, rate)
        for buf, value in zip(bufs, new):
            buf[at] = value

    def finish(group):
        start_all(moves(group, True))

    every = slice(None)
    wait_all(moves(head, False))

    @pl.loop(0, D // 128)
    def _(j):
        rows = pl.ds(pl.multiple_of(j * 128, 128), 128)
        gradient = dot(r.features[:, rows], r.d_logits[...], TN)
        step(head, (rows, every), gradient[:, :CLASSES], RATE_MATRIX)

    bias = jnp.sum(d_logits.astype(F32), 0, keepdims=True)[:, :CLASSES]
    step(head, (slice(D, D + 1), every), bias, RATE_MATRIX)
    r.bias_grad[...] = bias * clip
    finish(head)
    wait_all(moves(shrink, False))

    @pl.loop(0, LAYERS)
    def _(layer):
        unit = 3 * (LAYERS - 1 - layer)
        for k in range(4):
            gradient = r.owned[unit, k % 2, :, pl.ds(k // 2 * D, D)]
            step(shrink, (layer, pl.ds(k * HALF, HALF), every), gradient, RATE_MATRIX)

    finish(shrink)
    wait_all(moves(expand, False))

    @pl.loop(0, LAYERS)
    def _(layer):
        unit = 3 * (LAYERS - 1 - layer) + 1
        for k in range(2):
            step(expand, (layer, every, pl.ds(k * WIDTH, WIDTH)), r.owned[unit, k], RATE_MATRIX)

    finish(expand)
    wait_all(moves(triple, False))
    wait_all(moves(output, False))

    @pl.loop(0, LAYERS)
    def _(layer):
        unit = 3 * (LAYERS - 1 - layer) + 2
        step(triple, (layer, every, pl.ds(0, WIDTH)), r.owned[unit, 0], RATE_MATRIX)
        step(triple, (layer, every, pl.ds(WIDTH, D)), r.owned[unit, 1, :, pl.ds(0, D)], RATE_MATRIX)
        step(output, (layer, every, every), r.owned[unit, 1, :, pl.ds(D, D)], RATE_OUTPUT)

    finish(triple)
    finish(output)
    wait_all(moves(patch, False))
    for k in range(2):
        step(patch, (every, pl.ds(k * (D // 2), D // 2)), r.patch_grad[k], RATE_MATRIX)
    finish(patch)
    count = groups[vector][0][0].shape[0]
    for d in range(-(-count // 8)):
        for j in range(6):
            r.vector_grad[8 * d : 8 * d + 8, 128 * j : 128 * j + 128] = r.tails[d, 8 * j : 8 * j + 8, :]
    wait_all(moves(vector, False))
    step(vector, (every, every), r.vector_grad[:count], RATE_VECTOR)
    finish(vector)
    for group in order:
        wait_all(moves(group, True))


def update(plan, images, states, got):
    inputs, outputs, scratch = {}, {}, {}
    for name, state in zip(PARAMS, states):
        for kind, value in zip(KINDS, state):
            inputs[kind + name] = (value, ANY_SPEC)
            outputs["to_" + kind + name] = (value.shape, F32, ANY_SPEC)
            scratch["vm_" + kind + name] = pltpu.VMEM(value.shape, F32)
    inputs.update(
        given_in(
            VMEM_SPEC,
            owned=got.owned,
            patch_grad=got.patch,
            tails=got.vector_rows.reshape(plan.n, BLOCK + 8, 128),
            head_rows=got.head_rows.reshape(plan.n * HEAD_BLOCK, 128),
        )
    )
    outputs.update(scalars=((8, 128), F32, VMEM_SPEC), bias_grad=((1, CLASSES), F32, VMEM_SPEC))
    scratch.update(vmem(BF, features=(plan.n * images, D), d_logits=(plan.n * images, 1024)))
    scratch.update(vmem(F32, vector_grad=(VEC_ROWS, D)))
    scratch.update(dma(sems=(3 * len(PARAMS),)))
    new = pallas(functools.partial(update_kernel, images), "update", inputs, outputs, scratch)
    states = [[getattr(new, "to_" + kind + name) for kind in KINDS] for name in PARAMS]
    return new.scalars[0, 0], new.scalars[1, 0], states, new.bias_grad[0]


AXES = ("wide", "grp")


def update_whole(plan, images, states, got, done):
    full = got.full.reshape(UNITS + 1, 2, 16, BLOCK, WIDTH)
    layers = full[:UNITS].reshape(LAYERS, 3, 2, 16, BLOCK, WIDTH)[::-1]

    def scattered(whole):
        axis = whole.ndim - 2
        return lax.psum_scatter(whole, AXES, scatter_dimension=axis, tiled=True).astype(F32)

    def from_cols(part):
        joined = jnp.concatenate([part[..., 0, :, :, :], part[..., 1, :, :, :]], -1)
        return joined.reshape(part.shape[:-4] + (D, -1))

    shrink = layers[:, 0].reshape(LAYERS, 2, 16, BLOCK, 2, D).transpose(0, 2, 1, 4, 3, 5)
    joined = scattered(from_cols(layers[:, 2]))
    rows_all = lax.all_gather(done.head_block, AXES, axis=0)[:, : 14 * images]
    rows_all = rows_all.reshape(plan.n * images, 14 * 128).astype(BF)
    features, d_logits = rows_all[:, :D], rows_all[:, D : D + CLASSES]
    bias = jnp.sum(d_logits.astype(F32), 0)[None]
    split = [
        scattered(from_cols(full[UNITS, ..., : D // 2])),
        joined[:, :, : 3 * D],
        joined[:, :, 3 * D :],
        scattered(from_cols(layers[:, 1])),
        scattered(shrink.reshape(LAYERS, FF, D)),
    ]
    same = [
        lax.psum(got.vector_rows[: states[5][0].shape[0]], AXES),
        jnp.concatenate([dot(features, d_logits, TN), bias], 0),
    ]
    squares = lax.psum(sum(jnp.sum(g * g) for g in split), AXES) + sum(jnp.sum(g * g) for g in same)
    norm = jnp.sqrt(squares)
    clip = CLIP / jnp.maximum(norm, CLIP)
    rates = [RATE_MATRIX] * 2 + [RATE_OUTPUT] + [RATE_MATRIX] * 2 + [RATE_VECTOR, RATE_MATRIX]
    states = [
        adam_update(*state, gradient * clip, rate)
        for state, gradient, rate in zip(states, split + same, rates)
    ]
    return norm, lax.psum(done.tail[0, 0], AXES), states, bias[0] * clip


def per_device(plan, images, slot_mask, labels, *params):
    states = [params[3 * k : 3 * k + 3] for k in range(7)]
    patch, triple, output, expand, shrink, vector, head = (state[0] for state in states)
    count = images.shape[0]
    pad_rows = ((0, HEAD_ROWS - count), (0, 0))
    weights = slot_mask.astype(F32)
    args = dict(
        images=images,
        vectors=vector,
        head=head,
        labels=jnp.pad(labels[:, None], pad_rows),
        weights=jnp.pad(weights[:, None], pad_rows),
    )
    if plan.cube:
        shards = dict(patch=patch, triple=triple, output=output, expand=expand, shrink=shrink)
        done = forward(plan, shards, args, None, None)
    else:

        def whole(shard, shape):
            axis = shard.ndim - 2
            gathered = lax.all_gather(shard.astype(BF), AXES, axis=axis, tiled=True)
            return gathered.reshape(shard.shape[:axis] + shape)

        gathered = [
            whole(patch, cols_shape(D)),
            whole(jnp.concatenate([triple, output], 2), cols_shape(FF)),
            whole(expand, cols_shape(FF)),
            whole(shrink, ROWS_SHAPE),
        ]
        total = jnp.full((8, 128), lax.psum(jnp.sum(weights), AXES), F32)
        done = forward(plan, None, args, gathered, total)
    got = backward(plan, images, vector, done)
    if plan.cube:
        norm, loss, states, bias_grad = update(plan, count, states, got)
    else:
        norm, loss, states, bias_grad = update_whole(plan, count, states, got, done)
    return (
        loss,
        done.total[0, 0],
        norm,
        *(value for state in states for value in state),
        bias_grad,
    )


def solution(mesh):
    plan = Plan(mesh)
    rows = P(AXES, None)
    layers = P(None, AXES, None)
    in_specs = (P(AXES, None, None), P(AXES), P(AXES)) + (rows,) * 3 + (layers,) * 12 + (P(),) * 6
    out_specs = (P(),) * 3 + (rows,) * 3 + (layers,) * 12 + (P(),) * 7
    return jax.shard_map(
        functools.partial(per_device, plan),
        mesh=mesh,
        in_specs=in_specs,
        out_specs=out_specs,
        check_vma=False,
    )
```

```python
import functools
from types import SimpleNamespace

import jax
import jax.numpy as jnp
from jax import lax
from jax.experimental import pallas as pl
from jax.experimental.pallas import tpu as pltpu
from jax.sharding import PartitionSpec as P

D = 768
HEADS = 12
HEAD_DIM = 64
FF = 3072
CLASSES = 1000
LAYERS = 3
STEP_INDEX = 10
S = 197
PAD = 208

EPS_NORM = 1e-06
CLIP = 0.1
BETA_ONE = 0.9
BETA_TWO = 0.95
ADAM_EPS = 1e-08
DECAY = 0.05
RATE_MATRIX = 0.03
RATE_OUTPUT = 0.2
RATE_VECTOR = 0.3
SMOOTH = 0.1

F32 = jnp.float32
BF = jnp.bfloat16
NN = (((1,), (0,)), ((), ()))
NT = (((1,), (1,)), ((), ()))
TN = (((0,), (0,)), ((), ()))
VMEM_SPEC = pl.BlockSpec(memory_space=pltpu.VMEM)
ANY_SPEC = pl.BlockSpec(memory_space=pl.ANY)
LIMIT = 61 * 1024 * 1024


def dot(left, right, form=NN):
    return lax.dot_general(left, right, form, preferred_element_type=F32)


def normalize(values, gain_row, shift_row):
    center = values - jnp.mean(values, -1, keepdims=True)
    spread = jnp.mean(center * center, -1, keepdims=True)
    return center * lax.rsqrt(spread + EPS_NORM) * gain_row + shift_row


def normalize_back(values, gain_row, grad):
    center = values - jnp.mean(values, -1, keepdims=True)
    spread = jnp.mean(center * center, -1, keepdims=True)
    scale = lax.rsqrt(spread + EPS_NORM)
    unit = center * scale
    d_unit = grad * gain_row
    d_values = scale * (
        d_unit
        - jnp.mean(d_unit, -1, keepdims=True)
        - unit * jnp.mean(d_unit * unit, -1, keepdims=True)
    )
    return (
        d_values,
        jnp.sum(grad * unit, 0, keepdims=True),
        jnp.sum(grad, 0, keepdims=True),
    )


def gelu_and_slope(u):
    x = jnp.abs(u) * 0.7071067811865476
    t = 1.0 / (1.0 + 0.3275911 * x)
    series = t * (
        0.254829592
        + t * (-0.284496736 + t * (1.421413741 + t * (-1.453152027 + t * 1.061405429)))
    )
    bell = jnp.exp(-0.5 * u * u)
    tail = 0.5 * series * bell
    share = jnp.where(u >= 0.0, 1.0 - tail, tail)
    return u * share, share + u * bell * 0.3989422804014327


class Plan:
    def __init__(self, mesh):
        self.wide, self.grp = mesh.shape["wide"], mesh.shape["grp"]
        self.n = self.wide * self.grp
        self.cube = self.wide == 8 and self.grp == 4

    def where(self):
        if not self.cube:
            return 0, 0, 0, 0
        wide, grp = lax.axis_index("wide"), lax.axis_index("grp")
        return wide // 2, wide % 2, grp // 2, grp % 2


CHIPS = (4, 2, 2)
BLOCK = D // 16
BLOCK_FF = FF // 32


def cols_shape(columns):
    return CHIPS + (BLOCK, columns)


ROWS_SHAPE = CHIPS + (2, BLOCK_FF, D)


def other_part(width):
    return width // 6 // 128 * 128


def cut_of(columns):
    return columns // 2 // 128 * 128


def over_links(plan):
    z, x, y, c = plan.where()

    def at(z, x, y, c):
        return (z * 2 + x, y * 2 + c)

    return SimpleNamespace(
        z1=at(jnp.bitwise_xor(z, 1), x, y, c),
        z3=at(jnp.bitwise_xor(z, 3), x, y, c),
        x=at(z, 1 - x, y, c),
        y=at(z, x, 1 - y, c),
        core=at(z, x, y, 1 - c),
    )


def remote(src, dst, send, recv, to):
    return pltpu.make_async_remote_copy(
        src_ref=src,
        dst_ref=dst,
        send_sem=send,
        recv_sem=recv,
        device_id=to,
        device_id_type=pl.DeviceIdType.MESH,
    )


class Gather:
    def __init__(self, plan, by_cols, block, whole, send, recv):
        self.z, self.x, self.y, self.c = plan.where()
        self.to = over_links(plan)
        self.by_cols, self.block, self.whole = by_cols, block, whole
        self.send, self.recv = send, recv
        self.width = block.shape[-1]
        self.other = other_part(self.width)
        self.most = self.width - self.other

    def region(self, z, x, y, start, width):
        if self.by_cols:
            first = pl.multiple_of(self.c * self.width + start, 128)
            return self.whole.at[z, x, y, :, pl.ds(first, width)]
        return self.whole.at[z, x, y, self.c, :, pl.ds(start, width)]

    def part(self, start, width):
        return self.block.at[:, pl.ds(start, width)]

    def copy(self, at):
        z, x, y, to = self.z, self.x, self.y, self.to
        z1, z3, line = jnp.bitwise_xor(z, 1), jnp.bitwise_xor(z, 3), slice(None)
        most, other, region = self.most, self.other, self.region
        cut, cut_other = cut_of(most), most + max(cut_of(other), 128)
        landed = at
        if at in (0, 1):
            src, dst = self.part(0, most), region(z, x, y, 0, most)
            device = (to.z1, to.z3)[at]
        elif at in (8, 9):
            src, dst = self.part(most, other), region(z, x, y, most, other)
            device = (to.x, to.y)[at - 8]
        else:
            src, device = {
                2: lambda: (region(z3, x, y, 0, most), to.z1),
                3: lambda: (region(z1, x, y, 0, most), to.z3),
                4: lambda: (region(line, x, y, 0, most), to.x),
                5: lambda: (region(line, x, y, 0, most), to.y),
                6: lambda: (region(line, x, 1 - y, 0, cut), to.x),
                7: lambda: (region(line, 1 - x, y, cut, most - cut), to.y),
                10: lambda: (region(z, x, 1 - y, most, cut_other - most), to.x),
                11: lambda: (region(z, 1 - x, y, cut_other, self.width - cut_other), to.y),
                12: lambda: (region(z, line, line, most, other), to.z1),
                13: lambda: (region(z, line, line, most, other), to.z3),
                14: lambda: (region(z3, line, line, most, other), to.z1),
                15: lambda: (region(z1, line, line, most, other), to.z3),
                16: lambda: (region(line, x, y, 0, most), to.core),
                17: lambda: (region(line, 1 - x, y, 0, most), to.core),
                18: lambda: (region(line, x, 1 - y, 0, most), to.core),
                19: lambda: (region(line, 1 - x, 1 - y, 0, cut), to.core),
                20: lambda: (region(line, 1 - x, 1 - y, cut, most - cut), to.core),
                21: lambda: (region(line, line, line, most, other), to.core),
            }[at]()
            dst = src
            if at in (3, 15):
                landed = at - 1
        return remote(src, dst, self.send.at[at], self.recv.at[landed], device)

    def exists(self, at):
        if at in (8, 9, 10, 12, 13, 14, 15, 21):
            return self.other > 0
        return at != 11 or self.other > 128

    def keep(self):
        here = self.region(self.z, self.x, self.y, 0, self.width)
        return pltpu.make_async_copy(self.block, here, self.send.at[22])

    def start(self, *which):
        for at in which:
            if self.exists(at):
                self.copy(at).start()

    def arrived(self, *which):
        for at in which:
            if self.exists(at):
                self.copy(at).wait_recv()

    def in_middle(self, do):
        pl.when((self.z == 1) | (self.z == 2))(do)

    def stage0(self):
        self.start(0, 1, 8, 9)
        self.keep().start()

    def stage1(self):
        self.arrived(0, 1)
        self.in_middle(lambda: self.start(2, 3))
        self.arrived(8, 9)
        self.start(10, 11)
        self.keep().wait()

    def stage2(self):
        self.arrived(2)
        self.start(4, 5, 16)
        self.arrived(10, 11)
        self.start(12, 13)

    def stage3(self):
        self.arrived(4, 5)
        self.start(6, 7, 17, 18)
        self.arrived(12, 13)
        self.in_middle(lambda: self.start(14, 15))

    def stage4(self):
        self.arrived(6, 7)
        self.start(19, 20)
        self.arrived(14)
        self.start(21)

    def finish(self):
        self.arrived(16, 17, 18, 19, 20, 21)
        passed = (2, 3, 14, 15)

        def sent(which):
            for at in which:
                if self.exists(at):
                    self.copy(at).wait_send()

        sent([at for at in range(22) if at not in passed])
        self.in_middle(lambda: sent(passed))


def cube_barrier(plan):
    z, x, y, c = plan.where()
    barrier = pltpu.get_barrier_semaphore()
    partners = [(jnp.bitwise_xor(z, k) * 2 + x, y * 2 + c) for k in (1, 2, 3)]
    partners += [
        (z * 2 + 1 - x, y * 2 + c),
        (z * 2 + x, (1 - y) * 2 + c),
        (z * 2 + x, y * 2 + 1 - c),
    ]
    for partner in partners:
        pl.semaphore_signal(barrier, inc=1, device_id=partner, device_id_type=pl.DeviceIdType.MESH)
    pl.semaphore_wait(barrier, len(partners))


def load(source, target, sem):
    copy = pltpu.make_async_copy(source, target, sem)
    copy.start()
    return copy


def start_all(copies):
    for copy in copies:
        copy.start()


def wait_all(copies):
    for copy in copies:
        copy.wait()


def weight(ref, first, width):
    cols = pl.ds(first if isinstance(first, int) else pl.multiple_of(first, 128), width)
    return ref[:, :, :, :, cols].reshape(D, width)


class SmallGather:
    def __init__(self, plan, block, whole, send, recv):
        self.z, self.x, self.y, self.c = plan.where()
        self.block, self.whole, self.send, self.recv = block, whole, send, recv

    def copy(self, at):
        z, x, y, c = self.z, self.x, self.y, self.c
        line = slice(None)
        if at < 3:
            src, dst = self.block, self.whole.at[z, x, y, c]
            to = (jnp.bitwise_xor(z, at + 1) * 2 + x, y * 2 + c)
        elif at == 3:
            src = dst = self.whole.at[line, x, y, c]
            to = (z * 2 + 1 - x, y * 2 + c)
        elif at == 4:
            src = dst = self.whole.at[line, line, y, c]
            to = (z * 2 + x, (1 - y) * 2 + c)
        else:
            src = dst = self.whole.at[line, line, line, c]
            to = (z * 2 + x, y * 2 + 1 - c)
        return pltpu.make_async_remote_copy(
            src_ref=src,
            dst_ref=dst,
            send_sem=self.send.at[at],
            recv_sem=self.recv.at[at],
            device_id=to,
            device_id_type=pl.DeviceIdType.MESH,
        )

    def keep(self):
        here = self.whole.at[self.z, self.x, self.y, self.c]
        return pltpu.make_async_copy(self.block, here, self.send.at[6])

    def stage0(self):
        for at in range(3):
            self.copy(at).start()
        self.keep().start()

    def stage1(self):
        for at in range(3):
            self.copy(at).wait_recv()
        self.keep().wait()
        self.copy(3).start()

    def stage2(self):
        self.copy(3).wait_recv()
        self.copy(4).start()

    def stage3(self):
        self.copy(4).wait_recv()
        self.copy(5).start()

    def finish(self):
        self.copy(5).wait_recv()
        for at in range(6):
            self.copy(at).wait_send()


FF_TILE = 512
HALF = BLOCK // 2
WIDTH = FF // 2
HEAD_ROWS = 16
HEAD_BLOCK = 32
FINAL = S + 2 + 4 * LAYERS


def saved_shapes(rows):
    heads = rows // PAD * HEADS
    return dict(
        h=((rows, D), F32),
        a=((rows, D), BF),
        t=((rows, 3 * D), BF),
        o=((rows, D), BF),
        p=((heads, PAD, PAD), BF),
        h1=((rows, D), F32),
        m=((rows, D), BF),
        z=((rows, FF), BF),
        slope=((rows, FF), BF),
    )


SAVED = tuple(saved_shapes(PAD))


def row(ref, at):
    return ref[pl.ds(at, 1)]


def share_shards(plan, r):
    z, x, y, c = plan.where()
    r.joined_f[:, :, : 3 * D] = r.triple[...]
    r.joined_f[:, :, 3 * D :] = r.output[...]
    mine = pl.ds(pl.multiple_of(c * HALF, 8), HALF)

    def part(core, width):
        return pl.ds(pl.multiple_of(core * width, 128), width)

    moves = [
        (r.patch.at[:, part(1 - c, D // 2)], r.patch_f.at[mine]),
        (r.joined_f.at[:, :, part(1 - c, WIDTH)], r.joined_b.at[:, mine]),
        (r.expand.at[:, :, part(1 - c, WIDTH)], r.expand_b.at[:, mine]),
    ]
    copies = [
        pltpu.make_async_remote_copy(
            src_ref=src,
            dst_ref=dst,
            send_sem=r.share_send.at[i],
            recv_sem=r.share_recv.at[i],
            device_id=(z * 2 + x, y * 2 + 1 - c),
            device_id_type=pl.DeviceIdType.MESH,
        )
        for i, (src, dst) in enumerate(moves)
    ]
    start_all(copies)
    r.patch_f[mine] = r.patch[:, part(c, D // 2)]
    r.joined_b[:, mine] = r.joined_f[:, :, part(c, WIDTH)]
    r.expand_b[:, mine] = r.expand[:, :, part(c, WIDTH)]
    r.shrink_block[...] = r.shrink[...].astype(BF)
    for copy, src, dst in zip(
        copies,
        (r.patch_f, r.joined_b, r.expand_b),
        (r.patch_block, r.joined_block, r.expand_block),
    ):
        copy.wait_recv()
        dst[...] = src[...].astype(BF)
    for copy in copies:
        copy.wait_send()


def head_part(r, image_total):
    images = r.h.shape[0] // PAD
    table = r.head[:D].astype(BF)
    r.first[...] = jnp.zeros_like(r.first)
    for image in range(images):
        r.first[image : image + 1] = r.h[image * PAD : image * PAD + 1]
    first = r.first[...]
    gain, shift = r.vectors[FINAL : FINAL + 1], r.vectors[FINAL + 1 : FINAL + 2]
    feature = normalize(first, gain, shift).astype(BF)
    logits = dot(feature, table) + r.head[D : D + 1]
    ids = lax.broadcasted_iota(jnp.int32, logits.shape, 1)
    shifted = logits - jnp.max(logits, -1, keepdims=True)
    log_prob = shifted - jnp.log(jnp.sum(jnp.exp(shifted), -1, keepdims=True))
    target = jnp.where(ids == r.labels[...], 1.0 - SMOOTH, 0.0) + SMOOTH / CLASSES
    weights = r.weights[...]
    loss = jnp.sum(weights * -jnp.sum(target * log_prob, -1, keepdims=True))
    d_logits = ((weights / image_total) * (jnp.exp(log_prob) - target)).astype(BF)
    d_feature = dot(d_logits, table, NT)
    r.d_logits[...] = jnp.zeros_like(r.d_logits)
    r.d_logits[:, :CLASSES] = d_logits.astype(F32)
    r.head_block[...] = jnp.zeros_like(r.head_block)
    feature = feature.astype(F32)
    for image in range(images):
        for j in range(6):
            at = image * 14 + j
            r.head_block[at : at + 1] = feature[image : image + 1, j * 128 : j * 128 + 128]
        for j in range(8):
            at = image * 14 + 6 + j
            r.head_block[at : at + 1] = r.d_logits[image : image + 1, j * 128 : j * 128 + 128]
    d_first, d_gain, d_shift = normalize_back(first, gain, d_feature)
    r.g[...] = jnp.zeros_like(r.g)
    for image in range(images):
        r.g[image * PAD : image * PAD + 1] = d_first[image : image + 1]
    r.tail[...] = jnp.zeros_like(r.tail)
    r.tail[0:1] = jnp.full((1, D), loss, F32)
    r.tail[1:2] = d_gain
    r.tail[2:3] = d_shift


def forward_kernel(plan, names, *refs):
    r = SimpleNamespace(**dict(zip(names, refs)))
    cube = plan.cube
    images = r.images.shape[0]
    patch, joined, expand, shrink = range(4)
    wholes = (r.patch_whole, r.joined_whole, r.expand_whole, r.shrink_whole)
    weights = (r.patch_w, r.joined_w, r.expand_w, r.shrink_w)
    if cube:
        blocks = (r.patch_block, r.joined_block, r.expand_block, r.shrink_block)
        cube_barrier(plan)
        share_shards(plan, r)
        r.count[...] = jnp.full((8, 128), jnp.sum(r.weights[...]), F32)
        counting = SmallGather(plan, r.count, r.counts, r.count_send, r.count_recv)

    def unit(kind, layer):
        if kind == patch:
            return Gather(plan, True, blocks[0], wholes[0], r.send.at[0], r.recv.at[0])
        at = 3 * layer + kind
        block, whole = blocks[kind].at[layer], wholes[kind].at[layer]
        return Gather(plan, kind != shrink, block, whole, r.send.at[at], r.recv.at[at])

    def ready(kind, layer):
        if cube:
            unit(kind, layer).finish()
        whole = wholes[kind] if kind == patch else wholes[kind].at[layer]
        return load(whole, weights[kind], r.loads.at[kind])

    held = (r.h, r.a, r.t, r.o, r.p, r.h1, r.m, r.z, r.slope)
    kept = (r.keep_h, r.keep_a, r.keep_t, r.keep_o, r.keep_p, r.keep_h1, r.keep_m, r.keep_z, r.keep_slope)
    h_, a_, t_, o_, p_, h1_, m_, z_, slope_ = range(9)

    def saves(layer, *which):
        return [pltpu.make_async_copy(held[k], kept[k].at[layer], r.saves.at[k]) for k in which]

    if cube:
        first = [unit(patch, 0), unit(joined, 0), unit(expand, 0), unit(shrink, 0), unit(joined, 1)]
        first[0].stage0()
        counting.stage0()
        first[1].stage0()
        first[0].stage1()
        first[2].stage0()
        first[1].stage1()
        first[0].stage2()
        first[3].stage0()
        first[2].stage1()
        first[1].stage2()
        first[0].stage3()
        first[4].stage0()
        first[3].stage1()
        first[2].stage2()
        first[1].stage3()
        first[0].stage4()
    ready(patch, 0).wait()
    for image in range(images):
        at = image * PAD
        r.h[at : at + 1] = r.vectors[0:1] + r.vectors[S : S + 1]
        embedded = dot(r.images[image], weight(r.patch_w, 0, D))
        r.h[at + 1 : at + S] = embedded + r.vectors[S + 1 : S + 2] + r.vectors[1:S]
        r.h[at + S : at + PAD] = jnp.zeros((PAD - S, D), F32)

    low_lane = lax.broadcasted_iota(jnp.int32, (PAD, 128), 1) < HEAD_DIM
    real_key = lax.broadcasted_iota(jnp.int32, (PAD, PAD), 0) < S

    @pl.loop(0, LAYERS)
    def _(layer):
        more = layer < LAYERS - 1
        base = S + 2 + 4 * layer
        if cube:
            @pl.when(more)
            def _():
                unit(expand, layer + 1).stage0()
                unit(joined, layer + 1).stage1()

            unit(shrink, layer).stage2()
            unit(expand, layer).stage3()
            unit(joined, layer).stage4()
        start_all(saves(layer, h_))

        @pl.when(layer > 0)
        def _():
            wait_all(saves(layer, a_, t_, o_, p_, h1_, m_))

        r.a[...] = normalize(r.h[...], row(r.vectors, base), row(r.vectors, base + 1)).astype(BF)
        ready(joined, layer).wait()

        @pl.loop(0, 3)
        def _(j):
            cols = pl.ds(pl.multiple_of(j * D, 128), D)
            r.t[:, cols] = dot(r.a[...], weight(r.joined_w, j * D, D)).astype(BF)

        start_all(saves(layer, a_, t_))

        def heads(step):
            image, pair = step // (HEADS // 2), step % (HEADS // 2)
            rows = pl.ds(pl.multiple_of(image * PAD, 16), PAD)
            lanes = [pl.ds(pl.multiple_of(pair * 128 + part * D, 128), 128) for part in range(3)]
            q, key, v = (r.t[rows, lane] for lane in lanes)
            zero = jnp.zeros_like(key)
            outs = []
            for which in range(2):
                part = jnp.where(low_lane, key, zero) if which == 0 else jnp.where(low_lane, zero, key)
                scores = dot(part, q, NT) * HEAD_DIM**-0.5
                scores = jnp.where(real_key, scores, -1e30)
                top = jnp.max(scores, 0, keepdims=True)
                e = jnp.exp(scores - top)
                p = (e * (1.0 / jnp.sum(e, 0, keepdims=True))).astype(BF)
                r.p[step * 2 + which] = p
                outs.append(dot(p, v, TN))
            r.o[rows, lanes[0]] = jnp.where(low_lane, outs[0], outs[1]).astype(BF)

        half = images * (HEADS // 2) // 2
        pl.loop(0, half)(heads)
        if cube:
            @pl.when(more)
            def _():
                unit(shrink, layer + 1).stage0()
                unit(expand, layer + 1).stage1()
                unit(joined, layer + 1).stage2()

        pl.loop(half, 2 * half)(heads)
        start_all(saves(layer, o_, p_))
        r.h1[...] = r.h[...] + dot(r.o[...], weight(r.joined_w, 3 * D, D))
        start_all(saves(layer, h1_))
        if cube:
            unit(shrink, layer).stage3()
            unit(expand, layer).stage4()
            pl.when(layer == 0)(counting.stage1)
            pl.when(layer == 1)(counting.stage3)
        r.m[...] = normalize(r.h1[...], row(r.vectors, base + 2), row(r.vectors, base + 3)).astype(BF)
        start_all(saves(layer, m_))
        wait_all(saves(layer, h_))
        r.h[...] = r.h1[...]

        @pl.when(layer > 0)
        def _():
            wait_all(saves(layer, z_, slope_))

        ready(expand, layer).wait()

        @pl.loop(0, FF // FF_TILE)
        def _(j):
            cols = pl.ds(pl.multiple_of(j * FF_TILE, 128), FF_TILE)
            u = dot(r.m[...], weight(r.expand_w, j * FF_TILE, FF_TILE))
            z, slope = gelu_and_slope(u)
            r.z[:, cols] = z.astype(BF)
            r.slope[:, cols] = slope.astype(BF)

        start_all(saves(layer, z_, slope_))
        if cube:
            pl.when(layer < LAYERS - 2)(lambda: unit(joined, layer + 2).stage0())

            @pl.when(more)
            def _():
                unit(shrink, layer + 1).stage1()
                unit(expand, layer + 1).stage2()
                unit(joined, layer + 1).stage3()

            unit(shrink, layer).stage4()
            pl.when(layer == 0)(counting.stage2)
            pl.when(layer == 1)(counting.finish)
        ready(shrink, layer).wait()

        @pl.loop(0, 4)
        def _(j):
            cols = pl.ds(pl.multiple_of(j * D, 128), D)
            r.h[...] += dot(r.z[:, cols], r.shrink_w[j].reshape(D, D))

    if cube:
        r.total[...] = jnp.sum(r.counts[...].reshape(-1, 8, 128), 0)
        image_total = r.total[0:1, 0:1]
    else:
        image_total = r.count_in[0:1, 0:1]
    head_part(r, image_total)
    wait_all(saves(LAYERS - 1, a_, t_, o_, p_, h1_, m_, z_, slope_))


def pallas(kernel, name, inputs, outputs, scratch, **params):
    names = list(inputs) + list(outputs) + list(scratch)
    outs = pl.pallas_call(
        functools.partial(kernel, names),
        out_shape=[jax.ShapeDtypeStruct(shape, kind) for shape, kind, _ in outputs.values()],
        in_specs=[spec for _, spec in inputs.values()],
        out_specs=[spec for _, _, spec in outputs.values()],
        scratch_shapes=list(scratch.values()),
        compiler_params=pltpu.CompilerParams(vmem_limit_bytes=LIMIT, **params),
        name=name,
    )(*[value for value, _ in inputs.values()])
    return SimpleNamespace(**dict(zip(outputs, outs)))


def given_in(spec, **values):
    return {name: (value, spec) for name, value in values.items()}


def vmem(kind, **shapes):
    return {name: pltpu.VMEM(shape, kind) for name, shape in shapes.items()}


def dma(**counts):
    return {name: pltpu.SemaphoreType.DMA(count) for name, count in counts.items()}


def forward(plan, shards, args, gathered, count):
    rows = args["images"].shape[0] * PAD
    shapes = saved_shapes(rows)
    whole = dict(
        patch_whole=cols_shape(D),
        joined_whole=(LAYERS,) + cols_shape(FF),
        expand_whole=(LAYERS,) + cols_shape(FF),
        shrink_whole=(LAYERS,) + ROWS_SHAPE,
    )
    inputs = given_in(VMEM_SPEC, **args)
    outputs = {}
    if plan.cube:
        inputs.update(given_in(VMEM_SPEC, **shards))
        outputs.update({name: (shape, BF, ANY_SPEC) for name, shape in whole.items()})
    else:
        inputs.update(given_in(ANY_SPEC, **dict(zip(whole, gathered))))
        inputs.update(given_in(VMEM_SPEC, count_in=count))
    for name, (shape, kind) in shapes.items():
        outputs["keep_" + name] = ((LAYERS,) + shape, kind, ANY_SPEC)
    outputs.update(
        g=((rows, D), F32, VMEM_SPEC),
        tail=((8, D), F32, VMEM_SPEC),
        head_block=((HEAD_BLOCK, 128), F32, VMEM_SPEC),
        total=((8, 128), F32, VMEM_SPEC),
    )
    scratch = vmem(
        BF,
        patch_w=cols_shape(D),
        joined_w=cols_shape(FF),
        expand_w=cols_shape(FF),
        shrink_w=ROWS_SHAPE,
    )
    scratch.update({name: pltpu.VMEM(shape, kind) for name, (shape, kind) in shapes.items()})
    scratch.update(vmem(F32, first=(HEAD_ROWS, D), d_logits=(HEAD_ROWS, 1024)))
    scratch.update(dma(saves=(9,), loads=(4,)))
    extra = {}
    if plan.cube:
        scratch.update(
            vmem(
                F32,
                joined_f=(LAYERS, HALF, FF),
                joined_b=(LAYERS, BLOCK, WIDTH),
                expand_b=(LAYERS, BLOCK, WIDTH),
                patch_f=(BLOCK, D // 2),
                count=(8, 128),
                counts=CHIPS + (2, 8, 128),
            )
        )
        scratch.update(
            vmem(
                BF,
                patch_block=(BLOCK, D // 2),
                joined_block=(LAYERS, BLOCK, WIDTH),
                expand_block=(LAYERS, BLOCK, WIDTH),
                shrink_block=(LAYERS, BLOCK_FF, D),
            )
        )
        scratch.update(
            dma(send=(10, 23), recv=(10, 22), share_send=(3,), share_recv=(3,), count_send=(7,), count_recv=(7,))
        )
        extra = dict(collective_id=1, has_side_effects=True)
    got = pallas(functools.partial(forward_kernel, plan), "forward", inputs, outputs, scratch, **extra)
    if not plan.cube:
        for name, value in zip(whole, gathered):
            setattr(got, name, value)
        got.total = count
    return got


UNITS = 3 * LAYERS
TAIL = 512
SEND = 4
VEC_ROWS = 256


def relative(plan):
    z, x, y, c = plan.where()
    return c, (z * 2 + x) * 2 + y


def place(plan, slot, core, chip):
    my_core, my_chip = relative(plan)
    at = jnp.bitwise_xor(my_chip, chip)
    other = jnp.bitwise_xor(my_core, core)
    return slot + (SEND - slot) * other, at // 4, at % 4


def store_cols(plan, out, slot, tile, width, value, half=WIDTH):
    per_half = half // width
    lanes = pl.ds(pl.multiple_of((tile % per_half) * width, 128), width)
    for b in range(16):
        rows = value[b * BLOCK : (b + 1) * BLOCK].astype(BF)
        out[(*place(plan, slot, tile // per_half, b), slice(None), lanes)] = rows


def store_rows(plan, out, slot, tile, value):
    for b in range(4):
        at = place(plan, slot, b % 2, tile * 2 + b // 2)
        for part in range(2):
            first = b * BLOCK_FF + part * BLOCK
            out[(*at, slice(None), pl.ds(part * D, D))] = value[first : first + BLOCK].astype(BF)


def store_vectors(plan, out, slot, value):
    for b in range(32):
        rows = value[b * 8 : b * 8 + 8]
        block = jnp.concatenate([rows[:, j * 128 : j * 128 + 128] for j in range(6)], 0)
        out[(*place(plan, slot, b % 2, b // 2), slice(None), pl.ds(D // 2, 128))] = block.astype(BF)


class Reduce:
    def __init__(self, plan, bufs, unit, width=WIDTH):
        self.plan, self.bufs, self.unit, self.width = plan, bufs, unit, width
        self.z, self.x, self.y, self.c = plan.where()
        self.to = over_links(plan)
        self.other = other_part(width) if width == WIDTH else 0
        self.most = width - self.other
        self.cut, self.cut_other = cut_of(self.most), cut_of(self.other)
        self.slot, self.three, self.two = unit % 4, unit % 3, unit % 2

    def copy(self, at):
        b, slot, three, to, c = self.bufs, self.slot, self.three, self.to, self.c
        most, cut, cut_other = self.most, self.cut, self.cut_other
        line = slice(None)
        full, main = pl.ds(0, self.width), pl.ds(0, most)
        left, right, low = pl.ds(0, cut), pl.ds(cut, most - cut), pl.ds(0, most - cut)
        other = pl.ds(most, self.other)
        own = b.unit.at[slot]
        if at == 17:
            rows = pl.ds(pl.multiple_of((1 - c) * HALF, 8), HALF)
            if self.width == WIDTH:
                src, dst = b.total.at[self.two, rows], b.owned.at[self.unit, c]
            else:
                src, dst = b.total.at[self.two, rows, pl.ds(0, D // 2)], b.patch.at[c]
            device = to.core
        else:
            src, dst, device = {
                0: lambda: (b.unit.at[SEND, :, :, :, full], b.core.at[:, :, :, full], to.core),
                1: lambda: (own.at[:, 3, :, left], b.near.at[three, :, :, left], to.x),
                2: lambda: (own.at[:, 3, :, right], b.far.at[three, :, :, low], to.y),
                3: lambda: (own.at[:, 1, :, main], b.y.at[three, :, :, main], to.y),
                4: lambda: (own.at[:, 2, :, main], b.x.at[three, :, :, main], to.x),
                5: lambda: (b.line.at[three, 2, :, main], b.main_two.at[three, 0, :, main], to.z1),
                6: lambda: (b.line.at[three, 2, :, main], b.main_two.at[three, 1, :, main], to.z3),
                7: lambda: (b.line.at[three, 1, :, main], b.main_one.at[slot, 0, :, main], to.z1),
                8: lambda: (b.line.at[three, 3, :, main], b.main_one.at[slot, 1, :, main], to.z3),
                9: lambda: (own.at[2, :, :, other], b.other_two.at[three, 0], to.z1),
                10: lambda: (own.at[2, :, :, other], b.other_two.at[three, 1], to.z3),
                11: lambda: (own.at[1, :, :, other], b.other_one.at[slot, 0], to.z1),
                12: lambda: (own.at[3, :, :, other], b.other_one.at[slot, 1], to.z3),
                13: lambda: (b.plane.at[three, 3, :, pl.ds(0, cut_other)], b.other_near.at[three], to.x),
                14: lambda: (b.plane.at[three, 3, :, pl.ds(cut_other, cut_other)], b.other_far.at[three], to.y),
                15: lambda: (b.plane.at[three, 1], b.other_y.at[three], to.y),
                16: lambda: (b.plane.at[three, 2], b.other_x.at[three], to.x),
            }[at]()
        return remote(src, dst, b.send.at[slot, at], b.recv.at[slot, at], device)

    def own(self, by_rows):
        b, c = self.bufs, self.c
        total = b.total.at[self.two]
        if by_rows:
            moves = [(total.at[pl.ds(k * HALF, HALF)], b.owned.at[self.unit, k]) for k in range(2)]
        else:
            rows = pl.ds(pl.multiple_of(c * HALF, 8), HALF)
            if self.width == WIDTH:
                moves = [(total.at[rows], b.owned.at[self.unit, c])]
            else:
                moves = [(total.at[rows, pl.ds(0, D // 2)], b.patch.at[c])]
        return [
            pltpu.make_async_copy(src, dst, b.send.at[self.slot, 18 + k])
            for k, (src, dst) in enumerate(moves)
        ]

    def start(self, *which):
        for at in which:
            self.copy(at).start()

    def arrived(self, *which):
        for at in which:
            self.copy(at).wait_recv()

    def sent(self, *which):
        for at in which:
            self.copy(at).wait_send()

    def by_place(self, middle, end):
        inside = (self.z == 1) | (self.z == 2)
        if middle:
            pl.when(inside)(middle)
        if end:
            pl.when(jnp.logical_not(inside))(end)

    def stage0(self):
        @pl.when(self.unit > 0)
        def _():
            pl.semaphore_wait(self.bufs.credit, 1)

        self.start(0)

    def stage1(self):
        unit, core, slot = self.bufs.unit, self.bufs.core, self.slot
        cols = pl.ds(0, self.width)
        self.arrived(0)

        def add(z, chip):
            both = unit[slot, z, chip, :, cols].astype(F32) + core[z, chip, :, cols].astype(F32)
            unit[slot, z, chip, :, cols] = both.astype(BF)

        pl.loop(0, 4)(lambda z: add(z, 3))
        self.start(1, 2)
        pl.loop(0, 12)(lambda i: add(i // 3, i % 3))
        if self.other:
            self.by_place(lambda: self.start(10), lambda: self.start(9))

        @pl.when(self.unit < UNITS)
        def _():
            pl.semaphore_signal(
                self.bufs.credit, inc=1, device_id=self.to.core, device_id_type=pl.DeviceIdType.MESH
            )

    def stage2(self):
        b, slot, three, most, cut = self.bufs, self.slot, self.three, self.most, self.cut
        unit = b.unit
        left, right, low = pl.ds(0, cut), pl.ds(cut, most - cut), pl.ds(0, most - cut)
        self.arrived(1, 2)

        @pl.loop(0, 4)
        def _(z):
            got = b.near[three, z, :, left].astype(F32)
            unit[slot, z, 1, :, left] = (unit[slot, z, 1, :, left].astype(F32) + got).astype(BF)
            got = b.far[three, z, :, low].astype(F32)
            unit[slot, z, 2, :, right] = (unit[slot, z, 2, :, right].astype(F32) + got).astype(BF)

        self.start(3, 4)
        self.sent(1, 2)
        if not self.other:
            return
        other = pl.ds(most, self.other)

        def pass_on():
            self.arrived(9, 10)
            for z, k in ((3, 0), (1, 1)):
                for chip in range(4):
                    got = b.other_two[three, k, chip].astype(F32)
                    unit[slot, z, chip, :, other] = (
                        unit[slot, z, chip, :, other].astype(F32) + got
                    ).astype(BF)

        self.by_place(pass_on, None)
        self.start(11, 12)

    def stage3(self):
        b, slot, three, main = self.bufs, self.slot, self.three, pl.ds(0, self.most)
        self.arrived(3, 4)

        @pl.loop(0, 4)
        def _(z):
            b.line[three, z, :, main] = (
                b.unit[slot, z, 0, :, main].astype(F32)
                + b.y[three, z, :, main].astype(F32)
                + b.x[three, z, :, main].astype(F32)
            ).astype(BF)

        self.by_place(lambda: self.start(6), lambda: self.start(5))
        self.sent(3, 4)
        if not self.other:
            return
        self.arrived(11, 12)
        for chip in range(4):
            b.plane[three, chip] = (
                b.unit[slot, 0, chip, :, pl.ds(self.most, self.other)].astype(F32)
                + b.other_one[slot, 0, chip].astype(F32)
                + b.other_one[slot, 1, chip].astype(F32)
            ).astype(BF)
        self.start(13, 14)
        self.by_place(lambda: self.sent(10), lambda: self.sent(9))
        self.sent(11, 12)

    def stage4(self):
        b, three, main = self.bufs, self.three, pl.ds(0, self.most)

        def pass_on():
            self.arrived(5, 6)
            for z, k in ((3, 0), (1, 1)):
                got = b.main_two[three, k, :, main].astype(F32)
                b.line[three, z, :, main] = (b.line[three, z, :, main].astype(F32) + got).astype(BF)

        self.by_place(pass_on, None)
        self.start(7, 8)
        if not self.other:
            return
        self.arrived(13, 14)
        half = self.cut_other
        for chip, cols, got in (
            (1, pl.ds(0, half), b.other_near),
            (2, pl.ds(half, half), b.other_far),
        ):
            both = b.plane[three, chip, :, cols].astype(F32) + got[three].astype(F32)
            b.plane[three, chip, :, cols] = both.astype(BF)
        self.start(15, 16)
        self.sent(13, 14)

    def stage5(self, by_rows):
        b, slot, three, two = self.bufs, self.slot, self.three, self.two
        main = pl.ds(0, self.most)
        self.arrived(7, 8)
        total = b.line[three, 0, :, main].astype(F32)
        for k in range(2):
            total = total + b.main_one[slot, k, :, main].astype(F32)
        b.total[two, :, main] = total
        b.squares[0:1, main] += jnp.sum(total * total, 0, keepdims=True)
        if self.other:
            self.arrived(15, 16)
            other = pl.ds(self.most, self.other)
            total = (
                b.plane[three, 0].astype(F32)
                + b.other_y[three].astype(F32)
                + b.other_x[three].astype(F32)
            )
            b.total[two, :, other] = total
            b.squares[0:1, other] += jnp.sum(total * total, 0, keepdims=True)
        if not by_rows:
            self.start(17)
        start_all(self.own(by_rows))
        self.by_place(lambda: self.sent(6), lambda: self.sent(5))
        self.sent(7, 8)
        if self.other:
            self.sent(15, 16)

    def stage6(self, by_rows):
        if not by_rows:
            self.copy(17).wait()
        wait_all(self.own(by_rows))


POINTS = 4
ENTRY = (0, 1, 3)
STAGE_ORDER = (1, 0, 2, 3, 4, 6, 5)


def backward_kernel(plan, names, *refs):
    r = SimpleNamespace(**dict(zip(names, refs)))
    cube = plan.cube
    images = r.images.shape[0]
    loads = [
        (r.keep_z, r.vm_z),
        (r.shrink_whole, r.shrink_w),
        (r.keep_slope, r.vm_slope),
        (r.expand_whole, r.expand_w),
        (r.keep_m, r.vm_m),
        (r.keep_h1, r.vm_h1),
        (r.keep_o, r.vm_o),
        (r.keep_t, r.vm_t),
        (r.keep_p, r.vm_p),
        (r.keep_a, r.vm_a),
        (r.keep_h, r.vm_h),
        (r.joined_whole, r.expand_w),
    ]
    z_, shrink_, slope_, expand_, m_, h1_, o_, t_, p_, a_, h_, joined_ = range(12)
    top = LAYERS - 1

    def fetch(which, layer):
        src, dst = loads[which]
        return pltpu.make_async_copy(src.at[layer], dst, r.loads.at[which])

    def start(layer, *which):
        for k in which:
            fetch(k, layer).start()

    def wait(layer, *which):
        for k in which:
            fetch(k, layer).wait()

    first_g = load(r.g_in, r.g, r.loads.at[joined_ + 1])
    start(top, *range(joined_))
    if cube:
        cube_barrier(plan)
        r.squares[...] = jnp.zeros_like(r.squares)
        head_rows = SmallGather(plan, r.head_block, r.head_rows, r.head_send, r.head_recv)
        head_rows.stage0()
    r.vectors[...] = jnp.zeros_like(r.vectors)
    r.vectors[FINAL : FINAL + 2] = r.tail_in[1:3]
    first_g.wait()

    def run(unit, stage, by_rows, width=WIDTH):
        unit = Reduce(plan, r, unit, width)
        (
            unit.stage0,
            unit.stage1,
            unit.stage2,
            unit.stage3,
            unit.stage4,
            lambda: unit.stage5(by_rows),
            lambda: unit.stage6(by_rows),
        )[stage]()

    def point(it, at):
        if not cube:
            for kind in range(3):
                if ENTRY[kind] == at:
                    unit = 3 * it + kind
                    copies = [
                        pltpu.make_async_copy(
                            r.unit.at[(unit % 4, SEND)[i]],
                            r.full.at[unit, i],
                            r.loads.at[joined_ + 1 + i],
                        )
                        for i in range(2)
                    ]
                    start_all(copies)
                    wait_all(copies)
            return
        for stage in STAGE_ORDER:
            for kind in range(3):
                past, phase = divmod(ENTRY[kind] + stage, POINTS)
                if phase != at:
                    continue
                unit = 3 * (it - past) + kind
                if past:
                    pl.when(it >= past)(functools.partial(run, unit, stage, kind == 0))
                else:
                    run(unit, stage, kind == 0)

    def drain():
        at = 0
        while at <= 5:
            for stage in STAGE_ORDER:
                for past, kind in ((2, 0), (2, 1), (2, 2), (1, 0), (1, 1), (1, 2)):
                    if POINTS * past + at - ENTRY[kind] == stage:
                        run(jnp.int32(UNITS - 3 * past + kind), stage, kind == 0)
                if at == stage:
                    run(jnp.int32(UNITS), stage, False, TAIL)
            at += 1

    def sent(unit):
        if cube:
            pl.when(unit > 0)(lambda: Reduce(plan, r, unit - 1).copy(0).wait_send())

    low_lane = lax.broadcasted_iota(jnp.int32, (PAD, 128), 1) < HEAD_DIM
    scale = HEAD_DIM**-0.5

    @pl.loop(0, LAYERS)
    def _(it):
        layer = top - it
        below = it < LAYERS - 1
        base = S + 2 + 4 * layer
        r.gr[...] = r.g[...].astype(BF)
        wait(layer, z_)
        slot = (3 * it) % 4
        sent(3 * it)

        @pl.loop(0, 8)
        def _(j):
            cols = pl.ds(pl.multiple_of(j * (D // 2), 128), D // 2)
            store_rows(plan, r.unit, slot, j, dot(r.vm_z[:, cols], r.gr[...], TN))

        point(it, 0)
        if cube:
            pl.when(it == 0)(head_rows.stage1)
            pl.when(it == 1)(head_rows.finish)
        wait(layer, shrink_, slope_, expand_, m_, h1_)
        pl.when(below)(lambda: start(layer - 1, z_))
        slot_e = (3 * it + 1) % 4
        r.g1[...] = jnp.zeros_like(r.g1)
        sent(3 * it + 1)

        @pl.loop(0, 4)
        def _(j):
            cols = pl.ds(pl.multiple_of(j * D, 128), D)
            dz = dot(r.gr[...], r.shrink_w[j].reshape(D, D), NT)
            du = (dz * r.vm_slope[:, cols].astype(F32)).astype(BF)
            r.g1[...] += dot(du, weight(r.expand_w, j * D, D), NT)
            store_cols(plan, r.unit, slot_e, j, D, dot(r.vm_m[...], du, TN))

        start(layer, joined_)
        pl.when(below)(lambda: start(layer - 1, shrink_, slope_, m_))
        point(it, 1)
        if cube:
            pl.when(it == 0)(head_rows.stage2)
        d_h1, d_gain, d_shift = normalize_back(r.vm_h1[...], row(r.params, base + 2), r.g1[...])
        r.g1[...] = r.g[...] + d_h1
        r.vectors[pl.ds(base + 2, 1)] = d_gain
        r.vectors[pl.ds(base + 3, 1)] = d_shift
        pl.when(below)(lambda: start(layer - 1, h1_))

        r.gr[...] = r.g1[...].astype(BF)
        slot_t = (3 * it + 2) % 4
        wait(layer, o_)
        sent(3 * it + 2)
        store_cols(plan, r.unit, slot_t, 3, D, dot(r.vm_o[...], r.gr[...], TN))
        wait(layer, joined_)
        r.do[...] = dot(r.gr[...], weight(r.expand_w, 3 * D, D), NT).astype(BF)
        wait(layer, t_, p_, a_, h_)

        def heads(step):
            image, pair = step // (HEADS // 2), step % (HEADS // 2)
            rows = pl.ds(pl.multiple_of(image * PAD, 16), PAD)
            lanes = [pl.ds(pl.multiple_of(pair * 128 + part * D, 128), 128) for part in range(3)]
            q, key, v = (r.vm_t[rows, lane] for lane in lanes)
            do = r.do[rows, lanes[0]]
            zero = jnp.zeros_like(v)
            dqs, dks, dvs = [], [], []
            for which in range(2):
                part = jnp.where(low_lane, v, zero) if which == 0 else jnp.where(low_lane, zero, v)
                p_low = r.vm_p[step * 2 + which]
                p = p_low.astype(F32)
                dvs.append(dot(p_low, do))
                dp = dot(part, do, NT)
                ds = (p * (dp - jnp.sum(p * dp, 0, keepdims=True))).astype(BF)
                dqs.append(dot(ds, key, TN))
                dks.append(dot(ds, q))
            r.dt[rows, lanes[0]] = (jnp.where(low_lane, dqs[0], dqs[1]) * scale).astype(BF)
            r.dt[rows, lanes[1]] = (jnp.where(low_lane, dks[0], dks[1]) * scale).astype(BF)
            r.dt[rows, lanes[2]] = jnp.where(low_lane, dvs[0], dvs[1]).astype(BF)

        half = images * (HEADS // 2) // 2
        pl.loop(0, half)(heads)
        point(it, 2)
        pl.loop(half, 2 * half)(heads)
        pl.when(below)(lambda: start(layer - 1, o_, t_, p_))
        r.g[...] = jnp.zeros_like(r.g)

        @pl.loop(0, 3)
        def _(j):
            cols = pl.ds(pl.multiple_of(j * D, 128), D)
            store_cols(plan, r.unit, slot_t, j, D, dot(r.vm_a[...], r.dt[:, cols], TN))
            r.g[...] += dot(r.dt[:, cols], weight(r.expand_w, j * D, D), NT)

        point(it, 3)
        if cube:
            pl.when(it == 0)(head_rows.stage3)
        d_h, d_gain, d_shift = normalize_back(r.vm_h[...], row(r.params, base), r.g[...])
        r.g[...] = r.g1[...] + d_h
        r.vectors[pl.ds(base, 1)] = d_gain
        r.vectors[pl.ds(base + 1, 1)] = d_shift
        pl.when(below)(lambda: start(layer - 1, a_, h_, expand_))

    slot = UNITS % 4
    sent(jnp.int32(UNITS))
    for part in range(2):
        half = D // 2
        value = jnp.zeros((D, half), F32)
        for image in range(images):
            rows = r.g[image * PAD + 1 : image * PAD + S, part * half : (part + 1) * half]
            value = value + dot(r.images[image], rows.astype(BF), TN)
        store_cols(plan, r.unit, slot, part, half, value, half)
    pos = r.g[:PAD]
    for image in range(1, images):
        pos = pos + r.g[image * PAD : (image + 1) * PAD]
    r.vectors[:S] = pos[:S]
    r.vectors[S : S + 1] = pos[:1]
    r.vectors[S + 1 : S + 2] = jnp.sum(pos[1:S], 0, keepdims=True)
    if not cube:
        copies = [
            pltpu.make_async_copy(r.unit.at[(slot, SEND)[i]], r.full.at[UNITS, i], r.loads.at[i])
            for i in range(2)
        ]
        copies.append(pltpu.make_async_copy(r.vectors, r.vector_rows, r.loads.at[2]))
        start_all(copies)
        wait_all(copies)
        return
    store_vectors(plan, r.unit, slot, r.vectors[...])

    drain()
    r.tail_block[:BLOCK] = r.total[UNITS % 2, :, D // 2 : TAIL]
    line = lax.broadcasted_iota(jnp.int32, (8, 128), 0)
    squares, loss = jnp.sum(r.squares[...]), r.tail_in[0:1, 0:128]
    r.tail_block[BLOCK:] = jnp.where(line == 0, squares, jnp.where(line == 1, loss, 0.0))
    gather = SmallGather(plan, r.tail_block, r.vector_rows, r.tail_send, r.tail_recv)
    gather.stage0()
    gather.stage1()
    gather.stage2()
    gather.stage3()
    run(jnp.int32(UNITS), 6, False, TAIL)
    Reduce(plan, r, jnp.int32(UNITS), TAIL).copy(0).wait_send()
    gather.finish()


def backward(plan, images, params, done):
    rows = done.g.shape[0]
    shapes = saved_shapes(rows)
    inputs = given_in(VMEM_SPEC, images=images, params=params, tail_in=done.tail)
    if plan.cube:
        inputs.update(given_in(VMEM_SPEC, head_block=done.head_block))
    inputs.update(
        given_in(
            ANY_SPEC,
            g_in=done.g,
            joined_whole=done.joined_whole,
            expand_whole=done.expand_whole,
            shrink_whole=done.shrink_whole,
        )
    )
    inputs.update({"keep_" + name: (getattr(done, "keep_" + name), ANY_SPEC) for name in SAVED})
    if plan.cube:
        outputs = dict(
            owned=((UNITS, 2, HALF, WIDTH), F32, ANY_SPEC),
            patch=((2, HALF, D // 2), F32, ANY_SPEC),
            vector_rows=(CHIPS + (2, BLOCK + 8, 128), F32, ANY_SPEC),
            head_rows=(CHIPS + (2, HEAD_BLOCK, 128), F32, ANY_SPEC),
        )
    else:
        outputs = dict(
            full=((UNITS + 1, 2, 4, 4, BLOCK, WIDTH), BF, ANY_SPEC),
            vector_rows=((VEC_ROWS, D), F32, ANY_SPEC),
        )
    scratch = {"vm_" + name: pltpu.VMEM(shape, kind) for name, (shape, kind) in shapes.items()}
    scratch.update(
        vmem(
            BF,
            expand_w=cols_shape(FF),
            shrink_w=ROWS_SHAPE,
            gr=(rows, D),
            do=(rows, D),
            dt=(rows, 3 * D),
            unit=(SEND + 1, 4, 4, BLOCK, WIDTH),
        )
    )
    scratch.update(vmem(F32, g=(rows, D), g1=(rows, D), vectors=(VEC_ROWS, D)))
    scratch.update(dma(loads=(15,)))
    extra = {}
    if plan.cube:
        other = other_part(WIDTH)
        most = WIDTH - other
        scratch.update(
            vmem(
                BF,
                core=(4, 4, BLOCK, WIDTH),
                near=(3, 4, BLOCK, cut_of(most)),
                far=(3, 4, BLOCK, most - cut_of(most)),
                x=(3, 4, BLOCK, most),
                y=(3, 4, BLOCK, most),
                line=(3, 4, BLOCK, most),
                main_two=(3, 2, BLOCK, most),
                main_one=(4, 2, BLOCK, most),
                other_two=(3, 2, 4, BLOCK, other),
                other_one=(4, 2, 4, BLOCK, other),
                plane=(3, 4, BLOCK, other),
                other_near=(3, BLOCK, cut_of(other)),
                other_far=(3, BLOCK, other - cut_of(other)),
                other_x=(3, BLOCK, other),
                other_y=(3, BLOCK, other),
            )
        )
        scratch.update(
            vmem(F32, total=(2, BLOCK, WIDTH), squares=(8, WIDTH), tail_block=(BLOCK + 8, 128))
        )
        scratch.update(
            dma(send=(4, 20), recv=(4, 18), head_send=(7,), head_recv=(7,), tail_send=(7,), tail_recv=(7,))
        )
        scratch.update(credit=pltpu.SemaphoreType.REGULAR)
        extra = dict(collective_id=2, has_side_effects=True)
    return pallas(functools.partial(backward_kernel, plan), "backward", inputs, outputs, scratch, **extra)


PARAMS = ("patch", "triple", "output", "expand", "shrink", "vector", "head")
KINDS = ("w_", "m_", "s_")


def adam_update(master, moment, square, gradient, step_rate):
    moment_new = BETA_ONE * moment + (1.0 - BETA_ONE) * gradient
    square_new = BETA_TWO * square + (1.0 - BETA_TWO) * gradient * gradient
    moment_hat = moment_new / (1.0 - BETA_ONE**STEP_INDEX)
    square_hat = square_new / (1.0 - BETA_TWO**STEP_INDEX)
    master_new = master - step_rate * (
        moment_hat / (jnp.sqrt(square_hat) + ADAM_EPS) + DECAY * master
    )
    return (master_new, moment_new, square_new)


def head_matrices(ref, images):
    def take(first, count):
        devices = ref.shape[0] // HEAD_BLOCK
        pieces = [
            jnp.concatenate(
                [
                    ref[pl.ds(image * 14 + first + j, devices, stride=HEAD_BLOCK), :]
                    for j in range(count)
                ],
                1,
            )
            for image in range(images)
        ]
        return jnp.concatenate(pieces, 0).astype(BF)

    return take(0, 6), take(6, 8)


def update_kernel(images, names, *refs):
    r = SimpleNamespace(**dict(zip(names, refs)))
    named = dict(zip(names, refs))
    groups = [
        [(named[kind + name], named["vm_" + kind + name], named["to_" + kind + name]) for kind in KINDS]
        for name in PARAMS
    ]
    patch, triple, output, expand, shrink, vector, head = range(7)

    def moves(group, back):
        return [
            pltpu.make_async_copy(*((buf, out) if back else (src, buf)), r.sems.at[3 * group + k])
            for k, (src, buf, out) in enumerate(groups[group])
        ]

    order = (head, shrink, expand, triple, output, patch, vector)
    for group in order:
        start_all(moves(group, False))

    tile = jnp.sum(r.tails[:, BLOCK:, :], 0)
    features, d_logits = head_matrices(r.head_rows, images)
    r.features[...] = features
    r.d_logits[...] = d_logits
    alike = (dot(features, features, NT) + 1.0) * dot(d_logits, d_logits, NT)
    norm = jnp.sqrt(tile[0:1, 0:1] + jnp.sum(alike))
    clip = CLIP / jnp.maximum(norm, CLIP)
    line = lax.broadcasted_iota(jnp.int32, (8, 128), 0)
    r.scalars[...] = jnp.where(line == 0, norm, tile[1:2])

    def step(group, at, gradient, rate):
        bufs = [buf for _, buf, _ in groups[group]]
        new = adam_update(*[buf[at] for buf in bufs], gradient * clip, rate)
        for buf, value in zip(bufs, new):
            buf[at] = value

    def finish(group):
        start_all(moves(group, True))

    every = slice(None)
    wait_all(moves(head, False))

    @pl.loop(0, D // 128)
    def _(j):
        rows = pl.ds(pl.multiple_of(j * 128, 128), 128)
        gradient = dot(r.features[:, rows], r.d_logits[...], TN)
        step(head, (rows, every), gradient[:, :CLASSES], RATE_MATRIX)

    bias = jnp.sum(d_logits.astype(F32), 0, keepdims=True)[:, :CLASSES]
    step(head, (slice(D, D + 1), every), bias, RATE_MATRIX)
    r.bias_grad[...] = bias * clip
    finish(head)
    wait_all(moves(shrink, False))

    @pl.loop(0, LAYERS)
    def _(layer):
        unit = 3 * (LAYERS - 1 - layer)
        for k in range(4):
            gradient = r.owned[unit, k % 2, :, pl.ds(k // 2 * D, D)]
            step(shrink, (layer, pl.ds(k * HALF, HALF), every), gradient, RATE_MATRIX)

    finish(shrink)
    wait_all(moves(expand, False))

    @pl.loop(0, LAYERS)
    def _(layer):
        unit = 3 * (LAYERS - 1 - layer) + 1
        for k in range(2):
            step(expand, (layer, every, pl.ds(k * WIDTH, WIDTH)), r.owned[unit, k], RATE_MATRIX)

    finish(expand)
    wait_all(moves(triple, False))
    wait_all(moves(output, False))

    @pl.loop(0, LAYERS)
    def _(layer):
        unit = 3 * (LAYERS - 1 - layer) + 2
        step(triple, (layer, every, pl.ds(0, WIDTH)), r.owned[unit, 0], RATE_MATRIX)
        step(triple, (layer, every, pl.ds(WIDTH, D)), r.owned[unit, 1, :, pl.ds(0, D)], RATE_MATRIX)
        step(output, (layer, every, every), r.owned[unit, 1, :, pl.ds(D, D)], RATE_OUTPUT)

    finish(triple)
    finish(output)
    wait_all(moves(patch, False))
    for k in range(2):
        step(patch, (every, pl.ds(k * (D // 2), D // 2)), r.patch_grad[k], RATE_MATRIX)
    finish(patch)
    count = groups[vector][0][0].shape[0]
    for d in range(-(-count // 8)):
        for j in range(6):
            r.vector_grad[8 * d : 8 * d + 8, 128 * j : 128 * j + 128] = r.tails[d, 8 * j : 8 * j + 8, :]
    wait_all(moves(vector, False))
    step(vector, (every, every), r.vector_grad[:count], RATE_VECTOR)
    finish(vector)
    for group in order:
        wait_all(moves(group, True))


def update(plan, images, states, got):
    inputs, outputs, scratch = {}, {}, {}
    for name, state in zip(PARAMS, states):
        for kind, value in zip(KINDS, state):
            inputs[kind + name] = (value, ANY_SPEC)
            outputs["to_" + kind + name] = (value.shape, F32, ANY_SPEC)
            scratch["vm_" + kind + name] = pltpu.VMEM(value.shape, F32)
    inputs.update(
        given_in(
            VMEM_SPEC,
            owned=got.owned,
            patch_grad=got.patch,
            tails=got.vector_rows.reshape(plan.n, BLOCK + 8, 128),
            head_rows=got.head_rows.reshape(plan.n * HEAD_BLOCK, 128),
        )
    )
    outputs.update(scalars=((8, 128), F32, VMEM_SPEC), bias_grad=((1, CLASSES), F32, VMEM_SPEC))
    scratch.update(vmem(BF, features=(plan.n * images, D), d_logits=(plan.n * images, 1024)))
    scratch.update(vmem(F32, vector_grad=(VEC_ROWS, D)))
    scratch.update(dma(sems=(3 * len(PARAMS),)))
    new = pallas(functools.partial(update_kernel, images), "update", inputs, outputs, scratch)
    states = [[getattr(new, "to_" + kind + name) for kind in KINDS] for name in PARAMS]
    return new.scalars[0, 0], new.scalars[1, 0], states, new.bias_grad[0]


AXES = ("wide", "grp")


def update_whole(plan, images, states, got, done):
    full = got.full.reshape(UNITS + 1, 2, 16, BLOCK, WIDTH)
    layers = full[:UNITS].reshape(LAYERS, 3, 2, 16, BLOCK, WIDTH)[::-1]

    def scattered(whole):
        axis = whole.ndim - 2
        return lax.psum_scatter(whole, AXES, scatter_dimension=axis, tiled=True).astype(F32)

    def from_cols(part):
        joined = jnp.concatenate([part[..., 0, :, :, :], part[..., 1, :, :, :]], -1)
        return joined.reshape(part.shape[:-4] + (D, -1))

    shrink = layers[:, 0].reshape(LAYERS, 2, 16, BLOCK, 2, D).transpose(0, 2, 1, 4, 3, 5)
    joined = scattered(from_cols(layers[:, 2]))
    rows_all = lax.all_gather(done.head_block, AXES, axis=0)[:, : 14 * images]
    rows_all = rows_all.reshape(plan.n * images, 14 * 128).astype(BF)
    features, d_logits = rows_all[:, :D], rows_all[:, D : D + CLASSES]
    bias = jnp.sum(d_logits.astype(F32), 0)[None]
    split = [
        scattered(from_cols(full[UNITS, ..., : D // 2])),
        joined[:, :, : 3 * D],
        joined[:, :, 3 * D :],
        scattered(from_cols(layers[:, 1])),
        scattered(shrink.reshape(LAYERS, FF, D)),
    ]
    same = [
        lax.psum(got.vector_rows[: states[5][0].shape[0]], AXES),
        jnp.concatenate([dot(features, d_logits, TN), bias], 0),
    ]
    squares = lax.psum(sum(jnp.sum(g * g) for g in split), AXES) + sum(jnp.sum(g * g) for g in same)
    norm = jnp.sqrt(squares)
    clip = CLIP / jnp.maximum(norm, CLIP)
    rates = [RATE_MATRIX] * 2 + [RATE_OUTPUT] + [RATE_MATRIX] * 2 + [RATE_VECTOR, RATE_MATRIX]
    states = [
        adam_update(*state, gradient * clip, rate)
        for state, gradient, rate in zip(states, split + same, rates)
    ]
    return norm, lax.psum(done.tail[0, 0], AXES), states, bias[0] * clip


def per_device(plan, images, slot_mask, labels, *params):
    states = [params[3 * k : 3 * k + 3] for k in range(7)]
    patch, triple, output, expand, shrink, vector, head = (state[0] for state in states)
    count = images.shape[0]
    pad_rows = ((0, HEAD_ROWS - count), (0, 0))
    weights = slot_mask.astype(F32)
    args = dict(
        images=images,
        vectors=vector,
        head=head,
        labels=jnp.pad(labels[:, None], pad_rows),
        weights=jnp.pad(weights[:, None], pad_rows),
    )
    if plan.cube:
        shards = dict(patch=patch, triple=triple, output=output, expand=expand, shrink=shrink)
        done = forward(plan, shards, args, None, None)
    else:

        def whole(shard, shape):
            axis = shard.ndim - 2
            gathered = lax.all_gather(shard.astype(BF), AXES, axis=axis, tiled=True)
            return gathered.reshape(shard.shape[:axis] + shape)

        gathered = [
            whole(patch, cols_shape(D)),
            whole(jnp.concatenate([triple, output], 2), cols_shape(FF)),
            whole(expand, cols_shape(FF)),
            whole(shrink, ROWS_SHAPE),
        ]
        total = jnp.full((8, 128), lax.psum(jnp.sum(weights), AXES), F32)
        done = forward(plan, None, args, gathered, total)
    got = backward(plan, images, vector, done)
    if plan.cube:
        norm, loss, states, bias_grad = update(plan, count, states, got)
    else:
        norm, loss, states, bias_grad = update_whole(plan, count, states, got, done)
    return (
        loss,
        done.total[0, 0],
        norm,
        *(value for state in states for value in state),
        bias_grad,
    )


def solution(mesh):
    plan = Plan(mesh)
    rows = P(AXES, None)
    layers = P(None, AXES, None)
    in_specs = (P(AXES, None, None), P(AXES), P(AXES)) + (rows,) * 3 + (layers,) * 12 + (P(),) * 6
    out_specs = (P(),) * 3 + (rows,) * 3 + (layers,) * 12 + (P(),) * 7
    return jax.shard_map(
        functools.partial(per_device, plan),
        mesh=mesh,
        in_specs=in_specs,
        out_specs=out_specs,
        check_vma=False,
    )
```

```python
import functools
from types import SimpleNamespace

import jax
import jax.numpy as jnp
from jax import lax
from jax.experimental import pallas as pl
from jax.experimental.pallas import tpu as pltpu
from jax.sharding import PartitionSpec as P

D = 768
HEADS = 12
HEAD_DIM = 64
FF = 3072
CLASSES = 1000
LAYERS = 3
STEP_INDEX = 10
S = 197
PAD = 208

EPS_NORM = 1e-06
CLIP = 0.1
BETA_ONE = 0.9
BETA_TWO = 0.95
ADAM_EPS = 1e-08
DECAY = 0.05
RATE_MATRIX = 0.03
RATE_OUTPUT = 0.2
RATE_VECTOR = 0.3
SMOOTH = 0.1

F32 = jnp.float32
BF = jnp.bfloat16
NN = (((1,), (0,)), ((), ()))
NT = (((1,), (1,)), ((), ()))
TN = (((0,), (0,)), ((), ()))
VMEM_SPEC = pl.BlockSpec(memory_space=pltpu.VMEM)
ANY_SPEC = pl.BlockSpec(memory_space=pl.ANY)
LIMIT = 62 * 1024 * 1024


def dot(left, right, form=NN):
    return lax.dot_general(left, right, form, preferred_element_type=F32)


def normalize(values, gain_row, shift_row):
    center = values - jnp.mean(values, -1, keepdims=True)
    spread = jnp.mean(center * center, -1, keepdims=True)
    return center * lax.rsqrt(spread + EPS_NORM) * gain_row + shift_row


def normalize_back(values, gain_row, grad):
    center = values - jnp.mean(values, -1, keepdims=True)
    spread = jnp.mean(center * center, -1, keepdims=True)
    scale = lax.rsqrt(spread + EPS_NORM)
    unit = center * scale
    d_unit = grad * gain_row
    d_values = scale * (
        d_unit
        - jnp.mean(d_unit, -1, keepdims=True)
        - unit * jnp.mean(d_unit * unit, -1, keepdims=True)
    )
    return (
        d_values,
        jnp.sum(grad * unit, 0, keepdims=True),
        jnp.sum(grad, 0, keepdims=True),
    )


def gelu_and_slope(u):
    x = jnp.abs(u) * 0.7071067811865476
    t = 1.0 / (1.0 + 0.3275911 * x)
    series = t * (
        0.254829592
        + t * (-0.284496736 + t * (1.421413741 + t * (-1.453152027 + t * 1.061405429)))
    )
    bell = jnp.exp(-0.5 * u * u)
    tail = 0.5 * series * bell
    share = jnp.where(u >= 0.0, 1.0 - tail, tail)
    return u * share, share + u * bell * 0.3989422804014327


class Plan:
    def __init__(self, mesh):
        self.wide, self.grp = mesh.shape["wide"], mesh.shape["grp"]
        self.n = self.wide * self.grp
        self.cube = self.wide == 8 and self.grp == 4

    def me(self):
        return lax.axis_index("wide") * self.grp + lax.axis_index("grp")

    def where(self):
        if not self.cube:
            return 0, 0, 0, 0
        wide, grp = lax.axis_index("wide"), lax.axis_index("grp")
        return wide // 2, wide % 2, grp // 2, grp % 2


CHIPS = (4, 2, 2)
BLOCK = D // 16
BLOCK_FF = FF // 32


def cols_shape(columns):
    return CHIPS + (BLOCK, columns)


ROWS_SHAPE = CHIPS + (2, BLOCK_FF, D)


def other_part(width):
    return width // 6 // 128 * 128


def cut_of(columns):
    return columns // 2 // 128 * 128


def over_links(plan):
    z, x, y, c = plan.where()

    def at(z, x, y, c):
        return (z * 2 + x, y * 2 + c)

    return SimpleNamespace(
        z1=at(jnp.bitwise_xor(z, 1), x, y, c),
        z3=at(jnp.bitwise_xor(z, 3), x, y, c),
        x=at(z, 1 - x, y, c),
        y=at(z, x, 1 - y, c),
        core=at(z, x, y, 1 - c),
    )


def remote(src, dst, send, recv, to):
    return pltpu.make_async_remote_copy(
        src_ref=src,
        dst_ref=dst,
        send_sem=send,
        recv_sem=recv,
        device_id=to,
        device_id_type=pl.DeviceIdType.MESH,
    )


class Gather:
    def __init__(self, plan, by_cols, block, whole, send, recv):
        self.z, self.x, self.y, self.c = plan.where()
        self.to = over_links(plan)
        self.by_cols, self.block, self.whole = by_cols, block, whole
        self.send, self.recv = send, recv
        self.width = block.shape[-1]
        self.other = other_part(self.width)
        self.most = self.width - self.other

    def region(self, z, x, y, start, width):
        if self.by_cols:
            first = pl.multiple_of(self.c * self.width + start, 128)
            return self.whole.at[z, x, y, :, pl.ds(first, width)]
        return self.whole.at[z, x, y, self.c, :, pl.ds(start, width)]

    def part(self, start, width):
        return self.block.at[:, pl.ds(start, width)]

    def copy(self, at):
        z, x, y, to = self.z, self.x, self.y, self.to
        z1, z3, line = jnp.bitwise_xor(z, 1), jnp.bitwise_xor(z, 3), slice(None)
        most, other, region = self.most, self.other, self.region
        cut, cut_other = cut_of(most), most + max(cut_of(other), 128)
        landed = at
        if at in (0, 1):
            src, dst = self.part(0, most), region(z, x, y, 0, most)
            device = (to.z1, to.z3)[at]
        elif at in (8, 9):
            src, dst = self.part(most, other), region(z, x, y, most, other)
            device = (to.x, to.y)[at - 8]
        else:
            src, device = {
                2: lambda: (region(z3, x, y, 0, most), to.z1),
                3: lambda: (region(z1, x, y, 0, most), to.z3),
                4: lambda: (region(line, x, y, 0, most), to.x),
                5: lambda: (region(line, x, y, 0, most), to.y),
                6: lambda: (region(line, x, 1 - y, 0, cut), to.x),
                7: lambda: (region(line, 1 - x, y, cut, most - cut), to.y),
                10: lambda: (region(z, x, 1 - y, most, cut_other - most), to.x),
                11: lambda: (region(z, 1 - x, y, cut_other, self.width - cut_other), to.y),
                12: lambda: (region(z, line, line, most, other), to.z1),
                13: lambda: (region(z, line, line, most, other), to.z3),
                14: lambda: (region(z3, line, line, most, other), to.z1),
                15: lambda: (region(z1, line, line, most, other), to.z3),
                16: lambda: (region(line, x, y, 0, most), to.core),
                17: lambda: (region(line, 1 - x, y, 0, most), to.core),
                18: lambda: (region(line, x, 1 - y, 0, most), to.core),
                19: lambda: (region(line, 1 - x, 1 - y, 0, cut), to.core),
                20: lambda: (region(line, 1 - x, 1 - y, cut, most - cut), to.core),
                21: lambda: (region(line, line, line, most, other), to.core),
            }[at]()
            dst = src
            if at in (3, 15):
                landed = at - 1
        return remote(src, dst, self.send.at[at], self.recv.at[landed], device)

    def exists(self, at):
        if at in (8, 9, 10, 12, 13, 14, 15, 21):
            return self.other > 0
        return at != 11 or self.other > 128

    def keep(self):
        here = self.region(self.z, self.x, self.y, 0, self.width)
        return pltpu.make_async_copy(self.block, here, self.send.at[22])

    def start(self, *which):
        for at in which:
            if self.exists(at):
                self.copy(at).start()

    def arrived(self, *which):
        for at in which:
            if self.exists(at):
                self.copy(at).wait_recv()

    def in_middle(self, do):
        pl.when((self.z == 1) | (self.z == 2))(do)

    def stage0(self):
        self.start(0, 1, 8, 9)
        self.keep().start()

    def stage1(self):
        self.arrived(0, 1)
        self.in_middle(lambda: self.start(2, 3))
        self.arrived(8, 9)
        self.start(10, 11)
        self.keep().wait()

    def stage2(self):
        self.arrived(2)
        self.start(4, 5, 16)
        self.arrived(10, 11)
        self.start(12, 13)

    def stage3(self):
        self.arrived(4, 5)
        self.start(6, 7, 17, 18)
        self.arrived(12, 13)
        self.in_middle(lambda: self.start(14, 15))

    def stage4(self):
        self.arrived(6, 7)
        self.start(19, 20)
        self.arrived(14)
        self.start(21)

    def finish(self):
        self.arrived(16, 17, 18, 19, 20, 21)
        passed = (2, 3, 14, 15)

        def sent(which):
            for at in which:
                if self.exists(at):
                    self.copy(at).wait_send()

        sent([at for at in range(22) if at not in passed])
        self.in_middle(lambda: sent(passed))


def cube_barrier(plan):
    z, x, y, c = plan.where()
    barrier = pltpu.get_barrier_semaphore()
    partners = [(jnp.bitwise_xor(z, k) * 2 + x, y * 2 + c) for k in (1, 2, 3)]
    partners += [
        (z * 2 + 1 - x, y * 2 + c),
        (z * 2 + x, (1 - y) * 2 + c),
        (z * 2 + x, y * 2 + 1 - c),
    ]
    for partner in partners:
        pl.semaphore_signal(barrier, inc=1, device_id=partner, device_id_type=pl.DeviceIdType.MESH)
    pl.semaphore_wait(barrier, len(partners))


def load(source, target, sem):
    copy = pltpu.make_async_copy(source, target, sem)
    copy.start()
    return copy


def start_all(copies):
    for copy in copies:
        copy.start()


def wait_all(copies):
    for copy in copies:
        copy.wait()


def weight(ref, first, width):
    cols = pl.ds(first if isinstance(first, int) else pl.multiple_of(first, 128), width)
    return ref[:, :, :, :, cols].reshape(D, width)


class SmallGather:
    def __init__(self, plan, block, whole, send, recv):
        self.z, self.x, self.y, self.c = plan.where()
        self.block, self.whole, self.send, self.recv = block, whole, send, recv

    def copy(self, at):
        z, x, y, c = self.z, self.x, self.y, self.c
        line = slice(None)
        if at < 3:
            src, dst = self.block, self.whole.at[z, x, y, c]
            to = (jnp.bitwise_xor(z, at + 1) * 2 + x, y * 2 + c)
        elif at == 3:
            src = dst = self.whole.at[line, x, y, c]
            to = (z * 2 + 1 - x, y * 2 + c)
        elif at == 4:
            src = dst = self.whole.at[line, line, y, c]
            to = (z * 2 + x, (1 - y) * 2 + c)
        else:
            src = dst = self.whole.at[line, line, line, c]
            to = (z * 2 + x, y * 2 + 1 - c)
        return pltpu.make_async_remote_copy(
            src_ref=src,
            dst_ref=dst,
            send_sem=self.send.at[at],
            recv_sem=self.recv.at[at],
            device_id=to,
            device_id_type=pl.DeviceIdType.MESH,
        )

    def keep(self):
        here = self.whole.at[self.z, self.x, self.y, self.c]
        return pltpu.make_async_copy(self.block, here, self.send.at[6])

    def stage0(self):
        for at in range(3):
            self.copy(at).start()
        self.keep().start()

    def stage1(self):
        for at in range(3):
            self.copy(at).wait_recv()
        self.keep().wait()
        self.copy(3).start()

    def stage2(self):
        self.copy(3).wait_recv()
        self.copy(4).start()

    def stage3(self):
        self.copy(4).wait_recv()
        self.copy(5).start()

    def finish(self):
        self.copy(5).wait_recv()
        for at in range(6):
            self.copy(at).wait_send()


FF_TILE = 512
HALF = BLOCK // 2
WIDTH = FF // 2
HEAD_ROWS = 16
FINAL = S + 2 + 4 * LAYERS
TOP = LAYERS - 1
CLASS_PAD = 1024

Z_, M_, O_, Q_, A_ = (slice(0, FF),) + tuple(slice(FF + k * D, FF + k * D + D) for k in range(4))
FEATURE_, LOGIT_ = slice(FF + 4 * D, FF + 5 * D), slice(FF + 5 * D, FF + 5 * D + CLASS_PAD)
SLOPE_, H1_, G_ = slice(0, FF), slice(FF, FF + D), slice(FF + D, FF + 2 * D)
PIECES = (D, CLASS_PAD, FF, D, D, FF, D, D, D, D)
PER_IMAGE = sum(PIECES) // 128


def rows_block(images):
    return -(-PER_IMAGE * images // 16) * 16


def class_rows(ref, source):
    ref[...] = jnp.zeros_like(ref)
    for image in range(source.shape[0] // PAD):
        ref[image : image + 1] = source[image * PAD : image * PAD + 1]


def by_head(rows, image):
    head = lax.broadcasted_iota(jnp.int32, (16, D), 0)
    lane = lax.broadcasted_iota(jnp.int32, (16, D), 1)
    mine = (lane >= head * HEAD_DIM) & (lane < head * HEAD_DIM + HEAD_DIM)
    return mine, jnp.where(mine, rows[image : image + 1], 0.0)


def saved_shapes(rows):
    heads = rows // PAD * HEADS
    return dict(
        h=((rows, D), F32),
        a=((rows, D), BF),
        t=((rows, 3 * D), BF),
        o=((rows, D), BF),
        p=((heads, PAD, PAD), BF),
        h1=((rows, D), F32),
        m=((rows, D), BF),
        z=((rows, FF), BF),
        slope=((rows, FF), BF),
    )


SAVED = tuple(saved_shapes(PAD))


def row(ref, at):
    return ref[pl.ds(at, 1)]


def share_shards(plan, r):
    z, x, y, c = plan.where()
    r.joined_f[:, :, : 3 * D] = r.triple[...]
    r.joined_f[:, :, 3 * D :] = r.output[...]
    mine = pl.ds(pl.multiple_of(c * HALF, 8), HALF)

    def part(core, width):
        return pl.ds(pl.multiple_of(core * width, 128), width)

    moves = [
        (r.patch.at[:, part(1 - c, D // 2)], r.patch_f.at[mine]),
        (r.joined_f.at[:, :, part(1 - c, WIDTH)], r.joined_b.at[:, mine]),
        (r.expand.at[:, :, part(1 - c, WIDTH)], r.expand_b.at[:, mine]),
    ]
    copies = [
        pltpu.make_async_remote_copy(
            src_ref=src,
            dst_ref=dst,
            send_sem=r.share_send.at[i],
            recv_sem=r.share_recv.at[i],
            device_id=(z * 2 + x, y * 2 + 1 - c),
            device_id_type=pl.DeviceIdType.MESH,
        )
        for i, (src, dst) in enumerate(moves)
    ]
    start_all(copies)
    r.patch_f[mine] = r.patch[:, part(c, D // 2)]
    r.joined_b[:, mine] = r.joined_f[:, :, part(c, WIDTH)]
    r.expand_b[:, mine] = r.expand[:, :, part(c, WIDTH)]
    r.shrink_block[...] = r.shrink[...].astype(BF)
    for copy, src, dst in zip(
        copies,
        (r.patch_f, r.joined_b, r.expand_b),
        (r.patch_block, r.joined_block, r.expand_block),
    ):
        copy.wait_recv()
        dst[...] = src[...].astype(BF)
    for copy in copies:
        copy.wait_send()


def head_part(r, first, image_total):
    table = r.head[:D].astype(BF)
    gain, shift = r.vectors[FINAL : FINAL + 1], r.vectors[FINAL + 1 : FINAL + 2]
    feature = normalize(first, gain, shift).astype(BF)
    logits = dot(feature, table) + r.head[D : D + 1]
    ids = lax.broadcasted_iota(jnp.int32, logits.shape, 1)
    shifted = logits - jnp.max(logits, -1, keepdims=True)
    log_prob = shifted - jnp.log(jnp.sum(jnp.exp(shifted), -1, keepdims=True))
    target = jnp.where(ids == r.labels[...], 1.0 - SMOOTH, 0.0) + SMOOTH / CLASSES
    weights = r.weights[...]
    loss = jnp.sum(weights * -jnp.sum(target * log_prob, -1, keepdims=True))
    d_logits = ((weights / image_total) * (jnp.exp(log_prob) - target)).astype(BF)
    d_feature = dot(d_logits, table, NT)
    r.d_logits[...] = jnp.zeros_like(r.d_logits)
    r.d_logits[:, :CLASSES] = d_logits.astype(F32)
    r.top_b[:, FEATURE_] = feature
    r.top_b[:, LOGIT_] = r.d_logits[...].astype(BF)
    d_first, d_gain, d_shift = normalize_back(first, gain, d_feature)
    r.top_f[:, G_] = d_first
    r.tail[...] = jnp.zeros_like(r.tail)
    r.tail[0:1] = jnp.full((1, D), loss, F32)
    r.tail[1:2] = d_gain
    r.tail[2:3] = d_shift


def forward_kernel(plan, names, *refs):
    r = SimpleNamespace(**dict(zip(names, refs)))
    cube = plan.cube
    images = r.images.shape[0]
    patch, joined, expand, shrink = range(4)
    wholes = (r.patch_whole, r.joined_whole, r.expand_whole, r.shrink_whole)
    weights = (r.patch_w, r.joined_w, r.expand_w, r.shrink_w)
    if cube:
        blocks = (r.patch_block, r.joined_block, r.expand_block, r.shrink_block)
        cube_barrier(plan)
        share_shards(plan, r)
        r.count[...] = jnp.full((8, 128), jnp.sum(r.weights[...]), F32)
        counting = SmallGather(plan, r.count, r.counts, r.count_send, r.count_recv)

    def unit(kind, layer):
        if kind == patch:
            return Gather(plan, True, blocks[0], wholes[0], r.send.at[0], r.recv.at[0])
        at = 3 * layer + kind
        block, whole = blocks[kind].at[layer], wholes[kind].at[layer]
        return Gather(plan, kind != shrink, block, whole, r.send.at[at], r.recv.at[at])

    def ready(kind, layer):
        if cube:
            unit(kind, layer).finish()
        whole = wholes[kind] if kind == patch else wholes[kind].at[layer]
        return load(whole, weights[kind], r.loads.at[kind])

    held = (r.h, r.a, r.t, r.o, r.p, r.h1, r.m, r.z, r.slope)
    kept = (r.keep_h, r.keep_a, r.keep_t, r.keep_o, r.keep_p, r.keep_h1, r.keep_m, r.keep_z, r.keep_slope)
    h_, a_, t_, o_, p_, h1_, m_, z_, slope_ = range(9)

    def saves(layer, *which):
        return [pltpu.make_async_copy(held[k], kept[k].at[layer], r.saves.at[k]) for k in which]

    if cube:
        first = [unit(patch, 0), unit(joined, 0), unit(expand, 0), unit(shrink, 0), unit(joined, 1)]
        first[0].stage0()
        counting.stage0()
        first[1].stage0()
        first[0].stage1()
        first[2].stage0()
        first[1].stage1()
        first[0].stage2()
        first[3].stage0()
        first[2].stage1()
        first[1].stage2()
        first[0].stage3()
        first[4].stage0()
        first[3].stage1()
        first[2].stage2()
        first[1].stage3()
        first[0].stage4()
    ready(patch, 0).wait()
    for image in range(images):
        at = image * PAD
        r.h[at : at + 1] = r.vectors[0:1] + r.vectors[S : S + 1]
        embedded = dot(r.images[image], weight(r.patch_w, 0, D))
        r.h[at + 1 : at + S] = embedded + r.vectors[S + 1 : S + 2] + r.vectors[1:S]
        r.h[at + S : at + PAD] = jnp.zeros((PAD - S, D), F32)

    low_lane = lax.broadcasted_iota(jnp.int32, (PAD, 128), 1) < HEAD_DIM
    real_key = lax.broadcasted_iota(jnp.int32, (PAD, PAD), 0) < S

    @pl.loop(0, TOP)
    def _(layer):
        base = S + 2 + 4 * layer
        if cube:
            unit(expand, layer + 1).stage0()
            unit(joined, layer + 1).stage1()
            unit(shrink, layer).stage2()
            unit(expand, layer).stage3()
            unit(joined, layer).stage4()
        start_all(saves(layer, h_))

        @pl.when(layer > 0)
        def _():
            wait_all(saves(layer, a_, t_, o_, p_, h1_, m_))

        r.a[...] = normalize(r.h[...], row(r.vectors, base), row(r.vectors, base + 1)).astype(BF)
        ready(joined, layer).wait()

        @pl.loop(0, 3)
        def _(j):
            cols = pl.ds(pl.multiple_of(j * D, 128), D)
            r.t[:, cols] = dot(r.a[...], weight(r.joined_w, j * D, D)).astype(BF)

        start_all(saves(layer, a_, t_))

        def heads(step):
            image, pair = step // (HEADS // 2), step % (HEADS // 2)
            rows = pl.ds(pl.multiple_of(image * PAD, 16), PAD)
            lanes = [pl.ds(pl.multiple_of(pair * 128 + part * D, 128), 128) for part in range(3)]
            q, key, v = (r.t[rows, lane] for lane in lanes)
            zero = jnp.zeros_like(key)
            outs = []
            for which in range(2):
                part = jnp.where(low_lane, key, zero) if which == 0 else jnp.where(low_lane, zero, key)
                scores = dot(part, q, NT) * HEAD_DIM**-0.5
                scores = jnp.where(real_key, scores, -1e30)
                top = jnp.max(scores, 0, keepdims=True)
                e = jnp.exp(scores - top)
                p = (e * (1.0 / jnp.sum(e, 0, keepdims=True))).astype(BF)
                r.p[step * 2 + which] = p
                outs.append(dot(p, v, TN))
            r.o[rows, lanes[0]] = jnp.where(low_lane, outs[0], outs[1]).astype(BF)

        half = images * (HEADS // 2) // 2
        pl.loop(0, half)(heads)
        if cube:
            unit(shrink, layer + 1).stage0()
            unit(expand, layer + 1).stage1()
            unit(joined, layer + 1).stage2()

        pl.loop(half, 2 * half)(heads)
        start_all(saves(layer, o_, p_))
        r.h1[...] = r.h[...] + dot(r.o[...], weight(r.joined_w, 3 * D, D))
        start_all(saves(layer, h1_))
        if cube:
            unit(shrink, layer).stage3()
            unit(expand, layer).stage4()
            pl.when(layer == 0)(counting.stage1)
            pl.when(layer == 1)(counting.stage3)
        r.m[...] = normalize(r.h1[...], row(r.vectors, base + 2), row(r.vectors, base + 3)).astype(BF)
        start_all(saves(layer, m_))
        wait_all(saves(layer, h_))
        r.h[...] = r.h1[...]

        @pl.when(layer > 0)
        def _():
            wait_all(saves(layer, z_, slope_))

        ready(expand, layer).wait()

        @pl.loop(0, FF // FF_TILE)
        def _(j):
            cols = pl.ds(pl.multiple_of(j * FF_TILE, 128), FF_TILE)
            u = dot(r.m[...], weight(r.expand_w, j * FF_TILE, FF_TILE))
            z, slope = gelu_and_slope(u)
            r.z[:, cols] = z.astype(BF)
            r.slope[:, cols] = slope.astype(BF)

        start_all(saves(layer, z_, slope_))
        if cube:
            pl.when(layer < TOP - 1)(lambda: unit(joined, layer + 2).stage0())

            unit(shrink, layer + 1).stage1()
            unit(expand, layer + 1).stage2()
            unit(joined, layer + 1).stage3()
            unit(shrink, layer).stage4()
            pl.when(layer == 0)(counting.stage2)
            pl.when(layer == 1)(counting.finish)
        ready(shrink, layer).wait()

        @pl.loop(0, 4)
        def _(j):
            cols = pl.ds(pl.multiple_of(j * D, 128), D)
            r.h[...] += dot(r.z[:, cols], r.shrink_w[j].reshape(D, D))

    base = S + 2 + 4 * TOP
    if cube:
        unit(shrink, TOP).stage2()
        unit(expand, TOP).stage3()
        unit(joined, TOP).stage4()
    start_all(saves(TOP, h_))
    wait_all(saves(TOP, a_, t_) + saves(0, o_, p_, h1_, m_))
    r.a[...] = normalize(r.h[...], row(r.vectors, base), row(r.vectors, base + 1)).astype(BF)
    class_rows(r.first, r.h)
    first = r.first[...]
    r.top_b[:, A_] = normalize(first, row(r.vectors, base), row(r.vectors, base + 1)).astype(BF)
    ready(joined, TOP).wait()
    for j in (1, 2):
        r.t[:, j * D : j * D + D] = dot(r.a[...], weight(r.joined_w, j * D, D)).astype(BF)
    start_all(saves(TOP, a_, t_))
    query = dot(r.top_b[:, A_], weight(r.joined_w, 0, D)).astype(BF)
    r.top_b[:, Q_] = query
    if cube:
        unit(shrink, TOP).stage3()
        unit(expand, TOP).stage4()
    query = query.astype(F32)
    real = lax.broadcasted_iota(jnp.int32, (PAD, 16), 0) < S
    r.class_row[...] = jnp.zeros_like(r.class_row)
    for image in range(images):
        rows = slice(image * PAD, image * PAD + PAD)
        mine, spread = by_head(query, image)
        scores = dot(r.t[rows, D : 2 * D], spread.astype(BF), NT) * HEAD_DIM**-0.5
        scores = jnp.where(real, scores, -1e30)
        e = jnp.exp(scores - jnp.max(scores, 0, keepdims=True))
        p = (e * (1.0 / jnp.sum(e, 0, keepdims=True))).astype(BF)
        r.top_p[image] = p
        out = jnp.where(mine, dot(p, r.t[rows, 2 * D :], TN), 0.0)
        r.class_row[image : image + 1] = jnp.sum(out, 0, keepdims=True)
    attended = r.class_row[...].astype(BF)
    r.top_b[:, O_] = attended
    h1 = first + dot(attended, weight(r.joined_w, 3 * D, D))
    r.top_f[:, H1_] = h1
    r.top_b[:, M_] = normalize(h1, row(r.vectors, base + 2), row(r.vectors, base + 3)).astype(BF)
    ready(expand, TOP).wait()
    for j in range(4):
        cols = slice(j * D, j * D + D)
        z, slope = gelu_and_slope(dot(r.top_b[:, M_], weight(r.expand_w, j * D, D)))
        r.top_b[:, cols] = z.astype(BF)
        r.top_f[:, cols] = slope
    if cube:
        unit(shrink, TOP).stage4()
    ready(shrink, TOP).wait()
    last = h1
    for j in range(4):
        last = last + dot(r.top_b[:, j * D : j * D + D], r.shrink_w[j].reshape(D, D))

    if cube:
        r.total[...] = jnp.sum(r.counts[...].reshape(-1, 8, 128), 0)
        image_total = r.total[0:1, 0:1]
    else:
        image_total = r.count_in[0:1, 0:1]
    head_part(r, last, image_total)
    wait_all(saves(TOP, h_, a_, t_) + saves(0, z_, slope_))


def pallas(kernel, name, inputs, outputs, scratch, **params):
    names = list(inputs) + list(outputs) + list(scratch)
    outs = pl.pallas_call(
        functools.partial(kernel, names),
        out_shape=[jax.ShapeDtypeStruct(shape, kind) for shape, kind, _ in outputs.values()],
        in_specs=[spec for _, spec in inputs.values()],
        out_specs=[spec for _, _, spec in outputs.values()],
        scratch_shapes=list(scratch.values()),
        compiler_params=pltpu.CompilerParams(vmem_limit_bytes=LIMIT, **params),
        name=name,
    )(*[value for value, _ in inputs.values()])
    return SimpleNamespace(**dict(zip(outputs, outs)))


def given_in(spec, **values):
    return {name: (value, spec) for name, value in values.items()}


def vmem(kind, **shapes):
    return {name: pltpu.VMEM(shape, kind) for name, shape in shapes.items()}


def dma(**counts):
    return {name: pltpu.SemaphoreType.DMA(count) for name, count in counts.items()}


def forward(plan, shards, args, gathered, count):
    rows = args["images"].shape[0] * PAD
    shapes = saved_shapes(rows)
    whole = dict(
        patch_whole=cols_shape(D),
        joined_whole=(LAYERS,) + cols_shape(FF),
        expand_whole=(LAYERS,) + cols_shape(FF),
        shrink_whole=(LAYERS,) + ROWS_SHAPE,
    )
    inputs = given_in(VMEM_SPEC, **args)
    outputs = {}
    if plan.cube:
        inputs.update(given_in(VMEM_SPEC, **shards))
        outputs.update({name: (shape, BF, ANY_SPEC) for name, shape in whole.items()})
    else:
        inputs.update(given_in(ANY_SPEC, **dict(zip(whole, gathered))))
        inputs.update(given_in(VMEM_SPEC, count_in=count))
    for name, (shape, kind) in shapes.items():
        deep = LAYERS if name in ("h", "a", "t") else TOP
        outputs["keep_" + name] = ((deep,) + shape, kind, ANY_SPEC)
    outputs.update(
        top_b=((HEAD_ROWS, LOGIT_.stop), BF, VMEM_SPEC),
        top_f=((HEAD_ROWS, G_.stop), F32, VMEM_SPEC),
        top_p=((rows // PAD, PAD, 16), BF, VMEM_SPEC),
        tail=((8, D), F32, VMEM_SPEC),
        total=((8, 128), F32, VMEM_SPEC),
    )
    scratch = vmem(
        BF,
        patch_w=cols_shape(D),
        joined_w=cols_shape(FF),
        expand_w=cols_shape(FF),
        shrink_w=ROWS_SHAPE,
    )
    scratch.update({name: pltpu.VMEM(shape, kind) for name, (shape, kind) in shapes.items()})
    scratch.update(vmem(F32, first=(HEAD_ROWS, D), class_row=(HEAD_ROWS, D), d_logits=(HEAD_ROWS, CLASS_PAD)))
    scratch.update(dma(saves=(9,), loads=(4,)))
    extra = {}
    if plan.cube:
        scratch.update(
            vmem(
                F32,
                joined_f=(LAYERS, HALF, FF),
                joined_b=(LAYERS, BLOCK, WIDTH),
                expand_b=(LAYERS, BLOCK, WIDTH),
                patch_f=(BLOCK, D // 2),
                count=(8, 128),
                counts=CHIPS + (2, 8, 128),
            )
        )
        scratch.update(
            vmem(
                BF,
                patch_block=(BLOCK, D // 2),
                joined_block=(LAYERS, BLOCK, WIDTH),
                expand_block=(LAYERS, BLOCK, WIDTH),
                shrink_block=(LAYERS, BLOCK_FF, D),
            )
        )
        scratch.update(
            dma(send=(10, 23), recv=(10, 22), share_send=(3,), share_recv=(3,), count_send=(7,), count_recv=(7,))
        )
        extra = dict(collective_id=1, has_side_effects=True)
    got = pallas(functools.partial(forward_kernel, plan), "forward", inputs, outputs, scratch, **extra)
    if not plan.cube:
        for name, value in zip(whole, gathered):
            setattr(got, name, value)
        got.total = count
    return got


UNITS = 3 * TOP + 1
KEYS = D
TAIL = 512
SEND = 4
VEC_ROWS = 256


def relative(plan):
    z, x, y, c = plan.where()
    return c, (z * 2 + x) * 2 + y


def place(plan, slot, core, chip):
    my_core, my_chip = relative(plan)
    at = jnp.bitwise_xor(my_chip, chip)
    other = jnp.bitwise_xor(my_core, core)
    return slot + (SEND - slot) * other, at // 4, at % 4


def store_cols(plan, out, slot, tile, width, value, half=WIDTH):
    per_half = half // width
    lanes = pl.ds(pl.multiple_of((tile % per_half) * width, 128), width)
    for b in range(16):
        rows = value[b * BLOCK : (b + 1) * BLOCK].astype(BF)
        out[(*place(plan, slot, tile // per_half, b), slice(None), lanes)] = rows


def store_rows(plan, out, slot, tile, value):
    for b in range(4):
        at = place(plan, slot, b % 2, tile * 2 + b // 2)
        for part in range(2):
            first = b * BLOCK_FF + part * BLOCK
            out[(*at, slice(None), pl.ds(part * D, D))] = value[first : first + BLOCK].astype(BF)


def store_vectors(plan, out, slot, value):
    for b in range(32):
        rows = value[b * 8 : b * 8 + 8]
        block = jnp.concatenate([rows[:, j * 128 : j * 128 + 128] for j in range(6)], 0)
        out[(*place(plan, slot, b % 2, b // 2), slice(None), pl.ds(D // 2, 128))] = block.astype(BF)


class Reduce:
    def __init__(self, plan, bufs, unit, width=WIDTH):
        self.plan, self.bufs, self.unit, self.width = plan, bufs, unit, width
        self.z, self.x, self.y, self.c = plan.where()
        self.to = over_links(plan)
        self.other = other_part(width) if width == WIDTH else 0
        self.most = width - self.other
        self.cut, self.cut_other = cut_of(self.most), cut_of(self.other)
        self.slot, self.three, self.two = unit % 4, unit % 3, unit % 2

    def copy(self, at):
        b, slot, three, to, c = self.bufs, self.slot, self.three, self.to, self.c
        most, cut, cut_other = self.most, self.cut, self.cut_other
        line = slice(None)
        full, main = pl.ds(0, self.width), pl.ds(0, most)
        left, right, low = pl.ds(0, cut), pl.ds(cut, most - cut), pl.ds(0, most - cut)
        other = pl.ds(most, self.other)
        own = b.unit.at[slot]
        if at == 17:
            rows = pl.ds(pl.multiple_of((1 - c) * HALF, 8), HALF)
            src, dst = self.result(rows)
            device = to.core
        else:
            src, dst, device = {
                0: lambda: (b.unit.at[SEND, :, :, :, full], b.core.at[:, :, :, full], to.core),
                1: lambda: (own.at[:, 3, :, left], b.near.at[three, :, :, left], to.x),
                2: lambda: (own.at[:, 3, :, right], b.far.at[three, :, :, low], to.y),
                3: lambda: (own.at[:, 1, :, main], b.y.at[three, :, :, main], to.y),
                4: lambda: (own.at[:, 2, :, main], b.x.at[three, :, :, main], to.x),
                5: lambda: (b.line.at[three, 2, :, main], b.main_two.at[three, 0, :, main], to.z1),
                6: lambda: (b.line.at[three, 2, :, main], b.main_two.at[three, 1, :, main], to.z3),
                7: lambda: (b.line.at[three, 1, :, main], b.main_one.at[slot, 0, :, main], to.z1),
                8: lambda: (b.line.at[three, 3, :, main], b.main_one.at[slot, 1, :, main], to.z3),
                9: lambda: (own.at[2, :, :, other], b.other_two.at[three, 0], to.z1),
                10: lambda: (own.at[2, :, :, other], b.other_two.at[three, 1], to.z3),
                11: lambda: (own.at[1, :, :, other], b.other_one.at[slot, 0], to.z1),
                12: lambda: (own.at[3, :, :, other], b.other_one.at[slot, 1], to.z3),
                13: lambda: (b.plane.at[three, 3, :, pl.ds(0, cut_other)], b.other_near.at[three], to.x),
                14: lambda: (b.plane.at[three, 3, :, pl.ds(cut_other, cut_other)], b.other_far.at[three], to.y),
                15: lambda: (b.plane.at[three, 1], b.other_y.at[three], to.y),
                16: lambda: (b.plane.at[three, 2], b.other_x.at[three], to.x),
            }[at]()
        return remote(src, dst, b.send.at[slot, at], b.recv.at[slot, at], device)

    def result(self, rows):
        b, c = self.bufs, self.c
        total = b.total.at[self.two]
        if self.width == WIDTH:
            return total.at[rows], b.owned.at[self.unit - 1, c]
        if self.width == KEYS:
            return total.at[rows, pl.ds(0, KEYS)], b.keys.at[c]
        return total.at[rows, pl.ds(0, D // 2)], b.patch.at[c]

    def own(self, by_rows):
        b, c = self.bufs, self.c
        total = b.total.at[self.two]
        if by_rows:
            moves = [(total.at[pl.ds(k * HALF, HALF)], b.owned.at[self.unit - 1, k]) for k in range(2)]
        else:
            moves = [self.result(pl.ds(pl.multiple_of(c * HALF, 8), HALF))]
        return [
            pltpu.make_async_copy(src, dst, b.send.at[self.slot, 18 + k])
            for k, (src, dst) in enumerate(moves)
        ]

    def start(self, *which):
        for at in which:
            self.copy(at).start()

    def arrived(self, *which):
        for at in which:
            self.copy(at).wait_recv()

    def sent(self, *which):
        for at in which:
            self.copy(at).wait_send()

    def by_place(self, middle, end):
        inside = (self.z == 1) | (self.z == 2)
        if middle:
            pl.when(inside)(middle)
        if end:
            pl.when(jnp.logical_not(inside))(end)

    def stage0(self):
        @pl.when(self.unit > 0)
        def _():
            pl.semaphore_wait(self.bufs.credit, 1)

        self.start(0)

    def stage1(self):
        unit, core, slot = self.bufs.unit, self.bufs.core, self.slot
        cols = pl.ds(0, self.width)
        self.arrived(0)

        def add(z, chip):
            both = unit[slot, z, chip, :, cols].astype(F32) + core[z, chip, :, cols].astype(F32)
            unit[slot, z, chip, :, cols] = both.astype(BF)

        pl.loop(0, 4)(lambda z: add(z, 3))
        self.start(1, 2)
        pl.loop(0, 12)(lambda i: add(i // 3, i % 3))
        if self.other:
            self.by_place(lambda: self.start(10), lambda: self.start(9))

        @pl.when(self.unit < UNITS)
        def _():
            pl.semaphore_signal(
                self.bufs.credit, inc=1, device_id=self.to.core, device_id_type=pl.DeviceIdType.MESH
            )

    def stage2(self):
        b, slot, three, most, cut = self.bufs, self.slot, self.three, self.most, self.cut
        unit = b.unit
        left, right, low = pl.ds(0, cut), pl.ds(cut, most - cut), pl.ds(0, most - cut)
        self.arrived(1, 2)

        @pl.loop(0, 4)
        def _(z):
            got = b.near[three, z, :, left].astype(F32)
            unit[slot, z, 1, :, left] = (unit[slot, z, 1, :, left].astype(F32) + got).astype(BF)
            got = b.far[three, z, :, low].astype(F32)
            unit[slot, z, 2, :, right] = (unit[slot, z, 2, :, right].astype(F32) + got).astype(BF)

        self.start(3, 4)
        self.sent(1, 2)
        if not self.other:
            return
        other = pl.ds(most, self.other)

        def pass_on():
            self.arrived(9, 10)
            for z, k in ((3, 0), (1, 1)):
                for chip in range(4):
                    got = b.other_two[three, k, chip].astype(F32)
                    unit[slot, z, chip, :, other] = (
                        unit[slot, z, chip, :, other].astype(F32) + got
                    ).astype(BF)

        self.by_place(pass_on, None)
        self.start(11, 12)

    def stage3(self):
        b, slot, three, main = self.bufs, self.slot, self.three, pl.ds(0, self.most)
        self.arrived(3, 4)

        @pl.loop(0, 4)
        def _(z):
            b.line[three, z, :, main] = (
                b.unit[slot, z, 0, :, main].astype(F32)
                + b.y[three, z, :, main].astype(F32)
                + b.x[three, z, :, main].astype(F32)
            ).astype(BF)

        self.by_place(lambda: self.start(6), lambda: self.start(5))
        self.sent(3, 4)
        if not self.other:
            return
        self.arrived(11, 12)
        for chip in range(4):
            b.plane[three, chip] = (
                b.unit[slot, 0, chip, :, pl.ds(self.most, self.other)].astype(F32)
                + b.other_one[slot, 0, chip].astype(F32)
                + b.other_one[slot, 1, chip].astype(F32)
            ).astype(BF)
        self.start(13, 14)
        self.by_place(lambda: self.sent(10), lambda: self.sent(9))
        self.sent(11, 12)

    def stage4(self):
        b, three, main = self.bufs, self.three, pl.ds(0, self.most)

        def pass_on():
            self.arrived(5, 6)
            for z, k in ((3, 0), (1, 1)):
                got = b.main_two[three, k, :, main].astype(F32)
                b.line[three, z, :, main] = (b.line[three, z, :, main].astype(F32) + got).astype(BF)

        self.by_place(pass_on, None)
        self.start(7, 8)
        if not self.other:
            return
        self.arrived(13, 14)
        half = self.cut_other
        for chip, cols, got in (
            (1, pl.ds(0, half), b.other_near),
            (2, pl.ds(half, half), b.other_far),
        ):
            both = b.plane[three, chip, :, cols].astype(F32) + got[three].astype(F32)
            b.plane[three, chip, :, cols] = both.astype(BF)
        self.start(15, 16)
        self.sent(13, 14)

    def stage5(self, by_rows):
        b, slot, three, two = self.bufs, self.slot, self.three, self.two
        main = pl.ds(0, self.most)
        self.arrived(7, 8)
        total = b.line[three, 0, :, main].astype(F32)
        for k in range(2):
            total = total + b.main_one[slot, k, :, main].astype(F32)
        b.total[two, :, main] = total
        b.squares[0:1, main] += jnp.sum(total * total, 0, keepdims=True)
        if self.other:
            self.arrived(15, 16)
            other = pl.ds(self.most, self.other)
            total = (
                b.plane[three, 0].astype(F32)
                + b.other_y[three].astype(F32)
                + b.other_x[three].astype(F32)
            )
            b.total[two, :, other] = total
            b.squares[0:1, other] += jnp.sum(total * total, 0, keepdims=True)
        if not by_rows:
            self.start(17)
        start_all(self.own(by_rows))
        self.by_place(lambda: self.sent(6), lambda: self.sent(5))
        self.sent(7, 8)
        if self.other:
            self.sent(15, 16)

    def stage6(self, by_rows):
        if not by_rows:
            self.copy(17).wait()
        wait_all(self.own(by_rows))


POINTS = 4
ENTRY = (0, 1, 3)
STAGE_ORDER = (1, 0, 2, 3, 4, 6, 5)


def backward_kernel(plan, names, *refs):
    r = SimpleNamespace(**dict(zip(names, refs)))
    cube = plan.cube
    images = r.images.shape[0]
    loads = [
        (r.keep_z, r.vm_z),
        (r.shrink_whole, r.shrink_w),
        (r.keep_slope, r.vm_slope),
        (r.expand_whole, r.expand_w),
        (r.keep_m, r.vm_m),
        (r.keep_h1, r.vm_h1),
        (r.keep_o, r.vm_o),
        (r.keep_t, r.vm_t),
        (r.keep_p, r.vm_p),
        (r.keep_a, r.vm_a),
        (r.keep_h, r.vm_h),
        (r.joined_whole, r.expand_w),
    ]
    z_, shrink_, slope_, expand_, m_, h1_, o_, t_, p_, a_, h_, joined_ = range(12)

    def fetch(which, layer):
        src, dst = loads[which]
        return pltpu.make_async_copy(src.at[layer], dst, r.loads.at[which])

    def start(layer, *which):
        for k in which:
            fetch(k, layer).start()

    def wait(layer, *which):
        for k in which:
            fetch(k, layer).wait()

    start(TOP, shrink_, expand_, t_, a_, h_)
    start(TOP - 1, z_, slope_, m_, h1_, o_, p_)
    if cube:
        cube_barrier(plan)
        r.squares[...] = jnp.zeros_like(r.squares)
        top_rows = SmallGather(plan, r.rows_block, r.top_rows, r.rows_send, r.rows_recv)
    r.vectors[...] = jnp.zeros_like(r.vectors)
    r.vectors[FINAL : FINAL + 2] = r.tail_in[1:3]

    def run(unit, stage, by_rows, width=WIDTH):
        unit = Reduce(plan, r, unit, width)
        (
            unit.stage0,
            unit.stage1,
            unit.stage2,
            unit.stage3,
            unit.stage4,
            lambda: unit.stage5(by_rows),
            lambda: unit.stage6(by_rows),
        )[stage]()

    def point(it, at):
        if not cube:
            for kind in range(3):
                if ENTRY[kind] == at:
                    unit = 3 * it - 2 + kind
                    copies = [
                        pltpu.make_async_copy(
                            r.unit.at[(unit % 4, SEND)[i]],
                            r.full.at[unit, i],
                            r.loads.at[joined_ + 1 + i],
                        )
                        for i in range(2)
                    ]
                    start_all(copies)
                    wait_all(copies)
            return
        for stage in STAGE_ORDER:
            for kind in range(3):
                past, phase = divmod(ENTRY[kind] + stage, POINTS)
                if phase != at:
                    continue
                unit = 3 * (it - past) - 2 + kind
                if past:
                    pl.when(it > past)(functools.partial(run, unit, stage, kind == 0))
                else:
                    run(unit, stage, kind == 0)
                if past and kind == 2:
                    pl.when(it == past)(functools.partial(run, unit, stage, False, KEYS))

    def drain():
        at = 0
        while at <= 5:
            for stage in STAGE_ORDER:
                for past, kind in ((1, 0), (1, 1), (1, 2), (2, 0), (2, 1), (2, 2)):
                    if POINTS * past + at - ENTRY[kind] == stage:
                        run(jnp.int32(UNITS - 3 * past + kind), stage, kind == 0)
                if at == stage:
                    run(jnp.int32(UNITS), stage, False, TAIL)
            at += 1

    def sent(unit, width=WIDTH):
        if cube:
            Reduce(plan, r, unit - 1, width).copy(0).wait_send()

    low_lane = lax.broadcasted_iota(jnp.int32, (PAD, 128), 1) < HEAD_DIM
    scale = HEAD_DIM**-0.5

    base = S + 2 + 4 * TOP
    g = r.top_f[:, G_]
    g_low = g.astype(BF)
    wait(TOP, shrink_)
    for j in range(4):
        cols = slice(j * D, j * D + D)
        dz = dot(g_low, r.shrink_w[j].reshape(D, D), NT)
        r.top_du[:, cols] = (dz * r.top_f[:, cols]).astype(BF)
    start(TOP - 1, shrink_)
    wait(TOP, expand_)
    d_m = jnp.zeros((HEAD_ROWS, D), F32)
    for j in range(4):
        d_m = d_m + dot(r.top_du[:, j * D : j * D + D], weight(r.expand_w, j * D, D), NT)
    start(TOP, joined_)
    d_h1, d_gain, d_shift = normalize_back(r.top_f[:, H1_], row(r.params, base + 2), d_m)
    r.vectors[base + 2 : base + 3] = d_gain
    r.vectors[base + 3 : base + 4] = d_shift
    g1 = g + d_h1
    g1_low = g1.astype(BF)
    wait(TOP, joined_)
    d_o = dot(g1_low, weight(r.expand_w, 3 * D, D), NT).astype(BF).astype(F32)
    query = r.top_b[:, Q_].astype(F32)
    wait(TOP, t_, a_, h_)
    r.class_row[...] = jnp.zeros_like(r.class_row)
    for image in range(images):
        rows = slice(image * PAD, image * PAD + PAD)
        mine, spread_o = by_head(d_o, image)
        _, spread_q = by_head(query, image)
        spread_o, spread_q = spread_o.astype(BF), spread_q.astype(BF)
        p_low = r.top_p[image]
        p = p_low.astype(F32)
        r.dt[rows, 2 * D :] = dot(p_low, spread_o).astype(BF)
        dp = dot(r.vm_t[rows, 2 * D :], spread_o, NT)
        ds = (p * (dp - jnp.sum(p * dp, 0, keepdims=True))).astype(BF)
        r.dt[rows, D : 2 * D] = (dot(ds, spread_q) * HEAD_DIM**-0.5).astype(BF)
        d_q = jnp.where(mine, dot(ds, r.vm_t[rows, D : 2 * D], TN), 0.0)
        r.class_row[image : image + 1] = jnp.sum(d_q, 0, keepdims=True) * HEAD_DIM**-0.5
    start(TOP - 1, t_)
    for part in range(2):
        value = dot(r.vm_a[...], r.dt[:, (part + 1) * D : (part + 2) * D], TN)
        store_cols(plan, r.unit, 0, part, KEYS, value, KEYS)
    if cube:
        run(jnp.int32(0), 0, False, KEYS)
    else:
        copies = [
            pltpu.make_async_copy(r.unit.at[(0, SEND)[i]], r.full.at[0, i], r.loads.at[joined_ + 1 + i])
            for i in range(2)
        ]
        start_all(copies)
        wait_all(copies)
    start(TOP - 1, a_)
    d_q = r.class_row[...].astype(BF)
    sources = (
        r.top_b[:, FEATURE_],
        r.top_b[:, LOGIT_],
        r.top_b[:, Z_],
        g_low,
        r.top_b[:, M_],
        r.top_du[...],
        r.top_b[:, O_],
        g1_low,
        r.top_b[:, A_],
        d_q,
    )
    r.rows_f[...] = jnp.zeros_like(r.rows_f)
    first = 0
    for source in sources:
        value = source.astype(F32)
        for j in range(value.shape[1] // 128):
            for image in range(images):
                at = image * PER_IMAGE + first + j
                r.rows_f[at : at + 1] = value[image : image + 1, j * 128 : j * 128 + 128]
        first += value.shape[1] // 128
    r.rows_block[...] = r.rows_f[...].astype(BF)
    if cube:
        top_rows.stage0()
    else:
        save = load(r.rows_block, r.top_rows, r.loads.at[joined_ + 1])
        save.wait()
    r.g1[...] = dot(r.dt[:, D : 2 * D], weight(r.expand_w, D, D), NT)
    r.g1[...] += dot(r.dt[:, 2 * D :], weight(r.expand_w, 2 * D, D), NT)
    d_a = dot(d_q, weight(r.expand_w, 0, D), NT)
    for image in range(images):
        r.g1[image * PAD : image * PAD + 1] += d_a[image : image + 1]
    start(TOP - 1, expand_)
    d_h, d_gain, d_shift = normalize_back(r.vm_h[...], row(r.params, base), r.g1[...])
    r.g[...] = d_h
    for image in range(images):
        r.g[image * PAD : image * PAD + 1] += g1[image : image + 1]
    r.vectors[base : base + 1] = d_gain
    r.vectors[base + 1 : base + 2] = d_shift
    start(TOP - 1, h_)

    @pl.loop(1, LAYERS)
    def _(it):
        layer = TOP - it
        below = it < TOP
        unit_s = 3 * it - 2
        base = S + 2 + 4 * layer
        r.gr[...] = r.g[...].astype(BF)
        wait(layer, z_)
        slot = unit_s % 4
        pl.when(it == 1)(lambda: sent(unit_s, KEYS))
        pl.when(it > 1)(lambda: sent(unit_s))

        @pl.loop(0, 8)
        def _(j):
            cols = pl.ds(pl.multiple_of(j * (D // 2), 128), D // 2)
            store_rows(plan, r.unit, slot, j, dot(r.vm_z[:, cols], r.gr[...], TN))

        point(it, 0)
        if cube:
            pl.when(it == 1)(top_rows.stage1)
        wait(layer, shrink_, slope_, expand_, m_, h1_)
        pl.when(below)(lambda: start(layer - 1, z_))
        slot_e = (unit_s + 1) % 4
        r.g1[...] = jnp.zeros_like(r.g1)
        sent(unit_s + 1)

        @pl.loop(0, 4)
        def _(j):
            cols = pl.ds(pl.multiple_of(j * D, 128), D)
            dz = dot(r.gr[...], r.shrink_w[j].reshape(D, D), NT)
            du = (dz * r.vm_slope[:, cols].astype(F32)).astype(BF)
            r.vm_slope[:, cols] = du
            store_cols(plan, r.unit, slot_e, j, D, dot(r.vm_m[...], du, TN))

        pl.when(below)(lambda: start(layer - 1, shrink_, m_))
        point(it, 1)
        if cube:
            pl.when(it == 1)(top_rows.stage2)

        @pl.loop(0, 4)
        def _(j):
            cols = pl.ds(pl.multiple_of(j * D, 128), D)
            r.g1[...] += dot(r.vm_slope[:, cols], weight(r.expand_w, j * D, D), NT)

        start(layer, joined_)
        pl.when(below)(lambda: start(layer - 1, slope_))
        d_h1, d_gain, d_shift = normalize_back(r.vm_h1[...], row(r.params, base + 2), r.g1[...])
        r.g1[...] = r.g[...] + d_h1
        r.vectors[pl.ds(base + 2, 1)] = d_gain
        r.vectors[pl.ds(base + 3, 1)] = d_shift
        pl.when(below)(lambda: start(layer - 1, h1_))

        r.gr[...] = r.g1[...].astype(BF)
        slot_t = (unit_s + 2) % 4
        wait(layer, o_)
        sent(unit_s + 2)
        store_cols(plan, r.unit, slot_t, 3, D, dot(r.vm_o[...], r.gr[...], TN))
        wait(layer, joined_)
        r.do[...] = dot(r.gr[...], weight(r.expand_w, 3 * D, D), NT).astype(BF)
        wait(layer, t_, p_, a_, h_)

        def heads(step):
            image, pair = step // (HEADS // 2), step % (HEADS // 2)
            rows = pl.ds(pl.multiple_of(image * PAD, 16), PAD)
            lanes = [pl.ds(pl.multiple_of(pair * 128 + part * D, 128), 128) for part in range(3)]
            q, key, v = (r.vm_t[rows, lane] for lane in lanes)
            do = r.do[rows, lanes[0]]
            zero = jnp.zeros_like(v)
            dqs, dks, dvs = [], [], []
            for which in range(2):
                part = jnp.where(low_lane, v, zero) if which == 0 else jnp.where(low_lane, zero, v)
                p_low = r.vm_p[step * 2 + which]
                p = p_low.astype(F32)
                dvs.append(dot(p_low, do))
                dp = dot(part, do, NT)
                ds = (p * (dp - jnp.sum(p * dp, 0, keepdims=True))).astype(BF)
                dqs.append(dot(ds, key, TN))
                dks.append(dot(ds, q))
            r.dt[rows, lanes[0]] = (jnp.where(low_lane, dqs[0], dqs[1]) * scale).astype(BF)
            r.dt[rows, lanes[1]] = (jnp.where(low_lane, dks[0], dks[1]) * scale).astype(BF)
            r.dt[rows, lanes[2]] = jnp.where(low_lane, dvs[0], dvs[1]).astype(BF)

        half = images * (HEADS // 2) // 2
        pl.loop(0, half)(heads)
        point(it, 2)
        if cube:
            pl.when(it == 1)(top_rows.stage3)
        pl.loop(half, 2 * half)(heads)
        pl.when(below)(lambda: start(layer - 1, o_, t_, p_))
        r.g[...] = jnp.zeros_like(r.g)

        @pl.loop(0, 3)
        def _(j):
            cols = pl.ds(pl.multiple_of(j * D, 128), D)
            store_cols(plan, r.unit, slot_t, j, D, dot(r.vm_a[...], r.dt[:, cols], TN))

        point(it, 3)
        if cube:
            pl.when(it == 1)(top_rows.finish)

        @pl.loop(0, 3)
        def _(j):
            cols = pl.ds(pl.multiple_of(j * D, 128), D)
            r.g[...] += dot(r.dt[:, cols], weight(r.expand_w, j * D, D), NT)

        d_h, d_gain, d_shift = normalize_back(r.vm_h[...], row(r.params, base), r.g[...])
        r.g[...] = r.g1[...] + d_h
        r.vectors[pl.ds(base, 1)] = d_gain
        r.vectors[pl.ds(base + 1, 1)] = d_shift
        pl.when(below)(lambda: start(layer - 1, a_, h_, expand_))

    slot = UNITS % 4
    sent(jnp.int32(UNITS))
    for part in range(2):
        half = D // 2
        value = jnp.zeros((D, half), F32)
        for image in range(images):
            rows = r.g[image * PAD + 1 : image * PAD + S, part * half : (part + 1) * half]
            value = value + dot(r.images[image], rows.astype(BF), TN)
        store_cols(plan, r.unit, slot, part, half, value, half)
    pos = r.g[:PAD]
    for image in range(1, images):
        pos = pos + r.g[image * PAD : (image + 1) * PAD]
    r.vectors[:S] = pos[:S]
    r.vectors[S : S + 1] = pos[:1]
    r.vectors[S + 1 : S + 2] = jnp.sum(pos[1:S], 0, keepdims=True)
    if not cube:
        copies = [
            pltpu.make_async_copy(r.unit.at[(slot, SEND)[i]], r.full.at[UNITS, i], r.loads.at[i])
            for i in range(2)
        ]
        copies.append(pltpu.make_async_copy(r.vectors, r.vector_rows, r.loads.at[2]))
        start_all(copies)
        wait_all(copies)
        return
    store_vectors(plan, r.unit, slot, r.vectors[...])

    drain()
    r.tail_block[:BLOCK] = r.total[UNITS % 2, :, D // 2 : TAIL]
    line = lax.broadcasted_iota(jnp.int32, (8, 128), 0)
    squares, loss = jnp.sum(r.squares[...]), r.tail_in[0:1, 0:128]
    r.tail_block[BLOCK:] = jnp.where(line == 0, squares, jnp.where(line == 1, loss, 0.0))
    gather = SmallGather(plan, r.tail_block, r.vector_rows, r.tail_send, r.tail_recv)
    gather.stage0()
    gather.stage1()
    gather.stage2()
    gather.stage3()
    run(jnp.int32(UNITS), 6, False, TAIL)
    Reduce(plan, r, jnp.int32(UNITS), TAIL).copy(0).wait_send()
    gather.finish()


def backward(plan, images, params, done):
    rows = images.shape[0] * PAD
    shapes = saved_shapes(rows)
    inputs = given_in(
        VMEM_SPEC,
        images=images,
        params=params,
        tail_in=done.tail,
        top_b=done.top_b,
        top_f=done.top_f,
        top_p=done.top_p,
    )
    block = rows_block(images.shape[0])
    inputs.update(
        given_in(
            ANY_SPEC,
            joined_whole=done.joined_whole,
            expand_whole=done.expand_whole,
            shrink_whole=done.shrink_whole,
        )
    )
    inputs.update({"keep_" + name: (getattr(done, "keep_" + name), ANY_SPEC) for name in SAVED})
    if plan.cube:
        outputs = dict(
            owned=((UNITS - 1, 2, HALF, WIDTH), F32, ANY_SPEC),
            keys=((2, HALF, KEYS), F32, ANY_SPEC),
            patch=((2, HALF, D // 2), F32, ANY_SPEC),
            vector_rows=(CHIPS + (2, BLOCK + 8, 128), F32, ANY_SPEC),
            top_rows=(CHIPS + (2, block, 128), BF, ANY_SPEC),
        )
    else:
        outputs = dict(
            full=((UNITS + 1, 2, 4, 4, BLOCK, WIDTH), BF, ANY_SPEC),
            vector_rows=((VEC_ROWS, D), F32, ANY_SPEC),
            top_rows=((block, 128), BF, ANY_SPEC),
        )
    scratch = {"vm_" + name: pltpu.VMEM(shape, kind) for name, (shape, kind) in shapes.items()}
    scratch.update(
        vmem(
            BF,
            expand_w=cols_shape(FF),
            shrink_w=ROWS_SHAPE,
            gr=(rows, D),
            do=(rows, D),
            dt=(rows, 3 * D),
            unit=(SEND + 1, 4, 4, BLOCK, WIDTH),
            top_du=(HEAD_ROWS, FF),
            rows_block=(block, 128),
        )
    )
    scratch.update(
        vmem(
            F32,
            g=(rows, D),
            g1=(rows, D),
            vectors=(VEC_ROWS, D),
            class_row=(HEAD_ROWS, D),
            rows_f=(block, 128),
        )
    )
    scratch.update(dma(loads=(15,)))
    extra = {}
    if plan.cube:
        other = other_part(WIDTH)
        most = WIDTH - other
        scratch.update(
            vmem(
                BF,
                core=(4, 4, BLOCK, WIDTH),
                near=(3, 4, BLOCK, cut_of(most)),
                far=(3, 4, BLOCK, most - cut_of(most)),
                x=(3, 4, BLOCK, most),
                y=(3, 4, BLOCK, most),
                line=(3, 4, BLOCK, most),
                main_two=(3, 2, BLOCK, most),
                main_one=(4, 2, BLOCK, most),
                other_two=(3, 2, 4, BLOCK, other),
                other_one=(4, 2, 4, BLOCK, other),
                plane=(3, 4, BLOCK, other),
                other_near=(3, BLOCK, cut_of(other)),
                other_far=(3, BLOCK, other - cut_of(other)),
                other_x=(3, BLOCK, other),
                other_y=(3, BLOCK, other),
            )
        )
        scratch.update(
            vmem(F32, total=(2, BLOCK, WIDTH), squares=(8, WIDTH), tail_block=(BLOCK + 8, 128))
        )
        scratch.update(
            dma(send=(4, 20), recv=(4, 18), rows_send=(7,), rows_recv=(7,), tail_send=(7,), tail_recv=(7,))
        )
        scratch.update(credit=pltpu.SemaphoreType.REGULAR)
        extra = dict(collective_id=2, has_side_effects=True)
    return pallas(functools.partial(backward_kernel, plan), "backward", inputs, outputs, scratch, **extra)


PARAMS = ("patch", "triple", "output", "expand", "shrink", "vector", "head")
KINDS = ("w_", "m_", "s_")


def adam_update(master, moment, square, gradient, step_rate):
    moment_new = BETA_ONE * moment + (1.0 - BETA_ONE) * gradient
    square_new = BETA_TWO * square + (1.0 - BETA_TWO) * gradient * gradient
    moment_hat = moment_new / (1.0 - BETA_ONE**STEP_INDEX)
    square_hat = square_new / (1.0 - BETA_TWO**STEP_INDEX)
    master_new = master - step_rate * (
        moment_hat / (jnp.sqrt(square_hat) + ADAM_EPS) + DECAY * master
    )
    return (master_new, moment_new, square_new)


def class_matrices(ref, images, devices, stride):
    first, found = 0, []
    for columns in PIECES:
        count = columns // 128
        parts = [
            jnp.concatenate(
                [
                    ref[pl.ds(image * PER_IMAGE + first + j, devices, stride=stride), :]
                    for j in range(count)
                ],
                1,
            )
            for image in range(images)
        ]
        found.append(jnp.concatenate(parts, 0).astype(BF))
        first += count
    return found


def own_columns(value, first, count):
    at = lax.broadcasted_iota(jnp.int32, (value.shape[1], 128), 0)
    to = lax.broadcasted_iota(jnp.int32, (value.shape[1], 128), 1)
    chosen = jnp.where((at == to + first) & (to < count), 1.0, 0.0).astype(BF)
    return dot(value, chosen).astype(BF)


def update_kernel(plan, images, names, *refs):
    r = SimpleNamespace(**dict(zip(names, refs)))
    named = dict(zip(names, refs))
    groups = [
        [(named[kind + name], named["vm_" + kind + name], named["to_" + kind + name]) for kind in KINDS]
        for name in PARAMS
    ]
    patch, triple, output, expand, shrink, vector, head = range(7)

    def moves(group, back):
        return [
            pltpu.make_async_copy(*((buf, out) if back else (src, buf)), r.sems.at[3 * group + k])
            for k, (src, buf, out) in enumerate(groups[group])
        ]

    order = (head, shrink, expand, triple, output, patch, vector)
    for group in order:
        start_all(moves(group, False))

    tile = jnp.sum(r.tails[:, BLOCK:, :], 0)
    r.rows_f[...] = r.top_rows[...].astype(F32)
    stride = r.top_rows.shape[0] // plan.n
    found = class_matrices(r.rows_f, images, plan.n, stride)
    features, d_logits, z, g, m, du, o, g1, a, dq = found
    r.features[...] = features
    r.d_logits[...] = d_logits
    alike = (dot(features, features, NT) + 1.0) * dot(d_logits, d_logits, NT)
    for left, right in ((z, g), (m, du), (o, g1), (a, dq)):
        alike = alike + dot(left, left, NT) * dot(right, right, NT)
    norm = jnp.sqrt(tile[0:1, 0:1] + jnp.sum(alike))
    me = plan.me()

    def top_grad(left, right, rows):
        return dot(own_columns(left, me * rows, rows), right, TN)[:rows]

    clip = CLIP / jnp.maximum(norm, CLIP)
    line = lax.broadcasted_iota(jnp.int32, (8, 128), 0)
    r.scalars[...] = jnp.where(line == 0, norm, tile[1:2])

    def step(group, at, gradient, rate):
        bufs = [buf for _, buf, _ in groups[group]]
        new = adam_update(*[buf[at] for buf in bufs], gradient * clip, rate)
        for buf, value in zip(bufs, new):
            buf[at] = value

    def finish(group):
        start_all(moves(group, True))

    every = slice(None)
    wait_all(moves(head, False))

    @pl.loop(0, D // 128)
    def _(j):
        rows = pl.ds(pl.multiple_of(j * 128, 128), 128)
        gradient = dot(r.features[:, rows], r.d_logits[...], TN)
        step(head, (rows, every), gradient[:, :CLASSES], RATE_MATRIX)

    bias = jnp.sum(d_logits.astype(F32), 0, keepdims=True)[:, :CLASSES]
    step(head, (slice(D, D + 1), every), bias, RATE_MATRIX)
    r.bias_grad[...] = bias * clip
    finish(head)
    wait_all(moves(shrink, False))

    step(shrink, (TOP, every, every), top_grad(z, g, BLOCK_FF), RATE_MATRIX)

    @pl.loop(0, TOP)
    def _(layer):
        unit = 3 * (TOP - 1 - layer)
        for k in range(4):
            gradient = r.owned[unit, k % 2, :, pl.ds(k // 2 * D, D)]
            step(shrink, (layer, pl.ds(k * HALF, HALF), every), gradient, RATE_MATRIX)

    finish(shrink)
    wait_all(moves(expand, False))

    step(expand, (TOP, every, every), top_grad(m, du, HALF), RATE_MATRIX)

    @pl.loop(0, TOP)
    def _(layer):
        unit = 3 * (TOP - 1 - layer) + 1
        for k in range(2):
            step(expand, (layer, every, pl.ds(k * WIDTH, WIDTH)), r.owned[unit, k], RATE_MATRIX)

    finish(expand)
    wait_all(moves(triple, False))
    wait_all(moves(output, False))

    step(output, (TOP, every, every), top_grad(o, g1, HALF), RATE_OUTPUT)
    step(triple, (TOP, every, pl.ds(0, D)), top_grad(a, dq, HALF), RATE_MATRIX)
    for k in range(2):
        step(triple, (TOP, every, pl.ds((k + 1) * D, D)), r.keys[k], RATE_MATRIX)

    @pl.loop(0, TOP)
    def _(layer):
        unit = 3 * (TOP - 1 - layer) + 2
        step(triple, (layer, every, pl.ds(0, WIDTH)), r.owned[unit, 0], RATE_MATRIX)
        step(triple, (layer, every, pl.ds(WIDTH, D)), r.owned[unit, 1, :, pl.ds(0, D)], RATE_MATRIX)
        step(output, (layer, every, every), r.owned[unit, 1, :, pl.ds(D, D)], RATE_OUTPUT)

    finish(triple)
    finish(output)
    wait_all(moves(patch, False))
    for k in range(2):
        step(patch, (every, pl.ds(k * (D // 2), D // 2)), r.patch_grad[k], RATE_MATRIX)
    finish(patch)
    count = groups[vector][0][0].shape[0]
    for d in range(-(-count // 8)):
        for j in range(6):
            r.vector_grad[8 * d : 8 * d + 8, 128 * j : 128 * j + 128] = r.tails[d, 8 * j : 8 * j + 8, :]
    wait_all(moves(vector, False))
    step(vector, (every, every), r.vector_grad[:count], RATE_VECTOR)
    finish(vector)
    for group in order:
        wait_all(moves(group, True))


def update(plan, images, states, got):
    inputs, outputs, scratch = {}, {}, {}
    for name, state in zip(PARAMS, states):
        for kind, value in zip(KINDS, state):
            inputs[kind + name] = (value, ANY_SPEC)
            outputs["to_" + kind + name] = (value.shape, F32, ANY_SPEC)
            scratch["vm_" + kind + name] = pltpu.VMEM(value.shape, F32)
    inputs.update(
        given_in(
            VMEM_SPEC,
            owned=got.owned,
            patch_grad=got.patch,
            tails=got.vector_rows.reshape(plan.n, BLOCK + 8, 128),
            keys=got.keys,
            top_rows=got.top_rows.reshape(-1, 128),
        )
    )
    outputs.update(scalars=((8, 128), F32, VMEM_SPEC), bias_grad=((1, CLASSES), F32, VMEM_SPEC))
    scratch.update(vmem(BF, features=(plan.n * images, D), d_logits=(plan.n * images, 1024)))
    scratch.update(vmem(F32, vector_grad=(VEC_ROWS, D), rows_f=(plan.n * rows_block(images), 128)))
    scratch.update(dma(sems=(3 * len(PARAMS),)))
    new = pallas(functools.partial(update_kernel, plan, images), "update", inputs, outputs, scratch)
    states = [[getattr(new, "to_" + kind + name) for kind in KINDS] for name in PARAMS]
    return new.scalars[0, 0], new.scalars[1, 0], states, new.bias_grad[0]


AXES = ("wide", "grp")


def update_whole(plan, images, states, got, done):
    full = got.full.reshape(UNITS + 1, 2, 16, BLOCK, WIDTH)
    layers = full[1:UNITS].reshape(TOP, 3, 2, 16, BLOCK, WIDTH)[::-1]

    def scattered(whole):
        axis = whole.ndim - 2
        return lax.psum_scatter(whole, AXES, scatter_dimension=axis, tiled=True).astype(F32)

    def from_cols(part):
        joined = jnp.concatenate([part[..., 0, :, :, :], part[..., 1, :, :, :]], -1)
        return joined.reshape(part.shape[:-4] + (D, -1))

    shrink = layers[:, 0].reshape(TOP, 2, 16, BLOCK, 2, D).transpose(0, 2, 1, 4, 3, 5)
    joined = scattered(from_cols(layers[:, 2]))
    rows_all = lax.all_gather(got.top_rows, AXES, axis=0)[:, : PER_IMAGE * images]
    rows_all = rows_all.reshape(plan.n * images, PER_IMAGE * 128)
    ends = [sum(PIECES[: k + 1]) for k in range(len(PIECES))]
    features, d_logits, z, g, m, du, o, g1, a, dq = jnp.split(rows_all, ends[:-1], axis=1)
    d_logits = d_logits[:, :CLASSES]
    bias = jnp.sum(d_logits.astype(F32), 0)[None]

    def top_grad(left, right):
        whole = dot(left, right, TN)
        count = whole.shape[0] // plan.n
        return lax.dynamic_slice_in_dim(whole, plan.me() * count, count)

    def with_top(below, top):
        return jnp.concatenate([below, top[None]], 0)

    keys = scattered(from_cols(full[0, ..., :KEYS]))
    split = [
        scattered(from_cols(full[UNITS, ..., : D // 2])),
        with_top(joined[:, :, : 3 * D], jnp.concatenate([top_grad(a, dq), keys], 1)),
        with_top(joined[:, :, 3 * D :], top_grad(o, g1)),
        with_top(scattered(from_cols(layers[:, 1])), top_grad(m, du)),
        with_top(scattered(shrink.reshape(TOP, FF, D)), top_grad(z, g)),
    ]
    same = [
        lax.psum(got.vector_rows[: states[5][0].shape[0]], AXES),
        jnp.concatenate([dot(features, d_logits, TN), bias], 0),
    ]
    squares = lax.psum(sum(jnp.sum(g * g) for g in split), AXES) + sum(jnp.sum(g * g) for g in same)
    norm = jnp.sqrt(squares)
    clip = CLIP / jnp.maximum(norm, CLIP)
    rates = [RATE_MATRIX] * 2 + [RATE_OUTPUT] + [RATE_MATRIX] * 2 + [RATE_VECTOR, RATE_MATRIX]
    states = [
        adam_update(*state, gradient * clip, rate)
        for state, gradient, rate in zip(states, split + same, rates)
    ]
    return norm, lax.psum(done.tail[0, 0], AXES), states, bias[0] * clip


def per_device(plan, images, slot_mask, labels, *params):
    states = [params[3 * k : 3 * k + 3] for k in range(7)]
    patch, triple, output, expand, shrink, vector, head = (state[0] for state in states)
    count = images.shape[0]
    pad_rows = ((0, HEAD_ROWS - count), (0, 0))
    weights = slot_mask.astype(F32)
    args = dict(
        images=images,
        vectors=vector,
        head=head,
        labels=jnp.pad(labels[:, None], pad_rows),
        weights=jnp.pad(weights[:, None], pad_rows),
    )
    if plan.cube:
        shards = dict(patch=patch, triple=triple, output=output, expand=expand, shrink=shrink)
        done = forward(plan, shards, args, None, None)
    else:

        def whole(shard, shape):
            axis = shard.ndim - 2
            gathered = lax.all_gather(shard.astype(BF), AXES, axis=axis, tiled=True)
            return gathered.reshape(shard.shape[:axis] + shape)

        gathered = [
            whole(patch, cols_shape(D)),
            whole(jnp.concatenate([triple, output], 2), cols_shape(FF)),
            whole(expand, cols_shape(FF)),
            whole(shrink, ROWS_SHAPE),
        ]
        total = jnp.full((8, 128), lax.psum(jnp.sum(weights), AXES), F32)
        done = forward(plan, None, args, gathered, total)
    got = backward(plan, images, vector, done)
    if plan.cube:
        norm, loss, states, bias_grad = update(plan, count, states, got)
    else:
        norm, loss, states, bias_grad = update_whole(plan, count, states, got, done)
    return (
        loss,
        done.total[0, 0],
        norm,
        *(value for state in states for value in state),
        bias_grad,
    )


def solution(mesh):
    plan = Plan(mesh)
    rows = P(AXES, None)
    layers = P(None, AXES, None)
    in_specs = (P(AXES, None, None), P(AXES), P(AXES)) + (rows,) * 3 + (layers,) * 12 + (P(),) * 6
    out_specs = (P(),) * 3 + (rows,) * 3 + (layers,) * 12 + (P(),) * 7
    return jax.shard_map(
        functools.partial(per_device, plan),
        mesh=mesh,
        in_specs=in_specs,
        out_specs=out_specs,
        check_vma=False,
    )
```

```python
import functools
from types import SimpleNamespace

import jax
import jax.numpy as jnp
from jax import lax
from jax.experimental import pallas as pl
from jax.experimental.pallas import tpu as pltpu
from jax.sharding import PartitionSpec as P

D = 768
HEADS = 12
HEAD_DIM = 64
FF = 3072
CLASSES = 1000
LAYERS = 3
STEP_INDEX = 10
S = 197
PAD = 208

EPS_NORM = 1e-06
CLIP = 0.1
BETA_ONE = 0.9
BETA_TWO = 0.95
ADAM_EPS = 1e-08
DECAY = 0.05
RATE_MATRIX = 0.03
RATE_OUTPUT = 0.2
RATE_VECTOR = 0.3
SMOOTH = 0.1

F32 = jnp.float32
BF = jnp.bfloat16
NN = (((1,), (0,)), ((), ()))
NT = (((1,), (1,)), ((), ()))
TN = (((0,), (0,)), ((), ()))
VMEM_SPEC = pl.BlockSpec(memory_space=pltpu.VMEM)
ANY_SPEC = pl.BlockSpec(memory_space=pl.ANY)
LIMIT = 62 * 1024 * 1024


def dot(left, right, form=NN):
    return lax.dot_general(left, right, form, preferred_element_type=F32)


def normalize(values, gain_row, shift_row):
    center = values - jnp.mean(values, -1, keepdims=True)
    spread = jnp.mean(center * center, -1, keepdims=True)
    return center * lax.rsqrt(spread + EPS_NORM) * gain_row + shift_row


def normalize_back(values, gain_row, grad):
    center = values - jnp.mean(values, -1, keepdims=True)
    spread = jnp.mean(center * center, -1, keepdims=True)
    scale = lax.rsqrt(spread + EPS_NORM)
    unit = center * scale
    d_unit = grad * gain_row
    d_values = scale * (
        d_unit
        - jnp.mean(d_unit, -1, keepdims=True)
        - unit * jnp.mean(d_unit * unit, -1, keepdims=True)
    )
    return (
        d_values,
        jnp.sum(grad * unit, 0, keepdims=True),
        jnp.sum(grad, 0, keepdims=True),
    )


def gelu_and_slope(u):
    x = jnp.abs(u) * 0.7071067811865476
    t = 1.0 / (1.0 + 0.3275911 * x)
    series = t * (
        0.254829592
        + t * (-0.284496736 + t * (1.421413741 + t * (-1.453152027 + t * 1.061405429)))
    )
    bell = jnp.exp(-0.5 * u * u)
    tail = 0.5 * series * bell
    share = jnp.where(u >= 0.0, 1.0 - tail, tail)
    return u * share, share + u * bell * 0.3989422804014327


class Plan:
    def __init__(self, mesh):
        self.wide, self.grp = mesh.shape["wide"], mesh.shape["grp"]
        self.n = self.wide * self.grp
        self.cube = self.wide == 8 and self.grp == 4

    def me(self):
        return lax.axis_index("wide") * self.grp + lax.axis_index("grp")

    def where(self):
        if not self.cube:
            return 0, 0, 0, 0
        wide, grp = lax.axis_index("wide"), lax.axis_index("grp")
        return wide // 2, wide % 2, grp // 2, grp % 2


CHIPS = (4, 2, 2)
BLOCK = D // 16
BLOCK_FF = FF // 32


def cols_shape(columns):
    return CHIPS + (BLOCK, columns)


ROWS_SHAPE = CHIPS + (2, BLOCK_FF, D)


def other_part(width):
    return width // 6 // 128 * 128


def cut_of(columns):
    return columns // 2 // 128 * 128


def over_links(plan):
    z, x, y, c = plan.where()

    def at(z, x, y, c):
        return (z * 2 + x, y * 2 + c)

    return SimpleNamespace(
        z1=at(jnp.bitwise_xor(z, 1), x, y, c),
        z3=at(jnp.bitwise_xor(z, 3), x, y, c),
        x=at(z, 1 - x, y, c),
        y=at(z, x, 1 - y, c),
        core=at(z, x, y, 1 - c),
    )


def remote(src, dst, send, recv, to):
    return pltpu.make_async_remote_copy(
        src_ref=src,
        dst_ref=dst,
        send_sem=send,
        recv_sem=recv,
        device_id=to,
        device_id_type=pl.DeviceIdType.MESH,
    )


class Gather:
    def __init__(self, plan, by_cols, block, whole, send, recv):
        self.z, self.x, self.y, self.c = plan.where()
        self.to = over_links(plan)
        self.by_cols, self.block, self.whole = by_cols, block, whole
        self.send, self.recv = send, recv
        self.width = block.shape[-1]
        self.other = other_part(self.width)
        self.most = self.width - self.other
        self.cut = (self.most // 2 + 127) // 128 * 128

    def region(self, z, x, y, start, width):
        if self.by_cols:
            first = pl.multiple_of(self.c * self.width + start, 128)
            return self.whole.at[z, x, y, :, pl.ds(first, width)]
        return self.whole.at[z, x, y, self.c, :, pl.ds(start, width)]

    def part(self, start, width):
        return self.block.at[:, pl.ds(start, width)]

    def copy(self, at):
        z, x, y, to = self.z, self.x, self.y, self.to
        z1, z3, line = jnp.bitwise_xor(z, 1), jnp.bitwise_xor(z, 3), slice(None)
        most, other, region = self.most, self.other, self.region
        cut, cut_other = self.cut, most + max(cut_of(other), 128)
        landed = at
        if at in (0, 1):
            src, dst = self.part(0, most), region(z, x, y, 0, most)
            device = (to.z1, to.z3)[at]
        elif at in (8, 9):
            src, dst = self.part(most, other), region(z, x, y, most, other)
            device = (to.x, to.y)[at - 8]
        else:
            src, device = {
                2: lambda: (region(z3, x, y, 0, most), to.z1),
                3: lambda: (region(z1, x, y, 0, most), to.z3),
                4: lambda: (region(line, x, y, 0, most), to.x),
                5: lambda: (region(line, x, y, 0, most), to.y),
                6: lambda: (region(line, x, 1 - y, 0, cut), to.x),
                7: lambda: (region(line, 1 - x, y, cut, most - cut), to.y),
                10: lambda: (region(z, x, 1 - y, most, cut_other - most), to.x),
                11: lambda: (region(z, 1 - x, y, cut_other, self.width - cut_other), to.y),
                12: lambda: (region(z, line, line, most, other), to.z1),
                13: lambda: (region(z, line, line, most, other), to.z3),
                14: lambda: (region(z3, line, line, most, other), to.z1),
                15: lambda: (region(z1, line, line, most, other), to.z3),
                16: lambda: (region(line, x, y, 0, most), to.core),
                17: lambda: (region(line, 1 - x, y, 0, most), to.core),
                18: lambda: (region(line, x, 1 - y, 0, most), to.core),
                19: lambda: (region(line, 1 - x, 1 - y, 0, cut), to.core),
                20: lambda: (region(line, 1 - x, 1 - y, cut, most - cut), to.core),
                21: lambda: (region(line, line, line, most, other), to.core),
            }[at]()
            dst = src
            if at in (3, 15):
                landed = at - 1
        return remote(src, dst, self.send.at[at], self.recv.at[landed], device)

    def exists(self, at):
        if at in (8, 9, 10, 12, 13, 14, 15, 21):
            return self.other > 0
        return at != 11 or self.other > 128

    def keep(self):
        here = self.region(self.z, self.x, self.y, 0, self.width)
        return pltpu.make_async_copy(self.block, here, self.send.at[22])

    def start(self, *which):
        for at in which:
            if self.exists(at):
                self.copy(at).start()

    def arrived(self, *which):
        for at in which:
            if self.exists(at):
                self.copy(at).wait_recv()

    def in_middle(self, do):
        pl.when((self.z == 1) | (self.z == 2))(do)

    def stage0(self):
        self.start(0, 1, 8, 9)
        self.keep().start()

    def stage1(self):
        self.arrived(0, 1)
        self.in_middle(lambda: self.start(2, 3))
        self.arrived(8, 9)
        self.start(10, 11)
        self.keep().wait()

    def stage2(self):
        self.arrived(2)
        self.start(4, 5, 16)
        self.arrived(10, 11)
        self.start(12, 13)

    def stage3(self):
        self.arrived(4, 5)
        self.start(6, 7, 17, 18)
        self.arrived(12, 13)
        self.in_middle(lambda: self.start(14, 15))

    def stage4(self):
        self.arrived(6, 7)
        self.start(19, 20)
        self.arrived(14)
        self.start(21)

    def finish(self):
        self.arrived(16, 17, 18, 19, 20, 21)
        passed = (2, 3, 14, 15)

        def sent(which):
            for at in which:
                if self.exists(at):
                    self.copy(at).wait_send()

        sent([at for at in range(22) if at not in passed])
        self.in_middle(lambda: sent(passed))


def cube_barrier(plan):
    z, x, y, c = plan.where()
    barrier = pltpu.get_barrier_semaphore()
    partners = [(jnp.bitwise_xor(z, k) * 2 + x, y * 2 + c) for k in (1, 2, 3)]
    partners += [
        (z * 2 + 1 - x, y * 2 + c),
        (z * 2 + x, (1 - y) * 2 + c),
        (z * 2 + x, y * 2 + 1 - c),
    ]
    for partner in partners:
        pl.semaphore_signal(barrier, inc=1, device_id=partner, device_id_type=pl.DeviceIdType.MESH)
    pl.semaphore_wait(barrier, len(partners))


def load(source, target, sem):
    copy = pltpu.make_async_copy(source, target, sem)
    copy.start()
    return copy


def start_all(copies):
    for copy in copies:
        copy.start()


def wait_all(copies):
    for copy in copies:
        copy.wait()


def weight(ref, first, width):
    cols = pl.ds(first if isinstance(first, int) else pl.multiple_of(first, 128), width)
    return ref[:, :, :, :, cols].reshape(D, width)


class SmallGather:
    def __init__(self, plan, block, whole, send, recv):
        self.z, self.x, self.y, self.c = plan.where()
        self.block, self.whole, self.send, self.recv = block, whole, send, recv

    def copy(self, at):
        z, x, y, c = self.z, self.x, self.y, self.c
        line = slice(None)
        if at < 3:
            src, dst = self.block, self.whole.at[z, x, y, c]
            to = (jnp.bitwise_xor(z, at + 1) * 2 + x, y * 2 + c)
        elif at == 3:
            src = dst = self.whole.at[line, x, y, c]
            to = (z * 2 + 1 - x, y * 2 + c)
        elif at == 4:
            src = dst = self.whole.at[line, line, y, c]
            to = (z * 2 + x, (1 - y) * 2 + c)
        else:
            src = dst = self.whole.at[line, line, line, c]
            to = (z * 2 + x, y * 2 + 1 - c)
        return pltpu.make_async_remote_copy(
            src_ref=src,
            dst_ref=dst,
            send_sem=self.send.at[at],
            recv_sem=self.recv.at[at],
            device_id=to,
            device_id_type=pl.DeviceIdType.MESH,
        )

    def keep(self):
        here = self.whole.at[self.z, self.x, self.y, self.c]
        return pltpu.make_async_copy(self.block, here, self.send.at[6])

    def stage0(self):
        for at in range(3):
            self.copy(at).start()
        self.keep().start()

    def stage1(self):
        for at in range(3):
            self.copy(at).wait_recv()
        self.keep().wait()
        self.copy(3).start()

    def stage2(self):
        self.copy(3).wait_recv()
        self.copy(4).start()

    def stage3(self):
        self.copy(4).wait_recv()
        self.copy(5).start()

    def finish(self):
        self.copy(5).wait_recv()
        for at in range(6):
            self.copy(at).wait_send()


FF_TILE = 512
HALF = BLOCK // 2
WIDTH = FF // 2
HEAD_ROWS = 16
FINAL = S + 2 + 4 * LAYERS
TOP = LAYERS - 1
CLASS_PAD = 1024

Z_, M_, O_, Q_, A_ = (slice(0, FF),) + tuple(slice(FF + k * D, FF + k * D + D) for k in range(4))
FEATURE_, LOGIT_ = slice(FF + 4 * D, FF + 5 * D), slice(FF + 5 * D, FF + 5 * D + CLASS_PAD)
SLOPE_, H1_, G_ = slice(0, FF), slice(FF, FF + D), slice(FF + D, FF + 2 * D)
PIECES = (D, CLASS_PAD, FF, D, D, FF, D, D, D, D)
PER_IMAGE = sum(PIECES) // 128


def rows_block(images):
    return -(-PER_IMAGE * images // 16) * 16


def class_rows(ref, source):
    ref[...] = jnp.zeros_like(ref)
    for image in range(source.shape[0] // PAD):
        ref[image : image + 1] = source[image * PAD : image * PAD + 1]


def by_head(rows, image):
    head = lax.broadcasted_iota(jnp.int32, (16, D), 0)
    lane = lax.broadcasted_iota(jnp.int32, (16, D), 1)
    mine = (lane >= head * HEAD_DIM) & (lane < head * HEAD_DIM + HEAD_DIM)
    return mine, jnp.where(mine, rows[image : image + 1], 0.0)


def saved_shapes(rows):
    heads = rows // PAD * HEADS
    return dict(
        h=((rows, D), F32),
        a=((rows, D), BF),
        t=((rows, 3 * D), BF),
        o=((rows, D), BF),
        p=((heads, PAD, PAD), BF),
        h1=((rows, D), F32),
        m=((rows, D), BF),
        z=((rows, FF), BF),
        slope=((rows, FF), BF),
    )


SAVED = tuple(saved_shapes(PAD))


def row(ref, at):
    return ref[pl.ds(at, 1)]


def share_shards(plan, r):
    z, x, y, c = plan.where()
    r.joined_f[:, :, : 3 * D] = r.triple[...]
    r.joined_f[:, :, 3 * D :] = r.output[...]
    mine = pl.ds(pl.multiple_of(c * HALF, 8), HALF)

    def part(core, width):
        return pl.ds(pl.multiple_of(core * width, 128), width)

    moves = [
        (r.patch.at[:, part(1 - c, D // 2)], r.patch_f.at[mine]),
        (r.joined_f.at[:, :, part(1 - c, WIDTH)], r.joined_b.at[:, mine]),
        (r.expand.at[:, :, part(1 - c, WIDTH)], r.expand_b.at[:, mine]),
    ]
    copies = [
        pltpu.make_async_remote_copy(
            src_ref=src,
            dst_ref=dst,
            send_sem=r.share_send.at[i],
            recv_sem=r.share_recv.at[i],
            device_id=(z * 2 + x, y * 2 + 1 - c),
            device_id_type=pl.DeviceIdType.MESH,
        )
        for i, (src, dst) in enumerate(moves)
    ]
    start_all(copies)
    r.patch_f[mine] = r.patch[:, part(c, D // 2)]
    r.joined_b[:, mine] = r.joined_f[:, :, part(c, WIDTH)]
    r.expand_b[:, mine] = r.expand[:, :, part(c, WIDTH)]
    for copy, src, dst in zip(
        copies,
        (r.patch_f, r.joined_b, r.expand_b),
        (r.patch_block, r.joined_block, r.expand_block),
    ):
        copy.wait_recv()
        dst[...] = src[...].astype(BF)
    for copy in copies:
        copy.wait_send()


def class_column(ref, kind):
    line = lax.broadcasted_iota(jnp.int32, (HEAD_ROWS, 1), 0)
    column = jnp.zeros((HEAD_ROWS, 1), kind)
    for image in range(ref.shape[0]):
        column = jnp.where(line == image, ref[image].astype(kind), column)
    return column


def head_part(r, first, image_total):
    table = r.table[...]
    gain, shift = r.vectors[FINAL : FINAL + 1], r.vectors[FINAL + 1 : FINAL + 2]
    feature = normalize(first, gain, shift).astype(BF)
    logits = dot(feature, table) + r.head[D : D + 1]
    ids = lax.broadcasted_iota(jnp.int32, logits.shape, 1)
    shifted = logits - jnp.max(logits, -1, keepdims=True)
    log_prob = shifted - jnp.log(jnp.sum(jnp.exp(shifted), -1, keepdims=True))
    target = jnp.where(ids == class_column(r.labels, jnp.int32), 1.0 - SMOOTH, 0.0) + SMOOTH / CLASSES
    weights = class_column(r.mask, F32)
    loss = jnp.sum(weights * -jnp.sum(target * log_prob, -1, keepdims=True))
    d_logits = ((weights / image_total) * (jnp.exp(log_prob) - target)).astype(BF)
    d_feature = dot(d_logits, table, NT)
    r.d_logits[...] = jnp.zeros_like(r.d_logits)
    r.d_logits[:, :CLASSES] = d_logits.astype(F32)
    r.top_b[:, FEATURE_] = feature
    r.top_b[:, LOGIT_] = r.d_logits[...].astype(BF)
    d_first, d_gain, d_shift = normalize_back(first, gain, d_feature)
    r.top_f[:, G_] = d_first
    r.tail[...] = jnp.zeros_like(r.tail)
    r.tail[0:1] = jnp.full((1, D), loss, F32)
    r.tail[1:2] = d_gain
    r.tail[2:3] = d_shift


def top_backward(plan, r):
    images = r.images.shape[0]
    base = S + 2 + 4 * TOP
    g = r.top_f[:, G_]
    g_low = g.astype(BF)
    for j in range(4):
        cols = slice(j * D, j * D + D)
        dz = dot(g_low, r.shrink_w[j].reshape(D, D), NT)
        r.top_du[:, cols] = (dz * r.top_f[:, cols]).astype(BF)
    d_m = jnp.zeros((HEAD_ROWS, D), F32)
    for j in range(4):
        d_m = d_m + dot(r.top_du[:, j * D : j * D + D], weight(r.expand_w, j * D, D), NT)
    d_h1, d_gain, d_shift = normalize_back(r.top_f[:, H1_], row(r.vectors, base + 2), d_m)
    r.tail[5:6] = d_gain
    r.tail[6:7] = d_shift
    g1 = g + d_h1
    g1_low = g1.astype(BF)
    d_o = dot(g1_low, weight(r.joined_w, 3 * D, D), NT).astype(BF).astype(F32)
    query = r.top_b[:, Q_].astype(F32)
    r.class_row[...] = jnp.zeros_like(r.class_row)
    for image in range(images):
        rows = slice(image * PAD, image * PAD + PAD)
        mine, spread_o = by_head(d_o, image)
        _, spread_q = by_head(query, image)
        spread_o, spread_q = spread_o.astype(BF), spread_q.astype(BF)
        p_low = r.top_p[image]
        p = p_low.astype(F32)
        r.d_keys[rows, D:] = dot(p_low, spread_o).astype(BF)
        dp = dot(r.t[rows, 2 * D :], spread_o, NT)
        ds = (p * (dp - jnp.sum(p * dp, 0, keepdims=True))).astype(BF)
        r.d_keys[rows, :D] = (dot(ds, spread_q) * HEAD_DIM**-0.5).astype(BF)
        d_q = jnp.where(mine, dot(ds, r.t[rows, D : 2 * D], TN), 0.0)
        r.class_row[image : image + 1] = jnp.sum(d_q, 0, keepdims=True) * HEAD_DIM**-0.5
    for part in range(2):
        value = dot(r.a[...], r.d_keys[:, part * D : part * D + D], TN)
        store_cols(plan, r.keys_block, 0, part, D, value, D, 1)
    keys = load(r.keys_block, r.keys_out, r.loads.at[0])
    d_q = r.class_row[...].astype(BF)
    r.g[...] = dot(r.d_keys[:, :D], weight(r.joined_w, D, D), NT)
    r.g[...] += dot(r.d_keys[:, D:], weight(r.joined_w, 2 * D, D), NT)
    d_a = dot(d_q, weight(r.joined_w, 0, D), NT)
    for image in range(images):
        r.g[image * PAD : image * PAD + 1] += d_a[image : image + 1]
    d_h, d_gain, d_shift = normalize_back(r.h[...], row(r.vectors, base), r.g[...])
    r.g[...] = d_h
    for image in range(images):
        r.g[image * PAD : image * PAD + 1] += g1[image : image + 1]
    r.tail[3:4] = d_gain
    r.tail[4:5] = d_shift
    sources = (
        r.top_b[:, FEATURE_],
        r.top_b[:, LOGIT_],
        r.top_b[:, Z_],
        g_low,
        r.top_b[:, M_],
        r.top_du[...],
        r.top_b[:, O_],
        g1_low,
        r.top_b[:, A_],
        d_q,
    )
    r.rows_f[...] = jnp.zeros_like(r.rows_f)
    first = 0
    for source in sources:
        value = source.astype(F32)
        for j in range(value.shape[1] // 128):
            for image in range(images):
                at = image * PER_IMAGE + first + j
                r.rows_f[at : at + 1] = value[image : image + 1, j * 128 : j * 128 + 128]
        first += value.shape[1] // 128
    r.rows_block[...] = r.rows_f[...].astype(BF)
    keys.wait()


def forward_kernel(plan, names, *refs):
    r = SimpleNamespace(**dict(zip(names, refs)))
    cube = plan.cube
    images = r.images.shape[0]
    patch, joined, expand, shrink = range(4)
    wholes = (r.patch_whole, r.joined_whole, r.expand_whole, r.shrink_whole)
    weights = (r.patch_w, r.joined_w, r.expand_w, r.shrink_w)
    if cube:
        blocks = (r.patch_block, r.joined_block, r.expand_block, r.shrink_block)
        cube_barrier(plan)
        r.shrink_block[...] = r.shrink[...].astype(BF)
        share_shards(plan, r)
        r.count[...] = jnp.full((8, 128), jnp.sum(class_column(r.mask, F32)), F32)
        counting = SmallGather(plan, r.count, r.counts, r.count_send, r.count_recv)

    def unit(kind, layer):
        if kind == patch:
            return Gather(plan, True, blocks[0], wholes[0], r.send.at[0], r.recv.at[0])
        at = 3 * layer + kind
        block, whole = blocks[kind].at[layer], wholes[kind].at[layer]
        return Gather(plan, kind != shrink, block, whole, r.send.at[at], r.recv.at[at])

    def ready(kind, layer):
        if cube:
            unit(kind, layer).finish()
        whole = wholes[kind] if kind == patch else wholes[kind].at[layer]
        return load(whole, weights[kind], r.loads.at[kind])

    held = (r.h, r.a, r.t, r.o, r.p, r.h1, r.m, r.z, r.slope)
    kept = (r.keep_h, r.keep_a, r.keep_t, r.keep_o, r.keep_p, r.keep_h1, r.keep_m, r.keep_z, r.keep_slope)
    h_, a_, t_, o_, p_, h1_, m_, z_, slope_ = range(9)

    def saves(layer, *which):
        return [pltpu.make_async_copy(held[k], kept[k].at[layer], r.saves.at[k]) for k in which]

    if cube:
        first = [unit(patch, 0), unit(joined, 0), unit(expand, 0), unit(shrink, 0), unit(joined, 1)]
        first[0].stage0()
        counting.stage0()
        first[1].stage0()
        first[0].stage1()
        first[2].stage0()
        first[1].stage1()
        first[0].stage2()
        first[3].stage0()
        first[2].stage1()
        first[1].stage2()
        first[0].stage3()
        first[4].stage0()
        first[3].stage1()
        first[2].stage2()
        first[1].stage3()
        first[0].stage4()
    r.table[...] = r.head[:D].astype(BF)
    ready(patch, 0).wait()
    for image in range(images):
        at = image * PAD
        r.h[at : at + 1] = r.vectors[0:1] + r.vectors[S : S + 1]
        embedded = dot(r.images[image], weight(r.patch_w, 0, D))
        r.h[at + 1 : at + S] = embedded + r.vectors[S + 1 : S + 2] + r.vectors[1:S]
        r.h[at + S : at + PAD] = jnp.zeros((PAD - S, D), F32)

    low_lane = lax.broadcasted_iota(jnp.int32, (PAD, 128), 1) < HEAD_DIM
    real_key = lax.broadcasted_iota(jnp.int32, (PAD, PAD), 0) < S

    @pl.loop(0, TOP)
    def _(layer):
        base = S + 2 + 4 * layer
        if cube:
            unit(expand, layer + 1).stage0()
            unit(joined, layer + 1).stage1()
            unit(shrink, layer).stage2()
            unit(expand, layer).stage3()
            unit(joined, layer).stage4()
        start_all(saves(layer, h_))

        @pl.when(layer > 0)
        def _():
            wait_all(saves(layer, a_, t_, o_, p_, h1_, m_))

        r.a[...] = normalize(r.h[...], row(r.vectors, base), row(r.vectors, base + 1)).astype(BF)
        ready(joined, layer).wait()

        @pl.loop(0, 3)
        def _(j):
            cols = pl.ds(pl.multiple_of(j * D, 128), D)
            r.t[:, cols] = dot(r.a[...], weight(r.joined_w, j * D, D)).astype(BF)

        start_all(saves(layer, a_, t_))

        def heads(step):
            image, pair = step // (HEADS // 2), step % (HEADS // 2)
            rows = pl.ds(pl.multiple_of(image * PAD, 16), PAD)
            lanes = [pl.ds(pl.multiple_of(pair * 128 + part * D, 128), 128) for part in range(3)]
            q, key, v = (r.t[rows, lane] for lane in lanes)
            zero = jnp.zeros_like(key)
            outs = []
            for which in range(2):
                part = jnp.where(low_lane, key, zero) if which == 0 else jnp.where(low_lane, zero, key)
                scores = dot(part, q, NT) * HEAD_DIM**-0.5
                scores = jnp.where(real_key, scores, -1e30)
                top = jnp.max(scores, 0, keepdims=True)
                e = jnp.exp(scores - top)
                p = (e * (1.0 / jnp.sum(e, 0, keepdims=True))).astype(BF)
                r.p[step * 2 + which] = p
                outs.append(dot(p, v, TN))
            r.o[rows, lanes[0]] = jnp.where(low_lane, outs[0], outs[1]).astype(BF)

        half = images * (HEADS // 2) // 2
        pl.loop(0, half)(heads)
        if cube:
            unit(shrink, layer + 1).stage0()
            unit(expand, layer + 1).stage1()
            unit(joined, layer + 1).stage2()

        pl.loop(half, 2 * half)(heads)
        start_all(saves(layer, o_, p_))
        r.h1[...] = r.h[...] + dot(r.o[...], weight(r.joined_w, 3 * D, D))
        start_all(saves(layer, h1_))
        if cube:
            unit(shrink, layer).stage3()
            unit(expand, layer).stage4()
            pl.when(layer == 0)(counting.stage1)
            pl.when(layer == 1)(counting.stage3)
        r.m[...] = normalize(r.h1[...], row(r.vectors, base + 2), row(r.vectors, base + 3)).astype(BF)
        start_all(saves(layer, m_))
        wait_all(saves(layer, h_))
        r.h[...] = r.h1[...]

        @pl.when(layer > 0)
        def _():
            wait_all(saves(layer, z_, slope_))

        ready(expand, layer).wait()

        @pl.loop(0, FF // FF_TILE)
        def _(j):
            cols = pl.ds(pl.multiple_of(j * FF_TILE, 128), FF_TILE)
            u = dot(r.m[...], weight(r.expand_w, j * FF_TILE, FF_TILE))
            z, slope = gelu_and_slope(u)
            r.z[:, cols] = z.astype(BF)
            r.slope[:, cols] = slope.astype(BF)

        start_all(saves(layer, z_, slope_))
        if cube:
            pl.when(layer < TOP - 1)(lambda: unit(joined, layer + 2).stage0())

            unit(shrink, layer + 1).stage1()
            unit(expand, layer + 1).stage2()
            unit(joined, layer + 1).stage3()
            unit(shrink, layer).stage4()
            pl.when(layer == 0)(counting.stage2)
            pl.when(layer == 1)(counting.finish)
        ready(shrink, layer).wait()

        @pl.loop(0, 4)
        def _(j):
            cols = pl.ds(pl.multiple_of(j * D, 128), D)
            r.h[...] += dot(r.z[:, cols], r.shrink_w[j].reshape(D, D))

    base = S + 2 + 4 * TOP
    if cube:
        unit(shrink, TOP).stage2()
        unit(expand, TOP).stage3()
        unit(joined, TOP).stage4()
    start_all(saves(TOP, h_))
    wait_all(saves(TOP, a_, t_) + saves(0, o_, p_, h1_, m_))
    r.a[...] = normalize(r.h[...], row(r.vectors, base), row(r.vectors, base + 1)).astype(BF)
    class_rows(r.first, r.h)
    first = r.first[...]
    r.top_b[:, A_] = normalize(first, row(r.vectors, base), row(r.vectors, base + 1)).astype(BF)
    ready(joined, TOP).wait()
    for j in (1, 2):
        r.t[:, j * D : j * D + D] = dot(r.a[...], weight(r.joined_w, j * D, D)).astype(BF)
    start_all(saves(TOP, a_, t_))
    query = dot(r.top_b[:, A_], weight(r.joined_w, 0, D)).astype(BF)
    r.top_b[:, Q_] = query
    if cube:
        unit(shrink, TOP).stage3()
        unit(expand, TOP).stage4()
    query = query.astype(F32)
    real = lax.broadcasted_iota(jnp.int32, (PAD, 16), 0) < S
    r.class_row[...] = jnp.zeros_like(r.class_row)
    for image in range(images):
        rows = slice(image * PAD, image * PAD + PAD)
        mine, spread = by_head(query, image)
        scores = dot(r.t[rows, D : 2 * D], spread.astype(BF), NT) * HEAD_DIM**-0.5
        scores = jnp.where(real, scores, -1e30)
        e = jnp.exp(scores - jnp.max(scores, 0, keepdims=True))
        p = (e * (1.0 / jnp.sum(e, 0, keepdims=True))).astype(BF)
        r.top_p[image] = p
        out = jnp.where(mine, dot(p, r.t[rows, 2 * D :], TN), 0.0)
        r.class_row[image : image + 1] = jnp.sum(out, 0, keepdims=True)
    attended = r.class_row[...].astype(BF)
    r.top_b[:, O_] = attended
    h1 = first + dot(attended, weight(r.joined_w, 3 * D, D))
    r.top_f[:, H1_] = h1
    r.top_b[:, M_] = normalize(h1, row(r.vectors, base + 2), row(r.vectors, base + 3)).astype(BF)
    ready(expand, TOP).wait()
    for j in range(4):
        cols = slice(j * D, j * D + D)
        z, slope = gelu_and_slope(dot(r.top_b[:, M_], weight(r.expand_w, j * D, D)))
        r.top_b[:, cols] = z.astype(BF)
        r.top_f[:, cols] = slope
    if cube:
        unit(shrink, TOP).stage4()
    ready(shrink, TOP).wait()
    last = h1
    for j in range(4):
        last = last + dot(r.top_b[:, j * D : j * D + D], r.shrink_w[j].reshape(D, D))

    if cube:
        r.total[...] = jnp.sum(r.counts[...].reshape(-1, 8, 128), 0)
        image_total = r.total[0:1, 0:1]
    else:
        image_total = r.count_in[0:1, 0:1]
    head_part(r, last, image_total)
    top_backward(plan, r)
    wait_all(saves(TOP, h_, a_, t_) + saves(0, z_, slope_))


def pallas(kernel, name, inputs, outputs, scratch, **params):
    names = list(inputs) + list(outputs) + list(scratch)
    outs = pl.pallas_call(
        functools.partial(kernel, names),
        out_shape=[jax.ShapeDtypeStruct(shape, kind) for shape, kind, _ in outputs.values()],
        in_specs=[spec for _, spec in inputs.values()],
        out_specs=[spec for _, _, spec in outputs.values()],
        scratch_shapes=list(scratch.values()),
        compiler_params=pltpu.CompilerParams(vmem_limit_bytes=LIMIT, **params),
        name=name,
    )(*[value for value, _ in inputs.values()])
    return SimpleNamespace(**dict(zip(outputs, outs)))


def given_in(spec, **values):
    return {name: (value, spec) for name, value in values.items()}


def vmem(kind, **shapes):
    return {name: pltpu.VMEM(shape, kind) for name, shape in shapes.items()}


def dma(**counts):
    return {name: pltpu.SemaphoreType.DMA(count) for name, count in counts.items()}


def forward(plan, shards, args, scalars, gathered, count):
    rows = args["images"].shape[0] * PAD
    shapes = saved_shapes(rows)
    whole = dict(
        patch_whole=cols_shape(D),
        joined_whole=(LAYERS,) + cols_shape(FF),
        expand_whole=(LAYERS,) + cols_shape(FF),
        shrink_whole=(LAYERS,) + ROWS_SHAPE,
    )
    inputs = given_in(VMEM_SPEC, **args)
    inputs.update(given_in(pl.BlockSpec(memory_space=pltpu.SMEM), **scalars))
    outputs = {}
    if plan.cube:
        inputs.update(given_in(VMEM_SPEC, **shards))
        outputs.update({name: (shape, BF, ANY_SPEC) for name, shape in whole.items()})
    else:
        inputs.update(given_in(ANY_SPEC, **dict(zip(whole, gathered))))
        inputs.update(given_in(VMEM_SPEC, count_in=count))
    for name, (shape, kind) in shapes.items():
        deep = LAYERS if name in ("h", "a", "t") else TOP
        outputs["keep_" + name] = ((deep,) + shape, kind, ANY_SPEC)
    outputs.update(
        g=((rows, D), F32, VMEM_SPEC),
        rows_block=((rows_block(rows // PAD), 128), BF, VMEM_SPEC),
        keys_out=((2, 4, 4, BLOCK, D), BF, ANY_SPEC),
        tail=((8, D), F32, VMEM_SPEC),
        total=((8, 128), F32, VMEM_SPEC),
    )
    scratch = vmem(
        BF,
        table=(D, CLASSES),
        top_b=(HEAD_ROWS, LOGIT_.stop),
        top_p=(rows // PAD, PAD, 16),
        top_du=(HEAD_ROWS, FF),
        d_keys=(rows, 2 * D),
        keys_block=(2, 4, 4, BLOCK, D),
        patch_w=cols_shape(D),
        joined_w=cols_shape(FF),
        expand_w=cols_shape(FF),
        shrink_w=ROWS_SHAPE,
    )
    scratch.update({name: pltpu.VMEM(shape, kind) for name, (shape, kind) in shapes.items()})
    scratch.update(
        vmem(
            F32,
            first=(HEAD_ROWS, D),
            class_row=(HEAD_ROWS, D),
            d_logits=(HEAD_ROWS, CLASS_PAD),
            top_f=(HEAD_ROWS, G_.stop),
            rows_f=(rows_block(rows // PAD), 128),
        )
    )
    scratch.update(dma(saves=(9,), loads=(4,)))
    extra = {}
    if plan.cube:
        scratch.update(
            vmem(
                F32,
                joined_f=(LAYERS, HALF, FF),
                joined_b=(LAYERS, BLOCK, WIDTH),
                expand_b=(LAYERS, BLOCK, WIDTH),
                patch_f=(BLOCK, D // 2),
                count=(8, 128),
                counts=CHIPS + (2, 8, 128),
            )
        )
        scratch.update(
            vmem(
                BF,
                patch_block=(BLOCK, D // 2),
                joined_block=(LAYERS, BLOCK, WIDTH),
                expand_block=(LAYERS, BLOCK, WIDTH),
                shrink_block=(LAYERS, BLOCK_FF, D),
            )
        )
        scratch.update(
            dma(send=(10, 23), recv=(10, 22), share_send=(3,), share_recv=(3,), count_send=(7,), count_recv=(7,))
        )
        extra = dict(collective_id=1, has_side_effects=True)
    got = pallas(functools.partial(forward_kernel, plan), "forward", inputs, outputs, scratch, **extra)
    if not plan.cube:
        for name, value in zip(whole, gathered):
            setattr(got, name, value)
        got.total = count
    return got


UNITS = 3 * TOP + 1
KEYS = D
TAIL = 512
SEND = 4
VEC_ROWS = 256


def relative(plan):
    z, x, y, c = plan.where()
    return c, (z * 2 + x) * 2 + y


def place(plan, slot, core, chip, send=SEND):
    my_core, my_chip = relative(plan)
    at = jnp.bitwise_xor(my_chip, chip)
    other = jnp.bitwise_xor(my_core, core)
    return slot + (send - slot) * other, at // 4, at % 4


def store_cols(plan, out, slot, tile, width, value, half=WIDTH, send=SEND):
    per_half = half // width
    lanes = pl.ds(pl.multiple_of((tile % per_half) * width, 128), width)
    for b in range(16):
        rows = value[b * BLOCK : (b + 1) * BLOCK].astype(BF)
        out[(*place(plan, slot, tile // per_half, b, send), slice(None), lanes)] = rows


def store_rows(plan, out, slot, tile, value):
    for b in range(4):
        at = place(plan, slot, b % 2, tile * 2 + b // 2)
        for part in range(2):
            first = b * BLOCK_FF + part * BLOCK
            out[(*at, slice(None), pl.ds(part * D, D))] = value[first : first + BLOCK].astype(BF)


def store_vectors(plan, out, slot, value):
    for b in range(32):
        rows = value[b * 8 : b * 8 + 8]
        block = jnp.concatenate([rows[:, j * 128 : j * 128 + 128] for j in range(6)], 0)
        out[(*place(plan, slot, b % 2, b // 2), slice(None), pl.ds(D // 2, 128))] = block.astype(BF)


class Reduce:
    def __init__(self, plan, bufs, unit, width=WIDTH):
        self.plan, self.bufs, self.unit, self.width = plan, bufs, unit, width
        self.z, self.x, self.y, self.c = plan.where()
        self.to = over_links(plan)
        self.other = other_part(width) if width == WIDTH else 0
        self.most = width - self.other
        self.cut, self.cut_other = cut_of(self.most), cut_of(self.other)
        self.slot, self.three, self.two = unit % 4, unit % 3, unit % 2

    def copy(self, at):
        b, slot, three, to, c = self.bufs, self.slot, self.three, self.to, self.c
        most, cut, cut_other = self.most, self.cut, self.cut_other
        line = slice(None)
        full, main = pl.ds(0, self.width), pl.ds(0, most)
        left, right, low = pl.ds(0, cut), pl.ds(cut, most - cut), pl.ds(0, most - cut)
        other = pl.ds(most, self.other)
        own = b.unit.at[slot]
        if at == 17:
            rows = pl.ds(pl.multiple_of((1 - c) * HALF, 8), HALF)
            src, dst = self.result(rows)
            device = to.core
        else:
            src, dst, device = {
                0: lambda: (b.unit.at[SEND, :, :, :, full], b.core.at[:, :, :, full], to.core),
                1: lambda: (own.at[:, 3, :, left], b.near.at[three, :, :, left], to.x),
                2: lambda: (own.at[:, 3, :, right], b.far.at[three, :, :, low], to.y),
                3: lambda: (own.at[:, 1, :, main], b.y.at[three, :, :, main], to.y),
                4: lambda: (own.at[:, 2, :, main], b.x.at[three, :, :, main], to.x),
                5: lambda: (b.line.at[three, 2, :, main], b.main_two.at[three, 0, :, main], to.z1),
                6: lambda: (b.line.at[three, 2, :, main], b.main_two.at[three, 1, :, main], to.z3),
                7: lambda: (b.line.at[three, 1, :, main], b.main_one.at[slot, 0, :, main], to.z1),
                8: lambda: (b.line.at[three, 3, :, main], b.main_one.at[slot, 1, :, main], to.z3),
                9: lambda: (own.at[2, :, :, other], b.other_two.at[three, 0], to.z1),
                10: lambda: (own.at[2, :, :, other], b.other_two.at[three, 1], to.z3),
                11: lambda: (own.at[1, :, :, other], b.other_one.at[slot, 0], to.z1),
                12: lambda: (own.at[3, :, :, other], b.other_one.at[slot, 1], to.z3),
                13: lambda: (b.plane.at[three, 3, :, pl.ds(0, cut_other)], b.other_near.at[three], to.x),
                14: lambda: (b.plane.at[three, 3, :, pl.ds(cut_other, cut_other)], b.other_far.at[three], to.y),
                15: lambda: (b.plane.at[three, 1], b.other_y.at[three], to.y),
                16: lambda: (b.plane.at[three, 2], b.other_x.at[three], to.x),
            }[at]()
        return remote(src, dst, b.send.at[slot, at], b.recv.at[slot, at], device)

    def result(self, rows):
        b, c = self.bufs, self.c
        total = b.total.at[self.two]
        if self.width == WIDTH:
            return total.at[rows], b.owned.at[self.unit - 1, c]
        if self.width == KEYS:
            return total.at[rows, pl.ds(0, KEYS)], b.keys.at[c]
        return total.at[rows, pl.ds(0, D // 2)], b.patch.at[c]

    def own(self, by_rows):
        b, c = self.bufs, self.c
        total = b.total.at[self.two]
        if by_rows:
            moves = [(total.at[pl.ds(k * HALF, HALF)], b.owned.at[self.unit - 1, k]) for k in range(2)]
        else:
            moves = [self.result(pl.ds(pl.multiple_of(c * HALF, 8), HALF))]
        return [
            pltpu.make_async_copy(src, dst, b.send.at[self.slot, 18 + k])
            for k, (src, dst) in enumerate(moves)
        ]

    def start(self, *which):
        for at in which:
            self.copy(at).start()

    def arrived(self, *which):
        for at in which:
            self.copy(at).wait_recv()

    def sent(self, *which):
        for at in which:
            self.copy(at).wait_send()

    def by_place(self, middle, end):
        inside = (self.z == 1) | (self.z == 2)
        if middle:
            pl.when(inside)(middle)
        if end:
            pl.when(jnp.logical_not(inside))(end)

    def stage0(self):
        @pl.when(self.unit > 0)
        def _():
            pl.semaphore_wait(self.bufs.credit, 1)

        self.start(0)

    def stage1(self):
        unit, core, slot = self.bufs.unit, self.bufs.core, self.slot
        cols = pl.ds(0, self.width)
        self.arrived(0)

        def add(z, chip):
            both = unit[slot, z, chip, :, cols].astype(F32) + core[z, chip, :, cols].astype(F32)
            unit[slot, z, chip, :, cols] = both.astype(BF)

        pl.loop(0, 4)(lambda z: add(z, 3))
        self.start(1, 2)
        pl.loop(0, 12)(lambda i: add(i // 3, i % 3))
        if self.other:
            self.by_place(lambda: self.start(10), lambda: self.start(9))

        @pl.when(self.unit < UNITS)
        def _():
            pl.semaphore_signal(
                self.bufs.credit, inc=1, device_id=self.to.core, device_id_type=pl.DeviceIdType.MESH
            )

    def stage2(self):
        b, slot, three, most, cut = self.bufs, self.slot, self.three, self.most, self.cut
        unit = b.unit
        left, right, low = pl.ds(0, cut), pl.ds(cut, most - cut), pl.ds(0, most - cut)
        self.arrived(1, 2)

        @pl.loop(0, 4)
        def _(z):
            got = b.near[three, z, :, left].astype(F32)
            unit[slot, z, 1, :, left] = (unit[slot, z, 1, :, left].astype(F32) + got).astype(BF)
            got = b.far[three, z, :, low].astype(F32)
            unit[slot, z, 2, :, right] = (unit[slot, z, 2, :, right].astype(F32) + got).astype(BF)

        self.start(3, 4)
        self.sent(1, 2)
        if not self.other:
            return
        other = pl.ds(most, self.other)

        def pass_on():
            self.arrived(9, 10)
            for z, k in ((3, 0), (1, 1)):
                for chip in range(4):
                    got = b.other_two[three, k, chip].astype(F32)
                    unit[slot, z, chip, :, other] = (
                        unit[slot, z, chip, :, other].astype(F32) + got
                    ).astype(BF)

        self.by_place(pass_on, None)
        self.start(11, 12)

    def stage3(self):
        b, slot, three, main = self.bufs, self.slot, self.three, pl.ds(0, self.most)
        self.arrived(3, 4)

        @pl.loop(0, 4)
        def _(z):
            b.line[three, z, :, main] = (
                b.unit[slot, z, 0, :, main].astype(F32)
                + b.y[three, z, :, main].astype(F32)
                + b.x[three, z, :, main].astype(F32)
            ).astype(BF)

        self.by_place(lambda: self.start(6), lambda: self.start(5))
        self.sent(3, 4)
        if not self.other:
            return
        self.arrived(11, 12)
        for chip in range(4):
            b.plane[three, chip] = (
                b.unit[slot, 0, chip, :, pl.ds(self.most, self.other)].astype(F32)
                + b.other_one[slot, 0, chip].astype(F32)
                + b.other_one[slot, 1, chip].astype(F32)
            ).astype(BF)
        self.start(13, 14)
        self.by_place(lambda: self.sent(10), lambda: self.sent(9))
        self.sent(11, 12)

    def stage4(self):
        b, three, main = self.bufs, self.three, pl.ds(0, self.most)

        def pass_on():
            self.arrived(5, 6)
            for z, k in ((3, 0), (1, 1)):
                got = b.main_two[three, k, :, main].astype(F32)
                b.line[three, z, :, main] = (b.line[three, z, :, main].astype(F32) + got).astype(BF)

        self.by_place(pass_on, None)
        self.start(7, 8)
        if not self.other:
            return
        self.arrived(13, 14)
        half = self.cut_other
        for chip, cols, got in (
            (1, pl.ds(0, half), b.other_near),
            (2, pl.ds(half, half), b.other_far),
        ):
            both = b.plane[three, chip, :, cols].astype(F32) + got[three].astype(F32)
            b.plane[three, chip, :, cols] = both.astype(BF)
        self.start(15, 16)
        self.sent(13, 14)

    def stage5(self, by_rows):
        b, slot, three, two = self.bufs, self.slot, self.three, self.two
        main = pl.ds(0, self.most)
        self.arrived(7, 8)
        total = b.line[three, 0, :, main].astype(F32)
        for k in range(2):
            total = total + b.main_one[slot, k, :, main].astype(F32)
        b.total[two, :, main] = total
        b.squares[0:1, main] += jnp.sum(total * total, 0, keepdims=True)
        if self.other:
            self.arrived(15, 16)
            other = pl.ds(self.most, self.other)
            total = (
                b.plane[three, 0].astype(F32)
                + b.other_y[three].astype(F32)
                + b.other_x[three].astype(F32)
            )
            b.total[two, :, other] = total
            b.squares[0:1, other] += jnp.sum(total * total, 0, keepdims=True)
        if not by_rows:
            self.start(17)
        start_all(self.own(by_rows))
        self.by_place(lambda: self.sent(6), lambda: self.sent(5))
        self.sent(7, 8)
        if self.other:
            self.sent(15, 16)

    def stage6(self, by_rows):
        if not by_rows:
            self.copy(17).wait()
        wait_all(self.own(by_rows))


POINTS = 4
ENTRY = (0, 1, 3)
STAGE_ORDER = (1, 0, 2, 3, 4, 6, 5)


def backward_kernel(plan, names, *refs):
    r = SimpleNamespace(**dict(zip(names, refs)))
    cube = plan.cube
    images = r.images.shape[0]
    loads = [
        (r.keep_z, r.vm_z),
        (r.shrink_whole, r.shrink_w),
        (r.keep_slope, r.vm_slope),
        (r.expand_whole, r.expand_w),
        (r.keep_m, r.vm_m),
        (r.keep_h1, r.vm_h1),
        (r.keep_o, r.vm_o),
        (r.keep_t, r.vm_t),
        (r.keep_p, r.vm_p),
        (r.keep_a, r.vm_a),
        (r.keep_h, r.vm_h),
        (r.joined_whole, r.expand_w),
    ]
    z_, shrink_, slope_, expand_, m_, h1_, o_, t_, p_, a_, h_, joined_ = range(12)

    def fetch(which, layer):
        src, dst = loads[which]
        return pltpu.make_async_copy(src.at[layer], dst, r.loads.at[which])

    def start(layer, *which):
        for k in which:
            fetch(k, layer).start()

    def wait(layer, *which):
        for k in which:
            fetch(k, layer).wait()

    loaded = [
        load(r.g_in, r.g, r.loads.at[joined_ + 1]),
        load(r.keys_in.at[0], r.unit.at[0, :, :, :, pl.ds(0, KEYS)], r.loads.at[joined_ + 2]),
        load(r.keys_in.at[1], r.unit.at[SEND, :, :, :, pl.ds(0, KEYS)], r.loads.at[joined_ + 3]),
    ]
    start(TOP - 1, *range(joined_))
    if cube:
        cube_barrier(plan)
        r.squares[...] = jnp.zeros_like(r.squares)
        top_rows = SmallGather(plan, r.rows_block, r.top_rows, r.rows_send, r.rows_recv)
    r.vectors[...] = jnp.zeros_like(r.vectors)
    r.vectors[FINAL : FINAL + 2] = r.tail_in[1:3]
    r.vectors[FINAL - 4 : FINAL] = r.tail_in[3:7]

    def run(unit, stage, by_rows, width=WIDTH):
        unit = Reduce(plan, r, unit, width)
        (
            unit.stage0,
            unit.stage1,
            unit.stage2,
            unit.stage3,
            unit.stage4,
            lambda: unit.stage5(by_rows),
            lambda: unit.stage6(by_rows),
        )[stage]()

    def point(it, at):
        if not cube:
            for kind in range(3):
                if ENTRY[kind] == at:
                    unit = 3 * it - 2 + kind
                    copies = [
                        pltpu.make_async_copy(
                            r.unit.at[(unit % 4, SEND)[i]],
                            r.full.at[unit, i],
                            r.loads.at[joined_ + 1 + i],
                        )
                        for i in range(2)
                    ]
                    start_all(copies)
                    wait_all(copies)
            return
        for stage in STAGE_ORDER:
            for kind in range(3):
                past, phase = divmod(ENTRY[kind] + stage, POINTS)
                if phase != at:
                    continue
                unit = 3 * (it - past) - 2 + kind
                if past:
                    pl.when(it > past)(functools.partial(run, unit, stage, kind == 0))
                else:
                    run(unit, stage, kind == 0)
                if past and kind == 2:
                    pl.when(it == past)(functools.partial(run, unit, stage, False, KEYS))

    def drain():
        at = 0
        while at <= 5:
            for stage in STAGE_ORDER:
                for past, kind in ((1, 0), (1, 1), (1, 2), (2, 0), (2, 1), (2, 2)):
                    if POINTS * past + at - ENTRY[kind] == stage:
                        run(jnp.int32(UNITS - 3 * past + kind), stage, kind == 0)
                if at == stage:
                    run(jnp.int32(UNITS), stage, False, TAIL)
            at += 1

    def sent(unit, width=WIDTH):
        if cube:
            Reduce(plan, r, unit - 1, width).copy(0).wait_send()

    low_lane = lax.broadcasted_iota(jnp.int32, (PAD, 128), 1) < HEAD_DIM
    scale = HEAD_DIM**-0.5

    wait_all(loaded)
    if cube:
        run(jnp.int32(0), 0, False, KEYS)
        top_rows.stage0()
    else:
        copies = [
            pltpu.make_async_copy(r.unit.at[(0, SEND)[i]], r.full.at[0, i], r.loads.at[joined_ + 1 + i])
            for i in range(2)
        ]
        start_all(copies)
        wait_all(copies)

    @pl.loop(1, LAYERS)
    def _(it):
        layer = TOP - it
        below = it < TOP
        unit_s = 3 * it - 2
        base = S + 2 + 4 * layer
        r.gr[...] = r.g[...].astype(BF)
        wait(layer, z_)
        slot = unit_s % 4
        pl.when(it == 1)(lambda: sent(unit_s, KEYS))
        pl.when(it > 1)(lambda: sent(unit_s))

        @pl.loop(0, 8)
        def _(j):
            cols = pl.ds(pl.multiple_of(j * (D // 2), 128), D // 2)
            store_rows(plan, r.unit, slot, j, dot(r.vm_z[:, cols], r.gr[...], TN))

        point(it, 0)
        if cube:
            pl.when(it == 1)(top_rows.stage1)
        wait(layer, shrink_, slope_, expand_, m_, h1_)
        pl.when(below)(lambda: start(layer - 1, z_))
        slot_e = (unit_s + 1) % 4
        r.g1[...] = jnp.zeros_like(r.g1)
        sent(unit_s + 1)

        @pl.loop(0, 4)
        def _(j):
            cols = pl.ds(pl.multiple_of(j * D, 128), D)
            dz = dot(r.gr[...], r.shrink_w[j].reshape(D, D), NT)
            du = (dz * r.vm_slope[:, cols].astype(F32)).astype(BF)
            r.vm_slope[:, cols] = du
            store_cols(plan, r.unit, slot_e, j, D, dot(r.vm_m[...], du, TN))

        pl.when(below)(lambda: start(layer - 1, shrink_, m_))
        point(it, 1)
        if cube:
            pl.when(it == 1)(top_rows.stage2)

        @pl.loop(0, 4)
        def _(j):
            cols = pl.ds(pl.multiple_of(j * D, 128), D)
            r.g1[...] += dot(r.vm_slope[:, cols], weight(r.expand_w, j * D, D), NT)

        start(layer, joined_)
        pl.when(below)(lambda: start(layer - 1, slope_))
        d_h1, d_gain, d_shift = normalize_back(r.vm_h1[...], row(r.params, base + 2), r.g1[...])
        r.g1[...] = r.g[...] + d_h1
        r.vectors[pl.ds(base + 2, 1)] = d_gain
        r.vectors[pl.ds(base + 3, 1)] = d_shift
        pl.when(below)(lambda: start(layer - 1, h1_))

        r.gr[...] = r.g1[...].astype(BF)
        slot_t = (unit_s + 2) % 4
        wait(layer, o_)
        sent(unit_s + 2)
        store_cols(plan, r.unit, slot_t, 3, D, dot(r.vm_o[...], r.gr[...], TN))
        wait(layer, joined_)
        r.do[...] = dot(r.gr[...], weight(r.expand_w, 3 * D, D), NT).astype(BF)
        wait(layer, t_, p_, a_, h_)

        def heads(step):
            image, pair = step // (HEADS // 2), step % (HEADS // 2)
            rows = pl.ds(pl.multiple_of(image * PAD, 16), PAD)
            lanes = [pl.ds(pl.multiple_of(pair * 128 + part * D, 128), 128) for part in range(3)]
            q, key, v = (r.vm_t[rows, lane] for lane in lanes)
            do = r.do[rows, lanes[0]]
            zero = jnp.zeros_like(v)
            dqs, dks, dvs = [], [], []
            for which in range(2):
                part = jnp.where(low_lane, v, zero) if which == 0 else jnp.where(low_lane, zero, v)
                p_low = r.vm_p[step * 2 + which]
                p = p_low.astype(F32)
                dvs.append(dot(p_low, do))
                dp = dot(part, do, NT)
                ds = (p * (dp - jnp.sum(p * dp, 0, keepdims=True))).astype(BF)
                dqs.append(dot(ds, key, TN))
                dks.append(dot(ds, q))
            r.dt[rows, lanes[0]] = (jnp.where(low_lane, dqs[0], dqs[1]) * scale).astype(BF)
            r.dt[rows, lanes[1]] = (jnp.where(low_lane, dks[0], dks[1]) * scale).astype(BF)
            r.dt[rows, lanes[2]] = jnp.where(low_lane, dvs[0], dvs[1]).astype(BF)

        half = images * (HEADS // 2) // 2
        pl.loop(0, half)(heads)
        point(it, 2)
        if cube:
            pl.when(it == 1)(top_rows.stage3)
        pl.loop(half, 2 * half)(heads)
        pl.when(below)(lambda: start(layer - 1, o_, t_, p_))
        r.g[...] = jnp.zeros_like(r.g)

        @pl.loop(0, 3)
        def _(j):
            cols = pl.ds(pl.multiple_of(j * D, 128), D)
            store_cols(plan, r.unit, slot_t, j, D, dot(r.vm_a[...], r.dt[:, cols], TN))

        point(it, 3)
        if cube:
            pl.when(it == 1)(top_rows.finish)

        @pl.loop(0, 3)
        def _(j):
            cols = pl.ds(pl.multiple_of(j * D, 128), D)
            r.g[...] += dot(r.dt[:, cols], weight(r.expand_w, j * D, D), NT)

        d_h, d_gain, d_shift = normalize_back(r.vm_h[...], row(r.params, base), r.g[...])
        r.g[...] = r.g1[...] + d_h
        r.vectors[pl.ds(base, 1)] = d_gain
        r.vectors[pl.ds(base + 1, 1)] = d_shift
        pl.when(below)(lambda: start(layer - 1, a_, h_, expand_))

    slot = UNITS % 4
    sent(jnp.int32(UNITS))
    for part in range(2):
        half = D // 2
        value = jnp.zeros((D, half), F32)
        for image in range(images):
            rows = r.g[image * PAD + 1 : image * PAD + S, part * half : (part + 1) * half]
            value = value + dot(r.images[image], rows.astype(BF), TN)
        store_cols(plan, r.unit, slot, part, half, value, half)
    pos = r.g[:PAD]
    for image in range(1, images):
        pos = pos + r.g[image * PAD : (image + 1) * PAD]
    r.vectors[:S] = pos[:S]
    r.vectors[S : S + 1] = pos[:1]
    r.vectors[S + 1 : S + 2] = jnp.sum(pos[1:S], 0, keepdims=True)
    if not cube:
        copies = [
            pltpu.make_async_copy(r.unit.at[(slot, SEND)[i]], r.full.at[UNITS, i], r.loads.at[i])
            for i in range(2)
        ]
        copies.append(pltpu.make_async_copy(r.vectors, r.vector_rows, r.loads.at[2]))
        start_all(copies)
        wait_all(copies)
        return
    store_vectors(plan, r.unit, slot, r.vectors[...])

    drain()
    r.tail_block[:BLOCK] = r.total[UNITS % 2, :, D // 2 : TAIL].astype(BF)
    line = lax.broadcasted_iota(jnp.int32, (16, 128), 0)
    terms = jnp.zeros((16, 128), F32)
    for k, rest in enumerate((jnp.full((16, 128), jnp.sum(r.squares[...]), F32), r.tail_in[0:1, 0:128])):
        for j in range(3):
            term = rest.astype(BF).astype(F32)
            rest = rest - term
            terms = jnp.where(line == 3 * k + j, term, terms)
    r.tail_block[BLOCK:] = terms.astype(BF)
    gather = SmallGather(plan, r.tail_block, r.vector_rows, r.tail_send, r.tail_recv)
    gather.stage0()
    gather.stage1()
    gather.stage2()
    gather.stage3()
    run(jnp.int32(UNITS), 6, False, TAIL)
    Reduce(plan, r, jnp.int32(UNITS), TAIL).copy(0).wait_send()
    gather.finish()


def backward(plan, images, params, done):
    rows = images.shape[0] * PAD
    shapes = saved_shapes(rows)
    inputs = given_in(
        VMEM_SPEC,
        images=images,
        params=params,
        tail_in=done.tail,
        rows_block=done.rows_block,
    )
    block = rows_block(images.shape[0])
    inputs.update(
        given_in(
            ANY_SPEC,
            g_in=done.g,
            keys_in=done.keys_out,
            joined_whole=done.joined_whole,
            expand_whole=done.expand_whole,
            shrink_whole=done.shrink_whole,
        )
    )
    inputs.update({"keep_" + name: (getattr(done, "keep_" + name), ANY_SPEC) for name in SAVED})
    if plan.cube:
        outputs = dict(
            owned=((UNITS - 1, 2, HALF, WIDTH), F32, ANY_SPEC),
            keys=((2, HALF, KEYS), F32, ANY_SPEC),
            patch=((2, HALF, D // 2), F32, ANY_SPEC),
            vector_rows=(CHIPS + (2, BLOCK + 16, 128), BF, ANY_SPEC),
            top_rows=(CHIPS + (2, block, 128), BF, ANY_SPEC),
        )
    else:
        outputs = dict(
            full=((UNITS + 1, 2, 4, 4, BLOCK, WIDTH), BF, ANY_SPEC),
            vector_rows=((VEC_ROWS, D), F32, ANY_SPEC),
        )
    scratch = {"vm_" + name: pltpu.VMEM(shape, kind) for name, (shape, kind) in shapes.items()}
    scratch.update(
        vmem(
            BF,
            expand_w=cols_shape(FF),
            shrink_w=ROWS_SHAPE,
            gr=(rows, D),
            do=(rows, D),
            dt=(rows, 3 * D),
            unit=(SEND + 1, 4, 4, BLOCK, WIDTH),
        )
    )
    scratch.update(vmem(F32, g=(rows, D), g1=(rows, D), vectors=(VEC_ROWS, D)))
    scratch.update(dma(loads=(16,)))
    extra = {}
    if plan.cube:
        other = other_part(WIDTH)
        most = WIDTH - other
        scratch.update(
            vmem(
                BF,
                core=(4, 4, BLOCK, WIDTH),
                tail_block=(BLOCK + 16, 128),
                near=(3, 4, BLOCK, cut_of(most)),
                far=(3, 4, BLOCK, most - cut_of(most)),
                x=(3, 4, BLOCK, most),
                y=(3, 4, BLOCK, most),
                line=(3, 4, BLOCK, most),
                main_two=(3, 2, BLOCK, most),
                main_one=(4, 2, BLOCK, most),
                other_two=(3, 2, 4, BLOCK, other),
                other_one=(4, 2, 4, BLOCK, other),
                plane=(3, 4, BLOCK, other),
                other_near=(3, BLOCK, cut_of(other)),
                other_far=(3, BLOCK, other - cut_of(other)),
                other_x=(3, BLOCK, other),
                other_y=(3, BLOCK, other),
            )
        )
        scratch.update(
            vmem(F32, total=(2, BLOCK, WIDTH), squares=(8, WIDTH))
        )
        scratch.update(
            dma(send=(4, 20), recv=(4, 18), rows_send=(7,), rows_recv=(7,), tail_send=(7,), tail_recv=(7,))
        )
        scratch.update(credit=pltpu.SemaphoreType.REGULAR)
        extra = dict(collective_id=2, has_side_effects=True)
    return pallas(functools.partial(backward_kernel, plan), "backward", inputs, outputs, scratch, **extra)


PARAMS = ("patch", "triple", "output", "expand", "shrink", "vector", "head")
KINDS = ("w_", "m_", "s_")


def adam_update(master, moment, square, gradient, step_rate):
    moment_new = BETA_ONE * moment + (1.0 - BETA_ONE) * gradient
    square_new = BETA_TWO * square + (1.0 - BETA_TWO) * gradient * gradient
    moment_hat = moment_new / (1.0 - BETA_ONE**STEP_INDEX)
    square_hat = square_new / (1.0 - BETA_TWO**STEP_INDEX)
    master_new = master - step_rate * (
        moment_hat / (jnp.sqrt(square_hat) + ADAM_EPS) + DECAY * master
    )
    return (master_new, moment_new, square_new)


def class_matrices(ref, images, devices, stride):
    first, found = 0, []
    for columns in PIECES:
        count = columns // 128
        parts = [
            jnp.concatenate(
                [
                    ref[pl.ds(image * PER_IMAGE + first + j, devices, stride=stride), :]
                    for j in range(count)
                ],
                1,
            )
            for image in range(images)
        ]
        found.append(jnp.concatenate(parts, 0).astype(BF))
        first += count
    return found


def own_columns(value, first, count):
    at = lax.broadcasted_iota(jnp.int32, (value.shape[1], 128), 0)
    to = lax.broadcasted_iota(jnp.int32, (value.shape[1], 128), 1)
    chosen = jnp.where((at == to + first) & (to < count), 1.0, 0.0).astype(BF)
    return dot(value, chosen).astype(BF)


def update_kernel(plan, images, names, *refs):
    r = SimpleNamespace(**dict(zip(names, refs)))
    named = dict(zip(names, refs))
    groups = [
        [(named[kind + name], named["vm_" + kind + name], named["to_" + kind + name]) for kind in KINDS]
        for name in PARAMS
    ]
    patch, triple, output, expand, shrink, vector, head = range(7)

    def moves(group, back):
        return [
            pltpu.make_async_copy(*((buf, out) if back else (src, buf)), r.sems.at[3 * group + k])
            for k, (src, buf, out) in enumerate(groups[group])
        ]

    order = (head, shrink, expand, triple, output, patch, vector)
    for group in order:
        start_all(moves(group, False))

    tile = jnp.sum(r.tails[:, BLOCK:, :].astype(F32), 0)
    square_sum = tile[0:1, 0:1] + tile[1:2, 0:1] + tile[2:3, 0:1]
    loss = tile[3:4] + tile[4:5] + tile[5:6]
    r.rows_f[...] = r.top_rows[...].astype(F32)
    stride = r.top_rows.shape[0] // plan.n
    found = class_matrices(r.rows_f, images, plan.n, stride)
    features, d_logits, z, g, m, du, o, g1, a, dq = found
    r.features[...] = features
    r.d_logits[...] = d_logits
    alike = (dot(features, features, NT) + 1.0) * dot(d_logits, d_logits, NT)
    for left, right in ((z, g), (m, du), (o, g1), (a, dq)):
        alike = alike + dot(left, left, NT) * dot(right, right, NT)
    norm = jnp.sqrt(square_sum + jnp.sum(alike))
    me = plan.me()

    def top_grad(left, right, rows):
        return dot(own_columns(left, me * rows, rows), right, TN)[:rows]

    clip = CLIP / jnp.maximum(norm, CLIP)
    line = lax.broadcasted_iota(jnp.int32, (8, 128), 0)
    r.scalars[...] = jnp.where(line == 0, norm, loss)

    def step(group, at, gradient, rate):
        bufs = [buf for _, buf, _ in groups[group]]
        new = adam_update(*[buf[at] for buf in bufs], gradient * clip, rate)
        for buf, value in zip(bufs, new):
            buf[at] = value

    def finish(group):
        start_all(moves(group, True))

    every = slice(None)
    wait_all(moves(head, False))

    @pl.loop(0, D // 128)
    def _(j):
        rows = pl.ds(pl.multiple_of(j * 128, 128), 128)
        gradient = dot(r.features[:, rows], r.d_logits[...], TN)
        step(head, (rows, every), gradient[:, :CLASSES], RATE_MATRIX)

    bias = jnp.sum(d_logits.astype(F32), 0, keepdims=True)[:, :CLASSES]
    step(head, (slice(D, D + 1), every), bias, RATE_MATRIX)
    r.bias_grad[...] = bias * clip
    finish(head)
    wait_all(moves(shrink, False))

    step(shrink, (TOP, every, every), top_grad(z, g, BLOCK_FF), RATE_MATRIX)

    @pl.loop(0, TOP)
    def _(layer):
        unit = 3 * (TOP - 1 - layer)
        for k in range(4):
            gradient = r.owned[unit, k % 2, :, pl.ds(k // 2 * D, D)]
            step(shrink, (layer, pl.ds(k * HALF, HALF), every), gradient, RATE_MATRIX)

    finish(shrink)
    wait_all(moves(expand, False))

    step(expand, (TOP, every, every), top_grad(m, du, HALF), RATE_MATRIX)

    @pl.loop(0, TOP)
    def _(layer):
        unit = 3 * (TOP - 1 - layer) + 1
        for k in range(2):
            step(expand, (layer, every, pl.ds(k * WIDTH, WIDTH)), r.owned[unit, k], RATE_MATRIX)

    finish(expand)
    wait_all(moves(triple, False))
    wait_all(moves(output, False))

    step(output, (TOP, every, every), top_grad(o, g1, HALF), RATE_OUTPUT)
    step(triple, (TOP, every, pl.ds(0, D)), top_grad(a, dq, HALF), RATE_MATRIX)
    for k in range(2):
        step(triple, (TOP, every, pl.ds((k + 1) * D, D)), r.keys[k], RATE_MATRIX)

    @pl.loop(0, TOP)
    def _(layer):
        unit = 3 * (TOP - 1 - layer) + 2
        step(triple, (layer, every, pl.ds(0, WIDTH)), r.owned[unit, 0], RATE_MATRIX)
        step(triple, (layer, every, pl.ds(WIDTH, D)), r.owned[unit, 1, :, pl.ds(0, D)], RATE_MATRIX)
        step(output, (layer, every, every), r.owned[unit, 1, :, pl.ds(D, D)], RATE_OUTPUT)

    finish(triple)
    finish(output)
    wait_all(moves(patch, False))
    for k in range(2):
        step(patch, (every, pl.ds(k * (D // 2), D // 2)), r.patch_grad[k], RATE_MATRIX)
    finish(patch)
    count = groups[vector][0][0].shape[0]
    for d in range(-(-count // 8)):
        block = r.tails[d].astype(F32)
        for j in range(6):
            r.vector_grad[8 * d : 8 * d + 8, 128 * j : 128 * j + 128] = block[8 * j : 8 * j + 8]
    wait_all(moves(vector, False))
    step(vector, (every, every), r.vector_grad[:count], RATE_VECTOR)
    finish(vector)
    for group in order:
        wait_all(moves(group, True))


def update(plan, images, states, got):
    inputs, outputs, scratch = {}, {}, {}
    for name, state in zip(PARAMS, states):
        for kind, value in zip(KINDS, state):
            inputs[kind + name] = (value, ANY_SPEC)
            outputs["to_" + kind + name] = (value.shape, F32, ANY_SPEC)
            scratch["vm_" + kind + name] = pltpu.VMEM(value.shape, F32)
    inputs.update(
        given_in(
            VMEM_SPEC,
            owned=got.owned,
            patch_grad=got.patch,
            tails=got.vector_rows.reshape(plan.n, BLOCK + 16, 128),
            keys=got.keys,
            top_rows=got.top_rows.reshape(-1, 128),
        )
    )
    outputs.update(scalars=((8, 128), F32, VMEM_SPEC), bias_grad=((1, CLASSES), F32, VMEM_SPEC))
    scratch.update(vmem(BF, features=(plan.n * images, D), d_logits=(plan.n * images, 1024)))
    scratch.update(vmem(F32, vector_grad=(VEC_ROWS, D), rows_f=(plan.n * rows_block(images), 128)))
    scratch.update(dma(sems=(3 * len(PARAMS),)))
    new = pallas(functools.partial(update_kernel, plan, images), "update", inputs, outputs, scratch)
    states = [[getattr(new, "to_" + kind + name) for kind in KINDS] for name in PARAMS]
    return new.scalars[0, 0], new.scalars[1, 0], states, new.bias_grad[0]


AXES = ("wide", "grp")


def update_whole(plan, images, states, got, done):
    full = got.full.reshape(UNITS + 1, 2, 16, BLOCK, WIDTH)
    layers = full[1:UNITS].reshape(TOP, 3, 2, 16, BLOCK, WIDTH)[::-1]

    def scattered(whole):
        axis = whole.ndim - 2
        return lax.psum_scatter(whole, AXES, scatter_dimension=axis, tiled=True).astype(F32)

    def from_cols(part):
        joined = jnp.concatenate([part[..., 0, :, :, :], part[..., 1, :, :, :]], -1)
        return joined.reshape(part.shape[:-4] + (D, -1))

    shrink = layers[:, 0].reshape(TOP, 2, 16, BLOCK, 2, D).transpose(0, 2, 1, 4, 3, 5)
    joined = scattered(from_cols(layers[:, 2]))
    rows_all = lax.all_gather(done.rows_block, AXES, axis=0)[:, : PER_IMAGE * images]
    rows_all = rows_all.reshape(plan.n * images, PER_IMAGE * 128)
    ends = [sum(PIECES[: k + 1]) for k in range(len(PIECES))]
    features, d_logits, z, g, m, du, o, g1, a, dq = jnp.split(rows_all, ends[:-1], axis=1)
    d_logits = d_logits[:, :CLASSES]
    bias = jnp.sum(d_logits.astype(F32), 0)[None]

    def top_grad(left, right):
        whole = dot(left, right, TN)
        count = whole.shape[0] // plan.n
        return lax.dynamic_slice_in_dim(whole, plan.me() * count, count)

    def with_top(below, top):
        return jnp.concatenate([below, top[None]], 0)

    keys = scattered(from_cols(full[0, ..., :KEYS]))
    split = [
        scattered(from_cols(full[UNITS, ..., : D // 2])),
        with_top(joined[:, :, : 3 * D], jnp.concatenate([top_grad(a, dq), keys], 1)),
        with_top(joined[:, :, 3 * D :], top_grad(o, g1)),
        with_top(scattered(from_cols(layers[:, 1])), top_grad(m, du)),
        with_top(scattered(shrink.reshape(TOP, FF, D)), top_grad(z, g)),
    ]
    same = [
        lax.psum(got.vector_rows[: states[5][0].shape[0]], AXES),
        jnp.concatenate([dot(features, d_logits, TN), bias], 0),
    ]
    squares = lax.psum(sum(jnp.sum(g * g) for g in split), AXES) + sum(jnp.sum(g * g) for g in same)
    norm = jnp.sqrt(squares)
    clip = CLIP / jnp.maximum(norm, CLIP)
    rates = [RATE_MATRIX] * 2 + [RATE_OUTPUT] + [RATE_MATRIX] * 2 + [RATE_VECTOR, RATE_MATRIX]
    states = [
        adam_update(*state, gradient * clip, rate)
        for state, gradient, rate in zip(states, split + same, rates)
    ]
    return norm, lax.psum(done.tail[0, 0], AXES), states, bias[0] * clip


def per_device(plan, images, slot_mask, labels, *params):
    states = [params[3 * k : 3 * k + 3] for k in range(7)]
    patch, triple, output, expand, shrink, vector, head = (state[0] for state in states)
    count = images.shape[0]
    weights = slot_mask.astype(F32)
    args = dict(images=images, vectors=vector, head=head)
    scalars = dict(labels=labels, mask=slot_mask)
    if plan.cube:
        shards = dict(patch=patch, triple=triple, output=output, expand=expand, shrink=shrink)
        done = forward(plan, shards, args, scalars, None, None)
    else:

        def whole(shard, shape):
            axis = shard.ndim - 2
            gathered = lax.all_gather(shard.astype(BF), AXES, axis=axis, tiled=True)
            return gathered.reshape(shard.shape[:axis] + shape)

        gathered = [
            whole(patch, cols_shape(D)),
            whole(jnp.concatenate([triple, output], 2), cols_shape(FF)),
            whole(expand, cols_shape(FF)),
            whole(shrink, ROWS_SHAPE),
        ]
        total = jnp.full((8, 128), lax.psum(jnp.sum(weights), AXES), F32)
        done = forward(plan, None, args, scalars, gathered, total)
    got = backward(plan, images, vector, done)
    if plan.cube:
        norm, loss, states, bias_grad = update(plan, count, states, got)
    else:
        norm, loss, states, bias_grad = update_whole(plan, count, states, got, done)
    return (
        loss,
        done.total[0, 0],
        norm,
        *(value for state in states for value in state),
        bias_grad,
    )


def solution(mesh):
    plan = Plan(mesh)
    rows = P(AXES, None)
    layers = P(None, AXES, None)
    in_specs = (P(AXES, None, None), P(AXES), P(AXES)) + (rows,) * 3 + (layers,) * 12 + (P(),) * 6
    out_specs = (P(),) * 3 + (rows,) * 3 + (layers,) * 12 + (P(),) * 7
    return jax.shard_map(
        functools.partial(per_device, plan),
        mesh=mesh,
        in_specs=in_specs,
        out_specs=out_specs,
        check_vma=False,
    )
```

```python
import functools
from types import SimpleNamespace

import jax
import jax.numpy as jnp
from jax import lax
from jax.experimental import pallas as pl
from jax.experimental.pallas import tpu as pltpu
from jax.sharding import PartitionSpec as P

D = 768
HEADS = 12
HEAD_DIM = 64
FF = 3072
CLASSES = 1000
LAYERS = 3
STEP_INDEX = 10
S = 197
PAD = 208

EPS_NORM = 1e-06
CLIP = 0.1
BETA_ONE = 0.9
BETA_TWO = 0.95
ADAM_EPS = 1e-08
DECAY = 0.05
RATE_MATRIX = 0.03
RATE_OUTPUT = 0.2
RATE_VECTOR = 0.3
SMOOTH = 0.1

F32 = jnp.float32
BF = jnp.bfloat16
NN = (((1,), (0,)), ((), ()))
NT = (((1,), (1,)), ((), ()))
TN = (((0,), (0,)), ((), ()))
VMEM_SPEC = pl.BlockSpec(memory_space=pltpu.VMEM)
ANY_SPEC = pl.BlockSpec(memory_space=pl.ANY)
LIMIT = 62 * 1024 * 1024


def dot(left, right, form=NN):
    return lax.dot_general(left, right, form, preferred_element_type=F32)


def normalize(values, gain_row, shift_row):
    center = values - jnp.mean(values, -1, keepdims=True)
    spread = jnp.mean(center * center, -1, keepdims=True)
    return center * lax.rsqrt(spread + EPS_NORM) * gain_row + shift_row


def normalize_back(values, gain_row, grad):
    center = values - jnp.mean(values, -1, keepdims=True)
    spread = jnp.mean(center * center, -1, keepdims=True)
    scale = lax.rsqrt(spread + EPS_NORM)
    unit = center * scale
    d_unit = grad * gain_row
    d_values = scale * (
        d_unit
        - jnp.mean(d_unit, -1, keepdims=True)
        - unit * jnp.mean(d_unit * unit, -1, keepdims=True)
    )
    return (
        d_values,
        jnp.sum(grad * unit, 0, keepdims=True),
        jnp.sum(grad, 0, keepdims=True),
    )


def gelu_and_slope(u):
    x = jnp.abs(u) * 0.7071067811865476
    t = 1.0 / (1.0 + 0.3275911 * x)
    series = t * (
        0.254829592
        + t * (-0.284496736 + t * (1.421413741 + t * (-1.453152027 + t * 1.061405429)))
    )
    bell = jnp.exp(-0.5 * u * u)
    tail = 0.5 * series * bell
    share = jnp.where(u >= 0.0, 1.0 - tail, tail)
    return u * share, share + u * bell * 0.3989422804014327


class Plan:
    def __init__(self, mesh):
        self.wide, self.grp = mesh.shape["wide"], mesh.shape["grp"]
        self.n = self.wide * self.grp
        self.cube = self.wide == 8 and self.grp == 4

    def me(self):
        return lax.axis_index("wide") * self.grp + lax.axis_index("grp")

    def where(self):
        if not self.cube:
            return 0, 0, 0, 0
        wide, grp = lax.axis_index("wide"), lax.axis_index("grp")
        return wide // 2, wide % 2, grp // 2, grp % 2


CHIPS = (4, 2, 2)
BLOCK = D // 16
BLOCK_FF = FF // 32


def cols_shape(columns):
    return CHIPS + (BLOCK, columns)


ROWS_SHAPE = CHIPS + (2, BLOCK_FF, D)


def other_part(width):
    return width // 6 // 128 * 128


def cut_of(columns):
    return columns // 2 // 128 * 128


def over_links(plan):
    z, x, y, c = plan.where()

    def at(z, x, y, c):
        return (z * 2 + x, y * 2 + c)

    return SimpleNamespace(
        z1=at(jnp.bitwise_xor(z, 1), x, y, c),
        z3=at(jnp.bitwise_xor(z, 3), x, y, c),
        x=at(z, 1 - x, y, c),
        y=at(z, x, 1 - y, c),
        core=at(z, x, y, 1 - c),
    )


def remote(src, dst, send, recv, to):
    return pltpu.make_async_remote_copy(
        src_ref=src,
        dst_ref=dst,
        send_sem=send,
        recv_sem=recv,
        device_id=to,
        device_id_type=pl.DeviceIdType.MESH,
    )


class Gather:
    def __init__(self, plan, by_cols, block, whole, send, recv):
        self.z, self.x, self.y, self.c = plan.where()
        self.to = over_links(plan)
        self.by_cols, self.block, self.whole = by_cols, block, whole
        self.send, self.recv = send, recv
        self.width = block.shape[-1]
        self.other = other_part(self.width)
        self.most = self.width - self.other
        self.cut = (self.most // 2 + 127) // 128 * 128

    def region(self, z, x, y, start, width):
        if self.by_cols:
            first = pl.multiple_of(self.c * self.width + start, 128)
            return self.whole.at[z, x, y, :, pl.ds(first, width)]
        return self.whole.at[z, x, y, self.c, :, pl.ds(start, width)]

    def part(self, start, width):
        return self.block.at[:, pl.ds(start, width)]

    def copy(self, at):
        z, x, y, to = self.z, self.x, self.y, self.to
        z1, z3, line = jnp.bitwise_xor(z, 1), jnp.bitwise_xor(z, 3), slice(None)
        most, other, region = self.most, self.other, self.region
        cut, cut_other = self.cut, most + max(cut_of(other), 128)
        landed = at
        if at in (0, 1):
            src, dst = self.part(0, most), region(z, x, y, 0, most)
            device = (to.z1, to.z3)[at]
        elif at in (8, 9):
            src, dst = self.part(most, other), region(z, x, y, most, other)
            device = (to.x, to.y)[at - 8]
        else:
            src, device = {
                2: lambda: (region(z3, x, y, 0, most), to.z1),
                3: lambda: (region(z1, x, y, 0, most), to.z3),
                4: lambda: (region(line, x, y, 0, most), to.x),
                5: lambda: (region(line, x, y, 0, most), to.y),
                6: lambda: (region(line, x, 1 - y, 0, cut), to.x),
                7: lambda: (region(line, 1 - x, y, cut, most - cut), to.y),
                10: lambda: (region(z, x, 1 - y, most, cut_other - most), to.x),
                11: lambda: (region(z, 1 - x, y, cut_other, self.width - cut_other), to.y),
                12: lambda: (region(z, line, line, most, other), to.z1),
                13: lambda: (region(z, line, line, most, other), to.z3),
                14: lambda: (region(z3, line, line, most, other), to.z1),
                15: lambda: (region(z1, line, line, most, other), to.z3),
                16: lambda: (region(line, x, y, 0, most), to.core),
                17: lambda: (region(line, 1 - x, y, 0, most), to.core),
                18: lambda: (region(line, x, 1 - y, 0, most), to.core),
                19: lambda: (region(line, 1 - x, 1 - y, 0, cut), to.core),
                20: lambda: (region(line, 1 - x, 1 - y, cut, most - cut), to.core),
                21: lambda: (region(line, line, line, most, other), to.core),
            }[at]()
            dst = src
            if at in (3, 15):
                landed = at - 1
        return remote(src, dst, self.send.at[at], self.recv.at[landed], device)

    def exists(self, at):
        if at in (8, 9, 10, 12, 13, 14, 15, 21):
            return self.other > 0
        return at != 11 or self.other > 128

    def keep(self):
        here = self.region(self.z, self.x, self.y, 0, self.width)
        return pltpu.make_async_copy(self.block, here, self.send.at[22])

    def start(self, *which):
        for at in which:
            if self.exists(at):
                self.copy(at).start()

    def arrived(self, *which):
        for at in which:
            if self.exists(at):
                self.copy(at).wait_recv()

    def in_middle(self, do):
        pl.when((self.z == 1) | (self.z == 2))(do)

    def stage0(self):
        self.start(0, 1, 8, 9)
        self.keep().start()

    def stage1(self):
        self.arrived(0, 1)
        self.in_middle(lambda: self.start(2, 3))
        self.arrived(8, 9)
        self.start(10, 11)
        self.keep().wait()

    def stage2(self):
        self.arrived(2)
        self.start(4, 5, 16)
        self.arrived(10, 11)
        self.start(12, 13)

    def stage3(self):
        self.arrived(4, 5)
        self.start(6, 7, 17, 18)
        self.arrived(12, 13)
        self.in_middle(lambda: self.start(14, 15))

    def stage4(self):
        self.arrived(6, 7)
        self.start(19, 20)
        self.arrived(14)
        self.start(21)

    def finish(self):
        self.arrived(16, 17, 18, 19, 20, 21)
        passed = (2, 3, 14, 15)

        def sent(which):
            for at in which:
                if self.exists(at):
                    self.copy(at).wait_send()

        sent([at for at in range(22) if at not in passed])
        self.in_middle(lambda: sent(passed))


def cube_barrier(plan):
    z, x, y, c = plan.where()
    barrier = pltpu.get_barrier_semaphore()
    partners = [(jnp.bitwise_xor(z * 2 + x, k), y * 2 + c) for k in range(1, 8)]
    partners += [(z * 2 + x, (1 - y) * 2 + c), (z * 2 + x, y * 2 + 1 - c)]
    for partner in partners:
        pl.semaphore_signal(barrier, inc=1, device_id=partner, device_id_type=pl.DeviceIdType.MESH)
    pl.semaphore_wait(barrier, len(partners))


def load(source, target, sem):
    copy = pltpu.make_async_copy(source, target, sem)
    copy.start()
    return copy


def start_all(copies):
    for copy in copies:
        copy.start()


def wait_all(copies):
    for copy in copies:
        copy.wait()


def weight(ref, first, width):
    cols = pl.ds(first if isinstance(first, int) else pl.multiple_of(first, 128), width)
    return ref[:, :, :, :, cols].reshape(D, width)


class SmallGather:
    def __init__(self, plan, block, whole, send, recv):
        self.z, self.x, self.y, self.c = plan.where()
        self.to = over_links(plan)
        self.block, self.whole, self.send, self.recv = block, whole, send, recv

    def copy(self, at):
        z, x, y, c = self.z, self.x, self.y, self.c
        line = slice(None)
        if at < 7:
            src, dst = self.block, self.whole.at[z, x, y, c]
            device = (jnp.bitwise_xor(z * 2 + x, at + 1), y * 2 + c)
        elif at == 7:
            src = dst = self.whole.at[line, line, y, c]
            device = self.to.y
        else:
            src = dst = self.whole.at[line, line, line, c]
            device = self.to.core
        return remote(src, dst, self.send.at[at], self.recv.at[at], device)

    def keep(self):
        here = self.whole.at[self.z, self.x, self.y, self.c]
        return pltpu.make_async_copy(self.block, here, self.send.at[9])

    def stage0(self):
        for at in range(7):
            self.copy(at).start()
        self.keep().start()

    def stage1(self):
        for at in range(7):
            self.copy(at).wait_recv()
        self.keep().wait()
        self.copy(7).start()

    def stage2(self):
        self.copy(7).wait_recv()
        self.copy(8).start()

    def finish(self):
        self.copy(8).wait_recv()
        for at in range(9):
            self.copy(at).wait_send()


FF_TILE = 512
HALF = BLOCK // 2
WIDTH = FF // 2
HEAD_ROWS = 16
FINAL = S + 2 + 4 * LAYERS
TOP = LAYERS - 1
CLASS_PAD = 1024

Z_, M_, O_, Q_, A_ = (slice(0, FF),) + tuple(slice(FF + k * D, FF + k * D + D) for k in range(4))
FEATURE_, LOGIT_ = slice(FF + 4 * D, FF + 5 * D), slice(FF + 5 * D, FF + 5 * D + CLASS_PAD)
SLOPE_, H1_, G_ = slice(0, FF), slice(FF, FF + D), slice(FF + D, FF + 2 * D)
PIECES = (D, CLASS_PAD, FF, D, D, FF, D, D, D, D)
PER_IMAGE = sum(PIECES) // 128


def rows_block(images):
    return -(-PER_IMAGE * images // 16) * 16


def class_rows(ref, source):
    ref[...] = jnp.zeros_like(ref)
    for image in range(source.shape[0] // PAD):
        ref[image : image + 1] = source[image * PAD : image * PAD + 1]


def by_head(rows, image):
    head = lax.broadcasted_iota(jnp.int32, (16, D), 0)
    lane = lax.broadcasted_iota(jnp.int32, (16, D), 1)
    mine = (lane >= head * HEAD_DIM) & (lane < head * HEAD_DIM + HEAD_DIM)
    return mine, jnp.where(mine, rows[image : image + 1], 0.0)


def saved_shapes(rows):
    heads = rows // PAD * HEADS
    return dict(
        h=((rows, D), F32),
        a=((rows, D), BF),
        t=((rows, 3 * D), BF),
        o=((rows, D), BF),
        p=((heads, PAD, PAD), BF),
        h1=((rows, D), F32),
        m=((rows, D), BF),
        z=((rows, FF), BF),
        slope=((rows, FF), BF),
    )


SAVED = tuple(saved_shapes(PAD))


def row(ref, at):
    return ref[pl.ds(at, 1)]


def share_shards(plan, r):
    z, x, y, c = plan.where()
    r.joined_f[:, :, : 3 * D] = r.triple[...]
    r.joined_f[:, :, 3 * D :] = r.output[...]
    mine = pl.ds(pl.multiple_of(c * HALF, 8), HALF)

    def part(core, width):
        return pl.ds(pl.multiple_of(core * width, 128), width)

    moves = [
        (r.patch.at[:, part(1 - c, D // 2)], r.patch_f.at[mine]),
        (r.joined_f.at[:, :, part(1 - c, WIDTH)], r.joined_b.at[:, mine]),
        (r.expand.at[:, :, part(1 - c, WIDTH)], r.expand_b.at[:, mine]),
    ]
    copies = [
        pltpu.make_async_remote_copy(
            src_ref=src,
            dst_ref=dst,
            send_sem=r.share_send.at[i],
            recv_sem=r.share_recv.at[i],
            device_id=(z * 2 + x, y * 2 + 1 - c),
            device_id_type=pl.DeviceIdType.MESH,
        )
        for i, (src, dst) in enumerate(moves)
    ]
    start_all(copies)
    r.patch_f[mine] = r.patch[:, part(c, D // 2)]
    r.joined_b[:, mine] = r.joined_f[:, :, part(c, WIDTH)]
    r.expand_b[:, mine] = r.expand[:, :, part(c, WIDTH)]
    targets = (
        (r.patch_f, r.patch_block),
        (r.joined_b, r.joined_block),
        (r.expand_b, r.expand_block),
    )

    def arrive(which):
        src, dst = targets[which]
        copies[which].wait_recv()
        dst[...] = src[...].astype(BF)
        copies[which].wait_send()

    return arrive


def class_column(ref, kind):
    line = lax.broadcasted_iota(jnp.int32, (HEAD_ROWS, 1), 0)
    column = jnp.zeros((HEAD_ROWS, 1), kind)
    for image in range(ref.shape[0]):
        column = jnp.where(line == image, ref[image].astype(kind), column)
    return column


def head_part(r, first, image_total):
    table = r.table[...]
    gain, shift = r.vectors[FINAL : FINAL + 1], r.vectors[FINAL + 1 : FINAL + 2]
    feature = normalize(first, gain, shift).astype(BF)
    logits = dot(feature, table) + r.head[D : D + 1]
    ids = lax.broadcasted_iota(jnp.int32, logits.shape, 1)
    shifted = logits - jnp.max(logits, -1, keepdims=True)
    log_prob = shifted - jnp.log(jnp.sum(jnp.exp(shifted), -1, keepdims=True))
    target = jnp.where(ids == class_column(r.labels, jnp.int32), 1.0 - SMOOTH, 0.0) + SMOOTH / CLASSES
    weights = class_column(r.mask, F32)
    loss = jnp.sum(weights * -jnp.sum(target * log_prob, -1, keepdims=True))
    d_logits = ((weights / image_total) * (jnp.exp(log_prob) - target)).astype(BF)
    d_feature = dot(d_logits, table, NT)
    r.d_logits[...] = jnp.zeros_like(r.d_logits)
    r.d_logits[:, :CLASSES] = d_logits.astype(F32)
    r.top_b[:, FEATURE_] = feature
    r.top_b[:, LOGIT_] = r.d_logits[...].astype(BF)
    d_first, d_gain, d_shift = normalize_back(first, gain, d_feature)
    r.top_f[:, G_] = d_first
    r.tail[...] = jnp.zeros_like(r.tail)
    r.tail[0:1] = jnp.full((1, D), loss, F32)
    r.tail[1:2] = d_gain
    r.tail[2:3] = d_shift


def pack_rows(r, kind, *sources):
    first = sum(PIECES[:kind]) // 128
    for source in sources:
        value = source.astype(F32)
        for j in range(value.shape[1] // 128):
            for image in range(r.images.shape[0]):
                at = image * PER_IMAGE + first + j
                r.rows_f[at : at + 1] = value[image : image + 1, j * 128 : j * 128 + 128]
        first += value.shape[1] // 128


def top_backward(plan, r):
    images = r.images.shape[0]
    base = S + 2 + 4 * TOP
    g = r.top_f[:, G_]
    g_low = g.astype(BF)
    for j in range(4):
        cols = slice(j * D, j * D + D)
        dz = dot(g_low, r.shrink_w[j].reshape(D, D), NT)
        r.top_du[:, cols] = (dz * r.top_f[:, cols]).astype(BF)
    d_m = jnp.zeros((HEAD_ROWS, D), F32)
    for j in range(4):
        d_m = d_m + dot(r.top_du[:, j * D : j * D + D], weight(r.expand_w, j * D, D), NT)
    d_h1, d_gain, d_shift = normalize_back(r.top_f[:, H1_], row(r.vectors, base + 2), d_m)
    r.tail[5:6] = d_gain
    r.tail[6:7] = d_shift
    g1 = g + d_h1
    g1_low = g1.astype(BF)
    d_o = dot(g1_low, weight(r.joined_w, 3 * D, D), NT).astype(BF).astype(F32)
    query = r.top_b[:, Q_].astype(F32)
    r.class_row[...] = jnp.zeros_like(r.class_row)
    for image in range(images):
        rows = slice(image * PAD, image * PAD + PAD)
        mine, spread_o = by_head(d_o, image)
        _, spread_q = by_head(query, image)
        spread_o, spread_q = spread_o.astype(BF), spread_q.astype(BF)
        p_low = r.top_p[image]
        p = p_low.astype(F32)
        r.d_keys[rows, D:] = dot(p_low, spread_o).astype(BF)
        dp = dot(r.t[rows, 2 * D :], spread_o, NT)
        ds = (p * (dp - jnp.sum(p * dp, 0, keepdims=True))).astype(BF)
        r.d_keys[rows, :D] = (dot(ds, spread_q) * HEAD_DIM**-0.5).astype(BF)
        d_q = jnp.where(mine, dot(ds, r.t[rows, D : 2 * D], TN), 0.0)
        r.class_row[image : image + 1] = jnp.sum(d_q, 0, keepdims=True) * HEAD_DIM**-0.5
    for part in range(2):
        value = dot(r.a[...], r.d_keys[:, part * D : part * D + D], TN)
        store_cols(plan, r.keys_block, 0, part, D, value, D, 1)
    keys = load(r.keys_block, r.keys_out, r.loads.at[0])
    d_q = r.class_row[...].astype(BF)
    r.g[...] = dot(r.d_keys[:, :D], weight(r.joined_w, D, D), NT)
    r.g[...] += dot(r.d_keys[:, D:], weight(r.joined_w, 2 * D, D), NT)
    d_a = dot(d_q, weight(r.joined_w, 0, D), NT)
    for image in range(images):
        r.g[image * PAD : image * PAD + 1] += d_a[image : image + 1]
    d_h, d_gain, d_shift = normalize_back(r.h[...], row(r.vectors, base), r.g[...])
    r.g[...] = d_h
    for image in range(images):
        r.g[image * PAD : image * PAD + 1] += g1[image : image + 1]
    r.tail[3:4] = d_gain
    r.tail[4:5] = d_shift
    pack_rows(r, 0, r.top_b[:, FEATURE_], r.top_b[:, LOGIT_])
    pack_rows(r, 3, g_low)
    pack_rows(r, 5, r.top_du[...])
    pack_rows(r, 7, g1_low)
    pack_rows(r, 9, d_q)
    r.rows_block[...] = r.rows_f[...].astype(BF)
    keys.wait()


def forward_kernel(plan, names, *refs):
    r = SimpleNamespace(**dict(zip(names, refs)))
    cube = plan.cube
    images = r.images.shape[0]
    patch, joined, expand, shrink = range(4)
    pixels = load(r.images_in, r.images, r.loads.at[4])
    wholes = (r.patch_whole, r.joined_whole, r.expand_whole, r.shrink_whole)
    weights = (r.patch_w, r.joined_w, r.expand_w, r.shrink_w)
    if cube:
        blocks = (r.patch_block, r.joined_block, r.expand_block, r.shrink_block)
        cube_barrier(plan)
        r.shrink_block[...] = r.shrink[...].astype(BF)
        arrive = share_shards(plan, r)
        r.count[...] = jnp.full((8, 128), jnp.sum(class_column(r.mask, F32)), F32)
        counting = SmallGather(plan, r.count, r.counts, r.count_send, r.count_recv)

    def unit(kind, layer):
        if kind == patch:
            return Gather(plan, True, blocks[0], wholes[0], r.send.at[0], r.recv.at[0])
        at = 3 * layer + kind
        block, whole = blocks[kind].at[layer], wholes[kind].at[layer]
        return Gather(plan, kind != shrink, block, whole, r.send.at[at], r.recv.at[at])

    def ready(kind, layer):
        if cube:
            unit(kind, layer).finish()
        whole = wholes[kind] if kind == patch else wholes[kind].at[layer]
        return load(whole, weights[kind], r.loads.at[kind])

    held = (r.h, r.a, r.t, r.o, r.p, r.h1, r.m, r.z, r.slope)
    kept = (r.keep_h, r.keep_a, r.keep_t, r.keep_o, r.keep_p, r.keep_h1, r.keep_m, r.keep_z, r.keep_slope)
    h_, a_, t_, o_, p_, h1_, m_, z_, slope_ = range(9)

    def saves(layer, *which):
        return [pltpu.make_async_copy(held[k], kept[k].at[layer], r.saves.at[k]) for k in which]

    if cube:
        first = [unit(patch, 0), unit(joined, 0), unit(expand, 0), unit(shrink, 0), unit(joined, 1)]
        arrive(0)
        first[0].stage0()
        counting.stage0()
        arrive(1)
        first[1].stage0()
        first[0].stage1()
        arrive(2)
        first[2].stage0()
        first[1].stage1()
        first[0].stage2()
        first[3].stage0()
        first[2].stage1()
        first[1].stage2()
        first[0].stage3()
        first[4].stage0()
        first[3].stage1()
        first[2].stage2()
        first[1].stage3()
        first[0].stage4()
    r.table[...] = r.head[:D].astype(BF)
    ready(patch, 0).wait()
    pixels.wait()
    for image in range(images):
        at = image * PAD
        r.h[at : at + 1] = r.vectors[0:1] + r.vectors[S : S + 1]
        embedded = dot(r.images[image], weight(r.patch_w, 0, D))
        r.h[at + 1 : at + S] = embedded + r.vectors[S + 1 : S + 2] + r.vectors[1:S]
        r.h[at + S : at + PAD] = jnp.zeros((PAD - S, D), F32)

    low_lane = lax.broadcasted_iota(jnp.int32, (PAD, 128), 1) < HEAD_DIM
    real_key = lax.broadcasted_iota(jnp.int32, (PAD, PAD), 0) < S

    @pl.loop(0, TOP)
    def _(layer):
        base = S + 2 + 4 * layer
        if cube:
            unit(expand, layer + 1).stage0()
            unit(joined, layer + 1).stage1()
            unit(shrink, layer).stage2()
            unit(expand, layer).stage3()
            unit(joined, layer).stage4()
        start_all(saves(layer, h_))

        @pl.when(layer > 0)
        def _():
            wait_all(saves(layer, a_, t_, o_, p_, h1_, m_))

        r.a[...] = normalize(r.h[...], row(r.vectors, base), row(r.vectors, base + 1)).astype(BF)
        ready(joined, layer).wait()

        @pl.loop(0, 3)
        def _(j):
            cols = pl.ds(pl.multiple_of(j * D, 128), D)
            r.t[:, cols] = dot(r.a[...], weight(r.joined_w, j * D, D)).astype(BF)

        start_all(saves(layer, a_, t_))

        def heads(step):
            image, pair = step // (HEADS // 2), step % (HEADS // 2)
            rows = pl.ds(pl.multiple_of(image * PAD, 16), PAD)
            lanes = [pl.ds(pl.multiple_of(pair * 128 + part * D, 128), 128) for part in range(3)]
            q, key, v = (r.t[rows, lane] for lane in lanes)
            zero = jnp.zeros_like(key)
            outs = []
            for which in range(2):
                part = jnp.where(low_lane, key, zero) if which == 0 else jnp.where(low_lane, zero, key)
                scores = dot(part, q, NT) * HEAD_DIM**-0.5
                scores = jnp.where(real_key, scores, -1e30)
                top = jnp.max(scores, 0, keepdims=True)
                e = jnp.exp(scores - top)
                p = (e * (1.0 / jnp.sum(e, 0, keepdims=True))).astype(BF)
                r.p[step * 2 + which] = p
                outs.append(dot(p, v, TN))
            r.o[rows, lanes[0]] = jnp.where(low_lane, outs[0], outs[1]).astype(BF)

        half = images * (HEADS // 2) // 2
        pl.loop(0, half)(heads)
        if cube:
            unit(shrink, layer + 1).stage0()
            unit(expand, layer + 1).stage1()
            unit(joined, layer + 1).stage2()

        pl.loop(half, 2 * half)(heads)
        start_all(saves(layer, o_, p_))
        r.h1[...] = r.h[...] + dot(r.o[...], weight(r.joined_w, 3 * D, D))
        start_all(saves(layer, h1_))
        if cube:
            unit(shrink, layer).stage3()
            unit(expand, layer).stage4()
            pl.when(layer == 0)(counting.stage1)
            pl.when(layer == 1)(counting.finish)
        r.m[...] = normalize(r.h1[...], row(r.vectors, base + 2), row(r.vectors, base + 3)).astype(BF)
        start_all(saves(layer, m_))
        wait_all(saves(layer, h_))
        r.h[...] = r.h1[...]

        @pl.when(layer > 0)
        def _():
            wait_all(saves(layer, z_, slope_))

        ready(expand, layer).wait()

        @pl.loop(0, FF // FF_TILE)
        def _(j):
            cols = pl.ds(pl.multiple_of(j * FF_TILE, 128), FF_TILE)
            u = dot(r.m[...], weight(r.expand_w, j * FF_TILE, FF_TILE))
            z, slope = gelu_and_slope(u)
            r.z[:, cols] = z.astype(BF)
            r.slope[:, cols] = slope.astype(BF)

        start_all(saves(layer, z_, slope_))
        if cube:
            pl.when(layer < TOP - 1)(lambda: unit(joined, layer + 2).stage0())

            unit(shrink, layer + 1).stage1()
            unit(expand, layer + 1).stage2()
            unit(joined, layer + 1).stage3()
            unit(shrink, layer).stage4()
            pl.when(layer == 0)(counting.stage2)
        ready(shrink, layer).wait()

        @pl.loop(0, 4)
        def _(j):
            cols = pl.ds(pl.multiple_of(j * D, 128), D)
            r.h[...] += dot(r.z[:, cols], r.shrink_w[j].reshape(D, D))

    base = S + 2 + 4 * TOP
    if cube:
        unit(shrink, TOP).stage2()
        unit(expand, TOP).stage3()
        unit(joined, TOP).stage4()
    start_all(saves(TOP, h_))
    wait_all(saves(TOP, a_, t_) + saves(0, o_, p_, h1_, m_))
    r.a[...] = normalize(r.h[...], row(r.vectors, base), row(r.vectors, base + 1)).astype(BF)
    class_rows(r.first, r.h)
    first = r.first[...]
    r.top_b[:, A_] = normalize(first, row(r.vectors, base), row(r.vectors, base + 1)).astype(BF)
    ready(joined, TOP).wait()
    for j in (1, 2):
        r.t[:, j * D : j * D + D] = dot(r.a[...], weight(r.joined_w, j * D, D)).astype(BF)
    start_all(saves(TOP, a_, t_))
    query = dot(r.top_b[:, A_], weight(r.joined_w, 0, D)).astype(BF)
    r.top_b[:, Q_] = query
    if cube:
        unit(shrink, TOP).stage3()
        unit(expand, TOP).stage4()
    query = query.astype(F32)
    real = lax.broadcasted_iota(jnp.int32, (PAD, 16), 0) < S
    r.class_row[...] = jnp.zeros_like(r.class_row)
    for image in range(images):
        rows = slice(image * PAD, image * PAD + PAD)
        mine, spread = by_head(query, image)
        scores = dot(r.t[rows, D : 2 * D], spread.astype(BF), NT) * HEAD_DIM**-0.5
        scores = jnp.where(real, scores, -1e30)
        e = jnp.exp(scores - jnp.max(scores, 0, keepdims=True))
        p = (e * (1.0 / jnp.sum(e, 0, keepdims=True))).astype(BF)
        r.top_p[image] = p
        out = jnp.where(mine, dot(p, r.t[rows, 2 * D :], TN), 0.0)
        r.class_row[image : image + 1] = jnp.sum(out, 0, keepdims=True)
    attended = r.class_row[...].astype(BF)
    r.top_b[:, O_] = attended
    h1 = first + dot(attended, weight(r.joined_w, 3 * D, D))
    r.top_f[:, H1_] = h1
    r.top_b[:, M_] = normalize(h1, row(r.vectors, base + 2), row(r.vectors, base + 3)).astype(BF)
    ready(expand, TOP).wait()
    for j in range(4):
        cols = slice(j * D, j * D + D)
        z, slope = gelu_and_slope(dot(r.top_b[:, M_], weight(r.expand_w, j * D, D)))
        r.top_b[:, cols] = z.astype(BF)
        r.top_f[:, cols] = slope
    if cube:
        unit(shrink, TOP).stage4()
    r.rows_f[...] = jnp.zeros_like(r.rows_f)
    pack_rows(r, 2, r.top_b[:, Z_])
    pack_rows(r, 4, r.top_b[:, M_])
    pack_rows(r, 6, r.top_b[:, O_])
    pack_rows(r, 8, r.top_b[:, A_])
    ready(shrink, TOP).wait()
    last = h1
    for j in range(4):
        last = last + dot(r.top_b[:, j * D : j * D + D], r.shrink_w[j].reshape(D, D))

    if cube:
        r.total[...] = jnp.sum(r.counts[...].reshape(-1, 8, 128), 0)
        image_total = r.total[0:1, 0:1]
    else:
        image_total = r.count_in[0:1, 0:1]
    head_part(r, last, image_total)
    top_backward(plan, r)
    wait_all(saves(TOP, h_, a_, t_) + saves(0, z_, slope_))


def pallas(kernel, name, inputs, outputs, scratch, **params):
    names = list(inputs) + list(outputs) + list(scratch)
    outs = pl.pallas_call(
        functools.partial(kernel, names),
        out_shape=[jax.ShapeDtypeStruct(shape, kind) for shape, kind, _ in outputs.values()],
        in_specs=[spec for _, spec in inputs.values()],
        out_specs=[spec for _, _, spec in outputs.values()],
        scratch_shapes=list(scratch.values()),
        compiler_params=pltpu.CompilerParams(vmem_limit_bytes=LIMIT, **params),
        name=name,
    )(*[value for value, _ in inputs.values()])
    return SimpleNamespace(**dict(zip(outputs, outs)))


def given_in(spec, **values):
    return {name: (value, spec) for name, value in values.items()}


def vmem(kind, **shapes):
    return {name: pltpu.VMEM(shape, kind) for name, shape in shapes.items()}


def dma(**counts):
    return {name: pltpu.SemaphoreType.DMA(count) for name, count in counts.items()}


def forward(plan, images, shards, args, scalars, gathered, count):
    rows = images.shape[0] * PAD
    shapes = saved_shapes(rows)
    whole = dict(
        patch_whole=cols_shape(D),
        joined_whole=(LAYERS,) + cols_shape(FF),
        expand_whole=(LAYERS,) + cols_shape(FF),
        shrink_whole=(LAYERS,) + ROWS_SHAPE,
    )
    inputs = given_in(VMEM_SPEC, **args)
    inputs.update(given_in(ANY_SPEC, images_in=images))
    inputs.update(given_in(pl.BlockSpec(memory_space=pltpu.SMEM), **scalars))
    outputs = {}
    if plan.cube:
        inputs.update(given_in(VMEM_SPEC, **shards))
        outputs.update({name: (shape, BF, ANY_SPEC) for name, shape in whole.items()})
    else:
        inputs.update(given_in(ANY_SPEC, **dict(zip(whole, gathered))))
        inputs.update(given_in(VMEM_SPEC, count_in=count))
    for name, (shape, kind) in shapes.items():
        deep = LAYERS if name in ("h", "a", "t") else TOP
        outputs["keep_" + name] = ((deep,) + shape, kind, ANY_SPEC)
    outputs.update(
        g=((rows, D), F32, VMEM_SPEC),
        rows_block=((rows_block(rows // PAD), 128), BF, VMEM_SPEC),
        keys_out=((2, 4, 4, BLOCK, D), BF, ANY_SPEC),
        tail=((8, D), F32, VMEM_SPEC),
        total=((8, 128), F32, VMEM_SPEC),
    )
    scratch = vmem(
        BF,
        table=(D, CLASSES),
        images=images.shape,
        top_b=(HEAD_ROWS, LOGIT_.stop),
        top_p=(rows // PAD, PAD, 16),
        top_du=(HEAD_ROWS, FF),
        d_keys=(rows, 2 * D),
        keys_block=(2, 4, 4, BLOCK, D),
        patch_w=cols_shape(D),
        joined_w=cols_shape(FF),
        expand_w=cols_shape(FF),
        shrink_w=ROWS_SHAPE,
    )
    scratch.update({name: pltpu.VMEM(shape, kind) for name, (shape, kind) in shapes.items()})
    scratch.update(
        vmem(
            F32,
            first=(HEAD_ROWS, D),
            class_row=(HEAD_ROWS, D),
            d_logits=(HEAD_ROWS, CLASS_PAD),
            top_f=(HEAD_ROWS, G_.stop),
            rows_f=(rows_block(rows // PAD), 128),
        )
    )
    scratch.update(dma(saves=(9,), loads=(5,)))
    extra = {}
    if plan.cube:
        scratch.update(
            vmem(
                F32,
                joined_f=(LAYERS, HALF, FF),
                joined_b=(LAYERS, BLOCK, WIDTH),
                expand_b=(LAYERS, BLOCK, WIDTH),
                patch_f=(BLOCK, D // 2),
                count=(8, 128),
                counts=CHIPS + (2, 8, 128),
            )
        )
        scratch.update(
            vmem(
                BF,
                patch_block=(BLOCK, D // 2),
                joined_block=(LAYERS, BLOCK, WIDTH),
                expand_block=(LAYERS, BLOCK, WIDTH),
                shrink_block=(LAYERS, BLOCK_FF, D),
            )
        )
        scratch.update(
            dma(send=(10, 23), recv=(10, 22), share_send=(3,), share_recv=(3,), count_send=(10,), count_recv=(9,))
        )
        extra = dict(collective_id=1, has_side_effects=True)
    got = pallas(functools.partial(forward_kernel, plan), "forward", inputs, outputs, scratch, **extra)
    if not plan.cube:
        for name, value in zip(whole, gathered):
            setattr(got, name, value)
        got.total = count
    return got


UNITS = 4 * TOP + 1
WIDTHS = (WIDTH, WIDTH, D // 2, 3 * D // 2)
SHRINK, EXPAND, OUTPUT, TRIPLE = range(4)
KEYS = D
TAIL = 512
SEND = 4
VEC_ROWS = 256


def relative(plan):
    z, x, y, c = plan.where()
    return c, (z * 2 + x) * 2 + y


def place(plan, slot, core, chip, send=SEND):
    my_core, my_chip = relative(plan)
    at = jnp.bitwise_xor(my_chip, chip)
    other = jnp.bitwise_xor(my_core, core)
    return slot + (send - slot) * other, at // 4, at % 4


def store_cols(plan, out, slot, tile, width, value, half=WIDTH, send=SEND):
    per_half = half // width
    lanes = pl.ds(pl.multiple_of((tile % per_half) * width, 128), width)
    for b in range(16):
        rows = value[b * BLOCK : (b + 1) * BLOCK].astype(BF)
        out[(*place(plan, slot, tile // per_half, b, send), slice(None), lanes)] = rows


def store_rows(plan, out, slot, tile, value):
    for b in range(4):
        at = place(plan, slot, b % 2, tile * 2 + b // 2)
        for part in range(2):
            first = b * BLOCK_FF + part * BLOCK
            out[(*at, slice(None), pl.ds(part * D, D))] = value[first : first + BLOCK].astype(BF)


def store_vectors(plan, out, slot, value):
    for b in range(32):
        rows = value[b * 8 : b * 8 + 8]
        block = jnp.concatenate([rows[:, j * 128 : j * 128 + 128] for j in range(6)], 0)
        out[(*place(plan, slot, b % 2, b // 2), slice(None), pl.ds(D // 2, 128))] = block.astype(BF)


class Reduce:
    def __init__(self, plan, bufs, unit, width=WIDTH):
        self.plan, self.bufs, self.unit, self.width = plan, bufs, unit, width
        self.z, self.x, self.y, self.c = plan.where()
        self.to = over_links(plan)
        self.other = other_part(width) if width > KEYS else 0
        self.most = width - self.other
        self.cut, self.cut_other = cut_of(self.most), max(cut_of(self.other), 128)
        self.slot, self.three, self.two = unit % 4, unit % 3, unit % 2

    def copy(self, at):
        b, slot, three, to, c = self.bufs, self.slot, self.three, self.to, self.c
        most, cut, cut_other = self.most, self.cut, self.cut_other
        line = slice(None)
        full, main = pl.ds(0, self.width), pl.ds(0, most)
        left, right, low = pl.ds(0, cut), pl.ds(cut, most - cut), pl.ds(0, most - cut)
        other, all_other = pl.ds(most, self.other), pl.ds(0, self.other)
        own = b.unit.at[slot]
        if at == 17:
            rows = pl.ds(pl.multiple_of((1 - c) * HALF, 8), HALF)
            src, dst = self.result(rows)
            device = to.core
        else:
            src, dst, device = {
                0: lambda: (b.unit.at[SEND, :, :, :, full], b.core.at[:, :, :, full], to.core),
                1: lambda: (own.at[:, 3, :, left], b.near.at[three, :, :, left], to.x),
                2: lambda: (own.at[:, 3, :, right], b.far.at[three, :, :, low], to.y),
                3: lambda: (own.at[:, 1, :, main], b.y.at[three, :, :, main], to.y),
                4: lambda: (own.at[:, 2, :, main], b.x.at[three, :, :, main], to.x),
                5: lambda: (b.line.at[three, 2, :, main], b.main_two.at[three, 0, :, main], to.z1),
                6: lambda: (b.line.at[three, 2, :, main], b.main_two.at[three, 1, :, main], to.z3),
                7: lambda: (b.line.at[three, 1, :, main], b.main_one.at[slot, 0, :, main], to.z1),
                8: lambda: (b.line.at[three, 3, :, main], b.main_one.at[slot, 1, :, main], to.z3),
                9: lambda: (own.at[2, :, :, other], b.other_two.at[three, 0, :, :, all_other], to.z1),
                10: lambda: (own.at[2, :, :, other], b.other_two.at[three, 1, :, :, all_other], to.z3),
                11: lambda: (own.at[1, :, :, other], b.other_one.at[slot, 0, :, :, all_other], to.z1),
                12: lambda: (own.at[3, :, :, other], b.other_one.at[slot, 1, :, :, all_other], to.z3),
                13: lambda: (b.plane.at[three, 3, :, pl.ds(0, cut_other)], b.other_near.at[three], to.x),
                14: lambda: (b.plane.at[three, 3, :, pl.ds(cut_other, cut_other)], b.other_far.at[three], to.y),
                15: lambda: (b.plane.at[three, 1, :, all_other], b.other_y.at[three, :, all_other], to.y),
                16: lambda: (b.plane.at[three, 2, :, all_other], b.other_x.at[three, :, all_other], to.x),
            }[at]()
        return remote(src, dst, b.send.at[slot, at], b.recv.at[slot, at], device)

    def result(self, rows):
        b, c = self.bufs, self.c
        total, at = b.total.at[self.two], (self.unit - 1) // 4
        if self.width == WIDTH:
            return total.at[rows], b.expand_grad.at[at, c]
        if self.width == TAIL:
            return total.at[rows, pl.ds(0, D // 2)], b.patch.at[c]
        total = total.at[rows, pl.ds(0, self.width)]
        if self.width == KEYS:
            return total, b.keys.at[c]
        return total, (b.output_grad if self.width == WIDTHS[OUTPUT] else b.triple_grad).at[at, c]

    def own(self, by_rows):
        b, c = self.bufs, self.c
        total = b.total.at[self.two]
        if by_rows:
            at = (self.unit - 1) // 4
            moves = [(total.at[pl.ds(k * HALF, HALF)], b.shrink_grad.at[at, k]) for k in range(2)]
        else:
            moves = [self.result(pl.ds(pl.multiple_of(c * HALF, 8), HALF))]
        return [
            pltpu.make_async_copy(src, dst, b.send.at[self.slot, 18 + k])
            for k, (src, dst) in enumerate(moves)
        ]

    def start(self, *which):
        for at in which:
            self.copy(at).start()

    def arrived(self, *which):
        for at in which:
            self.copy(at).wait_recv()

    def sent(self, *which):
        for at in which:
            self.copy(at).wait_send()

    def corner(self):
        return (13, 14) if self.other > self.cut_other else (13,)

    def by_place(self, middle, end):
        inside = (self.z == 1) | (self.z == 2)
        if middle:
            pl.when(inside)(middle)
        if end:
            pl.when(jnp.logical_not(inside))(end)

    def stage0(self):
        @pl.when(self.unit > 0)
        def _():
            pl.semaphore_wait(self.bufs.credit, 1)

        self.start(0)

    def stage1(self):
        unit, core, slot = self.bufs.unit, self.bufs.core, self.slot
        cols = pl.ds(0, self.width)
        self.arrived(0)

        def add(z, chip):
            both = unit[slot, z, chip, :, cols].astype(F32) + core[z, chip, :, cols].astype(F32)
            unit[slot, z, chip, :, cols] = both.astype(BF)

        pl.loop(0, 4)(lambda z: add(z, 3))
        self.start(1, 2)
        pl.loop(0, 12)(lambda i: add(i // 3, i % 3))
        if self.other:
            self.by_place(lambda: self.start(10), lambda: self.start(9))

        @pl.when(self.unit < UNITS)
        def _():
            pl.semaphore_signal(
                self.bufs.credit, inc=1, device_id=self.to.core, device_id_type=pl.DeviceIdType.MESH
            )

    def stage2(self):
        b, slot, three, most, cut = self.bufs, self.slot, self.three, self.most, self.cut
        unit = b.unit
        left, right, low = pl.ds(0, cut), pl.ds(cut, most - cut), pl.ds(0, most - cut)
        self.arrived(1, 2)

        @pl.loop(0, 4)
        def _(z):
            got = b.near[three, z, :, left].astype(F32)
            unit[slot, z, 1, :, left] = (unit[slot, z, 1, :, left].astype(F32) + got).astype(BF)
            got = b.far[three, z, :, low].astype(F32)
            unit[slot, z, 2, :, right] = (unit[slot, z, 2, :, right].astype(F32) + got).astype(BF)

        self.start(3, 4)
        self.sent(1, 2)
        if not self.other:
            return
        other = pl.ds(most, self.other)

        def pass_on():
            self.arrived(9, 10)
            for z, k in ((3, 0), (1, 1)):
                for chip in range(4):
                    got = b.other_two[three, k, chip, :, pl.ds(0, self.other)].astype(F32)
                    unit[slot, z, chip, :, other] = (
                        unit[slot, z, chip, :, other].astype(F32) + got
                    ).astype(BF)

        self.by_place(pass_on, None)
        self.start(11, 12)

    def stage3(self):
        b, slot, three, main = self.bufs, self.slot, self.three, pl.ds(0, self.most)
        self.arrived(3, 4)

        @pl.loop(0, 4)
        def _(z):
            b.line[three, z, :, main] = (
                b.unit[slot, z, 0, :, main].astype(F32)
                + b.y[three, z, :, main].astype(F32)
                + b.x[three, z, :, main].astype(F32)
            ).astype(BF)

        self.by_place(lambda: self.start(6), lambda: self.start(5))
        self.sent(3, 4)
        if not self.other:
            return
        self.arrived(11, 12)
        for chip in range(4):
            every = pl.ds(0, self.other)
            b.plane[three, chip, :, every] = (
                b.unit[slot, 0, chip, :, pl.ds(self.most, self.other)].astype(F32)
                + b.other_one[slot, 0, chip, :, every].astype(F32)
                + b.other_one[slot, 1, chip, :, every].astype(F32)
            ).astype(BF)
        self.start(*self.corner())
        self.by_place(lambda: self.sent(10), lambda: self.sent(9))
        self.sent(11, 12)

    def stage4(self):
        b, three, main = self.bufs, self.three, pl.ds(0, self.most)

        def pass_on():
            self.arrived(5, 6)
            for z, k in ((3, 0), (1, 1)):
                got = b.main_two[three, k, :, main].astype(F32)
                b.line[three, z, :, main] = (b.line[three, z, :, main].astype(F32) + got).astype(BF)

        self.by_place(pass_on, None)
        self.start(7, 8)
        if not self.other:
            return
        self.arrived(*self.corner())
        half = self.cut_other
        for chip, cols, got in (
            (1, pl.ds(0, half), b.other_near),
            (2, pl.ds(half, half), b.other_far),
        )[: len(self.corner())]:
            both = b.plane[three, chip, :, cols].astype(F32) + got[three].astype(F32)
            b.plane[three, chip, :, cols] = both.astype(BF)
        self.start(15, 16)
        self.sent(*self.corner())

    def stage5(self, by_rows):
        b, slot, three, two = self.bufs, self.slot, self.three, self.two
        main = pl.ds(0, self.most)
        self.arrived(7, 8)
        total = b.line[three, 0, :, main].astype(F32)
        for k in range(2):
            total = total + b.main_one[slot, k, :, main].astype(F32)
        b.total[two, :, main] = total
        b.squares[0:1, main] += jnp.sum(total * total, 0, keepdims=True)
        if self.other:
            self.arrived(15, 16)
            other = pl.ds(self.most, self.other)
            every = pl.ds(0, self.other)
            total = (
                b.plane[three, 0, :, every].astype(F32)
                + b.other_y[three, :, every].astype(F32)
                + b.other_x[three, :, every].astype(F32)
            )
            b.total[two, :, other] = total
            b.squares[0:1, other] += jnp.sum(total * total, 0, keepdims=True)
        if not by_rows:
            self.start(17)
        start_all(self.own(by_rows))
        self.by_place(lambda: self.sent(6), lambda: self.sent(5))
        self.sent(7, 8)
        if self.other:
            self.sent(15, 16)

    def stage6(self, by_rows):
        if not by_rows:
            self.copy(17).wait()
        wait_all(self.own(by_rows))


POINTS = 4
STAGE_ORDER = (1, 0, 2, 3, 4, 6, 5)


def backward_kernel(plan, names, *refs):
    r = SimpleNamespace(**dict(zip(names, refs)))
    cube = plan.cube
    images = r.images.shape[0]
    loads = [
        (r.keep_z, r.vm_z),
        (r.shrink_whole, r.shrink_w),
        (r.keep_slope, r.vm_slope),
        (r.expand_whole, r.expand_w),
        (r.keep_m, r.vm_m),
        (r.keep_h1, r.vm_h1),
        (r.keep_o, r.vm_o),
        (r.keep_t, r.vm_t),
        (r.keep_p, r.vm_p),
        (r.keep_a, r.vm_a),
        (r.keep_h, r.vm_h),
        (r.joined_whole, r.expand_w),
    ]
    z_, shrink_, slope_, expand_, m_, h1_, o_, t_, p_, a_, h_, joined_ = range(12)

    def fetch(which, layer):
        src, dst = loads[which]
        return pltpu.make_async_copy(src.at[layer], dst, r.loads.at[which])

    def start(layer, *which):
        for k in which:
            fetch(k, layer).start()

    def wait(layer, *which):
        for k in which:
            fetch(k, layer).wait()

    loaded = [
        load(r.g_in, r.g, r.loads.at[joined_ + 1]),
        load(r.keys_in.at[0], r.unit.at[0, :, :, :, pl.ds(0, KEYS)], r.loads.at[joined_ + 2]),
        load(r.keys_in.at[1], r.unit.at[SEND, :, :, :, pl.ds(0, KEYS)], r.loads.at[joined_ + 3]),
    ]
    start(TOP - 1, *range(joined_))
    pixels = load(r.images_in, r.images, r.loads.at[joined_ + 4])
    if cube:
        cube_barrier(plan)
        r.squares[...] = jnp.zeros_like(r.squares)
        top_rows = SmallGather(plan, r.rows_block, r.top_rows, r.rows_send, r.rows_recv)
    r.vectors[...] = jnp.zeros_like(r.vectors)
    r.vectors[FINAL : FINAL + 2] = r.tail_in[1:3]
    r.vectors[FINAL - 4 : FINAL] = r.tail_in[3:7]

    def run(unit, stage, by_rows, width=WIDTH):
        unit = Reduce(plan, r, unit, width)
        (
            unit.stage0,
            unit.stage1,
            unit.stage2,
            unit.stage3,
            unit.stage4,
            lambda: unit.stage5(by_rows),
            lambda: unit.stage6(by_rows),
        )[stage]()

    def point(it, at):
        if not cube:
            unit = 4 * it - 3 + at
            copies = [
                pltpu.make_async_copy(
                    r.unit.at[(unit % 4, SEND)[i]], r.full.at[unit, i], r.loads.at[joined_ + 1 + i]
                )
                for i in range(2)
            ]
            start_all(copies)
            wait_all(copies)
            return
        for stage in STAGE_ORDER:
            kind = (at - stage) % POINTS
            past = (kind + stage) // POINTS
            unit = 4 * (it - past) - 3 + kind
            go = functools.partial(run, unit, stage, kind == SHRINK, WIDTHS[kind])
            if past:
                pl.when(it > past)(go)
            else:
                go()
            if past and kind == TRIPLE:
                pl.when(it == past)(functools.partial(run, unit, stage, False, KEYS))

    def drain():
        for at in range(6):
            for stage in STAGE_ORDER:
                unit = UNITS + at - stage
                if UNITS - 2 * POINTS <= unit < UNITS:
                    kind = (unit - 1) % POINTS
                    run(jnp.int32(unit), stage, kind == SHRINK, WIDTHS[kind])
                if unit == UNITS:
                    run(jnp.int32(UNITS), stage, False, TAIL)

    def sent(unit, width=WIDTH):
        if cube:
            Reduce(plan, r, unit - 1, width).copy(0).wait_send()

    low_lane = lax.broadcasted_iota(jnp.int32, (PAD, 128), 1) < HEAD_DIM
    scale = HEAD_DIM**-0.5

    wait_all(loaded)
    if cube:
        run(jnp.int32(0), 0, False, KEYS)
        top_rows.stage0()
    else:
        copies = [
            pltpu.make_async_copy(r.unit.at[(0, SEND)[i]], r.full.at[0, i], r.loads.at[joined_ + 1 + i])
            for i in range(2)
        ]
        start_all(copies)
        wait_all(copies)

    @pl.loop(1, LAYERS)
    def _(it):
        layer = TOP - it
        below = it < TOP
        unit_s = 4 * it - 3
        base = S + 2 + 4 * layer
        r.gr[...] = r.g[...].astype(BF)
        wait(layer, z_)
        slot = unit_s % 4
        pl.when(it == 1)(lambda: sent(unit_s, KEYS))
        pl.when(it > 1)(lambda: sent(unit_s, WIDTHS[TRIPLE]))

        @pl.loop(0, 8)
        def _(j):
            cols = pl.ds(pl.multiple_of(j * (D // 2), 128), D // 2)
            store_rows(plan, r.unit, slot, j, dot(r.vm_z[:, cols], r.gr[...], TN))

        point(it, 0)
        if cube:
            pl.when(it == 1)(top_rows.stage1)
        wait(layer, shrink_, slope_, expand_, m_, h1_)
        pl.when(below)(lambda: start(layer - 1, z_))
        slot_e = (unit_s + 1) % 4
        r.g1[...] = jnp.zeros_like(r.g1)
        sent(unit_s + 1)

        @pl.loop(0, 4)
        def _(j):
            cols = pl.ds(pl.multiple_of(j * D, 128), D)
            dz = dot(r.gr[...], r.shrink_w[j].reshape(D, D), NT)
            du = (dz * r.vm_slope[:, cols].astype(F32)).astype(BF)
            r.vm_slope[:, cols] = du
            store_cols(plan, r.unit, slot_e, j, D, dot(r.vm_m[...], du, TN))

        pl.when(below)(lambda: start(layer - 1, shrink_, m_))
        point(it, 1)
        if cube:
            pl.when(it == 1)(top_rows.stage2)

        @pl.loop(0, 4)
        def _(j):
            cols = pl.ds(pl.multiple_of(j * D, 128), D)
            r.g1[...] += dot(r.vm_slope[:, cols], weight(r.expand_w, j * D, D), NT)

        start(layer, joined_)
        pl.when(below)(lambda: start(layer - 1, slope_))
        d_h1, d_gain, d_shift = normalize_back(r.vm_h1[...], row(r.params, base + 2), r.g1[...])
        r.g1[...] = r.g[...] + d_h1
        r.vectors[pl.ds(base + 2, 1)] = d_gain
        r.vectors[pl.ds(base + 3, 1)] = d_shift
        pl.when(below)(lambda: start(layer - 1, h1_))

        r.gr[...] = r.g1[...].astype(BF)
        slot_t = (unit_s + TRIPLE) % 4
        wait(layer, o_)
        sent(unit_s + 2)
        for part in range(2):
            half = D // 2
            value = dot(r.vm_o[...], r.gr[:, part * half : part * half + half], TN)
            store_cols(plan, r.unit, (unit_s + OUTPUT) % 4, part, half, value, half)
        wait(layer, joined_)
        r.do[...] = dot(r.gr[...], weight(r.expand_w, 3 * D, D), NT).astype(BF)
        wait(layer, t_, p_, a_, h_)

        def heads(step):
            image, pair = step // (HEADS // 2), step % (HEADS // 2)
            rows = pl.ds(pl.multiple_of(image * PAD, 16), PAD)
            lanes = [pl.ds(pl.multiple_of(pair * 128 + part * D, 128), 128) for part in range(3)]
            q, key, v = (r.vm_t[rows, lane] for lane in lanes)
            do = r.do[rows, lanes[0]]
            zero = jnp.zeros_like(v)
            dqs, dks, dvs = [], [], []
            for which in range(2):
                part = jnp.where(low_lane, v, zero) if which == 0 else jnp.where(low_lane, zero, v)
                p_low = r.vm_p[step * 2 + which]
                p = p_low.astype(F32)
                dvs.append(dot(p_low, do))
                dp = dot(part, do, NT)
                ds = (p * (dp - jnp.sum(p * dp, 0, keepdims=True))).astype(BF)
                dqs.append(dot(ds, key, TN))
                dks.append(dot(ds, q))
            r.dt[rows, lanes[0]] = (jnp.where(low_lane, dqs[0], dqs[1]) * scale).astype(BF)
            r.dt[rows, lanes[1]] = (jnp.where(low_lane, dks[0], dks[1]) * scale).astype(BF)
            r.dt[rows, lanes[2]] = jnp.where(low_lane, dvs[0], dvs[1]).astype(BF)

        half = images * (HEADS // 2) // 2
        pl.loop(0, half)(heads)
        point(it, 2)
        if cube:
            pl.when(it == 1)(top_rows.finish)
        pl.loop(half, 2 * half)(heads)
        pl.when(below)(lambda: start(layer - 1, o_, t_, p_))
        r.g[...] = jnp.zeros_like(r.g)

        sent(unit_s + TRIPLE, WIDTHS[OUTPUT])

        @pl.loop(0, 6)
        def _(j):
            cols = pl.ds(pl.multiple_of(j * (D // 2), 128), D // 2)
            value = dot(r.vm_a[...], r.dt[:, cols], TN)
            store_cols(plan, r.unit, slot_t, j, D // 2, value, WIDTHS[TRIPLE])

        point(it, 3)

        @pl.loop(0, 3)
        def _(j):
            cols = pl.ds(pl.multiple_of(j * D, 128), D)
            r.g[...] += dot(r.dt[:, cols], weight(r.expand_w, j * D, D), NT)

        d_h, d_gain, d_shift = normalize_back(r.vm_h[...], row(r.params, base), r.g[...])
        r.g[...] = r.g1[...] + d_h
        r.vectors[pl.ds(base, 1)] = d_gain
        r.vectors[pl.ds(base + 1, 1)] = d_shift
        pl.when(below)(lambda: start(layer - 1, a_, h_, expand_))

    pixels.wait()
    slot = UNITS % 4
    sent(jnp.int32(UNITS), WIDTHS[TRIPLE])
    for part in range(2):
        half = D // 2
        value = jnp.zeros((D, half), F32)
        for image in range(images):
            rows = r.g[image * PAD + 1 : image * PAD + S, part * half : (part + 1) * half]
            value = value + dot(r.images[image], rows.astype(BF), TN)
        store_cols(plan, r.unit, slot, part, half, value, half)
    pos = r.g[:PAD]
    for image in range(1, images):
        pos = pos + r.g[image * PAD : (image + 1) * PAD]
    r.vectors[:S] = pos[:S]
    r.vectors[S : S + 1] = pos[:1]
    r.vectors[S + 1 : S + 2] = jnp.sum(pos[1:S], 0, keepdims=True)
    if not cube:
        copies = [
            pltpu.make_async_copy(r.unit.at[(slot, SEND)[i]], r.full.at[UNITS, i], r.loads.at[i])
            for i in range(2)
        ]
        copies.append(pltpu.make_async_copy(r.vectors, r.vector_rows, r.loads.at[2]))
        start_all(copies)
        wait_all(copies)
        return
    store_vectors(plan, r.unit, slot, r.vectors[...])

    drain()
    r.tail_block[:BLOCK] = r.total[UNITS % 2, :, D // 2 : TAIL].astype(BF)
    line = lax.broadcasted_iota(jnp.int32, (16, 128), 0)
    terms = jnp.zeros((16, 128), F32)
    for k, rest in enumerate((jnp.full((16, 128), jnp.sum(r.squares[...]), F32), r.tail_in[0:1, 0:128])):
        for j in range(3):
            term = rest.astype(BF).astype(F32)
            rest = rest - term
            terms = jnp.where(line == 3 * k + j, term, terms)
    r.tail_block[BLOCK:] = terms.astype(BF)
    gather = SmallGather(plan, r.tail_block, r.vector_rows, r.tail_send, r.tail_recv)
    gather.stage0()
    gather.stage1()
    gather.stage2()
    run(jnp.int32(UNITS), 6, False, TAIL)
    Reduce(plan, r, jnp.int32(UNITS), TAIL).copy(0).wait_send()
    gather.finish()


def backward(plan, images, params, done):
    rows = images.shape[0] * PAD
    shapes = saved_shapes(rows)
    inputs = given_in(
        VMEM_SPEC,
        params=params,
        tail_in=done.tail,
        rows_block=done.rows_block,
    )
    block = rows_block(images.shape[0])
    inputs.update(
        given_in(
            ANY_SPEC,
            images_in=images,
            g_in=done.g,
            keys_in=done.keys_out,
            joined_whole=done.joined_whole,
            expand_whole=done.expand_whole,
            shrink_whole=done.shrink_whole,
        )
    )
    inputs.update({"keep_" + name: (getattr(done, "keep_" + name), ANY_SPEC) for name in SAVED})
    if plan.cube:
        outputs = dict(
            shrink_grad=((TOP, 2, HALF, WIDTH), F32, ANY_SPEC),
            expand_grad=((TOP, 2, HALF, WIDTH), F32, ANY_SPEC),
            output_grad=((TOP, 2, HALF, WIDTHS[OUTPUT]), F32, ANY_SPEC),
            triple_grad=((TOP, 2, HALF, WIDTHS[TRIPLE]), F32, ANY_SPEC),
            keys=((2, HALF, KEYS), F32, ANY_SPEC),
            patch=((2, HALF, D // 2), F32, ANY_SPEC),
            vector_rows=(CHIPS + (2, BLOCK + 16, 128), BF, ANY_SPEC),
            top_rows=(CHIPS + (2, block, 128), BF, ANY_SPEC),
        )
    else:
        outputs = dict(
            full=((UNITS + 1, 2, 4, 4, BLOCK, WIDTH), BF, ANY_SPEC),
            vector_rows=((VEC_ROWS, D), F32, ANY_SPEC),
        )
    scratch = {"vm_" + name: pltpu.VMEM(shape, kind) for name, (shape, kind) in shapes.items()}
    scratch.update(
        vmem(
            BF,
            expand_w=cols_shape(FF),
            shrink_w=ROWS_SHAPE,
            gr=(rows, D),
            do=(rows, D),
            dt=(rows, 3 * D),
            unit=(SEND + 1, 4, 4, BLOCK, WIDTH),
            images=images.shape,
        )
    )
    scratch.update(vmem(F32, g=(rows, D), g1=(rows, D), vectors=(VEC_ROWS, D)))
    scratch.update(dma(loads=(17,)))
    extra = {}
    if plan.cube:
        other = other_part(WIDTH)
        most = WIDTH - other
        scratch.update(
            vmem(
                BF,
                core=(4, 4, BLOCK, WIDTH),
                tail_block=(BLOCK + 16, 128),
                near=(3, 4, BLOCK, cut_of(most)),
                far=(3, 4, BLOCK, most - cut_of(most)),
                x=(3, 4, BLOCK, most),
                y=(3, 4, BLOCK, most),
                line=(3, 4, BLOCK, most),
                main_two=(3, 2, BLOCK, most),
                main_one=(4, 2, BLOCK, most),
                other_two=(3, 2, 4, BLOCK, other),
                other_one=(4, 2, 4, BLOCK, other),
                plane=(3, 4, BLOCK, other),
                other_near=(3, BLOCK, cut_of(other)),
                other_far=(3, BLOCK, other - cut_of(other)),
                other_x=(3, BLOCK, other),
                other_y=(3, BLOCK, other),
            )
        )
        scratch.update(
            vmem(F32, total=(2, BLOCK, WIDTH), squares=(8, WIDTH))
        )
        scratch.update(
            dma(send=(4, 20), recv=(4, 18), rows_send=(10,), rows_recv=(9,), tail_send=(10,), tail_recv=(9,))
        )
        scratch.update(credit=pltpu.SemaphoreType.REGULAR)
        extra = dict(collective_id=2, has_side_effects=True)
    return pallas(functools.partial(backward_kernel, plan), "backward", inputs, outputs, scratch, **extra)


PARAMS = ("patch", "triple", "output", "expand", "shrink", "vector", "head")
KINDS = ("w_", "m_", "s_")


def adam_update(master, moment, square, gradient, step_rate):
    moment_new = BETA_ONE * moment + (1.0 - BETA_ONE) * gradient
    square_new = BETA_TWO * square + (1.0 - BETA_TWO) * gradient * gradient
    moment_hat = moment_new * (1.0 / (1.0 - BETA_ONE**STEP_INDEX))
    square_hat = square_new * (1.0 / (1.0 - BETA_TWO**STEP_INDEX))
    master_new = master - step_rate * (
        moment_hat / (jnp.sqrt(square_hat) + ADAM_EPS) + DECAY * master
    )
    return (master_new, moment_new, square_new)


def class_matrices(ref, images, devices, stride):
    first, found = 0, []
    for columns in PIECES:
        count = columns // 128
        parts = [
            jnp.concatenate(
                [
                    ref[pl.ds(image * PER_IMAGE + first + j, devices, stride=stride), :]
                    for j in range(count)
                ],
                1,
            )
            for image in range(images)
        ]
        found.append(jnp.concatenate(parts, 0).astype(BF))
        first += count
    return found


def own_columns(value, first, count):
    at = lax.broadcasted_iota(jnp.int32, (value.shape[1], 128), 0)
    to = lax.broadcasted_iota(jnp.int32, (value.shape[1], 128), 1)
    chosen = jnp.where((at == to + first) & (to < count), 1.0, 0.0).astype(BF)
    return dot(value, chosen).astype(BF)


def update_kernel(plan, images, names, *refs):
    r = SimpleNamespace(**dict(zip(names, refs)))
    named = dict(zip(names, refs))
    groups = [
        [(named[kind + name], named["vm_" + kind + name], named["to_" + kind + name]) for kind in KINDS]
        for name in PARAMS
    ]
    patch, triple, output, expand, shrink, vector, head = range(7)

    def moves(group, back):
        return [
            pltpu.make_async_copy(*((buf, out) if back else (src, buf)), r.sems.at[3 * group + k])
            for k, (src, buf, out) in enumerate(groups[group])
        ]

    order = (head, shrink, expand, triple, output, patch, vector)
    for group in order:
        start_all(moves(group, False))

    tile = jnp.sum(r.tails[:, BLOCK:, :].astype(F32), 0)
    square_sum = tile[0:1, 0:1] + tile[1:2, 0:1] + tile[2:3, 0:1]
    loss = tile[3:4] + tile[4:5] + tile[5:6]
    r.rows_f[...] = r.top_rows[...].astype(F32)
    stride = r.top_rows.shape[0] // plan.n
    found = class_matrices(r.rows_f, images, plan.n, stride)
    features, d_logits, z, g, m, du, o, g1, a, dq = found
    r.features[...] = features
    r.d_logits[...] = d_logits
    alike = (dot(features, features, NT) + 1.0) * dot(d_logits, d_logits, NT)
    for left, right in ((z, g), (m, du), (o, g1), (a, dq)):
        alike = alike + dot(left, left, NT) * dot(right, right, NT)
    norm = jnp.sqrt(square_sum + jnp.sum(alike))
    me = plan.me()

    def top_grad(left, right, rows):
        return dot(own_columns(left, me * rows, rows), right, TN)[:rows]

    clip = CLIP / jnp.maximum(norm, CLIP)
    line = lax.broadcasted_iota(jnp.int32, (8, 128), 0)
    r.scalars[...] = jnp.where(line == 0, norm, jnp.where(line == 1, loss, r.total[...]))

    def step(group, at, gradient, rate):
        bufs = [buf for _, buf, _ in groups[group]]
        new = adam_update(*[buf[at] for buf in bufs], gradient * clip, rate)
        for buf, value in zip(bufs, new):
            buf[at] = value

    def finish(group):
        start_all(moves(group, True))

    every = slice(None)
    wait_all(moves(head, False))

    @pl.loop(0, D // 128)
    def _(j):
        rows = pl.ds(pl.multiple_of(j * 128, 128), 128)
        gradient = dot(r.features[:, rows], r.d_logits[...], TN)
        step(head, (rows, every), gradient[:, :CLASSES], RATE_MATRIX)

    bias = jnp.sum(d_logits.astype(F32), 0, keepdims=True)[:, :CLASSES]
    step(head, (slice(D, D + 1), every), bias, RATE_MATRIX)
    r.bias_grad[...] = bias * clip
    finish(head)
    wait_all(moves(shrink, False))

    step(shrink, (TOP, every, every), top_grad(z, g, BLOCK_FF), RATE_MATRIX)

    @pl.loop(0, TOP)
    def _(layer):
        at = TOP - 1 - layer
        for k in range(4):
            gradient = r.shrink_grad[at, k % 2, :, pl.ds(k // 2 * D, D)]
            step(shrink, (layer, pl.ds(k * HALF, HALF), every), gradient, RATE_MATRIX)

    finish(shrink)
    wait_all(moves(expand, False))

    step(expand, (TOP, every, every), top_grad(m, du, HALF), RATE_MATRIX)

    @pl.loop(0, TOP)
    def _(layer):
        at = TOP - 1 - layer
        for k in range(2):
            step(expand, (layer, every, pl.ds(k * WIDTH, WIDTH)), r.expand_grad[at, k], RATE_MATRIX)

    finish(expand)
    wait_all(moves(triple, False))
    wait_all(moves(output, False))

    step(output, (TOP, every, every), top_grad(o, g1, HALF), RATE_OUTPUT)
    step(triple, (TOP, every, pl.ds(0, D)), top_grad(a, dq, HALF), RATE_MATRIX)
    for k in range(2):
        step(triple, (TOP, every, pl.ds((k + 1) * D, D)), r.keys[k], RATE_MATRIX)

    @pl.loop(0, TOP)
    def _(layer):
        at = TOP - 1 - layer
        for k in range(2):
            width = WIDTHS[TRIPLE]
            step(triple, (layer, every, pl.ds(k * width, width)), r.triple_grad[at, k], RATE_MATRIX)
            width = WIDTHS[OUTPUT]
            step(output, (layer, every, pl.ds(k * width, width)), r.output_grad[at, k], RATE_OUTPUT)

    finish(triple)
    finish(output)
    wait_all(moves(patch, False))
    for k in range(2):
        step(patch, (every, pl.ds(k * (D // 2), D // 2)), r.patch_grad[k], RATE_MATRIX)
    finish(patch)
    count = groups[vector][0][0].shape[0]
    for d in range(-(-count // 8)):
        block = r.tails[d].astype(F32)
        for j in range(6):
            r.vector_grad[8 * d : 8 * d + 8, 128 * j : 128 * j + 128] = block[8 * j : 8 * j + 8]
    wait_all(moves(vector, False))
    step(vector, (every, every), r.vector_grad[:count], RATE_VECTOR)
    finish(vector)
    for group in order:
        wait_all(moves(group, True))


def update(plan, images, states, got, done):
    inputs, outputs, scratch = {}, {}, {}
    for name, state in zip(PARAMS, states):
        for kind, value in zip(KINDS, state):
            inputs[kind + name] = (value, ANY_SPEC)
            outputs["to_" + kind + name] = (value.shape, F32, ANY_SPEC)
            scratch["vm_" + kind + name] = pltpu.VMEM(value.shape, F32)
    inputs.update(
        given_in(
            VMEM_SPEC,
            total=done.total,
            tails=got.vector_rows.reshape(plan.n, BLOCK + 16, 128),
            top_rows=got.top_rows.reshape(-1, 128),
            shrink_grad=got.shrink_grad,
            expand_grad=got.expand_grad,
            output_grad=got.output_grad,
            triple_grad=got.triple_grad,
            patch_grad=got.patch,
            keys=got.keys,
        )
    )
    outputs.update(scalars=((8, 128), F32, VMEM_SPEC), bias_grad=((1, CLASSES), F32, VMEM_SPEC))
    scratch.update(vmem(BF, features=(plan.n * images, D), d_logits=(plan.n * images, 1024)))
    scratch.update(vmem(F32, vector_grad=(VEC_ROWS, D), rows_f=(plan.n * rows_block(images), 128)))
    scratch.update(dma(sems=(3 * len(PARAMS),)))
    new = pallas(functools.partial(update_kernel, plan, images), "update", inputs, outputs, scratch)
    states = [[getattr(new, "to_" + kind + name) for kind in KINDS] for name in PARAMS]
    return new.scalars[0, 0], new.scalars[1, 0], new.scalars[2, 0], states, new.bias_grad[0]


AXES = ("wide", "grp")


def update_whole(plan, images, states, got, done):
    full = got.full.reshape(UNITS + 1, 2, 16, BLOCK, WIDTH)
    layers = full[1:UNITS].reshape(TOP, 4, 2, 16, BLOCK, WIDTH)[::-1]

    def scattered(whole):
        axis = whole.ndim - 2
        return lax.psum_scatter(whole, AXES, scatter_dimension=axis, tiled=True).astype(F32)

    def from_cols(part):
        joined = jnp.concatenate([part[..., 0, :, :, :], part[..., 1, :, :, :]], -1)
        return joined.reshape(part.shape[:-4] + (D, -1))

    shrink = layers[:, 0].reshape(TOP, 2, 16, BLOCK, 2, D).transpose(0, 2, 1, 4, 3, 5)
    output = scattered(from_cols(layers[:, OUTPUT, ..., : WIDTHS[OUTPUT]]))
    triple = scattered(from_cols(layers[:, TRIPLE, ..., : WIDTHS[TRIPLE]]))
    rows_all = lax.all_gather(done.rows_block, AXES, axis=0)[:, : PER_IMAGE * images]
    rows_all = rows_all.reshape(plan.n * images, PER_IMAGE * 128)
    ends = [sum(PIECES[: k + 1]) for k in range(len(PIECES))]
    features, d_logits, z, g, m, du, o, g1, a, dq = jnp.split(rows_all, ends[:-1], axis=1)
    d_logits = d_logits[:, :CLASSES]
    bias = jnp.sum(d_logits.astype(F32), 0)[None]

    def top_grad(left, right):
        whole = dot(left, right, TN)
        count = whole.shape[0] // plan.n
        return lax.dynamic_slice_in_dim(whole, plan.me() * count, count)

    def with_top(below, top):
        return jnp.concatenate([below, top[None]], 0)

    keys = scattered(from_cols(full[0, ..., :KEYS]))
    split = [
        scattered(from_cols(full[UNITS, ..., : D // 2])),
        with_top(triple, jnp.concatenate([top_grad(a, dq), keys], 1)),
        with_top(output, top_grad(o, g1)),
        with_top(scattered(from_cols(layers[:, 1])), top_grad(m, du)),
        with_top(scattered(shrink.reshape(TOP, FF, D)), top_grad(z, g)),
    ]
    same = [
        lax.psum(got.vector_rows[: states[5][0].shape[0]], AXES),
        jnp.concatenate([dot(features, d_logits, TN), bias], 0),
    ]
    squares = lax.psum(sum(jnp.sum(g * g) for g in split), AXES) + sum(jnp.sum(g * g) for g in same)
    norm = jnp.sqrt(squares)
    clip = CLIP / jnp.maximum(norm, CLIP)
    rates = [RATE_MATRIX] * 2 + [RATE_OUTPUT] + [RATE_MATRIX] * 2 + [RATE_VECTOR, RATE_MATRIX]
    states = [
        adam_update(*state, gradient * clip, rate)
        for state, gradient, rate in zip(states, split + same, rates)
    ]
    return norm, lax.psum(done.tail[0, 0], AXES), done.total[0, 0], states, bias[0] * clip


def per_device(plan, images, slot_mask, labels, *params):
    states = [params[3 * k : 3 * k + 3] for k in range(7)]
    patch, triple, output, expand, shrink, vector, head = (state[0] for state in states)
    count = images.shape[0]
    weights = slot_mask.astype(F32)
    args = dict(vectors=vector, head=head)
    scalars = dict(labels=labels, mask=slot_mask)
    if plan.cube:
        shards = dict(patch=patch, triple=triple, output=output, expand=expand, shrink=shrink)
        done = forward(plan, images, shards, args, scalars, None, None)
    else:

        def whole(shard, shape):
            axis = shard.ndim - 2
            gathered = lax.all_gather(shard.astype(BF), AXES, axis=axis, tiled=True)
            return gathered.reshape(shard.shape[:axis] + shape)

        gathered = [
            whole(patch, cols_shape(D)),
            whole(jnp.concatenate([triple, output], 2), cols_shape(FF)),
            whole(expand, cols_shape(FF)),
            whole(shrink, ROWS_SHAPE),
        ]
        total = jnp.full((8, 128), lax.psum(jnp.sum(weights), AXES), F32)
        done = forward(plan, images, None, args, scalars, gathered, total)
    got = backward(plan, images, vector, done)
    if plan.cube:
        norm, loss, total, states, bias_grad = update(plan, count, states, got, done)
    else:
        norm, loss, total, states, bias_grad = update_whole(plan, count, states, got, done)
    return (
        loss,
        total,
        norm,
        *(value for state in states for value in state),
        bias_grad,
    )


def solution(mesh):
    plan = Plan(mesh)
    rows = P(AXES, None)
    layers = P(None, AXES, None)
    in_specs = (P(AXES, None, None), P(AXES), P(AXES)) + (rows,) * 3 + (layers,) * 12 + (P(),) * 6
    out_specs = (P(),) * 3 + (rows,) * 3 + (layers,) * 12 + (P(),) * 7
    return jax.shard_map(
        functools.partial(per_device, plan),
        mesh=mesh,
        in_specs=in_specs,
        out_specs=out_specs,
        check_vma=False,
    )
```

```python
import functools
from types import SimpleNamespace

import jax
import jax.numpy as jnp
from jax import lax
from jax.experimental import pallas as pl
from jax.experimental.pallas import tpu as pltpu
from jax.sharding import PartitionSpec as P

D = 768
HEADS = 12
HEAD_DIM = 64
FF = 3072
CLASSES = 1000
LAYERS = 3
STEP_INDEX = 10
S = 197
PAD = 208

EPS_NORM = 1e-06
CLIP = 0.1
BETA_ONE = 0.9
BETA_TWO = 0.95
ADAM_EPS = 1e-08
DECAY = 0.05
RATE_MATRIX = 0.03
RATE_OUTPUT = 0.2
RATE_VECTOR = 0.3
SMOOTH = 0.1

F32 = jnp.float32
BF = jnp.bfloat16
NN = (((1,), (0,)), ((), ()))
NT = (((1,), (1,)), ((), ()))
TN = (((0,), (0,)), ((), ()))
VMEM_SPEC = pl.BlockSpec(memory_space=pltpu.VMEM)
ANY_SPEC = pl.BlockSpec(memory_space=pl.ANY)
LIMIT = 62 * 1024 * 1024


def dot(left, right, form=NN):
    return lax.dot_general(left, right, form, preferred_element_type=F32)


def normalize(values, gain_row, shift_row):
    center = values - jnp.mean(values, -1, keepdims=True)
    spread = jnp.mean(center * center, -1, keepdims=True)
    return center * lax.rsqrt(spread + EPS_NORM) * gain_row + shift_row


def normalize_back(values, gain_row, grad):
    center = values - jnp.mean(values, -1, keepdims=True)
    spread = jnp.mean(center * center, -1, keepdims=True)
    scale = lax.rsqrt(spread + EPS_NORM)
    unit = center * scale
    d_unit = grad * gain_row
    d_values = scale * (
        d_unit
        - jnp.mean(d_unit, -1, keepdims=True)
        - unit * jnp.mean(d_unit * unit, -1, keepdims=True)
    )
    return (
        d_values,
        jnp.sum(grad * unit, 0, keepdims=True),
        jnp.sum(grad, 0, keepdims=True),
    )


def gelu_and_slope(u):
    x = jnp.abs(u) * 0.7071067811865476
    t = 1.0 / (1.0 + 0.3275911 * x)
    series = t * (
        0.254829592
        + t * (-0.284496736 + t * (1.421413741 + t * (-1.453152027 + t * 1.061405429)))
    )
    bell = jnp.exp(-0.5 * u * u)
    tail = 0.5 * series * bell
    share = jnp.where(u >= 0.0, 1.0 - tail, tail)
    return u * share, share + u * bell * 0.3989422804014327


class Plan:
    def __init__(self, mesh):
        self.wide, self.grp = mesh.shape["wide"], mesh.shape["grp"]
        self.n = self.wide * self.grp
        self.cube = self.wide == 8 and self.grp == 4

    def me(self):
        return lax.axis_index("wide") * self.grp + lax.axis_index("grp")

    def where(self):
        if not self.cube:
            return 0, 0, 0, 0
        wide, grp = lax.axis_index("wide"), lax.axis_index("grp")
        return wide // 2, wide % 2, grp // 2, grp % 2


CHIPS = (4, 2, 2)
BLOCK = D // 16
BLOCK_FF = FF // 32


def cols_shape(columns):
    return CHIPS + (BLOCK, columns)


ROWS_SHAPE = CHIPS + (2, BLOCK_FF, D)


def other_part(width):
    return width * 2 // 9 // 128 * 128


def cut_of(columns):
    return columns // 2 // 128 * 128


def over_links(plan):
    z, x, y, c = plan.where()

    def at(z, x, y, c):
        return (z * 2 + x, y * 2 + c)

    return SimpleNamespace(
        z1=at(jnp.bitwise_xor(z, 1), x, y, c),
        z3=at(jnp.bitwise_xor(z, 3), x, y, c),
        x=at(z, 1 - x, y, c),
        y=at(z, x, 1 - y, c),
        core=at(z, x, y, 1 - c),
    )


def remote(src, dst, send, recv, to):
    return pltpu.make_async_remote_copy(
        src_ref=src,
        dst_ref=dst,
        send_sem=send,
        recv_sem=recv,
        device_id=to,
        device_id_type=pl.DeviceIdType.MESH,
    )


class Gather:
    def __init__(self, plan, by_cols, block, whole, send, recv):
        self.z, self.x, self.y, self.c = plan.where()
        self.to = over_links(plan)
        self.by_cols, self.block, self.whole = by_cols, block, whole
        self.send, self.recv = send, recv
        self.width = block.shape[-1]
        self.other = other_part(self.width)
        self.most = self.width - self.other
        self.cut = (self.most // 2 + 127) // 128 * 128

    def region(self, z, x, y, start, width):
        if self.by_cols:
            first = pl.multiple_of(self.c * self.width + start, 128)
            return self.whole.at[z, x, y, :, pl.ds(first, width)]
        return self.whole.at[z, x, y, self.c, :, pl.ds(start, width)]

    def part(self, start, width):
        return self.block.at[:, pl.ds(start, width)]

    def copy(self, at):
        z, x, y, to = self.z, self.x, self.y, self.to
        z1, z3, line = jnp.bitwise_xor(z, 1), jnp.bitwise_xor(z, 3), slice(None)
        most, other, region = self.most, self.other, self.region
        cut, cut_other = self.cut, most + max(cut_of(other), 128)
        landed = at
        if at in (0, 1):
            src, dst = self.part(0, most), region(z, x, y, 0, most)
            device = (to.z1, to.z3)[at]
        elif at in (8, 9):
            src, dst = self.part(most, other), region(z, x, y, most, other)
            device = (to.x, to.y)[at - 8]
        else:
            src, device = {
                2: lambda: (region(z3, x, y, 0, most), to.z1),
                3: lambda: (region(z1, x, y, 0, most), to.z3),
                4: lambda: (region(line, x, y, 0, most), to.x),
                5: lambda: (region(line, x, y, 0, most), to.y),
                6: lambda: (region(line, x, 1 - y, 0, cut), to.x),
                7: lambda: (region(line, 1 - x, y, cut, most - cut), to.y),
                10: lambda: (region(z, x, 1 - y, most, cut_other - most), to.x),
                11: lambda: (region(z, 1 - x, y, cut_other, self.width - cut_other), to.y),
                12: lambda: (region(z, line, line, most, other), to.z1),
                13: lambda: (region(z, line, line, most, other), to.z3),
                14: lambda: (region(z3, line, line, most, other), to.z1),
                15: lambda: (region(z1, line, line, most, other), to.z3),
                16: lambda: (region(line, x, y, 0, most), to.core),
                17: lambda: (region(line, 1 - x, y, 0, most), to.core),
                18: lambda: (region(line, x, 1 - y, 0, most), to.core),
                19: lambda: (region(line, 1 - x, 1 - y, 0, cut), to.core),
                20: lambda: (region(line, 1 - x, 1 - y, cut, most - cut), to.core),
                21: lambda: (region(line, line, line, most, other), to.core),
            }[at]()
            dst = src
            if at in (3, 15):
                landed = at - 1
        return remote(src, dst, self.send.at[at], self.recv.at[landed], device)

    def exists(self, at):
        if at in (8, 9, 10, 12, 13, 14, 15, 21):
            return self.other > 0
        return at != 11 or self.other > 128

    def keep(self):
        here = self.region(self.z, self.x, self.y, 0, self.width)
        return pltpu.make_async_copy(self.block, here, self.send.at[22])

    def start(self, *which):
        for at in which:
            if self.exists(at):
                self.copy(at).start()

    def arrived(self, *which):
        for at in which:
            if self.exists(at):
                self.copy(at).wait_recv()

    def in_middle(self, do):
        pl.when((self.z == 1) | (self.z == 2))(do)

    def stage0(self):
        self.start(0, 1, 8, 9)
        self.keep().start()

    def stage1(self):
        self.arrived(0, 1)
        self.in_middle(lambda: self.start(2, 3))
        self.arrived(8, 9)
        self.start(10, 11)
        self.keep().wait()

    def stage2(self):
        self.arrived(2)
        self.start(4, 5, 16)
        self.arrived(10, 11)
        self.start(12, 13)

    def stage3(self):
        self.arrived(4, 5)
        self.start(6, 7, 17, 18)
        self.arrived(12, 13)
        self.in_middle(lambda: self.start(14, 15))

    def stage4(self):
        self.arrived(6, 7)
        self.start(19, 20)
        self.arrived(14)
        self.start(21)

    def finish(self):
        self.arrived(16, 17, 18, 19, 20, 21)
        passed = (2, 3, 14, 15)

        def sent(which):
            for at in which:
                if self.exists(at):
                    self.copy(at).wait_send()

        sent([at for at in range(22) if at not in passed])
        self.in_middle(lambda: sent(passed))


def cube_barrier(plan):
    z, x, y, c = plan.where()
    barrier = pltpu.get_barrier_semaphore()
    partners = [(jnp.bitwise_xor(z * 2 + x, k), y * 2 + c) for k in range(1, 8)]
    partners += [(z * 2 + x, (1 - y) * 2 + c), (z * 2 + x, y * 2 + 1 - c)]
    for partner in partners:
        pl.semaphore_signal(barrier, inc=1, device_id=partner, device_id_type=pl.DeviceIdType.MESH)
    pl.semaphore_wait(barrier, len(partners))


def load(source, target, sem):
    copy = pltpu.make_async_copy(source, target, sem)
    copy.start()
    return copy


def start_all(copies):
    for copy in copies:
        copy.start()


def wait_all(copies):
    for copy in copies:
        copy.wait()


def weight(ref, first, width):
    cols = pl.ds(first if isinstance(first, int) else pl.multiple_of(first, 128), width)
    return ref[:, :, :, :, cols].reshape(D, width)


class SmallGather:
    def __init__(self, plan, block, whole, send, recv):
        self.z, self.x, self.y, self.c = plan.where()
        self.to = over_links(plan)
        self.block, self.whole, self.send, self.recv = block, whole, send, recv

    def copy(self, at):
        z, x, y, c = self.z, self.x, self.y, self.c
        line = slice(None)
        if at < 7:
            src, dst = self.block, self.whole.at[z, x, y, c]
            device = (jnp.bitwise_xor(z * 2 + x, at + 1), y * 2 + c)
        elif at == 7:
            src = dst = self.whole.at[line, line, y, c]
            device = self.to.y
        else:
            src = dst = self.whole.at[line, line, line, c]
            device = self.to.core
        return remote(src, dst, self.send.at[at], self.recv.at[at], device)

    def keep(self):
        here = self.whole.at[self.z, self.x, self.y, self.c]
        return pltpu.make_async_copy(self.block, here, self.send.at[9])

    def stage0(self):
        for at in range(7):
            self.copy(at).start()
        self.keep().start()

    def stage1(self):
        for at in range(7):
            self.copy(at).wait_recv()
        self.keep().wait()
        self.copy(7).start()

    def stage2(self):
        self.copy(7).wait_recv()
        self.copy(8).start()

    def finish(self):
        self.copy(8).wait_recv()
        for at in range(9):
            self.copy(at).wait_send()


FF_TILE = 512
HALF = BLOCK // 2
WIDTH = FF // 2
HEAD_ROWS = 16
FINAL = S + 2 + 4 * LAYERS
TOP = LAYERS - 1
CLASS_PAD = 1024

Z_, M_, O_, Q_, A_ = (slice(0, FF),) + tuple(slice(FF + k * D, FF + k * D + D) for k in range(4))
FEATURE_, LOGIT_ = slice(FF + 4 * D, FF + 5 * D), slice(FF + 5 * D, FF + 5 * D + CLASS_PAD)
SLOPE_, H1_, G_ = slice(0, FF), slice(FF, FF + D), slice(FF + D, FF + 2 * D)
PIECES = (D, CLASS_PAD, FF, D, D, FF, D, D, D, D)
PER_IMAGE = sum(PIECES) // 128


def rows_block(images):
    return -(-PER_IMAGE * images // 16) * 16


def class_rows(ref, source):
    ref[...] = jnp.zeros_like(ref)
    for image in range(source.shape[0] // PAD):
        ref[image : image + 1] = source[image * PAD : image * PAD + 1]


def by_head(rows, image):
    head = lax.broadcasted_iota(jnp.int32, (16, D), 0)
    lane = lax.broadcasted_iota(jnp.int32, (16, D), 1)
    mine = (lane >= head * HEAD_DIM) & (lane < head * HEAD_DIM + HEAD_DIM)
    return mine, jnp.where(mine, rows[image : image + 1], 0.0)


def saved_shapes(rows):
    heads = rows // PAD * HEADS
    return dict(
        h=((rows, D), F32),
        a=((rows, D), BF),
        t=((rows, 3 * D), BF),
        o=((rows, D), BF),
        p=((heads, PAD, PAD), BF),
        h1=((rows, D), F32),
        m=((rows, D), BF),
        z=((rows, FF), BF),
        slope=((rows, FF), BF),
    )


SAVED = tuple(saved_shapes(PAD))


def row(ref, at):
    return ref[pl.ds(at, 1)]


def share_shards(plan, r):
    z, x, y, c = plan.where()
    r.joined_f[:, :, : 3 * D] = r.triple[...]
    r.joined_f[:, :, 3 * D :] = r.output[...]
    mine = pl.ds(pl.multiple_of(c * HALF, 8), HALF)

    def part(core, width):
        return pl.ds(pl.multiple_of(core * width, 128), width)

    moves = [
        (r.patch.at[:, part(1 - c, D // 2)], r.patch_f.at[mine]),
        (r.joined_f.at[:, :, part(1 - c, WIDTH)], r.joined_b.at[:, mine]),
        (r.expand.at[:, :, part(1 - c, WIDTH)], r.expand_b.at[:, mine]),
    ]
    copies = [
        pltpu.make_async_remote_copy(
            src_ref=src,
            dst_ref=dst,
            send_sem=r.share_send.at[i],
            recv_sem=r.share_recv.at[i],
            device_id=(z * 2 + x, y * 2 + 1 - c),
            device_id_type=pl.DeviceIdType.MESH,
        )
        for i, (src, dst) in enumerate(moves)
    ]
    start_all(copies)
    r.patch_f[mine] = r.patch[:, part(c, D // 2)]
    r.joined_b[:, mine] = r.joined_f[:, :, part(c, WIDTH)]
    r.expand_b[:, mine] = r.expand[:, :, part(c, WIDTH)]
    targets = (
        (r.patch_f, r.patch_block),
        (r.joined_b, r.joined_block),
        (r.expand_b, r.expand_block),
    )

    def arrive(which):
        src, dst = targets[which]
        copies[which].wait_recv()
        dst[...] = src[...].astype(BF)
        copies[which].wait_send()

    return arrive


def class_column(ref, kind):
    line = lax.broadcasted_iota(jnp.int32, (HEAD_ROWS, 1), 0)
    column = jnp.zeros((HEAD_ROWS, 1), kind)
    for image in range(ref.shape[0]):
        column = jnp.where(line == image, ref[image].astype(kind), column)
    return column


def head_part(r, first, image_total):
    table = r.table[...]
    gain, shift = r.vectors[FINAL : FINAL + 1], r.vectors[FINAL + 1 : FINAL + 2]
    feature = normalize(first, gain, shift).astype(BF)
    logits = dot(feature, table) + r.head[D : D + 1]
    ids = lax.broadcasted_iota(jnp.int32, logits.shape, 1)
    shifted = logits - jnp.max(logits, -1, keepdims=True)
    log_prob = shifted - jnp.log(jnp.sum(jnp.exp(shifted), -1, keepdims=True))
    target = jnp.where(ids == class_column(r.labels, jnp.int32), 1.0 - SMOOTH, 0.0) + SMOOTH / CLASSES
    weights = class_column(r.mask, F32)
    loss = jnp.sum(weights * -jnp.sum(target * log_prob, -1, keepdims=True))
    d_logits = ((weights / image_total) * (jnp.exp(log_prob) - target)).astype(BF)
    d_feature = dot(d_logits, table, NT)
    r.d_logits[...] = jnp.zeros_like(r.d_logits)
    r.d_logits[:, :CLASSES] = d_logits.astype(F32)
    r.top_b[:, FEATURE_] = feature
    r.top_b[:, LOGIT_] = r.d_logits[...].astype(BF)
    d_first, d_gain, d_shift = normalize_back(first, gain, d_feature)
    r.top_f[:, G_] = d_first
    r.tail[...] = jnp.zeros_like(r.tail)
    r.tail[0:1] = jnp.full((1, D), loss, F32)
    r.tail[1:2] = d_gain
    r.tail[2:3] = d_shift


def pack_rows(r, kind, *sources):
    first = sum(PIECES[:kind]) // 128
    for source in sources:
        value = source.astype(F32)
        for j in range(value.shape[1] // 128):
            for image in range(r.images.shape[0]):
                at = image * PER_IMAGE + first + j
                r.rows_f[at : at + 1] = value[image : image + 1, j * 128 : j * 128 + 128]
        first += value.shape[1] // 128


def top_backward(plan, r):
    images = r.images.shape[0]
    base = S + 2 + 4 * TOP
    g = r.top_f[:, G_]
    g_low = g.astype(BF)
    for j in range(4):
        cols = slice(j * D, j * D + D)
        dz = dot(g_low, r.shrink_w[j].reshape(D, D), NT)
        r.top_du[:, cols] = (dz * r.top_f[:, cols]).astype(BF)
    d_m = jnp.zeros((HEAD_ROWS, D), F32)
    for j in range(4):
        d_m = d_m + dot(r.top_du[:, j * D : j * D + D], weight(r.expand_w, j * D, D), NT)
    d_h1, d_gain, d_shift = normalize_back(r.top_f[:, H1_], row(r.vectors, base + 2), d_m)
    r.tail[5:6] = d_gain
    r.tail[6:7] = d_shift
    g1 = g + d_h1
    g1_low = g1.astype(BF)
    d_o = dot(g1_low, weight(r.joined_w, 3 * D, D), NT).astype(BF).astype(F32)
    query = r.top_b[:, Q_].astype(F32)
    r.class_row[...] = jnp.zeros_like(r.class_row)
    for image in range(images):
        rows = slice(image * PAD, image * PAD + PAD)
        mine, spread_o = by_head(d_o, image)
        _, spread_q = by_head(query, image)
        spread_o, spread_q = spread_o.astype(BF), spread_q.astype(BF)
        p_low = r.top_p[image]
        p = p_low.astype(F32)
        r.d_keys[rows, D:] = dot(p_low, spread_o).astype(BF)
        dp = dot(r.t[rows, 2 * D :], spread_o, NT)
        ds = (p * (dp - jnp.sum(p * dp, 0, keepdims=True))).astype(BF)
        r.d_keys[rows, :D] = (dot(ds, spread_q) * HEAD_DIM**-0.5).astype(BF)
        d_q = jnp.where(mine, dot(ds, r.t[rows, D : 2 * D], TN), 0.0)
        r.class_row[image : image + 1] = jnp.sum(d_q, 0, keepdims=True) * HEAD_DIM**-0.5
    for part in range(2):
        value = dot(r.a[...], r.d_keys[:, part * D : part * D + D], TN)
        store_cols(plan, r.keys_block, 0, part, D, value, D, 1)
    keys = load(r.keys_block, r.keys_out, r.loads.at[0])
    d_q = r.class_row[...].astype(BF)
    r.g[...] = dot(r.d_keys[:, :D], weight(r.joined_w, D, D), NT)
    r.g[...] += dot(r.d_keys[:, D:], weight(r.joined_w, 2 * D, D), NT)
    d_a = dot(d_q, weight(r.joined_w, 0, D), NT)
    for image in range(images):
        r.g[image * PAD : image * PAD + 1] += d_a[image : image + 1]
    d_h, d_gain, d_shift = normalize_back(r.h[...], row(r.vectors, base), r.g[...])
    r.g[...] = d_h
    for image in range(images):
        r.g[image * PAD : image * PAD + 1] += g1[image : image + 1]
    r.tail[3:4] = d_gain
    r.tail[4:5] = d_shift
    pack_rows(r, 0, r.top_b[:, FEATURE_], r.top_b[:, LOGIT_])
    pack_rows(r, 3, g_low)
    pack_rows(r, 5, r.top_du[...])
    pack_rows(r, 7, g1_low)
    pack_rows(r, 9, d_q)
    r.rows_block[...] = r.rows_f[...].astype(BF)
    keys.wait()


def forward_kernel(plan, names, *refs):
    r = SimpleNamespace(**dict(zip(names, refs)))
    cube = plan.cube
    images = r.images.shape[0]
    patch, joined, expand, shrink = range(4)
    pixels = load(r.images_in, r.images, r.loads.at[4])
    wholes = (r.patch_whole, r.joined_whole, r.expand_whole, r.shrink_whole)
    weights = (r.patch_w, r.joined_w, r.expand_w, r.shrink_w)
    if cube:
        blocks = (r.patch_block, r.joined_block, r.expand_block, r.shrink_block)
        cube_barrier(plan)
        r.shrink_block[...] = r.shrink[...].astype(BF)
        arrive = share_shards(plan, r)
        r.count[...] = jnp.full((8, 128), jnp.sum(class_column(r.mask, F32)), F32)
        counting = SmallGather(plan, r.count, r.counts, r.count_send, r.count_recv)

    def unit(kind, layer):
        if kind == patch:
            return Gather(plan, True, blocks[0], wholes[0], r.send.at[0], r.recv.at[0])
        at = 3 * layer + kind
        block, whole = blocks[kind].at[layer], wholes[kind].at[layer]
        return Gather(plan, kind != shrink, block, whole, r.send.at[at], r.recv.at[at])

    def ready(kind, layer):
        if cube:
            unit(kind, layer).finish()
        whole = wholes[kind] if kind == patch else wholes[kind].at[layer]
        return load(whole, weights[kind], r.loads.at[kind])

    held = (r.h, r.a, r.t, r.o, r.p, r.h1, r.m, r.z, r.slope)
    kept = (r.keep_h, r.keep_a, r.keep_t, r.keep_o, r.keep_p, r.keep_h1, r.keep_m, r.keep_z, r.keep_slope)
    h_, a_, t_, o_, p_, h1_, m_, z_, slope_ = range(9)

    def saves(layer, *which):
        return [pltpu.make_async_copy(held[k], kept[k].at[layer], r.saves.at[k]) for k in which]

    if cube:
        first = [unit(patch, 0), unit(joined, 0), unit(expand, 0), unit(shrink, 0), unit(joined, 1)]
        arrive(0)
        first[0].stage0()
        counting.stage0()
        arrive(1)
        first[1].stage0()
        first[0].stage1()
        arrive(2)
        first[2].stage0()
        first[1].stage1()
        first[0].stage2()
        first[3].stage0()
        first[2].stage1()
        first[1].stage2()
        first[0].stage3()
        first[4].stage0()
        first[3].stage1()
        first[2].stage2()
        first[1].stage3()
        first[0].stage4()
    ready(patch, 0).wait()
    pixels.wait()
    classifier = load(r.head_in, r.head, r.loads.at[5])
    for image in range(images):
        at = image * PAD
        r.h[at : at + 1] = r.vectors[0:1] + r.vectors[S : S + 1]
        embedded = dot(r.images[image], weight(r.patch_w, 0, D))
        r.h[at + 1 : at + S] = embedded + r.vectors[S + 1 : S + 2] + r.vectors[1:S]
        r.h[at + S : at + PAD] = jnp.zeros((PAD - S, D), F32)

    low_lane = lax.broadcasted_iota(jnp.int32, (PAD, 128), 1) < HEAD_DIM
    real_key = lax.broadcasted_iota(jnp.int32, (PAD, PAD), 0) < S

    @pl.loop(0, TOP)
    def _(layer):
        base = S + 2 + 4 * layer
        if cube:
            unit(expand, layer + 1).stage0()
            unit(joined, layer + 1).stage1()
            unit(shrink, layer).stage2()
            unit(expand, layer).stage3()
            unit(joined, layer).stage4()
        start_all(saves(layer, h_))

        @pl.when(layer > 0)
        def _():
            wait_all(saves(layer, a_, t_, o_, p_, h1_, m_))

        r.a[...] = normalize(r.h[...], row(r.vectors, base), row(r.vectors, base + 1)).astype(BF)
        ready(joined, layer).wait()

        @pl.loop(0, 3)
        def _(j):
            cols = pl.ds(pl.multiple_of(j * D, 128), D)
            r.t[:, cols] = dot(r.a[...], weight(r.joined_w, j * D, D)).astype(BF)

        start_all(saves(layer, a_, t_))

        def heads(step):
            image, pair = step // (HEADS // 2), step % (HEADS // 2)
            rows = pl.ds(pl.multiple_of(image * PAD, 16), PAD)
            lanes = [pl.ds(pl.multiple_of(pair * 128 + part * D, 128), 128) for part in range(3)]
            q, key, v = (r.t[rows, lane] for lane in lanes)
            zero = jnp.zeros_like(key)
            outs = []
            for which in range(2):
                part = jnp.where(low_lane, key, zero) if which == 0 else jnp.where(low_lane, zero, key)
                scores = dot(part, q, NT) * HEAD_DIM**-0.5
                scores = jnp.where(real_key, scores, -1e30)
                top = jnp.max(scores, 0, keepdims=True)
                e = jnp.exp(scores - top)
                p = (e * (1.0 / jnp.sum(e, 0, keepdims=True))).astype(BF)
                r.p[step * 2 + which] = p
                outs.append(dot(p, v, TN))
            r.o[rows, lanes[0]] = jnp.where(low_lane, outs[0], outs[1]).astype(BF)

        half = images * (HEADS // 2) // 2
        pl.loop(0, half, unroll=2)(heads)
        if cube:
            unit(shrink, layer + 1).stage0()
            unit(expand, layer + 1).stage1()
            unit(joined, layer + 1).stage2()

        pl.loop(half, 2 * half, unroll=2)(heads)
        start_all(saves(layer, o_, p_))
        r.h1[...] = r.h[...] + dot(r.o[...], weight(r.joined_w, 3 * D, D))
        start_all(saves(layer, h1_))
        if cube:
            unit(shrink, layer).stage3()
            unit(expand, layer).stage4()
            pl.when(layer == 0)(counting.stage1)
            pl.when(layer == 1)(counting.finish)
        r.m[...] = normalize(r.h1[...], row(r.vectors, base + 2), row(r.vectors, base + 3)).astype(BF)
        start_all(saves(layer, m_))
        wait_all(saves(layer, h_))
        r.h[...] = r.h1[...]

        @pl.when(layer > 0)
        def _():
            wait_all(saves(layer, z_, slope_))

        ready(expand, layer).wait()

        @pl.loop(0, FF // FF_TILE)
        def _(j):
            cols = pl.ds(pl.multiple_of(j * FF_TILE, 128), FF_TILE)
            u = dot(r.m[...], weight(r.expand_w, j * FF_TILE, FF_TILE))
            z, slope = gelu_and_slope(u)
            r.z[:, cols] = z.astype(BF)
            r.slope[:, cols] = slope.astype(BF)

        start_all(saves(layer, z_, slope_))
        if cube:
            pl.when(layer < TOP - 1)(lambda: unit(joined, layer + 2).stage0())

            unit(shrink, layer + 1).stage1()
            unit(expand, layer + 1).stage2()
            unit(joined, layer + 1).stage3()
            unit(shrink, layer).stage4()
            pl.when(layer == 0)(counting.stage2)
        ready(shrink, layer).wait()

        @pl.loop(0, 4)
        def _(j):
            cols = pl.ds(pl.multiple_of(j * D, 128), D)
            r.h[...] += dot(r.z[:, cols], r.shrink_w[j].reshape(D, D))

    base = S + 2 + 4 * TOP
    if cube:
        unit(shrink, TOP).stage2()
        unit(expand, TOP).stage3()
        unit(joined, TOP).stage4()
    start_all(saves(TOP, h_))
    wait_all(saves(TOP, a_, t_) + saves(0, o_, p_, h1_, m_))
    r.a[...] = normalize(r.h[...], row(r.vectors, base), row(r.vectors, base + 1)).astype(BF)
    class_rows(r.first, r.h)
    first = r.first[...]
    r.top_b[:, A_] = normalize(first, row(r.vectors, base), row(r.vectors, base + 1)).astype(BF)
    ready(joined, TOP).wait()
    for j in (1, 2):
        r.t[:, j * D : j * D + D] = dot(r.a[...], weight(r.joined_w, j * D, D)).astype(BF)
    start_all(saves(TOP, a_, t_))
    query = dot(r.top_b[:, A_], weight(r.joined_w, 0, D)).astype(BF)
    r.top_b[:, Q_] = query
    if cube:
        unit(shrink, TOP).stage3()
        unit(expand, TOP).stage4()
    query = query.astype(F32)
    real = lax.broadcasted_iota(jnp.int32, (PAD, 16), 0) < S
    r.class_row[...] = jnp.zeros_like(r.class_row)
    for image in range(images):
        rows = slice(image * PAD, image * PAD + PAD)
        mine, spread = by_head(query, image)
        scores = dot(r.t[rows, D : 2 * D], spread.astype(BF), NT) * HEAD_DIM**-0.5
        scores = jnp.where(real, scores, -1e30)
        e = jnp.exp(scores - jnp.max(scores, 0, keepdims=True))
        p = (e * (1.0 / jnp.sum(e, 0, keepdims=True))).astype(BF)
        r.top_p[image] = p
        out = jnp.where(mine, dot(p, r.t[rows, 2 * D :], TN), 0.0)
        r.class_row[image : image + 1] = jnp.sum(out, 0, keepdims=True)
    attended = r.class_row[...].astype(BF)
    r.top_b[:, O_] = attended
    h1 = first + dot(attended, weight(r.joined_w, 3 * D, D))
    r.top_f[:, H1_] = h1
    r.top_b[:, M_] = normalize(h1, row(r.vectors, base + 2), row(r.vectors, base + 3)).astype(BF)
    ready(expand, TOP).wait()
    for j in range(4):
        cols = slice(j * D, j * D + D)
        z, slope = gelu_and_slope(dot(r.top_b[:, M_], weight(r.expand_w, j * D, D)))
        r.top_b[:, cols] = z.astype(BF)
        r.top_f[:, cols] = slope
    if cube:
        unit(shrink, TOP).stage4()
    classifier.wait()
    r.table[...] = r.head[:D].astype(BF)
    r.rows_f[...] = jnp.zeros_like(r.rows_f)
    pack_rows(r, 2, r.top_b[:, Z_])
    pack_rows(r, 4, r.top_b[:, M_])
    pack_rows(r, 6, r.top_b[:, O_])
    pack_rows(r, 8, r.top_b[:, A_])
    ready(shrink, TOP).wait()
    last = h1
    for j in range(4):
        last = last + dot(r.top_b[:, j * D : j * D + D], r.shrink_w[j].reshape(D, D))

    if cube:
        r.total[...] = jnp.sum(r.counts[...].reshape(-1, 8, 128), 0)
        image_total = r.total[0:1, 0:1]
    else:
        image_total = r.count_in[0:1, 0:1]
    head_part(r, last, image_total)
    top_backward(plan, r)
    wait_all(saves(TOP, h_, a_, t_) + saves(0, z_, slope_))


def pallas(kernel, name, inputs, outputs, scratch, **params):
    names = list(inputs) + list(outputs) + list(scratch)
    outs = pl.pallas_call(
        functools.partial(kernel, names),
        out_shape=[jax.ShapeDtypeStruct(shape, kind) for shape, kind, _ in outputs.values()],
        in_specs=[spec for _, spec in inputs.values()],
        out_specs=[spec for _, _, spec in outputs.values()],
        scratch_shapes=list(scratch.values()),
        compiler_params=pltpu.CompilerParams(vmem_limit_bytes=LIMIT, **params),
        name=name,
    )(*[value for value, _ in inputs.values()])
    return SimpleNamespace(**dict(zip(outputs, outs)))


def given_in(spec, **values):
    return {name: (value, spec) for name, value in values.items()}


def vmem(kind, **shapes):
    return {name: pltpu.VMEM(shape, kind) for name, shape in shapes.items()}


def dma(**counts):
    return {name: pltpu.SemaphoreType.DMA(count) for name, count in counts.items()}


def forward(plan, images, head, shards, args, scalars, gathered, count):
    rows = images.shape[0] * PAD
    shapes = saved_shapes(rows)
    whole = dict(
        patch_whole=cols_shape(D),
        joined_whole=(LAYERS,) + cols_shape(FF),
        expand_whole=(LAYERS,) + cols_shape(FF),
        shrink_whole=(LAYERS,) + ROWS_SHAPE,
    )
    inputs = given_in(VMEM_SPEC, **args)
    inputs.update(given_in(ANY_SPEC, images_in=images, head_in=head))
    inputs.update(given_in(pl.BlockSpec(memory_space=pltpu.SMEM), **scalars))
    outputs = {}
    if plan.cube:
        inputs.update(given_in(VMEM_SPEC, **shards))
        outputs.update({name: (shape, BF, ANY_SPEC) for name, shape in whole.items()})
    else:
        inputs.update(given_in(ANY_SPEC, **dict(zip(whole, gathered))))
        inputs.update(given_in(VMEM_SPEC, count_in=count))
    for name, (shape, kind) in shapes.items():
        deep = LAYERS if name in ("h", "a", "t") else TOP
        outputs["keep_" + name] = ((deep,) + shape, kind, ANY_SPEC)
    outputs.update(
        g=((rows, D), F32, VMEM_SPEC),
        rows_block=((rows_block(rows // PAD), 128), BF, VMEM_SPEC),
        keys_out=((2, 4, 4, BLOCK, D), BF, ANY_SPEC),
        tail=((8, D), F32, VMEM_SPEC),
        total=((8, 128), F32, VMEM_SPEC),
    )
    scratch = vmem(
        BF,
        table=(D, CLASSES),
        images=images.shape,
        top_b=(HEAD_ROWS, LOGIT_.stop),
        top_p=(rows // PAD, PAD, 16),
        top_du=(HEAD_ROWS, FF),
        d_keys=(rows, 2 * D),
        keys_block=(2, 4, 4, BLOCK, D),
        patch_w=cols_shape(D),
        joined_w=cols_shape(FF),
        expand_w=cols_shape(FF),
        shrink_w=ROWS_SHAPE,
    )
    scratch.update({name: pltpu.VMEM(shape, kind) for name, (shape, kind) in shapes.items()})
    scratch.update(
        vmem(
            F32,
            first=(HEAD_ROWS, D),
            class_row=(HEAD_ROWS, D),
            d_logits=(HEAD_ROWS, CLASS_PAD),
            head=head.shape,
            top_f=(HEAD_ROWS, G_.stop),
            rows_f=(rows_block(rows // PAD), 128),
        )
    )
    scratch.update(dma(saves=(9,), loads=(6,)))
    extra = {}
    if plan.cube:
        scratch.update(
            vmem(
                F32,
                joined_f=(LAYERS, HALF, FF),
                joined_b=(LAYERS, BLOCK, WIDTH),
                expand_b=(LAYERS, BLOCK, WIDTH),
                patch_f=(BLOCK, D // 2),
                count=(8, 128),
                counts=CHIPS + (2, 8, 128),
            )
        )
        scratch.update(
            vmem(
                BF,
                patch_block=(BLOCK, D // 2),
                joined_block=(LAYERS, BLOCK, WIDTH),
                expand_block=(LAYERS, BLOCK, WIDTH),
                shrink_block=(LAYERS, BLOCK_FF, D),
            )
        )
        scratch.update(
            dma(send=(10, 23), recv=(10, 22), share_send=(3,), share_recv=(3,), count_send=(10,), count_recv=(9,))
        )
        extra = dict(collective_id=1, has_side_effects=True)
    got = pallas(functools.partial(forward_kernel, plan), "forward", inputs, outputs, scratch, **extra)
    if not plan.cube:
        for name, value in zip(whole, gathered):
            setattr(got, name, value)
        got.total = count
    return got


UNITS = 4 * TOP + 1
WIDTHS = (WIDTH, WIDTH, D // 2, 3 * D // 2)
SHRINK, EXPAND, OUTPUT, TRIPLE = range(4)
KEYS = D
TAIL = 512
SEND = 4
VEC_ROWS = 256


def relative(plan):
    z, x, y, c = plan.where()
    return c, (z * 2 + x) * 2 + y


def place(plan, slot, core, chip, send=SEND):
    my_core, my_chip = relative(plan)
    at = jnp.bitwise_xor(my_chip, chip)
    other = jnp.bitwise_xor(my_core, core)
    return slot + (send - slot) * other, at // 4, at % 4


def store_cols(plan, out, slot, tile, width, value, half=WIDTH, send=SEND):
    per_half = half // width
    lanes = pl.ds(pl.multiple_of((tile % per_half) * width, 128), width)
    for b in range(16):
        rows = value[b * BLOCK : (b + 1) * BLOCK].astype(BF)
        out[(*place(plan, slot, tile // per_half, b, send), slice(None), lanes)] = rows


def store_rows(plan, out, slot, tile, value):
    for b in range(4):
        at = place(plan, slot, b % 2, tile * 2 + b // 2)
        for part in range(2):
            first = b * BLOCK_FF + part * BLOCK
            out[(*at, slice(None), pl.ds(part * D, D))] = value[first : first + BLOCK].astype(BF)


def store_vectors(plan, out, slot, value):
    for b in range(32):
        rows = value[b * 8 : b * 8 + 8]
        block = jnp.concatenate([rows[:, j * 128 : j * 128 + 128] for j in range(6)], 0)
        out[(*place(plan, slot, b % 2, b // 2), slice(None), pl.ds(D // 2, 128))] = block.astype(BF)


class Reduce:
    def __init__(self, plan, bufs, unit, width=WIDTH):
        self.plan, self.bufs, self.unit, self.width = plan, bufs, unit, width
        self.z, self.x, self.y, self.c = plan.where()
        self.to = over_links(plan)
        self.other = other_part(width)
        self.most = width - self.other
        self.cut, self.cut_other = cut_of(self.most), max(cut_of(self.other), 128)
        self.slot, self.three, self.two = unit % 4, unit % 3, unit % 2

    def copy(self, at):
        b, slot, three, to, c = self.bufs, self.slot, self.three, self.to, self.c
        most, cut, cut_other = self.most, self.cut, self.cut_other
        line = slice(None)
        full, main = pl.ds(0, self.width), pl.ds(0, most)
        left, right, low = pl.ds(0, cut), pl.ds(cut, most - cut), pl.ds(0, most - cut)
        other, all_other = pl.ds(most, self.other), pl.ds(0, self.other)
        own = b.unit.at[slot]
        if at == 17:
            rows = pl.ds(pl.multiple_of((1 - c) * HALF, 8), HALF)
            src, dst = self.result(rows)
            device = to.core
        else:
            src, dst, device = {
                0: lambda: (b.unit.at[SEND, :, :, :, full], b.core.at[:, :, :, full], to.core),
                1: lambda: (own.at[:, 3, :, left], b.near.at[three, :, :, left], to.x),
                2: lambda: (own.at[:, 3, :, right], b.far.at[three, :, :, low], to.y),
                3: lambda: (own.at[:, 1, :, main], b.y.at[three, :, :, main], to.y),
                4: lambda: (own.at[:, 2, :, main], b.x.at[three, :, :, main], to.x),
                5: lambda: (b.line.at[three, 2, :, main], b.main_two.at[three, 0, :, main], to.z1),
                6: lambda: (b.line.at[three, 2, :, main], b.main_two.at[three, 1, :, main], to.z3),
                7: lambda: (b.line.at[three, 1, :, main], b.main_one.at[slot, 0, :, main], to.z1),
                8: lambda: (b.line.at[three, 3, :, main], b.main_one.at[slot, 1, :, main], to.z3),
                9: lambda: (own.at[2, :, :, other], b.other_two.at[three, 0, :, :, all_other], to.z1),
                10: lambda: (own.at[2, :, :, other], b.other_two.at[three, 1, :, :, all_other], to.z3),
                11: lambda: (own.at[1, :, :, other], b.other_one.at[slot, 0, :, :, all_other], to.z1),
                12: lambda: (own.at[3, :, :, other], b.other_one.at[slot, 1, :, :, all_other], to.z3),
                13: lambda: (b.plane.at[three, 3, :, pl.ds(0, cut_other)], b.other_near.at[three], to.x),
                14: lambda: (b.plane.at[three, 3, :, pl.ds(cut_other, cut_other)], b.other_far.at[three], to.y),
                15: lambda: (b.plane.at[three, 1, :, all_other], b.other_y.at[three, :, all_other], to.y),
                16: lambda: (b.plane.at[three, 2, :, all_other], b.other_x.at[three, :, all_other], to.x),
            }[at]()
        return remote(src, dst, b.send.at[slot, at], b.recv.at[slot, at], device)

    def result(self, rows):
        b, c = self.bufs, self.c
        total, at = b.total.at[self.two], (self.unit - 1) // 4
        if self.width == WIDTH:
            return total.at[rows], b.expand_grad.at[at, c]
        if self.width == TAIL:
            return total.at[rows, pl.ds(0, D // 2)], b.patch.at[c]
        total = total.at[rows, pl.ds(0, self.width)]
        if self.width == KEYS:
            return total, b.keys.at[c]
        return total, (b.output_grad if self.width == WIDTHS[OUTPUT] else b.triple_grad).at[at, c]

    def own(self, by_rows):
        b, c = self.bufs, self.c
        total = b.total.at[self.two]
        if by_rows:
            at = (self.unit - 1) // 4
            moves = [(total.at[pl.ds(k * HALF, HALF)], b.shrink_grad.at[at, k]) for k in range(2)]
        else:
            moves = [self.result(pl.ds(pl.multiple_of(c * HALF, 8), HALF))]
        return [
            pltpu.make_async_copy(src, dst, b.send.at[self.slot, 18 + k])
            for k, (src, dst) in enumerate(moves)
        ]

    def start(self, *which):
        for at in which:
            self.copy(at).start()

    def arrived(self, *which):
        for at in which:
            self.copy(at).wait_recv()

    def sent(self, *which):
        for at in which:
            self.copy(at).wait_send()

    def corner(self):
        return (13, 14) if self.other > self.cut_other else (13,)

    def by_place(self, middle, end):
        inside = (self.z == 1) | (self.z == 2)
        if middle:
            pl.when(inside)(middle)
        if end:
            pl.when(jnp.logical_not(inside))(end)

    def stage0(self):
        @pl.when(self.unit > 0)
        def _():
            pl.semaphore_wait(self.bufs.credit, 1)

        self.start(0)

    def stage1(self):
        unit, core, slot = self.bufs.unit, self.bufs.core, self.slot
        cols = pl.ds(0, self.width)
        self.arrived(0)

        def add(z, chip):
            both = unit[slot, z, chip, :, cols].astype(F32) + core[z, chip, :, cols].astype(F32)
            unit[slot, z, chip, :, cols] = both.astype(BF)

        pl.loop(0, 4)(lambda z: add(z, 3))
        self.start(1, 2)
        pl.loop(0, 12)(lambda i: add(i // 3, i % 3))
        if self.other:
            self.by_place(lambda: self.start(10), lambda: self.start(9))

        @pl.when(self.unit < UNITS)
        def _():
            pl.semaphore_signal(
                self.bufs.credit, inc=1, device_id=self.to.core, device_id_type=pl.DeviceIdType.MESH
            )

    def stage2(self):
        b, slot, three, most, cut = self.bufs, self.slot, self.three, self.most, self.cut
        unit = b.unit
        left, right, low = pl.ds(0, cut), pl.ds(cut, most - cut), pl.ds(0, most - cut)
        self.arrived(1, 2)

        @pl.loop(0, 4)
        def _(z):
            got = b.near[three, z, :, left].astype(F32)
            unit[slot, z, 1, :, left] = (unit[slot, z, 1, :, left].astype(F32) + got).astype(BF)
            got = b.far[three, z, :, low].astype(F32)
            unit[slot, z, 2, :, right] = (unit[slot, z, 2, :, right].astype(F32) + got).astype(BF)

        self.start(3, 4)
        self.sent(1, 2)
        if not self.other:
            return
        other = pl.ds(most, self.other)

        def pass_on():
            self.arrived(9, 10)
            for z, k in ((3, 0), (1, 1)):
                for chip in range(4):
                    got = b.other_two[three, k, chip, :, pl.ds(0, self.other)].astype(F32)
                    unit[slot, z, chip, :, other] = (
                        unit[slot, z, chip, :, other].astype(F32) + got
                    ).astype(BF)

        self.by_place(pass_on, None)
        self.start(11, 12)

    def stage3(self):
        b, slot, three, main = self.bufs, self.slot, self.three, pl.ds(0, self.most)
        self.arrived(3, 4)

        @pl.loop(0, 4)
        def _(z):
            b.line[three, z, :, main] = (
                b.unit[slot, z, 0, :, main].astype(F32)
                + b.y[three, z, :, main].astype(F32)
                + b.x[three, z, :, main].astype(F32)
            ).astype(BF)

        self.by_place(lambda: self.start(6), lambda: self.start(5))
        self.sent(3, 4)
        if not self.other:
            return
        self.arrived(11, 12)
        for chip in range(4):
            every = pl.ds(0, self.other)
            b.plane[three, chip, :, every] = (
                b.unit[slot, 0, chip, :, pl.ds(self.most, self.other)].astype(F32)
                + b.other_one[slot, 0, chip, :, every].astype(F32)
                + b.other_one[slot, 1, chip, :, every].astype(F32)
            ).astype(BF)
        self.start(*self.corner())
        self.by_place(lambda: self.sent(10), lambda: self.sent(9))
        self.sent(11, 12)

    def stage4(self):
        b, three, main = self.bufs, self.three, pl.ds(0, self.most)

        def pass_on():
            self.arrived(5, 6)
            for z, k in ((3, 0), (1, 1)):
                got = b.main_two[three, k, :, main].astype(F32)
                b.line[three, z, :, main] = (b.line[three, z, :, main].astype(F32) + got).astype(BF)

        self.by_place(pass_on, None)
        self.start(7, 8)
        if not self.other:
            return
        self.arrived(*self.corner())
        half = self.cut_other
        for chip, cols, got in (
            (1, pl.ds(0, half), b.other_near),
            (2, pl.ds(half, half), b.other_far),
        )[: len(self.corner())]:
            both = b.plane[three, chip, :, cols].astype(F32) + got[three].astype(F32)
            b.plane[three, chip, :, cols] = both.astype(BF)
        self.start(15, 16)
        self.sent(*self.corner())

    def stage5(self, by_rows):
        b, slot, three, two = self.bufs, self.slot, self.three, self.two
        main = pl.ds(0, self.most)
        self.arrived(7, 8)
        total = b.line[three, 0, :, main].astype(F32)
        for k in range(2):
            total = total + b.main_one[slot, k, :, main].astype(F32)
        b.total[two, :, main] = total
        b.squares[0:1, main] += jnp.sum(total * total, 0, keepdims=True)
        if self.other:
            self.arrived(15, 16)
            other = pl.ds(self.most, self.other)
            every = pl.ds(0, self.other)
            total = (
                b.plane[three, 0, :, every].astype(F32)
                + b.other_y[three, :, every].astype(F32)
                + b.other_x[three, :, every].astype(F32)
            )
            b.total[two, :, other] = total
            b.squares[0:1, other] += jnp.sum(total * total, 0, keepdims=True)
        if not by_rows:
            self.start(17)
        start_all(self.own(by_rows))
        self.by_place(lambda: self.sent(6), lambda: self.sent(5))
        self.sent(7, 8)
        if self.other:
            self.sent(15, 16)

    def stage6(self, by_rows):
        if not by_rows:
            self.copy(17).wait()
        wait_all(self.own(by_rows))


POINTS = 4
STAGE_ORDER = (1, 0, 2, 3, 4, 6, 5)


def backward_kernel(plan, names, *refs):
    r = SimpleNamespace(**dict(zip(names, refs)))
    cube = plan.cube
    images = r.images.shape[0]
    loads = [
        (r.keep_z, r.vm_z),
        (r.shrink_whole, r.shrink_w),
        (r.keep_slope, r.vm_slope),
        (r.expand_whole, r.expand_w),
        (r.keep_m, r.vm_m),
        (r.keep_h1, r.vm_h1),
        (r.keep_o, r.vm_o),
        (r.keep_t, r.vm_t),
        (r.keep_p, r.vm_p),
        (r.keep_a, r.vm_a),
        (r.keep_h, r.vm_h),
        (r.joined_whole, r.expand_w),
    ]
    z_, shrink_, slope_, expand_, m_, h1_, o_, t_, p_, a_, h_, joined_ = range(12)

    def fetch(which, layer):
        src, dst = loads[which]
        return pltpu.make_async_copy(src.at[layer], dst, r.loads.at[which])

    def start(layer, *which):
        for k in which:
            fetch(k, layer).start()

    def wait(layer, *which):
        for k in which:
            fetch(k, layer).wait()

    loaded = [
        load(r.g_in, r.g, r.loads.at[joined_ + 1]),
        load(r.keys_in.at[0], r.unit.at[0, :, :, :, pl.ds(0, KEYS)], r.loads.at[joined_ + 2]),
        load(r.keys_in.at[1], r.unit.at[SEND, :, :, :, pl.ds(0, KEYS)], r.loads.at[joined_ + 3]),
    ]
    start(TOP - 1, z_)
    if cube:
        cube_barrier(plan)
        r.squares[...] = jnp.zeros_like(r.squares)
        top_rows = SmallGather(plan, r.rows_block, r.top_rows, r.rows_send, r.rows_recv)
    r.vectors[...] = jnp.zeros_like(r.vectors)
    r.vectors[FINAL : FINAL + 2] = r.tail_in[1:3]
    r.vectors[FINAL - 4 : FINAL] = r.tail_in[3:7]

    def run(unit, stage, by_rows, width=WIDTH):
        unit = Reduce(plan, r, unit, width)
        (
            unit.stage0,
            unit.stage1,
            unit.stage2,
            unit.stage3,
            unit.stage4,
            lambda: unit.stage5(by_rows),
            lambda: unit.stage6(by_rows),
        )[stage]()

    def point(it, at):
        if not cube:
            unit = 4 * it - 3 + at
            copies = [
                pltpu.make_async_copy(
                    r.unit.at[(unit % 4, SEND)[i]], r.full.at[unit, i], r.loads.at[joined_ + 1 + i]
                )
                for i in range(2)
            ]
            start_all(copies)
            wait_all(copies)
            return
        for stage in STAGE_ORDER:
            kind = (at - stage) % POINTS
            past = (kind + stage) // POINTS
            unit = 4 * (it - past) - 3 + kind
            go = functools.partial(run, unit, stage, kind == SHRINK, WIDTHS[kind])
            if past:
                pl.when(it > past)(go)
            else:
                go()
            if past and kind == TRIPLE:
                pl.when(it == past)(functools.partial(run, unit, stage, False, KEYS))

    def drain():
        for at in range(6):
            for stage in STAGE_ORDER:
                unit = UNITS + at - stage
                if UNITS - 2 * POINTS <= unit < UNITS:
                    kind = (unit - 1) % POINTS
                    run(jnp.int32(unit), stage, kind == SHRINK, WIDTHS[kind])
                if unit == UNITS:
                    run(jnp.int32(UNITS), stage, False, TAIL)

    def sent(unit, width=WIDTH):
        if cube:
            Reduce(plan, r, unit - 1, width).copy(0).wait_send()

    low_lane = lax.broadcasted_iota(jnp.int32, (PAD, 128), 1) < HEAD_DIM
    scale = HEAD_DIM**-0.5

    wait_all(loaded)
    start(TOP - 1, shrink_, slope_, expand_, m_, h1_, o_, t_, p_, a_, h_)
    pixels = load(r.images_in, r.images, r.loads.at[joined_ + 4])
    if cube:
        run(jnp.int32(0), 0, False, KEYS)
        top_rows.stage0()
    else:
        copies = [
            pltpu.make_async_copy(r.unit.at[(0, SEND)[i]], r.full.at[0, i], r.loads.at[joined_ + 1 + i])
            for i in range(2)
        ]
        start_all(copies)
        wait_all(copies)

    @pl.loop(1, LAYERS)
    def _(it):
        layer = TOP - it
        below = it < TOP
        unit_s = 4 * it - 3
        base = S + 2 + 4 * layer
        r.gr[...] = r.g[...].astype(BF)
        wait(layer, z_)
        slot = unit_s % 4
        pl.when(it == 1)(lambda: sent(unit_s, KEYS))
        pl.when(it > 1)(lambda: sent(unit_s, WIDTHS[TRIPLE]))

        @pl.loop(0, 8)
        def _(j):
            cols = pl.ds(pl.multiple_of(j * (D // 2), 128), D // 2)
            store_rows(plan, r.unit, slot, j, dot(r.vm_z[:, cols], r.gr[...], TN))

        point(it, 0)
        if cube:
            pl.when(it == 1)(top_rows.stage1)
        wait(layer, shrink_, slope_, expand_, m_, h1_)
        pl.when(below)(lambda: start(layer - 1, z_))
        slot_e = (unit_s + 1) % 4
        r.g1[...] = jnp.zeros_like(r.g1)
        sent(unit_s + 1)

        @pl.loop(0, 4)
        def _(j):
            cols = pl.ds(pl.multiple_of(j * D, 128), D)
            dz = dot(r.gr[...], r.shrink_w[j].reshape(D, D), NT)
            du = (dz * r.vm_slope[:, cols].astype(F32)).astype(BF)
            r.vm_slope[:, cols] = du
            store_cols(plan, r.unit, slot_e, j, D, dot(r.vm_m[...], du, TN))

        pl.when(below)(lambda: start(layer - 1, shrink_, m_))
        point(it, 1)
        if cube:
            pl.when(it == 1)(top_rows.stage2)

        @pl.loop(0, 4)
        def _(j):
            cols = pl.ds(pl.multiple_of(j * D, 128), D)
            r.g1[...] += dot(r.vm_slope[:, cols], weight(r.expand_w, j * D, D), NT)

        start(layer, joined_)
        pl.when(below)(lambda: start(layer - 1, slope_))
        d_h1, d_gain, d_shift = normalize_back(r.vm_h1[...], row(r.params, base + 2), r.g1[...])
        r.g1[...] = r.g[...] + d_h1
        r.vectors[pl.ds(base + 2, 1)] = d_gain
        r.vectors[pl.ds(base + 3, 1)] = d_shift
        pl.when(below)(lambda: start(layer - 1, h1_))

        r.gr[...] = r.g1[...].astype(BF)
        slot_t = (unit_s + TRIPLE) % 4
        wait(layer, o_)
        sent(unit_s + 2)
        for part in range(2):
            half = D // 2
            value = dot(r.vm_o[...], r.gr[:, part * half : part * half + half], TN)
            store_cols(plan, r.unit, (unit_s + OUTPUT) % 4, part, half, value, half)
        wait(layer, joined_)
        r.do[...] = dot(r.gr[...], weight(r.expand_w, 3 * D, D), NT).astype(BF)
        wait(layer, t_, p_, a_, h_)

        def heads(step):
            image, pair = step // (HEADS // 2), step % (HEADS // 2)
            rows = pl.ds(pl.multiple_of(image * PAD, 16), PAD)
            lanes = [pl.ds(pl.multiple_of(pair * 128 + part * D, 128), 128) for part in range(3)]
            q, key, v = (r.vm_t[rows, lane] for lane in lanes)
            do = r.do[rows, lanes[0]]
            zero = jnp.zeros_like(v)
            dqs, dks, dvs = [], [], []
            for which in range(2):
                part = jnp.where(low_lane, v, zero) if which == 0 else jnp.where(low_lane, zero, v)
                p_low = r.vm_p[step * 2 + which]
                p = p_low.astype(F32)
                dvs.append(dot(p_low, do))
                dp = dot(part, do, NT)
                ds = (p * (dp - jnp.sum(p * dp, 0, keepdims=True))).astype(BF)
                dqs.append(dot(ds, key, TN))
                dks.append(dot(ds, q))
            r.dt[rows, lanes[0]] = (jnp.where(low_lane, dqs[0], dqs[1]) * scale).astype(BF)
            r.dt[rows, lanes[1]] = (jnp.where(low_lane, dks[0], dks[1]) * scale).astype(BF)
            r.dt[rows, lanes[2]] = jnp.where(low_lane, dvs[0], dvs[1]).astype(BF)

        half = images * (HEADS // 2) // 2
        pl.loop(0, half, unroll=2)(heads)
        point(it, 2)
        if cube:
            pl.when(it == 1)(top_rows.finish)
        pl.loop(half, 2 * half, unroll=2)(heads)
        pl.when(below)(lambda: start(layer - 1, o_, t_, p_))
        r.g[...] = jnp.zeros_like(r.g)

        sent(unit_s + TRIPLE, WIDTHS[OUTPUT])

        @pl.loop(0, 6)
        def _(j):
            cols = pl.ds(pl.multiple_of(j * (D // 2), 128), D // 2)
            value = dot(r.vm_a[...], r.dt[:, cols], TN)
            store_cols(plan, r.unit, slot_t, j, D // 2, value, WIDTHS[TRIPLE])

        point(it, 3)

        @pl.loop(0, 3)
        def _(j):
            cols = pl.ds(pl.multiple_of(j * D, 128), D)
            r.g[...] += dot(r.dt[:, cols], weight(r.expand_w, j * D, D), NT)

        d_h, d_gain, d_shift = normalize_back(r.vm_h[...], row(r.params, base), r.g[...])
        r.g[...] = r.g1[...] + d_h
        r.vectors[pl.ds(base, 1)] = d_gain
        r.vectors[pl.ds(base + 1, 1)] = d_shift
        pl.when(below)(lambda: start(layer - 1, a_, h_, expand_))

    pixels.wait()
    slot = UNITS % 4
    sent(jnp.int32(UNITS), WIDTHS[TRIPLE])
    for part in range(2):
        half = D // 2
        value = jnp.zeros((D, half), F32)
        for image in range(images):
            rows = r.g[image * PAD + 1 : image * PAD + S, part * half : (part + 1) * half]
            value = value + dot(r.images[image], rows.astype(BF), TN)
        store_cols(plan, r.unit, slot, part, half, value, half)
    pos = r.g[:PAD]
    for image in range(1, images):
        pos = pos + r.g[image * PAD : (image + 1) * PAD]
    r.vectors[:S] = pos[:S]
    r.vectors[S : S + 1] = pos[:1]
    r.vectors[S + 1 : S + 2] = jnp.sum(pos[1:S], 0, keepdims=True)
    if not cube:
        copies = [
            pltpu.make_async_copy(r.unit.at[(slot, SEND)[i]], r.full.at[UNITS, i], r.loads.at[i])
            for i in range(2)
        ]
        copies.append(pltpu.make_async_copy(r.vectors, r.vector_rows, r.loads.at[2]))
        start_all(copies)
        wait_all(copies)
        return
    store_vectors(plan, r.unit, slot, r.vectors[...])

    drain()
    r.tail_block[:BLOCK] = r.total[UNITS % 2, :, D // 2 : TAIL].astype(BF)
    line = lax.broadcasted_iota(jnp.int32, (16, 128), 0)
    terms = jnp.zeros((16, 128), F32)
    for k, rest in enumerate((jnp.full((16, 128), jnp.sum(r.squares[...]), F32), r.tail_in[0:1, 0:128])):
        for j in range(3):
            term = rest.astype(BF).astype(F32)
            rest = rest - term
            terms = jnp.where(line == 3 * k + j, term, terms)
    r.tail_block[BLOCK:] = terms.astype(BF)
    gather = SmallGather(plan, r.tail_block, r.vector_rows, r.tail_send, r.tail_recv)
    gather.stage0()
    gather.stage1()
    gather.stage2()
    run(jnp.int32(UNITS), 6, False, TAIL)
    Reduce(plan, r, jnp.int32(UNITS), TAIL).copy(0).wait_send()
    gather.finish()


def backward(plan, images, params, done):
    rows = images.shape[0] * PAD
    shapes = saved_shapes(rows)
    inputs = given_in(
        VMEM_SPEC,
        params=params,
        tail_in=done.tail,
        rows_block=done.rows_block,
    )
    block = rows_block(images.shape[0])
    inputs.update(
        given_in(
            ANY_SPEC,
            images_in=images,
            g_in=done.g,
            keys_in=done.keys_out,
            joined_whole=done.joined_whole,
            expand_whole=done.expand_whole,
            shrink_whole=done.shrink_whole,
        )
    )
    inputs.update({"keep_" + name: (getattr(done, "keep_" + name), ANY_SPEC) for name in SAVED})
    if plan.cube:
        outputs = dict(
            shrink_grad=((TOP, 2, HALF, WIDTH), F32, ANY_SPEC),
            expand_grad=((TOP, 2, HALF, WIDTH), F32, ANY_SPEC),
            output_grad=((TOP, 2, HALF, WIDTHS[OUTPUT]), F32, ANY_SPEC),
            triple_grad=((TOP, 2, HALF, WIDTHS[TRIPLE]), F32, ANY_SPEC),
            keys=((2, HALF, KEYS), F32, ANY_SPEC),
            patch=((2, HALF, D // 2), F32, ANY_SPEC),
            vector_rows=(CHIPS + (2, BLOCK + 16, 128), BF, ANY_SPEC),
            top_rows=(CHIPS + (2, block, 128), BF, ANY_SPEC),
        )
    else:
        outputs = dict(
            full=((UNITS + 1, 2, 4, 4, BLOCK, WIDTH), BF, ANY_SPEC),
            vector_rows=((VEC_ROWS, D), F32, ANY_SPEC),
        )
    scratch = {"vm_" + name: pltpu.VMEM(shape, kind) for name, (shape, kind) in shapes.items()}
    scratch.update(
        vmem(
            BF,
            expand_w=cols_shape(FF),
            shrink_w=ROWS_SHAPE,
            gr=(rows, D),
            do=(rows, D),
            dt=(rows, 3 * D),
            unit=(SEND + 1, 4, 4, BLOCK, WIDTH),
            images=images.shape,
        )
    )
    scratch.update(vmem(F32, g=(rows, D), g1=(rows, D), vectors=(VEC_ROWS, D)))
    scratch.update(dma(loads=(17,)))
    extra = {}
    if plan.cube:
        other = other_part(WIDTH)
        most = WIDTH - other
        scratch.update(
            vmem(
                BF,
                core=(4, 4, BLOCK, WIDTH),
                tail_block=(BLOCK + 16, 128),
                near=(3, 4, BLOCK, cut_of(most)),
                far=(3, 4, BLOCK, most - cut_of(most)),
                x=(3, 4, BLOCK, most),
                y=(3, 4, BLOCK, most),
                line=(3, 4, BLOCK, most),
                main_two=(3, 2, BLOCK, most),
                main_one=(4, 2, BLOCK, most),
                other_two=(3, 2, 4, BLOCK, other),
                other_one=(4, 2, 4, BLOCK, other),
                plane=(3, 4, BLOCK, other),
                other_near=(3, BLOCK, cut_of(other)),
                other_far=(3, BLOCK, other - cut_of(other)),
                other_x=(3, BLOCK, other),
                other_y=(3, BLOCK, other),
            )
        )
        scratch.update(
            vmem(F32, total=(2, BLOCK, WIDTH), squares=(8, WIDTH))
        )
        scratch.update(
            dma(send=(4, 20), recv=(4, 18), rows_send=(10,), rows_recv=(9,), tail_send=(10,), tail_recv=(9,))
        )
        scratch.update(credit=pltpu.SemaphoreType.REGULAR)
        extra = dict(collective_id=2, has_side_effects=True)
    return pallas(functools.partial(backward_kernel, plan), "backward", inputs, outputs, scratch, **extra)


PARAMS = ("patch", "triple", "output", "expand", "shrink", "vector", "head")
KINDS = ("w_", "m_", "s_")


def adam_update(master, moment, square, gradient, step_rate):
    moment_new = BETA_ONE * moment + (1.0 - BETA_ONE) * gradient
    square_new = BETA_TWO * square + (1.0 - BETA_TWO) * gradient * gradient
    moment_hat = moment_new * (1.0 / (1.0 - BETA_ONE**STEP_INDEX))
    square_hat = square_new * (1.0 / (1.0 - BETA_TWO**STEP_INDEX))
    master_new = master - step_rate * (
        moment_hat / (jnp.sqrt(square_hat) + ADAM_EPS) + DECAY * master
    )
    return (master_new, moment_new, square_new)


def class_matrices(ref, images, devices, stride):
    first, found = 0, []
    for columns in PIECES:
        count = columns // 128
        parts = [
            jnp.concatenate(
                [
                    ref[pl.ds(image * PER_IMAGE + first + j, devices, stride=stride), :]
                    for j in range(count)
                ],
                1,
            )
            for image in range(images)
        ]
        found.append(jnp.concatenate(parts, 0).astype(BF))
        first += count
    return found


def own_columns(value, first, count):
    at = lax.broadcasted_iota(jnp.int32, (value.shape[1], 128), 0)
    to = lax.broadcasted_iota(jnp.int32, (value.shape[1], 128), 1)
    chosen = jnp.where((at == to + first) & (to < count), 1.0, 0.0).astype(BF)
    return dot(value, chosen).astype(BF)


def update_kernel(plan, images, names, *refs):
    r = SimpleNamespace(**dict(zip(names, refs)))
    named = dict(zip(names, refs))
    groups = [
        [(named[kind + name], named["vm_" + kind + name], named["to_" + kind + name]) for kind in KINDS]
        for name in PARAMS
    ]
    patch, triple, output, expand, shrink, vector, head = range(7)

    def moves(group, back):
        return [
            pltpu.make_async_copy(*((buf, out) if back else (src, buf)), r.sems.at[3 * group + k])
            for k, (src, buf, out) in enumerate(groups[group])
        ]

    order = (head, shrink, expand, triple, output, patch, vector)
    start_all(moves(head, False))

    tile = jnp.sum(r.tails[:, BLOCK:, :].astype(F32), 0)
    square_sum = tile[0:1, 0:1] + tile[1:2, 0:1] + tile[2:3, 0:1]
    loss = tile[3:4] + tile[4:5] + tile[5:6]
    r.rows_f[...] = r.top_rows[...].astype(F32)
    stride = r.top_rows.shape[0] // plan.n
    found = class_matrices(r.rows_f, images, plan.n, stride)
    features, d_logits, z, g, m, du, o, g1, a, dq = found
    r.features[...] = features
    r.d_logits[...] = d_logits
    alike = (dot(features, features, NT) + 1.0) * dot(d_logits, d_logits, NT)
    for left, right in ((z, g), (m, du), (o, g1), (a, dq)):
        alike = alike + dot(left, left, NT) * dot(right, right, NT)
    norm = jnp.sqrt(square_sum + jnp.sum(alike))
    me = plan.me()

    def top_grad(left, right, rows):
        return dot(own_columns(left, me * rows, rows), right, TN)[:rows]

    clip = CLIP / jnp.maximum(norm, CLIP)
    for group in order[1:]:
        start_all(moves(group, False))
    line = lax.broadcasted_iota(jnp.int32, (8, 128), 0)
    r.scalars[...] = jnp.where(line == 0, norm, jnp.where(line == 1, loss, r.total[...]))

    def step(group, at, gradient, rate):
        bufs = [buf for _, buf, _ in groups[group]]
        new = adam_update(*[buf[at] for buf in bufs], gradient * clip, rate)
        for buf, value in zip(bufs, new):
            buf[at] = value

    def finish(group):
        start_all(moves(group, True))

    every = slice(None)
    wait_all(moves(head, False))

    @pl.loop(0, D // 128)
    def _(j):
        rows = pl.ds(pl.multiple_of(j * 128, 128), 128)
        gradient = dot(r.features[:, rows], r.d_logits[...], TN)
        step(head, (rows, every), gradient[:, :CLASSES], RATE_MATRIX)

    bias = jnp.sum(d_logits.astype(F32), 0, keepdims=True)[:, :CLASSES]
    step(head, (slice(D, D + 1), every), bias, RATE_MATRIX)
    r.bias_grad[...] = bias * clip
    finish(head)
    wait_all(moves(shrink, False))

    step(shrink, (TOP, every, every), top_grad(z, g, BLOCK_FF), RATE_MATRIX)

    @pl.loop(0, TOP)
    def _(layer):
        at = TOP - 1 - layer
        for k in range(4):
            gradient = r.shrink_grad[at, k % 2, :, pl.ds(k // 2 * D, D)]
            step(shrink, (layer, pl.ds(k * HALF, HALF), every), gradient, RATE_MATRIX)

    finish(shrink)
    wait_all(moves(expand, False))

    step(expand, (TOP, every, every), top_grad(m, du, HALF), RATE_MATRIX)

    @pl.loop(0, TOP)
    def _(layer):
        at = TOP - 1 - layer
        for k in range(2):
            step(expand, (layer, every, pl.ds(k * WIDTH, WIDTH)), r.expand_grad[at, k], RATE_MATRIX)

    finish(expand)
    wait_all(moves(triple, False))
    wait_all(moves(output, False))

    step(output, (TOP, every, every), top_grad(o, g1, HALF), RATE_OUTPUT)
    step(triple, (TOP, every, pl.ds(0, D)), top_grad(a, dq, HALF), RATE_MATRIX)
    for k in range(2):
        step(triple, (TOP, every, pl.ds((k + 1) * D, D)), r.keys[k], RATE_MATRIX)

    @pl.loop(0, TOP)
    def _(layer):
        at = TOP - 1 - layer
        for k in range(2):
            width = WIDTHS[TRIPLE]
            step(triple, (layer, every, pl.ds(k * width, width)), r.triple_grad[at, k], RATE_MATRIX)
            width = WIDTHS[OUTPUT]
            step(output, (layer, every, pl.ds(k * width, width)), r.output_grad[at, k], RATE_OUTPUT)

    finish(triple)
    finish(output)
    wait_all(moves(patch, False))
    for k in range(2):
        step(patch, (every, pl.ds(k * (D // 2), D // 2)), r.patch_grad[k], RATE_MATRIX)
    finish(patch)
    count = groups[vector][0][0].shape[0]
    for d in range(-(-count // 8)):
        block = r.tails[d].astype(F32)
        for j in range(6):
            r.vector_grad[8 * d : 8 * d + 8, 128 * j : 128 * j + 128] = block[8 * j : 8 * j + 8]
    wait_all(moves(vector, False))
    step(vector, (every, every), r.vector_grad[:count], RATE_VECTOR)
    finish(vector)
    for group in order:
        wait_all(moves(group, True))


def update(plan, images, states, got, done):
    inputs, outputs, scratch = {}, {}, {}
    for name, state in zip(PARAMS, states):
        for kind, value in zip(KINDS, state):
            inputs[kind + name] = (value, ANY_SPEC)
            outputs["to_" + kind + name] = (value.shape, F32, ANY_SPEC)
            scratch["vm_" + kind + name] = pltpu.VMEM(value.shape, F32)
    inputs.update(
        given_in(
            VMEM_SPEC,
            total=done.total,
            tails=got.vector_rows.reshape(plan.n, BLOCK + 16, 128),
            top_rows=got.top_rows.reshape(-1, 128),
            shrink_grad=got.shrink_grad,
            expand_grad=got.expand_grad,
            output_grad=got.output_grad,
            triple_grad=got.triple_grad,
            patch_grad=got.patch,
            keys=got.keys,
        )
    )
    outputs.update(scalars=((8, 128), F32, VMEM_SPEC), bias_grad=((1, CLASSES), F32, VMEM_SPEC))
    scratch.update(vmem(BF, features=(plan.n * images, D), d_logits=(plan.n * images, 1024)))
    scratch.update(vmem(F32, vector_grad=(VEC_ROWS, D), rows_f=(plan.n * rows_block(images), 128)))
    scratch.update(dma(sems=(3 * len(PARAMS),)))
    new = pallas(functools.partial(update_kernel, plan, images), "update", inputs, outputs, scratch)
    states = [[getattr(new, "to_" + kind + name) for kind in KINDS] for name in PARAMS]
    return new.scalars[0, 0], new.scalars[1, 0], new.scalars[2, 0], states, new.bias_grad[0]


AXES = ("wide", "grp")


def update_whole(plan, images, states, got, done):
    full = got.full.reshape(UNITS + 1, 2, 16, BLOCK, WIDTH)
    layers = full[1:UNITS].reshape(TOP, 4, 2, 16, BLOCK, WIDTH)[::-1]

    def scattered(whole):
        axis = whole.ndim - 2
        return lax.psum_scatter(whole, AXES, scatter_dimension=axis, tiled=True).astype(F32)

    def from_cols(part):
        joined = jnp.concatenate([part[..., 0, :, :, :], part[..., 1, :, :, :]], -1)
        return joined.reshape(part.shape[:-4] + (D, -1))

    shrink = layers[:, 0].reshape(TOP, 2, 16, BLOCK, 2, D).transpose(0, 2, 1, 4, 3, 5)
    output = scattered(from_cols(layers[:, OUTPUT, ..., : WIDTHS[OUTPUT]]))
    triple = scattered(from_cols(layers[:, TRIPLE, ..., : WIDTHS[TRIPLE]]))
    rows_all = lax.all_gather(done.rows_block, AXES, axis=0)[:, : PER_IMAGE * images]
    rows_all = rows_all.reshape(plan.n * images, PER_IMAGE * 128)
    ends = [sum(PIECES[: k + 1]) for k in range(len(PIECES))]
    features, d_logits, z, g, m, du, o, g1, a, dq = jnp.split(rows_all, ends[:-1], axis=1)
    d_logits = d_logits[:, :CLASSES]
    bias = jnp.sum(d_logits.astype(F32), 0)[None]

    def top_grad(left, right):
        whole = dot(left, right, TN)
        count = whole.shape[0] // plan.n
        return lax.dynamic_slice_in_dim(whole, plan.me() * count, count)

    def with_top(below, top):
        return jnp.concatenate([below, top[None]], 0)

    keys = scattered(from_cols(full[0, ..., :KEYS]))
    split = [
        scattered(from_cols(full[UNITS, ..., : D // 2])),
        with_top(triple, jnp.concatenate([top_grad(a, dq), keys], 1)),
        with_top(output, top_grad(o, g1)),
        with_top(scattered(from_cols(layers[:, 1])), top_grad(m, du)),
        with_top(scattered(shrink.reshape(TOP, FF, D)), top_grad(z, g)),
    ]
    same = [
        lax.psum(got.vector_rows[: states[5][0].shape[0]], AXES),
        jnp.concatenate([dot(features, d_logits, TN), bias], 0),
    ]
    squares = lax.psum(sum(jnp.sum(g * g) for g in split), AXES) + sum(jnp.sum(g * g) for g in same)
    norm = jnp.sqrt(squares)
    clip = CLIP / jnp.maximum(norm, CLIP)
    rates = [RATE_MATRIX] * 2 + [RATE_OUTPUT] + [RATE_MATRIX] * 2 + [RATE_VECTOR, RATE_MATRIX]
    states = [
        adam_update(*state, gradient * clip, rate)
        for state, gradient, rate in zip(states, split + same, rates)
    ]
    return norm, lax.psum(done.tail[0, 0], AXES), done.total[0, 0], states, bias[0] * clip


def per_device(plan, images, slot_mask, labels, *params):
    states = [params[3 * k : 3 * k + 3] for k in range(7)]
    patch, triple, output, expand, shrink, vector, head = (state[0] for state in states)
    count = images.shape[0]
    weights = slot_mask.astype(F32)
    args = dict(vectors=vector)
    scalars = dict(labels=labels, mask=slot_mask)
    if plan.cube:
        shards = dict(patch=patch, triple=triple, output=output, expand=expand, shrink=shrink)
        done = forward(plan, images, head, shards, args, scalars, None, None)
    else:

        def whole(shard, shape):
            axis = shard.ndim - 2
            gathered = lax.all_gather(shard.astype(BF), AXES, axis=axis, tiled=True)
            return gathered.reshape(shard.shape[:axis] + shape)

        gathered = [
            whole(patch, cols_shape(D)),
            whole(jnp.concatenate([triple, output], 2), cols_shape(FF)),
            whole(expand, cols_shape(FF)),
            whole(shrink, ROWS_SHAPE),
        ]
        total = jnp.full((8, 128), lax.psum(jnp.sum(weights), AXES), F32)
        done = forward(plan, images, head, None, args, scalars, gathered, total)
    got = backward(plan, images, vector, done)
    if plan.cube:
        norm, loss, total, states, bias_grad = update(plan, count, states, got, done)
    else:
        norm, loss, total, states, bias_grad = update_whole(plan, count, states, got, done)
    return (
        loss,
        total,
        norm,
        *(value for state in states for value in state),
        bias_grad,
    )


def solution(mesh):
    plan = Plan(mesh)
    rows = P(AXES, None)
    layers = P(None, AXES, None)
    in_specs = (P(AXES, None, None), P(AXES), P(AXES)) + (rows,) * 3 + (layers,) * 12 + (P(),) * 6
    out_specs = (P(),) * 3 + (rows,) * 3 + (layers,) * 12 + (P(),) * 7
    return jax.shard_map(
        functools.partial(per_device, plan),
        mesh=mesh,
        in_specs=in_specs,
        out_specs=out_specs,
        check_vma=False,
    )
```

```python
import functools
from types import SimpleNamespace

import jax
import jax.numpy as jnp
from jax import lax
from jax.experimental import pallas as pl
from jax.experimental.pallas import tpu as pltpu
from jax.sharding import PartitionSpec as P

D = 768
HEADS = 12
HEAD_DIM = 64
FF = 3072
CLASSES = 1000
LAYERS = 3
STEP_INDEX = 10
S = 197
PAD = 208

EPS_NORM = 1e-06
CLIP = 0.1
BETA_ONE = 0.9
BETA_TWO = 0.95
ADAM_EPS = 1e-08
DECAY = 0.05
RATE_MATRIX = 0.03
RATE_OUTPUT = 0.2
RATE_VECTOR = 0.3
SMOOTH = 0.1

F32 = jnp.float32
BF = jnp.bfloat16
NN = (((1,), (0,)), ((), ()))
NT = (((1,), (1,)), ((), ()))
TN = (((0,), (0,)), ((), ()))
VMEM_SPEC = pl.BlockSpec(memory_space=pltpu.VMEM)
ANY_SPEC = pl.BlockSpec(memory_space=pl.ANY)
LIMIT = 62 * 1024 * 1024


def dot(left, right, form=NN):
    return lax.dot_general(left, right, form, preferred_element_type=F32)


def normalize(values, gain_row, shift_row):
    center = values - jnp.mean(values, -1, keepdims=True)
    spread = jnp.mean(center * center, -1, keepdims=True)
    return center * lax.rsqrt(spread + EPS_NORM) * gain_row + shift_row


def normalize_back(values, gain_row, grad):
    center = values - jnp.mean(values, -1, keepdims=True)
    spread = jnp.mean(center * center, -1, keepdims=True)
    scale = lax.rsqrt(spread + EPS_NORM)
    unit = center * scale
    d_unit = grad * gain_row
    d_values = scale * (
        d_unit
        - jnp.mean(d_unit, -1, keepdims=True)
        - unit * jnp.mean(d_unit * unit, -1, keepdims=True)
    )
    return (
        d_values,
        jnp.sum(grad * unit, 0, keepdims=True),
        jnp.sum(grad, 0, keepdims=True),
    )


def gelu_and_slope(u):
    x = jnp.abs(u) * 0.7071067811865476
    t = 1.0 / (1.0 + 0.3275911 * x)
    series = t * (
        0.254829592
        + t * (-0.284496736 + t * (1.421413741 + t * (-1.453152027 + t * 1.061405429)))
    )
    bell = jnp.exp(-0.5 * u * u)
    tail = 0.5 * series * bell
    share = jnp.where(u >= 0.0, 1.0 - tail, tail)
    return u * share, share + u * bell * 0.3989422804014327


class Plan:
    def __init__(self, mesh):
        self.wide, self.grp = mesh.shape["wide"], mesh.shape["grp"]
        self.n = self.wide * self.grp
        self.cube = self.wide == 8 and self.grp == 4

    def me(self):
        return lax.axis_index("wide") * self.grp + lax.axis_index("grp")

    def where(self):
        if not self.cube:
            return 0, 0, 0, 0
        wide, grp = lax.axis_index("wide"), lax.axis_index("grp")
        return wide // 2, wide % 2, grp // 2, grp % 2


CHIPS = (4, 2, 2)
BLOCK = D // 16
BLOCK_FF = FF // 32


def cols_shape(columns):
    return CHIPS + (BLOCK, columns)


ROWS_SHAPE = CHIPS + (2, BLOCK_FF, D)


def other_part(width):
    return width * 2 // 9 // 128 * 128


def cut_of(columns):
    return columns // 2 // 128 * 128


def over_links(plan):
    z, x, y, c = plan.where()

    def at(z, x, y, c):
        return (z * 2 + x, y * 2 + c)

    return SimpleNamespace(
        z1=at(jnp.bitwise_xor(z, 1), x, y, c),
        z3=at(jnp.bitwise_xor(z, 3), x, y, c),
        x=at(z, 1 - x, y, c),
        y=at(z, x, 1 - y, c),
        core=at(z, x, y, 1 - c),
    )


def remote(src, dst, send, recv, to):
    return pltpu.make_async_remote_copy(
        src_ref=src,
        dst_ref=dst,
        send_sem=send,
        recv_sem=recv,
        device_id=to,
        device_id_type=pl.DeviceIdType.MESH,
    )


class Gather:
    def __init__(self, plan, by_cols, block, whole, send, recv):
        self.z, self.x, self.y, self.c = plan.where()
        self.to = over_links(plan)
        self.by_cols, self.block, self.whole = by_cols, block, whole
        self.send, self.recv = send, recv
        self.width = block.shape[-1]
        self.other = other_part(self.width)
        self.most = self.width - self.other
        self.cut = (self.most // 2 + 127) // 128 * 128

    def region(self, z, x, y, start, width):
        if self.by_cols:
            first = pl.multiple_of(self.c * self.width + start, 128)
            return self.whole.at[z, x, y, :, pl.ds(first, width)]
        return self.whole.at[z, x, y, self.c, :, pl.ds(start, width)]

    def part(self, start, width):
        return self.block.at[:, pl.ds(start, width)]

    def copy(self, at):
        z, x, y, to = self.z, self.x, self.y, self.to
        z1, z3, line = jnp.bitwise_xor(z, 1), jnp.bitwise_xor(z, 3), slice(None)
        most, other, region = self.most, self.other, self.region
        cut, cut_other = self.cut, most + max(cut_of(other), 128)
        landed = at
        if at in (0, 1):
            src, dst = self.part(0, most), region(z, x, y, 0, most)
            device = (to.z1, to.z3)[at]
        elif at in (8, 9):
            src, dst = self.part(most, other), region(z, x, y, most, other)
            device = (to.x, to.y)[at - 8]
        else:
            src, device = {
                2: lambda: (region(z3, x, y, 0, most), to.z1),
                3: lambda: (region(z1, x, y, 0, most), to.z3),
                4: lambda: (region(line, x, y, 0, most), to.x),
                5: lambda: (region(line, x, y, 0, most), to.y),
                6: lambda: (region(line, x, 1 - y, 0, cut), to.x),
                7: lambda: (region(line, 1 - x, y, cut, most - cut), to.y),
                10: lambda: (region(z, x, 1 - y, most, cut_other - most), to.x),
                11: lambda: (region(z, 1 - x, y, cut_other, self.width - cut_other), to.y),
                12: lambda: (region(z, line, line, most, other), to.z1),
                13: lambda: (region(z, line, line, most, other), to.z3),
                14: lambda: (region(z3, line, line, most, other), to.z1),
                15: lambda: (region(z1, line, line, most, other), to.z3),
                16: lambda: (region(line, x, y, 0, most), to.core),
                17: lambda: (region(line, 1 - x, y, 0, most), to.core),
                18: lambda: (region(line, x, 1 - y, 0, most), to.core),
                19: lambda: (region(line, 1 - x, 1 - y, 0, cut), to.core),
                20: lambda: (region(line, 1 - x, 1 - y, cut, most - cut), to.core),
                21: lambda: (region(line, line, line, most, other), to.core),
            }[at]()
            dst = src
            if at in (3, 15):
                landed = at - 1
        return remote(src, dst, self.send.at[at], self.recv.at[landed], device)

    def exists(self, at):
        if at in (8, 9, 10, 12, 13, 14, 15, 21):
            return self.other > 0
        return at != 11 or self.other > 128

    def keep(self):
        here = self.region(self.z, self.x, self.y, 0, self.width)
        return pltpu.make_async_copy(self.block, here, self.send.at[22])

    def start(self, *which):
        for at in which:
            if self.exists(at):
                self.copy(at).start()

    def arrived(self, *which):
        for at in which:
            if self.exists(at):
                self.copy(at).wait_recv()

    def in_middle(self, do):
        pl.when((self.z == 1) | (self.z == 2))(do)

    def stage0(self):
        self.start(0, 1, 8, 9)
        self.keep().start()

    def stage1(self):
        self.arrived(0, 1)
        self.in_middle(lambda: self.start(2, 3))
        self.arrived(8, 9)
        self.start(10, 11)
        self.keep().wait()

    def stage2(self):
        self.arrived(2)
        self.start(4, 5, 16)
        self.arrived(10, 11)
        self.start(12, 13)

    def stage3(self):
        self.arrived(4, 5)
        self.start(6, 7, 17, 18)
        self.arrived(12, 13)
        self.in_middle(lambda: self.start(14, 15))

    def stage4(self):
        self.arrived(6, 7)
        self.start(19, 20)
        self.arrived(14)
        self.start(21)

    def finish(self):
        self.arrived(16, 17, 18, 19, 20, 21)
        passed = (2, 3, 14, 15)

        def sent(which):
            for at in which:
                if self.exists(at):
                    self.copy(at).wait_send()

        sent([at for at in range(22) if at not in passed])
        self.in_middle(lambda: sent(passed))


def cube_barrier(plan):
    z, x, y, c = plan.where()
    barrier = pltpu.get_barrier_semaphore()
    partners = [(jnp.bitwise_xor(z * 2 + x, k), y * 2 + c) for k in range(1, 8)]
    partners += [(z * 2 + x, (1 - y) * 2 + c), (z * 2 + x, y * 2 + 1 - c)]
    for partner in partners:
        pl.semaphore_signal(barrier, inc=1, device_id=partner, device_id_type=pl.DeviceIdType.MESH)
    pl.semaphore_wait(barrier, len(partners))


def load(source, target, sem):
    copy = pltpu.make_async_copy(source, target, sem)
    copy.start()
    return copy


def start_all(copies):
    for copy in copies:
        copy.start()


def wait_all(copies):
    for copy in copies:
        copy.wait()


def weight(ref, first, width):
    cols = pl.ds(first if isinstance(first, int) else pl.multiple_of(first, 128), width)
    return ref[:, :, :, :, cols].reshape(D, width)


class SmallGather:
    def __init__(self, plan, block, whole, send, recv):
        self.z, self.x, self.y, self.c = plan.where()
        self.to = over_links(plan)
        self.block, self.whole, self.send, self.recv = block, whole, send, recv

    def copy(self, at):
        z, x, y, c = self.z, self.x, self.y, self.c
        line = slice(None)
        if at < 7:
            src, dst = self.block, self.whole.at[z, x, y, c]
            device = (jnp.bitwise_xor(z * 2 + x, at + 1), y * 2 + c)
        elif at == 7:
            src = dst = self.whole.at[line, line, y, c]
            device = self.to.y
        else:
            src = dst = self.whole.at[line, line, line, c]
            device = self.to.core
        return remote(src, dst, self.send.at[at], self.recv.at[at], device)

    def keep(self):
        here = self.whole.at[self.z, self.x, self.y, self.c]
        return pltpu.make_async_copy(self.block, here, self.send.at[9])

    def stage0(self):
        for at in range(7):
            self.copy(at).start()
        self.keep().start()

    def stage1(self):
        for at in range(7):
            self.copy(at).wait_recv()
        self.keep().wait()
        self.copy(7).start()

    def stage2(self):
        self.copy(7).wait_recv()
        self.copy(8).start()

    def finish(self):
        self.copy(8).wait_recv()
        for at in range(9):
            self.copy(at).wait_send()


FF_TILE = 512
HALF = BLOCK // 2
WIDTH = FF // 2
HEAD_ROWS = 16
FINAL = S + 2 + 4 * LAYERS
TOP = LAYERS - 1
CLASS_PAD = 1024

Z_, M_, O_, Q_, A_ = (slice(0, FF),) + tuple(slice(FF + k * D, FF + k * D + D) for k in range(4))
FEATURE_, LOGIT_ = slice(FF + 4 * D, FF + 5 * D), slice(FF + 5 * D, FF + 5 * D + CLASS_PAD)
SLOPE_, H1_, G_ = slice(0, FF), slice(FF, FF + D), slice(FF + D, FF + 2 * D)
PIECES = (D, CLASS_PAD, FF, D, D, FF, D, D, D, D)
PER_IMAGE = sum(PIECES) // 128


def rows_block(images):
    return -(-PER_IMAGE * images // 16) * 16


def class_rows(ref, source):
    ref[...] = jnp.zeros_like(ref)
    for image in range(source.shape[0] // PAD):
        ref[image : image + 1] = source[image * PAD : image * PAD + 1]


def by_head(rows, image):
    head = lax.broadcasted_iota(jnp.int32, (16, D), 0)
    lane = lax.broadcasted_iota(jnp.int32, (16, D), 1)
    mine = (lane >= head * HEAD_DIM) & (lane < head * HEAD_DIM + HEAD_DIM)
    return mine, jnp.where(mine, rows[image : image + 1], 0.0)


def saved_shapes(rows):
    heads = rows // PAD * HEADS
    return dict(
        h=((rows, D), F32),
        a=((rows, D), BF),
        t=((rows, 3 * D), BF),
        o=((rows, D), BF),
        p=((heads, PAD, PAD), BF),
        h1=((rows, D), F32),
        m=((rows, D), BF),
        z=((rows, FF), BF),
        slope=((rows, FF), BF),
    )


SAVED = tuple(saved_shapes(PAD))


def row(ref, at):
    return ref[pl.ds(at, 1)]


def share_shards(plan, r):
    z, x, y, c = plan.where()
    r.joined_f[:, :, : 3 * D] = r.triple[...]
    r.joined_f[:, :, 3 * D :] = r.output[...]
    mine = pl.ds(pl.multiple_of(c * HALF, 8), HALF)

    def part(core, width):
        return pl.ds(pl.multiple_of(core * width, 128), width)

    moves = [
        (r.patch.at[:, part(1 - c, D // 2)], r.patch_f.at[mine]),
        (r.joined_f.at[:, :, part(1 - c, WIDTH)], r.joined_b.at[:, mine]),
        (r.expand.at[:, :, part(1 - c, WIDTH)], r.expand_b.at[:, mine]),
    ]
    copies = [
        pltpu.make_async_remote_copy(
            src_ref=src,
            dst_ref=dst,
            send_sem=r.share_send.at[i],
            recv_sem=r.share_recv.at[i],
            device_id=(z * 2 + x, y * 2 + 1 - c),
            device_id_type=pl.DeviceIdType.MESH,
        )
        for i, (src, dst) in enumerate(moves)
    ]
    start_all(copies)
    r.patch_f[mine] = r.patch[:, part(c, D // 2)]
    r.joined_b[:, mine] = r.joined_f[:, :, part(c, WIDTH)]
    r.expand_b[:, mine] = r.expand[:, :, part(c, WIDTH)]
    targets = (
        (r.patch_f, r.patch_block),
        (r.joined_b, r.joined_block),
        (r.expand_b, r.expand_block),
    )

    def arrive(which):
        src, dst = targets[which]
        copies[which].wait_recv()
        dst[...] = src[...].astype(BF)
        copies[which].wait_send()

    return arrive


def class_column(ref, kind):
    line = lax.broadcasted_iota(jnp.int32, (HEAD_ROWS, 1), 0)
    column = jnp.zeros((HEAD_ROWS, 1), kind)
    for image in range(ref.shape[0]):
        column = jnp.where(line == image, ref[image].astype(kind), column)
    return column


def head_part(r, first, image_total):
    table = r.table[...]
    gain, shift = r.vectors[FINAL : FINAL + 1], r.vectors[FINAL + 1 : FINAL + 2]
    feature = normalize(first, gain, shift).astype(BF)
    logits = dot(feature, table) + r.head[D : D + 1]
    ids = lax.broadcasted_iota(jnp.int32, logits.shape, 1)
    shifted = logits - jnp.max(logits, -1, keepdims=True)
    log_prob = shifted - jnp.log(jnp.sum(jnp.exp(shifted), -1, keepdims=True))
    target = jnp.where(ids == class_column(r.labels, jnp.int32), 1.0 - SMOOTH, 0.0) + SMOOTH / CLASSES
    weights = class_column(r.mask, F32)
    loss = jnp.sum(weights * -jnp.sum(target * log_prob, -1, keepdims=True))
    d_logits = ((weights / image_total) * (jnp.exp(log_prob) - target)).astype(BF)
    d_feature = dot(d_logits, table, NT)
    r.d_logits[...] = jnp.zeros_like(r.d_logits)
    r.d_logits[:, :CLASSES] = d_logits.astype(F32)
    r.top_b[:, FEATURE_] = feature
    r.top_b[:, LOGIT_] = r.d_logits[...].astype(BF)
    d_first, d_gain, d_shift = normalize_back(first, gain, d_feature)
    r.top_f[:, G_] = d_first
    r.tail[...] = jnp.zeros_like(r.tail)
    r.tail[0:1] = jnp.full((1, D), loss, F32)
    r.tail[1:2] = d_gain
    r.tail[2:3] = d_shift


def pack_rows(r, kind, *sources):
    first = sum(PIECES[:kind]) // 128
    for source in sources:
        value = source.astype(F32)
        for j in range(value.shape[1] // 128):
            for image in range(r.images.shape[0]):
                at = image * PER_IMAGE + first + j
                r.rows_f[at : at + 1] = value[image : image + 1, j * 128 : j * 128 + 128]
        first += value.shape[1] // 128


def top_backward(plan, r):
    images = r.images.shape[0]
    base = S + 2 + 4 * TOP
    g = r.top_f[:, G_]
    g_low = g.astype(BF)
    for j in range(4):
        cols = slice(j * D, j * D + D)
        dz = dot(g_low, r.shrink_w[j].reshape(D, D), NT)
        r.top_du[:, cols] = (dz * r.top_f[:, cols]).astype(BF)
    d_m = jnp.zeros((HEAD_ROWS, D), F32)
    for j in range(4):
        d_m = d_m + dot(r.top_du[:, j * D : j * D + D], weight(r.expand_w, j * D, D), NT)
    d_h1, d_gain, d_shift = normalize_back(r.top_f[:, H1_], row(r.vectors, base + 2), d_m)
    r.tail[5:6] = d_gain
    r.tail[6:7] = d_shift
    g1 = g + d_h1
    g1_low = g1.astype(BF)
    d_o = dot(g1_low, weight(r.joined_w, 3 * D, D), NT).astype(BF).astype(F32)
    query = r.top_b[:, Q_].astype(F32)
    r.class_row[...] = jnp.zeros_like(r.class_row)
    for image in range(images):
        rows = slice(image * PAD, image * PAD + PAD)
        mine, spread_o = by_head(d_o, image)
        _, spread_q = by_head(query, image)
        spread_o, spread_q = spread_o.astype(BF), spread_q.astype(BF)
        p_low = r.top_p[image]
        p = p_low.astype(F32)
        r.d_keys[rows, D:] = dot(p_low, spread_o).astype(BF)
        dp = dot(r.t[rows, 2 * D :], spread_o, NT)
        ds = (p * (dp - jnp.sum(p * dp, 0, keepdims=True))).astype(BF)
        r.d_keys[rows, :D] = (dot(ds, spread_q) * HEAD_DIM**-0.5).astype(BF)
        d_q = jnp.where(mine, dot(ds, r.t[rows, D : 2 * D], TN), 0.0)
        r.class_row[image : image + 1] = jnp.sum(d_q, 0, keepdims=True) * HEAD_DIM**-0.5
    for part in range(2):
        value = dot(r.a[...], r.d_keys[:, part * D : part * D + D], TN)
        store_cols(plan, r.keys_block, 0, part, D, value, D, 1)
    keys = load(r.keys_block, r.keys_out, r.loads.at[0])
    d_q = r.class_row[...].astype(BF)
    r.g[...] = dot(r.d_keys[:, :D], weight(r.joined_w, D, D), NT)
    r.g[...] += dot(r.d_keys[:, D:], weight(r.joined_w, 2 * D, D), NT)
    d_a = dot(d_q, weight(r.joined_w, 0, D), NT)
    for image in range(images):
        r.g[image * PAD : image * PAD + 1] += d_a[image : image + 1]
    d_h, d_gain, d_shift = normalize_back(r.h[...], row(r.vectors, base), r.g[...])
    r.g[...] = d_h
    for image in range(images):
        r.g[image * PAD : image * PAD + 1] += g1[image : image + 1]
    r.tail[3:4] = d_gain
    r.tail[4:5] = d_shift
    pack_rows(r, 0, r.top_b[:, FEATURE_], r.top_b[:, LOGIT_])
    pack_rows(r, 3, g_low)
    pack_rows(r, 5, r.top_du[...])
    pack_rows(r, 7, g1_low)
    pack_rows(r, 9, d_q)
    r.rows_block[...] = r.rows_f[...].astype(BF)
    keys.wait()


def forward_kernel(plan, names, *refs):
    r = SimpleNamespace(**dict(zip(names, refs)))
    cube = plan.cube
    images = r.images.shape[0]
    patch, joined, expand, shrink = range(4)
    pixels = load(r.images_in, r.images, r.loads.at[4])
    wholes = (r.patch_whole, r.joined_whole, r.expand_whole, r.shrink_whole)
    weights = (r.patch_w, r.joined_w, r.expand_w, r.shrink_w)
    if cube:
        blocks = (r.patch_block, r.joined_block, r.expand_block, r.shrink_block)
        cube_barrier(plan)
        r.shrink_block[...] = r.shrink[...].astype(BF)
        arrive = share_shards(plan, r)
        r.count[...] = jnp.full((8, 128), jnp.sum(class_column(r.mask, F32)), F32)
        counting = SmallGather(plan, r.count, r.counts, r.count_send, r.count_recv)

    def unit(kind, layer):
        if kind == patch:
            return Gather(plan, True, blocks[0], wholes[0], r.send.at[0], r.recv.at[0])
        at = 3 * layer + kind
        block, whole = blocks[kind].at[layer], wholes[kind].at[layer]
        return Gather(plan, kind != shrink, block, whole, r.send.at[at], r.recv.at[at])

    def ready(kind, layer):
        if cube:
            unit(kind, layer).finish()
        whole = wholes[kind] if kind == patch else wholes[kind].at[layer]
        return load(whole, weights[kind], r.loads.at[kind])

    held = (r.h, r.a, r.t, r.o, r.p, r.h1, r.m, r.z, r.slope)
    kept = (r.keep_h, r.keep_a, r.keep_t, r.keep_o, r.keep_p, r.keep_h1, r.keep_m, r.keep_z, r.keep_slope)
    h_, a_, t_, o_, p_, h1_, m_, z_, slope_ = range(9)

    def saves(layer, *which):
        return [pltpu.make_async_copy(held[k], kept[k].at[layer], r.saves.at[k]) for k in which]

    if cube:
        first = [unit(patch, 0), unit(joined, 0), unit(expand, 0), unit(shrink, 0), unit(joined, 1)]
        arrive(0)
        first[0].stage0()
        counting.stage0()
        arrive(1)
        first[1].stage0()
        first[0].stage1()
        arrive(2)
        first[2].stage0()
        first[1].stage1()
        first[0].stage2()
        first[3].stage0()
        first[2].stage1()
        first[1].stage2()
        first[0].stage3()
        first[4].stage0()
        first[3].stage1()
        first[2].stage2()
        first[1].stage3()
        first[0].stage4()
    ready(patch, 0).wait()
    pixels.wait()
    classifier = load(r.head_in, r.head, r.loads.at[5])
    for image in range(images):
        at = image * PAD
        r.h[at : at + 1] = r.vectors[0:1] + r.vectors[S : S + 1]
        embedded = dot(r.images[image], weight(r.patch_w, 0, D))
        r.h[at + 1 : at + S] = embedded + r.vectors[S + 1 : S + 2] + r.vectors[1:S]
        r.h[at + S : at + PAD] = jnp.zeros((PAD - S, D), F32)

    low_lane = lax.broadcasted_iota(jnp.int32, (PAD, 128), 1) < HEAD_DIM
    real_key = lax.broadcasted_iota(jnp.int32, (PAD, PAD), 0) < S

    @pl.loop(0, TOP)
    def _(layer):
        base = S + 2 + 4 * layer
        if cube:
            unit(expand, layer + 1).stage0()
            unit(joined, layer + 1).stage1()
            unit(shrink, layer).stage2()
            unit(expand, layer).stage3()
            unit(joined, layer).stage4()
        start_all(saves(layer, h_))

        @pl.when(layer > 0)
        def _():
            wait_all(saves(layer, a_, t_, o_, p_, h1_, m_))

        r.a[...] = normalize(r.h[...], row(r.vectors, base), row(r.vectors, base + 1)).astype(BF)
        ready(joined, layer).wait()

        @pl.loop(0, 3)
        def _(j):
            cols = pl.ds(pl.multiple_of(j * D, 128), D)
            r.t[:, cols] = dot(r.a[...], weight(r.joined_w, j * D, D)).astype(BF)

        start_all(saves(layer, a_, t_))

        def heads(step):
            image, pair = step // (HEADS // 2), step % (HEADS // 2)
            rows = pl.ds(pl.multiple_of(image * PAD, 16), PAD)
            lanes = [pl.ds(pl.multiple_of(pair * 128 + part * D, 128), 128) for part in range(3)]
            q, key, v = (r.t[rows, lane] for lane in lanes)
            zero = jnp.zeros_like(key)
            outs = []
            for which in range(2):
                part = jnp.where(low_lane, key, zero) if which == 0 else jnp.where(low_lane, zero, key)
                scores = dot(part, q, NT) * HEAD_DIM**-0.5
                scores = jnp.where(real_key, scores, -1e30)
                top = jnp.max(scores, 0, keepdims=True)
                e = jnp.exp(scores - top)
                p = (e * (1.0 / jnp.sum(e, 0, keepdims=True))).astype(BF)
                r.p[step * 2 + which] = p
                outs.append(dot(p, v, TN))
            r.o[rows, lanes[0]] = jnp.where(low_lane, outs[0], outs[1]).astype(BF)

        half = images * (HEADS // 2) // 2
        pl.loop(0, half, unroll=2)(heads)
        if cube:
            unit(shrink, layer + 1).stage0()
            unit(expand, layer + 1).stage1()
            unit(joined, layer + 1).stage2()

        pl.loop(half, 2 * half, unroll=2)(heads)
        start_all(saves(layer, o_, p_))
        r.h1[...] = r.h[...] + dot(r.o[...], weight(r.joined_w, 3 * D, D))
        start_all(saves(layer, h1_))
        if cube:
            unit(shrink, layer).stage3()
            unit(expand, layer).stage4()
            pl.when(layer == 0)(counting.stage1)
            pl.when(layer == 1)(counting.finish)
        r.m[...] = normalize(r.h1[...], row(r.vectors, base + 2), row(r.vectors, base + 3)).astype(BF)
        start_all(saves(layer, m_))
        wait_all(saves(layer, h_))
        r.h[...] = r.h1[...]

        @pl.when(layer > 0)
        def _():
            wait_all(saves(layer, z_, slope_))

        ready(expand, layer).wait()

        @pl.loop(0, FF // FF_TILE)
        def _(j):
            cols = pl.ds(pl.multiple_of(j * FF_TILE, 128), FF_TILE)
            u = dot(r.m[...], weight(r.expand_w, j * FF_TILE, FF_TILE))
            z, slope = gelu_and_slope(u)
            r.z[:, cols] = z.astype(BF)
            r.slope[:, cols] = slope.astype(BF)

        start_all(saves(layer, z_, slope_))
        if cube:
            pl.when(layer < TOP - 1)(lambda: unit(joined, layer + 2).stage0())

            unit(shrink, layer + 1).stage1()
            unit(expand, layer + 1).stage2()
            unit(joined, layer + 1).stage3()
            unit(shrink, layer).stage4()
            pl.when(layer == 0)(counting.stage2)
        ready(shrink, layer).wait()

        @pl.loop(0, 4)
        def _(j):
            cols = pl.ds(pl.multiple_of(j * D, 128), D)
            r.h[...] += dot(r.z[:, cols], r.shrink_w[j].reshape(D, D))

    base = S + 2 + 4 * TOP
    if cube:
        unit(shrink, TOP).stage2()
        unit(expand, TOP).stage3()
        unit(joined, TOP).stage4()
    start_all(saves(TOP, h_))
    wait_all(saves(TOP, a_, t_) + saves(0, o_, p_, h1_, m_))
    r.a[...] = normalize(r.h[...], row(r.vectors, base), row(r.vectors, base + 1)).astype(BF)
    class_rows(r.first, r.h)
    first = r.first[...]
    r.top_b[:, A_] = normalize(first, row(r.vectors, base), row(r.vectors, base + 1)).astype(BF)
    ready(joined, TOP).wait()
    for j in (1, 2):
        r.t[:, j * D : j * D + D] = dot(r.a[...], weight(r.joined_w, j * D, D)).astype(BF)
    start_all(saves(TOP, a_, t_))
    query = dot(r.top_b[:, A_], weight(r.joined_w, 0, D)).astype(BF)
    r.top_b[:, Q_] = query
    if cube:
        unit(shrink, TOP).stage3()
        unit(expand, TOP).stage4()
    query = query.astype(F32)
    real = lax.broadcasted_iota(jnp.int32, (PAD, 16), 0) < S
    r.class_row[...] = jnp.zeros_like(r.class_row)
    for image in range(images):
        rows = slice(image * PAD, image * PAD + PAD)
        mine, spread = by_head(query, image)
        scores = dot(r.t[rows, D : 2 * D], spread.astype(BF), NT) * HEAD_DIM**-0.5
        scores = jnp.where(real, scores, -1e30)
        e = jnp.exp(scores - jnp.max(scores, 0, keepdims=True))
        p = (e * (1.0 / jnp.sum(e, 0, keepdims=True))).astype(BF)
        r.top_p[image] = p
        out = jnp.where(mine, dot(p, r.t[rows, 2 * D :], TN), 0.0)
        r.class_row[image : image + 1] = jnp.sum(out, 0, keepdims=True)
    attended = r.class_row[...].astype(BF)
    r.top_b[:, O_] = attended
    h1 = first + dot(attended, weight(r.joined_w, 3 * D, D))
    r.top_f[:, H1_] = h1
    r.top_b[:, M_] = normalize(h1, row(r.vectors, base + 2), row(r.vectors, base + 3)).astype(BF)
    ready(expand, TOP).wait()
    for j in range(4):
        cols = slice(j * D, j * D + D)
        z, slope = gelu_and_slope(dot(r.top_b[:, M_], weight(r.expand_w, j * D, D)))
        r.top_b[:, cols] = z.astype(BF)
        r.top_f[:, cols] = slope
    if cube:
        unit(shrink, TOP).stage4()
    classifier.wait()
    r.table[...] = r.head[:D].astype(BF)
    r.rows_f[...] = jnp.zeros_like(r.rows_f)
    pack_rows(r, 2, r.top_b[:, Z_])
    pack_rows(r, 4, r.top_b[:, M_])
    pack_rows(r, 6, r.top_b[:, O_])
    pack_rows(r, 8, r.top_b[:, A_])
    ready(shrink, TOP).wait()
    last = h1
    for j in range(4):
        last = last + dot(r.top_b[:, j * D : j * D + D], r.shrink_w[j].reshape(D, D))

    if cube:
        r.total[...] = jnp.sum(r.counts[...].reshape(-1, 8, 128), 0)
        image_total = r.total[0:1, 0:1]
    else:
        image_total = r.count_in[0:1, 0:1]
    head_part(r, last, image_total)
    top_backward(plan, r)
    wait_all(saves(TOP, h_, a_, t_) + saves(0, z_, slope_))


def pallas(kernel, name, inputs, outputs, scratch, **params):
    names = list(inputs) + list(outputs) + list(scratch)
    outs = pl.pallas_call(
        functools.partial(kernel, names),
        out_shape=[jax.ShapeDtypeStruct(shape, kind) for shape, kind, _ in outputs.values()],
        in_specs=[spec for _, spec in inputs.values()],
        out_specs=[spec for _, _, spec in outputs.values()],
        scratch_shapes=list(scratch.values()),
        compiler_params=pltpu.CompilerParams(vmem_limit_bytes=LIMIT, **params),
        name=name,
    )(*[value for value, _ in inputs.values()])
    return SimpleNamespace(**dict(zip(outputs, outs)))


def given_in(spec, **values):
    return {name: (value, spec) for name, value in values.items()}


def vmem(kind, **shapes):
    return {name: pltpu.VMEM(shape, kind) for name, shape in shapes.items()}


def dma(**counts):
    return {name: pltpu.SemaphoreType.DMA(count) for name, count in counts.items()}


def forward(plan, images, head, shards, args, scalars, gathered, count):
    rows = images.shape[0] * PAD
    shapes = saved_shapes(rows)
    whole = dict(
        patch_whole=cols_shape(D),
        joined_whole=(LAYERS,) + cols_shape(FF),
        expand_whole=(LAYERS,) + cols_shape(FF),
        shrink_whole=(LAYERS,) + ROWS_SHAPE,
    )
    inputs = given_in(VMEM_SPEC, **args)
    inputs.update(given_in(ANY_SPEC, images_in=images, head_in=head))
    inputs.update(given_in(pl.BlockSpec(memory_space=pltpu.SMEM), **scalars))
    outputs = {}
    if plan.cube:
        inputs.update(given_in(VMEM_SPEC, **shards))
        outputs.update({name: (shape, BF, ANY_SPEC) for name, shape in whole.items()})
    else:
        inputs.update(given_in(ANY_SPEC, **dict(zip(whole, gathered))))
        inputs.update(given_in(VMEM_SPEC, count_in=count))
    for name, (shape, kind) in shapes.items():
        deep = LAYERS if name in ("h", "a", "t") else TOP
        outputs["keep_" + name] = ((deep,) + shape, kind, ANY_SPEC)
    outputs.update(
        g=((rows, D), F32, VMEM_SPEC),
        rows_block=((rows_block(rows // PAD), 128), BF, VMEM_SPEC),
        keys_out=((2, 4, 4, BLOCK, D), BF, ANY_SPEC),
        tail=((8, D), F32, VMEM_SPEC),
        total=((8, 128), F32, VMEM_SPEC),
    )
    scratch = vmem(
        BF,
        table=(D, CLASSES),
        images=images.shape,
        top_b=(HEAD_ROWS, LOGIT_.stop),
        top_p=(rows // PAD, PAD, 16),
        top_du=(HEAD_ROWS, FF),
        d_keys=(rows, 2 * D),
        keys_block=(2, 4, 4, BLOCK, D),
        patch_w=cols_shape(D),
        joined_w=cols_shape(FF),
        expand_w=cols_shape(FF),
        shrink_w=ROWS_SHAPE,
    )
    scratch.update({name: pltpu.VMEM(shape, kind) for name, (shape, kind) in shapes.items()})
    scratch.update(
        vmem(
            F32,
            first=(HEAD_ROWS, D),
            class_row=(HEAD_ROWS, D),
            d_logits=(HEAD_ROWS, CLASS_PAD),
            head=head.shape,
            top_f=(HEAD_ROWS, G_.stop),
            rows_f=(rows_block(rows // PAD), 128),
        )
    )
    scratch.update(dma(saves=(9,), loads=(6,)))
    extra = {}
    if plan.cube:
        scratch.update(
            vmem(
                F32,
                joined_f=(LAYERS, HALF, FF),
                joined_b=(LAYERS, BLOCK, WIDTH),
                expand_b=(LAYERS, BLOCK, WIDTH),
                patch_f=(BLOCK, D // 2),
                count=(8, 128),
                counts=CHIPS + (2, 8, 128),
            )
        )
        scratch.update(
            vmem(
                BF,
                patch_block=(BLOCK, D // 2),
                joined_block=(LAYERS, BLOCK, WIDTH),
                expand_block=(LAYERS, BLOCK, WIDTH),
                shrink_block=(LAYERS, BLOCK_FF, D),
            )
        )
        scratch.update(
            dma(send=(10, 23), recv=(10, 22), share_send=(3,), share_recv=(3,), count_send=(10,), count_recv=(9,))
        )
        extra = dict(collective_id=1, has_side_effects=True)
    got = pallas(functools.partial(forward_kernel, plan), "forward", inputs, outputs, scratch, **extra)
    if not plan.cube:
        for name, value in zip(whole, gathered):
            setattr(got, name, value)
        got.total = count
    return got


UNITS = 4 * TOP + 1
WIDTHS = (WIDTH, WIDTH, D // 2, 3 * D // 2)
SHRINK, EXPAND, OUTPUT, TRIPLE = range(4)
KEYS = D
TAIL = 512
SEND = 4
VEC_ROWS = 256


def relative(plan):
    z, x, y, c = plan.where()
    return c, (z * 2 + x) * 2 + y


def place(plan, slot, core, chip, send=SEND):
    my_core, my_chip = relative(plan)
    at = jnp.bitwise_xor(my_chip, chip)
    other = jnp.bitwise_xor(my_core, core)
    return slot + (send - slot) * other, at // 4, at % 4


def store_cols(plan, out, slot, tile, width, value, half=WIDTH, send=SEND):
    per_half = half // width
    lanes = pl.ds(pl.multiple_of((tile % per_half) * width, 128), width)
    for b in range(16):
        rows = value[b * BLOCK : (b + 1) * BLOCK].astype(BF)
        out[(*place(plan, slot, tile // per_half, b, send), slice(None), lanes)] = rows


def store_rows(plan, out, slot, tile, value):
    for b in range(4):
        at = place(plan, slot, b % 2, tile * 2 + b // 2)
        for part in range(2):
            first = b * BLOCK_FF + part * BLOCK
            out[(*at, slice(None), pl.ds(part * D, D))] = value[first : first + BLOCK].astype(BF)


def store_vectors(plan, out, slot, value):
    for b in range(32):
        rows = value[b * 8 : b * 8 + 8]
        block = jnp.concatenate([rows[:, j * 128 : j * 128 + 128] for j in range(6)], 0)
        out[(*place(plan, slot, b % 2, b // 2), slice(None), pl.ds(D // 2, 128))] = block.astype(BF)


class Reduce:
    def __init__(self, plan, bufs, unit, width=WIDTH):
        self.plan, self.bufs, self.unit, self.width = plan, bufs, unit, width
        self.z, self.x, self.y, self.c = plan.where()
        self.to = over_links(plan)
        self.other = other_part(width)
        self.most = width - self.other
        self.cut, self.cut_other = cut_of(self.most), max(cut_of(self.other), 128)
        self.slot, self.three, self.two = unit % 4, unit % 3, unit % 2

    def copy(self, at):
        b, slot, three, to, c = self.bufs, self.slot, self.three, self.to, self.c
        most, cut, cut_other = self.most, self.cut, self.cut_other
        line = slice(None)
        full, main = pl.ds(0, self.width), pl.ds(0, most)
        left, right, low = pl.ds(0, cut), pl.ds(cut, most - cut), pl.ds(0, most - cut)
        other, all_other = pl.ds(most, self.other), pl.ds(0, self.other)
        own = b.unit.at[slot]
        if at == 17:
            rows = pl.ds(pl.multiple_of((1 - c) * HALF, 8), HALF)
            src, dst = self.result(rows)
            device = to.core
        else:
            src, dst, device = {
                0: lambda: (b.unit.at[SEND, :, :, :, full], b.core.at[:, :, :, full], to.core),
                1: lambda: (own.at[:, 3, :, left], b.near.at[three, :, :, left], to.x),
                2: lambda: (own.at[:, 3, :, right], b.far.at[three, :, :, low], to.y),
                3: lambda: (own.at[:, 1, :, main], b.y.at[three, :, :, main], to.y),
                4: lambda: (own.at[:, 2, :, main], b.x.at[three, :, :, main], to.x),
                5: lambda: (b.line.at[three, 2, :, main], b.main_two.at[three, 0, :, main], to.z1),
                6: lambda: (b.line.at[three, 2, :, main], b.main_two.at[three, 1, :, main], to.z3),
                7: lambda: (b.line.at[three, 1, :, main], b.main_one.at[slot, 0, :, main], to.z1),
                8: lambda: (b.line.at[three, 3, :, main], b.main_one.at[slot, 1, :, main], to.z3),
                9: lambda: (own.at[2, :, :, other], b.other_two.at[three, 0, :, :, all_other], to.z1),
                10: lambda: (own.at[2, :, :, other], b.other_two.at[three, 1, :, :, all_other], to.z3),
                11: lambda: (own.at[1, :, :, other], b.other_one.at[slot, 0, :, :, all_other], to.z1),
                12: lambda: (own.at[3, :, :, other], b.other_one.at[slot, 1, :, :, all_other], to.z3),
                13: lambda: (b.plane.at[three, 3, :, pl.ds(0, cut_other)], b.other_near.at[three], to.x),
                14: lambda: (b.plane.at[three, 3, :, pl.ds(cut_other, cut_other)], b.other_far.at[three], to.y),
                15: lambda: (b.plane.at[three, 1, :, all_other], b.other_y.at[three, :, all_other], to.y),
                16: lambda: (b.plane.at[three, 2, :, all_other], b.other_x.at[three, :, all_other], to.x),
            }[at]()
        return remote(src, dst, b.send.at[slot, at], b.recv.at[slot, at], device)

    def result(self, rows):
        b, c = self.bufs, self.c
        total, at = b.total.at[self.two], (self.unit - 1) // 4
        if self.width == WIDTH:
            return total.at[rows], b.expand_grad.at[at, c]
        if self.width == TAIL:
            return total.at[rows, pl.ds(0, D // 2)], b.patch.at[c]
        total = total.at[rows, pl.ds(0, self.width)]
        if self.width == KEYS:
            return total, b.keys.at[c]
        return total, (b.output_grad if self.width == WIDTHS[OUTPUT] else b.triple_grad).at[at, c]

    def own(self, by_rows):
        b, c = self.bufs, self.c
        total = b.total.at[self.two]
        if by_rows:
            at = (self.unit - 1) // 4
            moves = [(total.at[pl.ds(k * HALF, HALF)], b.shrink_grad.at[at, k]) for k in range(2)]
        else:
            moves = [self.result(pl.ds(pl.multiple_of(c * HALF, 8), HALF))]
        return [
            pltpu.make_async_copy(src, dst, b.send.at[self.slot, 18 + k])
            for k, (src, dst) in enumerate(moves)
        ]

    def start(self, *which):
        for at in which:
            self.copy(at).start()

    def arrived(self, *which):
        for at in which:
            self.copy(at).wait_recv()

    def sent(self, *which):
        for at in which:
            self.copy(at).wait_send()

    def corner(self):
        return (13, 14) if self.other > self.cut_other else (13,)

    def by_place(self, middle, end):
        inside = (self.z == 1) | (self.z == 2)
        if middle:
            pl.when(inside)(middle)
        if end:
            pl.when(jnp.logical_not(inside))(end)

    def stage0(self):
        @pl.when(self.unit > 0)
        def _():
            pl.semaphore_wait(self.bufs.credit, 1)

        self.start(0)

    def stage1(self):
        unit, core, slot = self.bufs.unit, self.bufs.core, self.slot
        cols = pl.ds(0, self.width)
        self.arrived(0)

        def add(z, chip):
            both = unit[slot, z, chip, :, cols].astype(F32) + core[z, chip, :, cols].astype(F32)
            unit[slot, z, chip, :, cols] = both.astype(BF)

        pl.loop(0, 4)(lambda z: add(z, 3))
        self.start(1, 2)
        pl.loop(0, 12)(lambda i: add(i // 3, i % 3))
        if self.other:
            self.by_place(lambda: self.start(10), lambda: self.start(9))

        @pl.when(self.unit < UNITS)
        def _():
            pl.semaphore_signal(
                self.bufs.credit, inc=1, device_id=self.to.core, device_id_type=pl.DeviceIdType.MESH
            )

    def stage2(self):
        b, slot, three, most, cut = self.bufs, self.slot, self.three, self.most, self.cut
        unit = b.unit
        left, right, low = pl.ds(0, cut), pl.ds(cut, most - cut), pl.ds(0, most - cut)
        self.arrived(1, 2)

        @pl.loop(0, 4)
        def _(z):
            got = b.near[three, z, :, left].astype(F32)
            unit[slot, z, 1, :, left] = (unit[slot, z, 1, :, left].astype(F32) + got).astype(BF)
            got = b.far[three, z, :, low].astype(F32)
            unit[slot, z, 2, :, right] = (unit[slot, z, 2, :, right].astype(F32) + got).astype(BF)

        self.start(3, 4)
        self.sent(1, 2)
        if not self.other:
            return
        other = pl.ds(most, self.other)

        def pass_on():
            self.arrived(9, 10)
            for z, k in ((3, 0), (1, 1)):
                for chip in range(4):
                    got = b.other_two[three, k, chip, :, pl.ds(0, self.other)].astype(F32)
                    unit[slot, z, chip, :, other] = (
                        unit[slot, z, chip, :, other].astype(F32) + got
                    ).astype(BF)

        self.by_place(pass_on, None)
        self.start(11, 12)

    def stage3(self):
        b, slot, three, main = self.bufs, self.slot, self.three, pl.ds(0, self.most)
        self.arrived(3, 4)

        @pl.loop(0, 4)
        def _(z):
            b.line[three, z, :, main] = (
                b.unit[slot, z, 0, :, main].astype(F32)
                + b.y[three, z, :, main].astype(F32)
                + b.x[three, z, :, main].astype(F32)
            ).astype(BF)

        self.by_place(lambda: self.start(6), lambda: self.start(5))
        self.sent(3, 4)
        if not self.other:
            return
        self.arrived(11, 12)
        for chip in range(4):
            every = pl.ds(0, self.other)
            b.plane[three, chip, :, every] = (
                b.unit[slot, 0, chip, :, pl.ds(self.most, self.other)].astype(F32)
                + b.other_one[slot, 0, chip, :, every].astype(F32)
                + b.other_one[slot, 1, chip, :, every].astype(F32)
            ).astype(BF)
        self.start(*self.corner())
        self.by_place(lambda: self.sent(10), lambda: self.sent(9))
        self.sent(11, 12)

    def stage4(self):
        b, three, main = self.bufs, self.three, pl.ds(0, self.most)

        def pass_on():
            self.arrived(5, 6)
            for z, k in ((3, 0), (1, 1)):
                got = b.main_two[three, k, :, main].astype(F32)
                b.line[three, z, :, main] = (b.line[three, z, :, main].astype(F32) + got).astype(BF)

        self.by_place(pass_on, None)
        self.start(7, 8)
        if not self.other:
            return
        self.arrived(*self.corner())
        half = self.cut_other
        for chip, cols, got in (
            (1, pl.ds(0, half), b.other_near),
            (2, pl.ds(half, half), b.other_far),
        )[: len(self.corner())]:
            both = b.plane[three, chip, :, cols].astype(F32) + got[three].astype(F32)
            b.plane[three, chip, :, cols] = both.astype(BF)
        self.start(15, 16)
        self.sent(*self.corner())

    def stage5(self, by_rows):
        b, slot, three, two = self.bufs, self.slot, self.three, self.two
        main = pl.ds(0, self.most)
        self.arrived(7, 8)
        total = b.line[three, 0, :, main].astype(F32)
        for k in range(2):
            total = total + b.main_one[slot, k, :, main].astype(F32)
        b.total[two, :, main] = total
        b.squares[0:1, main] += jnp.sum(total * total, 0, keepdims=True)
        if self.other:
            self.arrived(15, 16)
            other = pl.ds(self.most, self.other)
            every = pl.ds(0, self.other)
            total = (
                b.plane[three, 0, :, every].astype(F32)
                + b.other_y[three, :, every].astype(F32)
                + b.other_x[three, :, every].astype(F32)
            )
            b.total[two, :, other] = total
            b.squares[0:1, other] += jnp.sum(total * total, 0, keepdims=True)
        if not by_rows:
            self.start(17)
        start_all(self.own(by_rows))
        self.by_place(lambda: self.sent(6), lambda: self.sent(5))
        self.sent(7, 8)
        if self.other:
            self.sent(15, 16)

    def stage6(self, by_rows):
        if not by_rows:
            self.copy(17).wait()
        wait_all(self.own(by_rows))


POINTS = 4
STAGE_ORDER = (1, 0, 2, 3, 4, 6, 5)


def backward_kernel(plan, names, *refs):
    r = SimpleNamespace(**dict(zip(names, refs)))
    cube = plan.cube
    images = r.images.shape[0]
    loads = [
        (r.keep_z, r.vm_z),
        (r.shrink_whole, r.shrink_w),
        (r.keep_slope, r.vm_slope),
        (r.expand_whole, r.expand_w),
        (r.keep_m, r.vm_m),
        (r.keep_h1, r.vm_h1),
        (r.keep_o, r.vm_o),
        (r.keep_t, r.vm_t),
        (r.keep_p, r.vm_p),
        (r.keep_a, r.vm_a),
        (r.keep_h, r.vm_h),
        (r.joined_whole, r.expand_w),
    ]
    z_, shrink_, slope_, expand_, m_, h1_, o_, t_, p_, a_, h_, joined_ = range(12)

    def fetch(which, layer):
        src, dst = loads[which]
        return pltpu.make_async_copy(src.at[layer], dst, r.loads.at[which])

    def start(layer, *which):
        for k in which:
            fetch(k, layer).start()

    def wait(layer, *which):
        for k in which:
            fetch(k, layer).wait()

    loaded = [
        load(r.g_in, r.g, r.loads.at[joined_ + 1]),
        load(r.keys_in.at[0], r.unit.at[0, :, :, :, pl.ds(0, KEYS)], r.loads.at[joined_ + 2]),
        load(r.keys_in.at[1], r.unit.at[SEND, :, :, :, pl.ds(0, KEYS)], r.loads.at[joined_ + 3]),
    ]
    start(TOP - 1, z_)
    if cube:
        cube_barrier(plan)
        r.squares[...] = jnp.zeros_like(r.squares)
        top_rows = SmallGather(plan, r.rows_block, r.top_rows, r.rows_send, r.rows_recv)
    r.vectors[...] = jnp.zeros_like(r.vectors)
    r.vectors[FINAL : FINAL + 2] = r.tail_in[1:3]
    r.vectors[FINAL - 4 : FINAL] = r.tail_in[3:7]

    def run(unit, stage, by_rows, width=WIDTH):
        unit = Reduce(plan, r, unit, width)
        (
            unit.stage0,
            unit.stage1,
            unit.stage2,
            unit.stage3,
            unit.stage4,
            lambda: unit.stage5(by_rows),
            lambda: unit.stage6(by_rows),
        )[stage]()

    def point(it, at):
        if not cube:
            unit = 4 * it - 3 + at
            copies = [
                pltpu.make_async_copy(
                    r.unit.at[(unit % 4, SEND)[i]], r.full.at[unit, i], r.loads.at[joined_ + 1 + i]
                )
                for i in range(2)
            ]
            start_all(copies)
            wait_all(copies)
            return
        for stage in STAGE_ORDER:
            kind = (at - stage) % POINTS
            past = (kind + stage) // POINTS
            unit = 4 * (it - past) - 3 + kind
            go = functools.partial(run, unit, stage, kind == SHRINK, WIDTHS[kind])
            if past:
                pl.when(it > past)(go)
            else:
                go()
            if past and kind == TRIPLE:
                pl.when(it == past)(functools.partial(run, unit, stage, False, KEYS))

    def drain():
        for at in range(6):
            for stage in STAGE_ORDER:
                unit = UNITS + at - stage
                if UNITS - 2 * POINTS <= unit < UNITS:
                    kind = (unit - 1) % POINTS
                    run(jnp.int32(unit), stage, kind == SHRINK, WIDTHS[kind])
                if unit == UNITS:
                    run(jnp.int32(UNITS), stage, False, TAIL)

    def sent(unit, width=WIDTH):
        if cube:
            Reduce(plan, r, unit - 1, width).copy(0).wait_send()

    low_lane = lax.broadcasted_iota(jnp.int32, (PAD, 128), 1) < HEAD_DIM
    scale = HEAD_DIM**-0.5

    wait_all(loaded)
    start(TOP - 1, shrink_, slope_, expand_, m_, h1_, o_, t_, p_, a_, h_)
    pixels = load(r.images_in, r.images, r.loads.at[joined_ + 4])
    if cube:
        run(jnp.int32(0), 0, False, KEYS)
        top_rows.stage0()
    else:
        copies = [
            pltpu.make_async_copy(r.unit.at[(0, SEND)[i]], r.full.at[0, i], r.loads.at[joined_ + 1 + i])
            for i in range(2)
        ]
        start_all(copies)
        wait_all(copies)

    @pl.loop(1, LAYERS)
    def _(it):
        layer = TOP - it
        below = it < TOP
        unit_s = 4 * it - 3
        base = S + 2 + 4 * layer
        r.gr[...] = r.g[...].astype(BF)
        wait(layer, z_)
        slot = unit_s % 4
        pl.when(it == 1)(lambda: sent(unit_s, KEYS))
        pl.when(it > 1)(lambda: sent(unit_s, WIDTHS[TRIPLE]))

        @pl.loop(0, 8, unroll=2)
        def _(j):
            cols = pl.ds(pl.multiple_of(j * (D // 2), 128), D // 2)
            store_rows(plan, r.unit, slot, j, dot(r.vm_z[:, cols], r.gr[...], TN))

        point(it, 0)
        if cube:
            pl.when(it == 1)(top_rows.stage1)
        wait(layer, shrink_, slope_, expand_, m_, h1_)
        pl.when(below)(lambda: start(layer - 1, z_))
        slot_e = (unit_s + 1) % 4
        r.g1[...] = jnp.zeros_like(r.g1)
        sent(unit_s + 1)

        @pl.loop(0, 4)
        def _(j):
            cols = pl.ds(pl.multiple_of(j * D, 128), D)
            dz = dot(r.gr[...], r.shrink_w[j].reshape(D, D), NT)
            du = (dz * r.vm_slope[:, cols].astype(F32)).astype(BF)
            r.vm_slope[:, cols] = du
            store_cols(plan, r.unit, slot_e, j, D, dot(r.vm_m[...], du, TN))

        pl.when(below)(lambda: start(layer - 1, shrink_, m_))
        point(it, 1)
        if cube:
            pl.when(it == 1)(top_rows.stage2)

        @pl.loop(0, 4, unroll=2)
        def _(j):
            cols = pl.ds(pl.multiple_of(j * D, 128), D)
            r.g1[...] += dot(r.vm_slope[:, cols], weight(r.expand_w, j * D, D), NT)

        start(layer, joined_)
        pl.when(below)(lambda: start(layer - 1, slope_))
        d_h1, d_gain, d_shift = normalize_back(r.vm_h1[...], row(r.params, base + 2), r.g1[...])
        r.g1[...] = r.g[...] + d_h1
        r.vectors[pl.ds(base + 2, 1)] = d_gain
        r.vectors[pl.ds(base + 3, 1)] = d_shift
        pl.when(below)(lambda: start(layer - 1, h1_))

        r.gr[...] = r.g1[...].astype(BF)
        slot_t = (unit_s + TRIPLE) % 4
        wait(layer, o_)
        sent(unit_s + 2)
        for part in range(2):
            half = D // 2
            value = dot(r.vm_o[...], r.gr[:, part * half : part * half + half], TN)
            store_cols(plan, r.unit, (unit_s + OUTPUT) % 4, part, half, value, half)
        wait(layer, joined_)
        r.do[...] = dot(r.gr[...], weight(r.expand_w, 3 * D, D), NT).astype(BF)
        wait(layer, t_, p_, a_, h_)

        def heads(step):
            image, pair = step // (HEADS // 2), step % (HEADS // 2)
            rows = pl.ds(pl.multiple_of(image * PAD, 16), PAD)
            lanes = [pl.ds(pl.multiple_of(pair * 128 + part * D, 128), 128) for part in range(3)]
            q, key, v = (r.vm_t[rows, lane] for lane in lanes)
            do = r.do[rows, lanes[0]]
            zero = jnp.zeros_like(v)
            dqs, dks, dvs = [], [], []
            for which in range(2):
                part = jnp.where(low_lane, v, zero) if which == 0 else jnp.where(low_lane, zero, v)
                p_low = r.vm_p[step * 2 + which]
                p = p_low.astype(F32)
                dvs.append(dot(p_low, do))
                dp = dot(part, do, NT)
                ds = (p * (dp - jnp.sum(p * dp, 0, keepdims=True))).astype(BF)
                dqs.append(dot(ds, key, TN))
                dks.append(dot(ds, q))
            r.dt[rows, lanes[0]] = (jnp.where(low_lane, dqs[0], dqs[1]) * scale).astype(BF)
            r.dt[rows, lanes[1]] = (jnp.where(low_lane, dks[0], dks[1]) * scale).astype(BF)
            r.dt[rows, lanes[2]] = jnp.where(low_lane, dvs[0], dvs[1]).astype(BF)

        half = images * (HEADS // 2) // 2
        pl.loop(0, half, unroll=2)(heads)
        point(it, 2)
        if cube:
            pl.when(it == 1)(top_rows.finish)
        pl.loop(half, 2 * half, unroll=2)(heads)
        pl.when(below)(lambda: start(layer - 1, o_, t_, p_))
        r.g[...] = jnp.zeros_like(r.g)

        sent(unit_s + TRIPLE, WIDTHS[OUTPUT])

        @pl.loop(0, 6, unroll=2)
        def _(j):
            cols = pl.ds(pl.multiple_of(j * (D // 2), 128), D // 2)
            value = dot(r.vm_a[...], r.dt[:, cols], TN)
            store_cols(plan, r.unit, slot_t, j, D // 2, value, WIDTHS[TRIPLE])

        point(it, 3)

        @pl.loop(0, 3)
        def _(j):
            cols = pl.ds(pl.multiple_of(j * D, 128), D)
            r.g[...] += dot(r.dt[:, cols], weight(r.expand_w, j * D, D), NT)

        d_h, d_gain, d_shift = normalize_back(r.vm_h[...], row(r.params, base), r.g[...])
        r.g[...] = r.g1[...] + d_h
        r.vectors[pl.ds(base, 1)] = d_gain
        r.vectors[pl.ds(base + 1, 1)] = d_shift
        pl.when(below)(lambda: start(layer - 1, a_, h_, expand_))

    pixels.wait()
    slot = UNITS % 4
    sent(jnp.int32(UNITS), WIDTHS[TRIPLE])
    for part in range(2):
        half = D // 2
        value = jnp.zeros((D, half), F32)
        for image in range(images):
            rows = r.g[image * PAD + 1 : image * PAD + S, part * half : (part + 1) * half]
            value = value + dot(r.images[image], rows.astype(BF), TN)
        store_cols(plan, r.unit, slot, part, half, value, half)
    pos = r.g[:PAD]
    for image in range(1, images):
        pos = pos + r.g[image * PAD : (image + 1) * PAD]
    r.vectors[:S] = pos[:S]
    r.vectors[S : S + 1] = pos[:1]
    r.vectors[S + 1 : S + 2] = jnp.sum(pos[1:S], 0, keepdims=True)
    if not cube:
        copies = [
            pltpu.make_async_copy(r.unit.at[(slot, SEND)[i]], r.full.at[UNITS, i], r.loads.at[i])
            for i in range(2)
        ]
        copies.append(pltpu.make_async_copy(r.vectors, r.vector_rows, r.loads.at[2]))
        start_all(copies)
        wait_all(copies)
        return
    store_vectors(plan, r.unit, slot, r.vectors[...])

    drain()
    r.tail_block[:BLOCK] = r.total[UNITS % 2, :, D // 2 : TAIL].astype(BF)
    line = lax.broadcasted_iota(jnp.int32, (16, 128), 0)
    terms = jnp.zeros((16, 128), F32)
    for k, rest in enumerate((jnp.full((16, 128), jnp.sum(r.squares[...]), F32), r.tail_in[0:1, 0:128])):
        for j in range(3):
            term = rest.astype(BF).astype(F32)
            rest = rest - term
            terms = jnp.where(line == 3 * k + j, term, terms)
    r.tail_block[BLOCK:] = terms.astype(BF)
    gather = SmallGather(plan, r.tail_block, r.vector_rows, r.tail_send, r.tail_recv)
    gather.stage0()
    gather.stage1()
    gather.stage2()
    run(jnp.int32(UNITS), 6, False, TAIL)
    Reduce(plan, r, jnp.int32(UNITS), TAIL).copy(0).wait_send()
    gather.finish()


def backward(plan, images, params, done):
    rows = images.shape[0] * PAD
    shapes = saved_shapes(rows)
    inputs = given_in(
        VMEM_SPEC,
        params=params,
        tail_in=done.tail,
        rows_block=done.rows_block,
    )
    block = rows_block(images.shape[0])
    inputs.update(
        given_in(
            ANY_SPEC,
            images_in=images,
            g_in=done.g,
            keys_in=done.keys_out,
            joined_whole=done.joined_whole,
            expand_whole=done.expand_whole,
            shrink_whole=done.shrink_whole,
        )
    )
    inputs.update({"keep_" + name: (getattr(done, "keep_" + name), ANY_SPEC) for name in SAVED})
    if plan.cube:
        outputs = dict(
            shrink_grad=((TOP, 2, HALF, WIDTH), F32, ANY_SPEC),
            expand_grad=((TOP, 2, HALF, WIDTH), F32, ANY_SPEC),
            output_grad=((TOP, 2, HALF, WIDTHS[OUTPUT]), F32, ANY_SPEC),
            triple_grad=((TOP, 2, HALF, WIDTHS[TRIPLE]), F32, ANY_SPEC),
            keys=((2, HALF, KEYS), F32, ANY_SPEC),
            patch=((2, HALF, D // 2), F32, ANY_SPEC),
            vector_rows=(CHIPS + (2, BLOCK + 16, 128), BF, ANY_SPEC),
            top_rows=(CHIPS + (2, block, 128), BF, ANY_SPEC),
        )
    else:
        outputs = dict(
            full=((UNITS + 1, 2, 4, 4, BLOCK, WIDTH), BF, ANY_SPEC),
            vector_rows=((VEC_ROWS, D), F32, ANY_SPEC),
        )
    scratch = {"vm_" + name: pltpu.VMEM(shape, kind) for name, (shape, kind) in shapes.items()}
    scratch.update(
        vmem(
            BF,
            expand_w=cols_shape(FF),
            shrink_w=ROWS_SHAPE,
            gr=(rows, D),
            do=(rows, D),
            dt=(rows, 3 * D),
            unit=(SEND + 1, 4, 4, BLOCK, WIDTH),
            images=images.shape,
        )
    )
    scratch.update(vmem(F32, g=(rows, D), g1=(rows, D), vectors=(VEC_ROWS, D)))
    scratch.update(dma(loads=(17,)))
    extra = {}
    if plan.cube:
        other = other_part(WIDTH)
        most = WIDTH - other
        scratch.update(
            vmem(
                BF,
                core=(4, 4, BLOCK, WIDTH),
                tail_block=(BLOCK + 16, 128),
                near=(3, 4, BLOCK, cut_of(most)),
                far=(3, 4, BLOCK, most - cut_of(most)),
                x=(3, 4, BLOCK, most),
                y=(3, 4, BLOCK, most),
                line=(3, 4, BLOCK, most),
                main_two=(3, 2, BLOCK, most),
                main_one=(4, 2, BLOCK, most),
                other_two=(3, 2, 4, BLOCK, other),
                other_one=(4, 2, 4, BLOCK, other),
                plane=(3, 4, BLOCK, other),
                other_near=(3, BLOCK, cut_of(other)),
                other_far=(3, BLOCK, other - cut_of(other)),
                other_x=(3, BLOCK, other),
                other_y=(3, BLOCK, other),
            )
        )
        scratch.update(
            vmem(F32, total=(2, BLOCK, WIDTH), squares=(8, WIDTH))
        )
        scratch.update(
            dma(send=(4, 20), recv=(4, 18), rows_send=(10,), rows_recv=(9,), tail_send=(10,), tail_recv=(9,))
        )
        scratch.update(credit=pltpu.SemaphoreType.REGULAR)
        extra = dict(collective_id=2, has_side_effects=True)
    return pallas(functools.partial(backward_kernel, plan), "backward", inputs, outputs, scratch, **extra)


PARAMS = ("patch", "triple", "output", "expand", "shrink", "vector", "head")
KINDS = ("w_", "m_", "s_")


def adam_update(master, moment, square, gradient, step_rate):
    moment_new = BETA_ONE * moment + (1.0 - BETA_ONE) * gradient
    square_new = BETA_TWO * square + (1.0 - BETA_TWO) * gradient * gradient
    moment_hat = moment_new * (1.0 / (1.0 - BETA_ONE**STEP_INDEX))
    square_hat = square_new * (1.0 / (1.0 - BETA_TWO**STEP_INDEX))
    master_new = master - step_rate * (
        moment_hat / (jnp.sqrt(square_hat) + ADAM_EPS) + DECAY * master
    )
    return (master_new, moment_new, square_new)


def class_matrices(ref, images, devices, stride):
    first, found = 0, []
    for columns in PIECES:
        count = columns // 128
        parts = [
            jnp.concatenate(
                [
                    ref[pl.ds(image * PER_IMAGE + first + j, devices, stride=stride), :]
                    for j in range(count)
                ],
                1,
            )
            for image in range(images)
        ]
        found.append(jnp.concatenate(parts, 0).astype(BF))
        first += count
    return found


def own_columns(value, first, count):
    at = lax.broadcasted_iota(jnp.int32, (value.shape[1], 128), 0)
    to = lax.broadcasted_iota(jnp.int32, (value.shape[1], 128), 1)
    chosen = jnp.where((at == to + first) & (to < count), 1.0, 0.0).astype(BF)
    return dot(value, chosen).astype(BF)


def update_kernel(plan, images, names, *refs):
    r = SimpleNamespace(**dict(zip(names, refs)))
    named = dict(zip(names, refs))
    groups = [
        [(named[kind + name], named["vm_" + kind + name], named["to_" + kind + name]) for kind in KINDS]
        for name in PARAMS
    ]
    patch, triple, output, expand, shrink, vector, head = range(7)

    def moves(group, back):
        return [
            pltpu.make_async_copy(*((buf, out) if back else (src, buf)), r.sems.at[3 * group + k])
            for k, (src, buf, out) in enumerate(groups[group])
        ]

    order = (head, shrink, expand, triple, output, patch, vector)
    start_all(moves(head, False))

    tile = jnp.sum(r.tails[:, BLOCK:, :].astype(F32), 0)
    square_sum = tile[0:1, 0:1] + tile[1:2, 0:1] + tile[2:3, 0:1]
    loss = tile[3:4] + tile[4:5] + tile[5:6]
    r.rows_f[...] = r.top_rows[...].astype(F32)
    stride = r.top_rows.shape[0] // plan.n
    found = class_matrices(r.rows_f, images, plan.n, stride)
    features, d_logits, z, g, m, du, o, g1, a, dq = found
    r.features[...] = features
    r.d_logits[...] = d_logits
    alike = (dot(features, features, NT) + 1.0) * dot(d_logits, d_logits, NT)
    for left, right in ((z, g), (m, du), (o, g1), (a, dq)):
        alike = alike + dot(left, left, NT) * dot(right, right, NT)
    norm = jnp.sqrt(square_sum + jnp.sum(alike))
    me = plan.me()

    def top_grad(left, right, rows):
        return dot(own_columns(left, me * rows, rows), right, TN)[:rows]

    clip = CLIP / jnp.maximum(norm, CLIP)
    for group in order[1:]:
        start_all(moves(group, False))
    line = lax.broadcasted_iota(jnp.int32, (8, 128), 0)
    r.scalars[...] = jnp.where(line == 0, norm, jnp.where(line == 1, loss, r.total[...]))

    def step(group, at, gradient, rate):
        bufs = [buf for _, buf, _ in groups[group]]
        new = adam_update(*[buf[at] for buf in bufs], gradient * clip, rate)
        for buf, value in zip(bufs, new):
            buf[at] = value

    def finish(group):
        start_all(moves(group, True))

    every = slice(None)
    wait_all(moves(head, False))

    @pl.loop(0, D // 128)
    def _(j):
        rows = pl.ds(pl.multiple_of(j * 128, 128), 128)
        gradient = dot(r.features[:, rows], r.d_logits[...], TN)
        step(head, (rows, every), gradient[:, :CLASSES], RATE_MATRIX)

    bias = jnp.sum(d_logits.astype(F32), 0, keepdims=True)[:, :CLASSES]
    step(head, (slice(D, D + 1), every), bias, RATE_MATRIX)
    r.bias_grad[...] = bias * clip
    finish(head)
    wait_all(moves(shrink, False))

    step(shrink, (TOP, every, every), top_grad(z, g, BLOCK_FF), RATE_MATRIX)

    @pl.loop(0, TOP)
    def _(layer):
        at = TOP - 1 - layer
        for k in range(4):
            gradient = r.shrink_grad[at, k % 2, :, pl.ds(k // 2 * D, D)]
            step(shrink, (layer, pl.ds(k * HALF, HALF), every), gradient, RATE_MATRIX)

    finish(shrink)
    wait_all(moves(expand, False))

    step(expand, (TOP, every, every), top_grad(m, du, HALF), RATE_MATRIX)

    @pl.loop(0, TOP)
    def _(layer):
        at = TOP - 1 - layer
        for k in range(2):
            step(expand, (layer, every, pl.ds(k * WIDTH, WIDTH)), r.expand_grad[at, k], RATE_MATRIX)

    finish(expand)
    wait_all(moves(triple, False))
    wait_all(moves(output, False))

    step(output, (TOP, every, every), top_grad(o, g1, HALF), RATE_OUTPUT)
    step(triple, (TOP, every, pl.ds(0, D)), top_grad(a, dq, HALF), RATE_MATRIX)
    for k in range(2):
        step(triple, (TOP, every, pl.ds((k + 1) * D, D)), r.keys[k], RATE_MATRIX)

    @pl.loop(0, TOP)
    def _(layer):
        at = TOP - 1 - layer
        for k in range(2):
            width = WIDTHS[TRIPLE]
            step(triple, (layer, every, pl.ds(k * width, width)), r.triple_grad[at, k], RATE_MATRIX)
            width = WIDTHS[OUTPUT]
            step(output, (layer, every, pl.ds(k * width, width)), r.output_grad[at, k], RATE_OUTPUT)

    finish(triple)
    finish(output)
    wait_all(moves(patch, False))
    for k in range(2):
        step(patch, (every, pl.ds(k * (D // 2), D // 2)), r.patch_grad[k], RATE_MATRIX)
    finish(patch)
    count = groups[vector][0][0].shape[0]
    for d in range(-(-count // 8)):
        block = r.tails[d].astype(F32)
        for j in range(6):
            r.vector_grad[8 * d : 8 * d + 8, 128 * j : 128 * j + 128] = block[8 * j : 8 * j + 8]
    wait_all(moves(vector, False))
    step(vector, (every, every), r.vector_grad[:count], RATE_VECTOR)
    finish(vector)
    for group in order:
        wait_all(moves(group, True))


def update(plan, images, states, got, done):
    inputs, outputs, scratch = {}, {}, {}
    for name, state in zip(PARAMS, states):
        for kind, value in zip(KINDS, state):
            inputs[kind + name] = (value, ANY_SPEC)
            outputs["to_" + kind + name] = (value.shape, F32, ANY_SPEC)
            scratch["vm_" + kind + name] = pltpu.VMEM(value.shape, F32)
    inputs.update(
        given_in(
            VMEM_SPEC,
            total=done.total,
            tails=got.vector_rows.reshape(plan.n, BLOCK + 16, 128),
            top_rows=got.top_rows.reshape(-1, 128),
            shrink_grad=got.shrink_grad,
            expand_grad=got.expand_grad,
            output_grad=got.output_grad,
            triple_grad=got.triple_grad,
            patch_grad=got.patch,
            keys=got.keys,
        )
    )
    outputs.update(scalars=((8, 128), F32, VMEM_SPEC), bias_grad=((1, CLASSES), F32, VMEM_SPEC))
    scratch.update(vmem(BF, features=(plan.n * images, D), d_logits=(plan.n * images, 1024)))
    scratch.update(vmem(F32, vector_grad=(VEC_ROWS, D), rows_f=(plan.n * rows_block(images), 128)))
    scratch.update(dma(sems=(3 * len(PARAMS),)))
    new = pallas(functools.partial(update_kernel, plan, images), "update", inputs, outputs, scratch)
    states = [[getattr(new, "to_" + kind + name) for kind in KINDS] for name in PARAMS]
    return new.scalars[0, 0], new.scalars[1, 0], new.scalars[2, 0], states, new.bias_grad[0]


AXES = ("wide", "grp")


def update_whole(plan, images, states, got, done):
    full = got.full.reshape(UNITS + 1, 2, 16, BLOCK, WIDTH)
    layers = full[1:UNITS].reshape(TOP, 4, 2, 16, BLOCK, WIDTH)[::-1]

    def scattered(whole):
        axis = whole.ndim - 2
        return lax.psum_scatter(whole, AXES, scatter_dimension=axis, tiled=True).astype(F32)

    def from_cols(part):
        joined = jnp.concatenate([part[..., 0, :, :, :], part[..., 1, :, :, :]], -1)
        return joined.reshape(part.shape[:-4] + (D, -1))

    shrink = layers[:, 0].reshape(TOP, 2, 16, BLOCK, 2, D).transpose(0, 2, 1, 4, 3, 5)
    output = scattered(from_cols(layers[:, OUTPUT, ..., : WIDTHS[OUTPUT]]))
    triple = scattered(from_cols(layers[:, TRIPLE, ..., : WIDTHS[TRIPLE]]))
    rows_all = lax.all_gather(done.rows_block, AXES, axis=0)[:, : PER_IMAGE * images]
    rows_all = rows_all.reshape(plan.n * images, PER_IMAGE * 128)
    ends = [sum(PIECES[: k + 1]) for k in range(len(PIECES))]
    features, d_logits, z, g, m, du, o, g1, a, dq = jnp.split(rows_all, ends[:-1], axis=1)
    d_logits = d_logits[:, :CLASSES]
    bias = jnp.sum(d_logits.astype(F32), 0)[None]

    def top_grad(left, right):
        whole = dot(left, right, TN)
        count = whole.shape[0] // plan.n
        return lax.dynamic_slice_in_dim(whole, plan.me() * count, count)

    def with_top(below, top):
        return jnp.concatenate([below, top[None]], 0)

    keys = scattered(from_cols(full[0, ..., :KEYS]))
    split = [
        scattered(from_cols(full[UNITS, ..., : D // 2])),
        with_top(triple, jnp.concatenate([top_grad(a, dq), keys], 1)),
        with_top(output, top_grad(o, g1)),
        with_top(scattered(from_cols(layers[:, 1])), top_grad(m, du)),
        with_top(scattered(shrink.reshape(TOP, FF, D)), top_grad(z, g)),
    ]
    same = [
        lax.psum(got.vector_rows[: states[5][0].shape[0]], AXES),
        jnp.concatenate([dot(features, d_logits, TN), bias], 0),
    ]
    squares = lax.psum(sum(jnp.sum(g * g) for g in split), AXES) + sum(jnp.sum(g * g) for g in same)
    norm = jnp.sqrt(squares)
    clip = CLIP / jnp.maximum(norm, CLIP)
    rates = [RATE_MATRIX] * 2 + [RATE_OUTPUT] + [RATE_MATRIX] * 2 + [RATE_VECTOR, RATE_MATRIX]
    states = [
        adam_update(*state, gradient * clip, rate)
        for state, gradient, rate in zip(states, split + same, rates)
    ]
    return norm, lax.psum(done.tail[0, 0], AXES), done.total[0, 0], states, bias[0] * clip


def per_device(plan, images, slot_mask, labels, *params):
    states = [params[3 * k : 3 * k + 3] for k in range(7)]
    patch, triple, output, expand, shrink, vector, head = (state[0] for state in states)
    count = images.shape[0]
    weights = slot_mask.astype(F32)
    args = dict(vectors=vector)
    scalars = dict(labels=labels, mask=slot_mask)
    if plan.cube:
        shards = dict(patch=patch, triple=triple, output=output, expand=expand, shrink=shrink)
        done = forward(plan, images, head, shards, args, scalars, None, None)
    else:

        def whole(shard, shape):
            axis = shard.ndim - 2
            gathered = lax.all_gather(shard.astype(BF), AXES, axis=axis, tiled=True)
            return gathered.reshape(shard.shape[:axis] + shape)

        gathered = [
            whole(patch, cols_shape(D)),
            whole(jnp.concatenate([triple, output], 2), cols_shape(FF)),
            whole(expand, cols_shape(FF)),
            whole(shrink, ROWS_SHAPE),
        ]
        total = jnp.full((8, 128), lax.psum(jnp.sum(weights), AXES), F32)
        done = forward(plan, images, head, None, args, scalars, gathered, total)
    got = backward(plan, images, vector, done)
    if plan.cube:
        norm, loss, total, states, bias_grad = update(plan, count, states, got, done)
    else:
        norm, loss, total, states, bias_grad = update_whole(plan, count, states, got, done)
    return (
        loss,
        total,
        norm,
        *(value for state in states for value in state),
        bias_grad,
    )


def solution(mesh):
    plan = Plan(mesh)
    rows = P(AXES, None)
    layers = P(None, AXES, None)
    in_specs = (P(AXES, None, None), P(AXES), P(AXES)) + (rows,) * 3 + (layers,) * 12 + (P(),) * 6
    out_specs = (P(),) * 3 + (rows,) * 3 + (layers,) * 12 + (P(),) * 7
    return jax.shard_map(
        functools.partial(per_device, plan),
        mesh=mesh,
        in_specs=in_specs,
        out_specs=out_specs,
        check_vma=False,
    )
```
